32 devices in a mesh: dp: 8 (over y, x, core), tensor: 4 (over z).
Axes of the slice: x: 2, y: 2, z: 4, core: 2. Of those that a mesh axis runs over, the one named last changes fastest.
Arguments:
- tokens: bfloat16 [128, 256, 768], P(None, 'dp'), may hold values from -6 to 6
- lengths: int32 [256], P('dp'), may hold values from 5 to 128, as said below
- partner: int32 [256], P('dp'), may hold values from 0 to 255, as said below
- w_qkv: bfloat16 [768, 2304], P(None, 'tensor'), may hold values from -0.21875 to 0.21875
- w_out: bfloat16 [768, 768], P('tensor'), may hold values from -0.625 to 0.625
- ln1_gain: float32 [768], replicated, may hold values from 0.25 to 1.75
- ln1_bias: float32 [768], replicated, may hold values from -4 to 4
- up_weight: bfloat16 [768, 3072], P(None, 'tensor'), may hold values from -0.21875 to 0.21875
- up_projection_bias: float32 [3072], P('tensor'), may hold values from -6 to 6
- down_weight: bfloat16 [3072, 768], P('tensor'), may hold values from -0.109375 to 0.109375
- ln2_gain: float32 [768], replicated, may hold values from 0.25 to 1.75
- ln2_bias: float32 [768], replicated, may hold values from -4 to 4
- cot_pooled: bfloat16 [256, 768], P('dp'), may hold values from -6 to 6
- cot_paired: bfloat16 [256, 768], P('dp'), may hold values from -6 to 6
Outputs:
- pooled: bfloat16 [256, 768], P('dp')
- paired: bfloat16 [256, 768], P('dp')
- input_grad: bfloat16 [128, 256, 768], P('tensor', 'dp')
- grad_w_qkv: float32 [768, 2304], P(None, 'tensor')
- grad_w_out: float32 [768, 768], P('tensor')
- grad_ln1_gain: float32 [768], replicated
- grad_ln1_bias: float32 [768], replicated
- grad_w_up: float32 [768, 3072], P(None, 'tensor')
- grad_b_up: float32 [3072], P('tensor')
- grad_w_down: float32 [3072, 768], P('tensor')
- grad_ln2_gain: float32 [768], replicated
- grad_ln2_bias: float32 [768], replicated
The draws below stay inside these ranges and needn't reach their ends.
Inputs may be any that keep to these rules, and one draw needn't show every extreme that they name: `lengths`: each device's block of 32 sentences holds one of length 128. Sentences come in pairs: partner[partner[s]] = s and partner[s] != s.
All inputs are finite; a program needn't handle non-finite values.
Results may differ from the reference program's by a relative error of at most 0.018.
Values may be sent and summed in bfloat16 or wider, within the bound.
No kernel may reach another device: no remote copies, remote signals or barrier semaphores. Data moves between devices by JAX's collectives and lax.ppermute only.
A program may use at most 256 MiB of HBM per device.

```python
import math
import jax
import jax.numpy as jnp
from jax import lax

D = 768
HEADS = 12
HD = 64
FF = 3072
LEN = 128
SENT_DEV = 32
SENTS = 256


def draw_lengths(key, part):
    key = jax.random.fold_in(key, 11)
    base_key, pick_key = jax.random.split(key)
    blocks = SENTS // SENT_DEV
    drawn = jax.random.randint(base_key, (blocks, SENT_DEV), 5, LEN + 1)
    chosen = jax.random.randint(pick_key, (blocks, 1), 0, SENT_DEV)
    slots = jnp.arange(SENT_DEV)[None, :]
    return jnp.where(slots == chosen, LEN, drawn).reshape(SENTS).astype(jnp.int32)


def draw_partner(key, part):
    key = jax.random.fold_in(key, 23)
    order = jax.random.permutation(key, SENTS).astype(jnp.int32)
    leading = order[0::2]
    trailing = order[1::2]
    mates = jnp.zeros((SENTS,), jnp.int32).at[leading].set(trailing).at[trailing].set(leading)
    return mates.astype(jnp.int32)


def block_scale(rng, extent, cuts, smallest, largest):
    level, own = 1.0, jax.random.fold_in(rng, 6)
    for dim, blocks in cuts:
        steps = jnp.exp(jax.random.uniform(jax.random.fold_in(own, dim), (blocks,), jnp.float32, smallest / len(cuts), largest / len(cuts)))
        level = level * jnp.repeat(steps, extent[dim] // blocks).reshape([-1 if axis == dim else 1 for axis in range(len(extent))])
    return level


def gaussian(key, dims, deviation, bound, cuts=(), held_as=jnp.bfloat16):
    values = jax.random.normal(key, dims, jnp.float32) * deviation
    if len(cuts) > 0:
        values = block_scale(key, dims, cuts, -0.22, 0.18) * values
    return jnp.clip(values, min=-bound, max=bound).astype(held_as)


def setup_inputs(seed: int = 0) -> dict:
    key_list = jax.random.split(jax.random.key(seed), 15)
    return {
        "tokens": gaussian(key_list[0], (LEN, SENTS, D), 1.0, 6.0, ((1, 8),)),
        "lengths": draw_lengths(jax.random.fold_in(key_list[14], 71), 0),
        "partner": draw_partner(jax.random.fold_in(key_list[14], 71), 0),
        "w_qkv": gaussian(key_list[3], (D, 3 * D), D ** -0.5, 0.21875, ((1, 4),)),
        "w_out": gaussian(key_list[4], (D, D), (D // 8) ** -0.5, 0.625, ((0, 4),)),
        "ln1_gain": jnp.clip(1.0 + 0.15 * jax.random.normal(key_list[5], (D,), jnp.float32), 0.25, 1.75),
        "ln1_bias": gaussian(key_list[6], (D,), 0.3, 4.0, (), jnp.float32),
        "up_weight": gaussian(key_list[7], (D, FF), D ** -0.5, 0.21875, ((1, 4),)),
        "up_projection_bias": gaussian(key_list[8], (FF,), 0.5, 6.0, ((0, 4),), jnp.float32),
        "down_weight": gaussian(key_list[9], (FF, D), FF ** -0.5, 0.109375, ((0, 4),)),
        "ln2_gain": jnp.clip(1.0 + 0.15 * jax.random.normal(key_list[10], (D,), jnp.float32), 0.25, 1.75),
        "ln2_bias": gaussian(key_list[11], (D,), 0.3, 4.0, (), jnp.float32),
        "cot_pooled": gaussian(key_list[12], (SENTS, D), 1.0, 6.0, ((0, 8),)),
        "cot_paired": gaussian(key_list[13], (SENTS, D), 1.0, 6.0, ((0, 8),)),
    }


@jax.custom_vjp
def low(v):
    return lax.optimization_barrier(v.astype(jnp.bfloat16)).astype(jnp.float32)

@jax.custom_vjp
def low_back(v):
    return v

def low_keep(v):
    return (low(v), None)

def low_pass(kept, grad):
    return (grad,)

def back_keep(v):
    return (v, None)

def back_low(kept, grad):
    return (low(grad),)
low.defvjp(low_keep, low_pass)
low_back.defvjp(back_keep, back_low)
HIGHEST = lax.Precision.HIGHEST
EPSILON = 1e-06

def norm_rows(values, gain, bias):
    center = values - lax.optimization_barrier(jnp.mean(values, axis=-1, keepdims=True))
    spread = lax.optimization_barrier(jnp.mean(center * center, axis=-1, keepdims=True))
    return center * lax.rsqrt(spread + EPSILON) * gain + bias

def sentence_group(inputs, counts, w_qkv, w_out, gain_one, bias_one, up_weight, up_projection_bias, down_weight, gain_two, bias_two):
    groups = inputs.shape[0]
    flat = inputs.reshape(groups * LEN, D)
    projected = low_back(low(jnp.dot(flat, w_qkv, precision=HIGHEST)))
    projected = projected.reshape(groups, LEN, HEADS, 3, HD)
    queries = projected[:, :, :, 0]
    keys_all = projected[:, :, :, 1]
    values = projected[:, :, :, 2]
    score_scale = 1.0 / math.sqrt(HD)
    scores = low_back(jnp.einsum('gqhe,gkhe->ghqk', queries, keys_all, precision=HIGHEST) * score_scale)
    valid_keys = jnp.arange(LEN)[None, :] < counts[:, None]
    scores = jnp.where(valid_keys[:, None, None, :], scores, -1000000000.0)
    probs_low = low(jax.nn.softmax(scores, axis=-1))
    context = low_back(low(jnp.einsum('ghqk,gkhe->gqhe', probs_low, values, precision=HIGHEST)))
    attended = low_back(jnp.dot(context.reshape(groups * LEN, D), w_out, precision=HIGHEST))
    normed_one = norm_rows(flat + attended, gain_one, bias_one)
    hidden_pre = low_back(jnp.dot(low(normed_one), up_weight, precision=HIGHEST) + up_projection_bias)
    active = low(jax.nn.gelu(hidden_pre, approximate=False))
    branch = low_back(jnp.dot(active, down_weight, precision=HIGHEST))
    normed_two = norm_rows(normed_one + branch, gain_two, bias_two).reshape(groups, LEN, D)
    row_mask = valid_keys.astype(normed_two.dtype)
    return lax.optimization_barrier(jnp.sum(normed_two * row_mask[:, :, None], axis=1)) / counts[:, None].astype(normed_two.dtype)

def reference(tokens, lengths, partner, w_qkv, w_out, ln1_gain, ln1_bias, up_weight, up_projection_bias, down_weight, ln2_gain, ln2_bias, cot_pooled, cot_paired):
    group_count = SENTS // SENT_DEV
    step_group = jax.checkpoint(sentence_group)

    def forward(inputs, *weights):
        stacked = inputs.reshape(group_count, SENT_DEV, LEN, D)
        grouped = lengths.reshape(group_count, SENT_DEV)

        def one_group(pieces):
            return step_group(pieces[0], pieces[1], *weights)
        pooled_full = lax.map(one_group, (stacked, grouped)).reshape(SENTS, D)
        kept = low(low_back(pooled_full))
        return (kept, kept * kept[partner])
    inputs = jnp.transpose(tokens.astype(jnp.float32), (1, 0, 2))
    floats = [item.astype(jnp.float32) for item in (w_qkv, w_out, ln1_gain, ln1_bias, up_weight, up_projection_bias, down_weight, ln2_gain, ln2_bias)]
    outputs, pull = jax.vjp(forward, inputs, *floats)
    grads = pull((cot_pooled.astype(jnp.float32), cot_paired.astype(jnp.float32)))
    input_grad = jnp.transpose(grads[0], (1, 0, 2)).astype(jnp.bfloat16)
    return (outputs[0].astype(jnp.bfloat16), outputs[1].astype(jnp.bfloat16), input_grad, grads[1], grads[2], grads[3], grads[4], grads[5], grads[6], grads[7], grads[8], grads[9])
```

```python
import jax
import jax.numpy as jnp
from jax import lax
from jax.sharding import PartitionSpec as P

HD = 64
EPSILON = 1e-06
LOW = jnp.bfloat16
F32 = jnp.float32
SQRT_HALF = 0.7071067811865476
INV_SQRT_2PI = 0.3989422804014327


def dot(spec, a, b):
    return jnp.einsum(spec, a, b, preferred_element_type=F32)


def normalize(values):
    center = values - jnp.mean(values, axis=-1, keepdims=True)
    spread = jnp.mean(center * center, axis=-1, keepdims=True)
    root = lax.rsqrt(spread + EPSILON)
    return center * root, root


def normalize_back(z, root, dz):
    return root * (dz - jnp.mean(dz, -1, keepdims=True) - z * jnp.mean(dz * z, -1, keepdims=True))


def halve(values, bit):
    dp_count = lax.axis_size("dp")
    other = [(i, i ^ bit) for i in range(dp_count)]
    side = (lax.axis_index("dp") // bit) % 2
    mine = lax.dynamic_index_in_dim(values, side, 0, False)
    theirs = lax.dynamic_index_in_dim(values, 1 - side, 0, False)
    got = lax.ppermute(theirs, "dp", other)
    return (mine.astype(F32) + got.astype(F32)).astype(LOW)


def reduce_plane(grad):
    dp_count = lax.axis_size("dp")
    bits = []
    bit = 1
    while bit < dp_count:
        bits.append(bit)
        bit *= 2
    rows, columns = grad.shape
    g = grad.reshape((2,) * len(bits) + (rows // dp_count, columns))
    g = halve(jnp.moveaxis(g, len(bits) - 1, 0), 1)
    rest = bits[1:]
    parts = []
    cut = columns // 2
    for part, order in ((g[..., :cut], rest), (g[..., cut:], rest[::-1])):
        left = list(rest[::-1])
        for b in order:
            part = halve(jnp.moveaxis(part, left.index(b), 0), b)
            left.remove(b)
        parts.append(part)
    return jnp.concatenate(parts, axis=-1)


def reduce_line(grad):
    n = lax.axis_size("tensor")
    me = lax.axis_index("tensor")
    total = lax.dynamic_index_in_dim(grad, me, 1, False).astype(F32)
    for k in range(1, n):
        piece = lax.dynamic_index_in_dim(grad, (me + k) % n, 1, False)
        got = lax.ppermute(piece, "tensor", [(i, (i + k) % n) for i in range(n)])
        total = total + got.astype(F32)
    return total.astype(LOW)


def reduce_weight(grad):
    rows, n, columns = grad.shape
    g = reduce_plane(grad.reshape(rows, n * columns).astype(LOW))
    g = reduce_line(g.reshape(g.shape[0], n, columns))
    return lax.all_gather(g, "dp", axis=0, tiled=True)


def shards(
    tokens,
    lengths,
    partner,
    w_qkv,
    w_out,
    ln1_gain,
    ln1_bias,
    up_weight,
    up_projection_bias,
    down_weight,
    ln2_gain,
    ln2_bias,
    cot_pooled,
    cot_paired,
):
    dp_count = lax.axis_size("dp")
    t_count = lax.axis_size("tensor")
    dp_me = lax.axis_index("dp")
    t_me = lax.axis_index("tensor")
    length, sentences, width = tokens.shape
    mine = sentences // t_count
    rows = mine * length
    slab = width // dp_count
    scale = HD ** (-0.5)
    head_cols = w_qkv.shape[1]
    heads = head_cols // (3 * HD)
    units = up_weight.shape[1]
    ctx = w_out.shape[0]

    def cut(weight):
        return lax.dynamic_slice_in_dim(weight, dp_me * slab, slab, 0)

    def cut_columns(weight):
        return lax.dynamic_slice_in_dim(weight, dp_me * slab, slab, 1).T

    attn_piece = jnp.concatenate([cut(w_qkv), cut_columns(w_out)], axis=1)
    ffn_piece = jnp.concatenate([cut(up_weight), cut_columns(down_weight)], axis=1)
    attn_all = lax.all_gather(attn_piece, ("tensor", "dp"), axis=0, tiled=True)
    attn_all = attn_all.reshape(t_count, width, head_cols + ctx)
    ffn_all = lax.all_gather(ffn_piece, ("tensor", "dp"), axis=0, tiled=True)
    ffn_all = ffn_all.reshape(t_count, width, 2 * units)
    bias_all = lax.all_gather(up_projection_bias, "tensor", axis=0, tiled=False)

    x = lax.dynamic_slice_in_dim(tokens, t_me * mine, mine, 1).transpose(1, 0, 2)
    counts = lax.dynamic_slice_in_dim(lengths, t_me * mine, mine, 0)
    valid = jnp.arange(length)[None, :] < counts[:, None]
    row_mask = valid.astype(F32)
    flat = x.reshape(rows, width)

    wq = attn_all[:, :, :head_cols]
    wo = attn_all[:, :, head_cols:]
    projected = dot("rd,tde->rte", flat, wq).astype(LOW)
    projected = projected.reshape(mine, length, t_count * heads, 3, HD)
    queries, keys_all, values = projected[:, :, :, 0], projected[:, :, :, 1], projected[:, :, :, 2]
    scores = dot("sqhe,skhe->shqk", queries, keys_all) * scale
    scores = jnp.where(valid[:, None, None, :], scores, -1000000000.0)
    probs = jnp.exp(scores - jnp.max(scores, -1, keepdims=True))
    probs = probs / jnp.sum(probs, -1, keepdims=True)
    probs_low = probs.astype(LOW)
    context = dot("shqk,skhe->sqhe", probs_low, values).astype(LOW).reshape(rows, t_count, ctx)
    attended = dot("rte,tde->rd", context, wo)
    z1, root1 = normalize(flat.astype(F32) + attended)
    first = z1 * ln1_gain + ln1_bias
    first_low = first.astype(LOW)
    up = ffn_all[:, :, :units]
    down = ffn_all[:, :, units:]
    pre = dot("rd,tdu->rtu", first_low, up) + bias_all[None]
    cdf = 0.5 * (1.0 + lax.erf(pre * SQRT_HALF))
    active = (pre * cdf).astype(LOW)
    slope = cdf + pre * (jnp.exp(-0.5 * pre * pre) * INV_SQRT_2PI)
    branch = dot("rtu,tdu->rd", active, down)
    z2, root2 = normalize(first + branch)
    second = (z2 * ln2_gain + ln2_bias).reshape(mine, length, width)
    pooled = (jnp.sum(second * row_mask[:, :, None], axis=1) / counts[:, None].astype(F32)).astype(LOW)

    returned = lax.all_gather(pooled, "tensor", axis=0, tiled=True)
    everyone = lax.all_gather(jnp.concatenate([returned, cot_paired], 1), "dp", axis=0, tiled=True)
    partner_rows = everyone[partner]
    partner_pooled = partner_rows[:, :width].astype(F32)
    paired = (returned.astype(F32) * partner_pooled).astype(LOW)
    pool_grad = cot_pooled.astype(F32) + partner_pooled * (
        cot_paired.astype(F32) + partner_rows[:, width:].astype(F32)
    )
    pool_grad = lax.dynamic_slice_in_dim(pool_grad.astype(LOW).astype(F32), t_me * mine, mine, 0)

    second_grad = row_mask[:, :, None] * (pool_grad / counts[:, None].astype(F32))[:, None]
    second_grad = second_grad.reshape(rows, width)
    gain_two = jnp.sum(second_grad * z2, 0)
    bias_two = jnp.sum(second_grad, 0)
    sum_grad = normalize_back(z2, root2, second_grad * ln2_gain)
    branch_low = sum_grad.astype(LOW)
    down_grad = dot("rd,rtu->dtu", branch_low, active)
    hidden = (slope * dot("rd,tdu->rtu", branch_low, down)).astype(LOW)
    up_bias = jnp.sum(hidden.astype(F32), 0)
    up_grad = dot("rd,rtu->dtu", first_low, hidden)
    ffn_grad = reduce_weight(jnp.concatenate([up_grad, down_grad], 2))
    first_grad = sum_grad + dot("rtu,tdu->rd", hidden, up)
    gain_one = jnp.sum(first_grad * z1, 0)
    bias_one = jnp.sum(first_grad, 0)
    attn_grad = normalize_back(z1, root1, first_grad * ln1_gain)
    attn_low = attn_grad.astype(LOW)
    out_grad = dot("rd,rte->dte", attn_low, context)
    context_grad = dot("rd,tde->rte", attn_low, wo).astype(LOW).reshape(mine, length, t_count * heads, HD)
    value_grad = dot("shqk,sqhe->skhe", probs_low, context_grad)
    prob_grad = dot("sqhe,skhe->shqk", context_grad, values)
    score_grad = (probs * (prob_grad - jnp.sum(probs * prob_grad, -1, keepdims=True))).astype(LOW)
    query_grad = dot("shqk,skhe->sqhe", score_grad, keys_all) * scale
    key_grad = dot("shqk,sqhe->skhe", score_grad, queries) * scale
    project_grad = jnp.stack((query_grad, key_grad, value_grad), axis=3).astype(LOW)
    project_grad = project_grad.reshape(rows, t_count, head_cols)
    qkv_grad = dot("rd,rte->dte", flat, project_grad)
    attn_w_grad = reduce_weight(jnp.concatenate([qkv_grad, out_grad], 2))
    input_grad = (attn_grad + dot("rte,tde->rd", project_grad, wq)).astype(LOW)
    input_grad = input_grad.reshape(mine, length, width)
    share = length // t_count
    blocks = [lax.dynamic_slice_in_dim(input_grad, t_me * share, share, 1)]
    for k in range(1, t_count):
        piece = lax.dynamic_slice_in_dim(input_grad, (t_me + k) % t_count * share, share, 1)
        blocks.append(
            lax.ppermute(piece, "tensor", [(i, (i + k) % t_count) for i in range(t_count)])
        )
    home = jnp.zeros((t_count, mine, share, width), LOW)
    for k in range(t_count):
        home = lax.dynamic_update_index_in_dim(home, blocks[k], (t_me - k) % t_count, 0)
    home = home.reshape(sentences, share, width).transpose(1, 0, 2)

    up_bias_sum, norm_sums = lax.psum((up_bias, (gain_one, bias_one, gain_two, bias_two)), ("dp", "tensor"))
    up_bias_sum = lax.dynamic_index_in_dim(up_bias_sum, t_me, 0, False)
    return (
        returned,
        paired,
        home,
        attn_w_grad[:, :head_cols].astype(F32),
        attn_w_grad[:, head_cols:].astype(F32).T,
        norm_sums[0],
        norm_sums[1],
        ffn_grad[:, :units].astype(F32),
        up_bias_sum,
        ffn_grad[:, units:].astype(F32).T,
        norm_sums[2],
        norm_sums[3],
    )


def solution(mesh):
    placed = (
        P(None, "dp", None),
        P("dp"),
        P("dp"),
        P(None, "tensor"),
        P("tensor", None),
        P(),
        P(),
        P(None, "tensor"),
        P("tensor"),
        P("tensor", None),
        P(),
        P(),
        P("dp", None),
        P("dp", None),
    )
    return jax.shard_map(
        shards,
        mesh=mesh,
        in_specs=placed,
        out_specs=(
            P("dp", None),
            P("dp", None),
            P("tensor", "dp", None),
            P(None, "tensor"),
            P("tensor", None),
            P(),
            P(),
            P(None, "tensor"),
            P("tensor"),
            P("tensor", None),
            P(),
            P(),
        ),
        check_vma=False,
    )
```

```python
import functools

import jax
import jax.numpy as jnp
from jax import lax
from jax.experimental import pallas as pl
from jax.experimental.pallas import tpu as pltpu
from jax.sharding import PartitionSpec as P

HD = 64
EPSILON = 1e-06
LOW = jnp.bfloat16
F32 = jnp.float32
INV_SQRT_2PI = 0.3989422804014327
SQRT_HALF = 0.7071067811865476
TILE = 256
MASKED = -1000000000.0
VMEM_BYTES = 60 * 2**20
NN = (((1,), (0,)), ((), ()))
NT = (((1,), (1,)), ((), ()))
PAIR = 2 * HD
LENS, TILES, CORE, MASKS = 16, 32, 33, 34


def mm(a, b, dims=NN):
    return lax.dot_general(a, b, dims, preferred_element_type=F32)


def rows_of(table, s):
    return pl.ds(pl.multiple_of(table[s], 16), 128)


def tile_at(i):
    return pl.ds(pl.multiple_of(i * TILE, TILE), TILE)


def normalize(values):
    center = values - jnp.mean(values, axis=-1, keepdims=True)
    spread = jnp.mean(center * center, axis=-1, keepdims=True)
    root = lax.rsqrt(spread + EPSILON)
    return center * root, root


def normalize_back(z, root, dz):
    return root * (
        dz - jnp.mean(dz, -1, keepdims=True) - z * jnp.mean(dz * z, -1, keepdims=True)
    )


def split_heads(pair):
    first = lax.broadcasted_iota(jnp.int32, pair.shape, 1) < HD
    zero = jnp.zeros_like(pair)
    return jnp.concatenate([jnp.where(first, pair, zero), jnp.where(first, zero, pair)], axis=0)


def join_heads(split):
    n = split.shape[0] // 2
    first = lax.broadcasted_iota(jnp.int32, (n, PAIR), 1) < HD
    return jnp.where(first, split[:n], split[n:])


def softmax_pair(queries, keys_split, count):
    length = queries.shape[0]
    scores = mm(queries, keys_split, NT) * (HD**-0.5)
    valid = lax.broadcasted_iota(jnp.int32, (length, length), 1) < count
    out = []
    for h in range(2):
        part = jnp.where(valid, scores[:, h * length : (h + 1) * length], MASKED)
        part = jnp.exp(part - jnp.max(part, axis=-1, keepdims=True))
        out.append(part * (1.0 / jnp.sum(part, axis=-1, keepdims=True)))
    return out


def attention_forward(table, x, w, proj, ctx, z1, root1, wide, packed):
    sents, length, width = x.shape
    count, _, block = w.shape
    part = block // 4
    for k in range(count):
        for p in range(4):
            wide[:, p * width + k * part : p * width + (k + 1) * part] = w[
                k, :, p * part : (p + 1) * part
            ]
    packed[...] = jnp.zeros_like(packed)
    ctx[...] = jnp.zeros_like(ctx)

    def place(s, _):
        packed[rows_of(table, s), :] = x[s]
        return 0

    lax.fori_loop(0, sents, place, 0)
    tiles = table[TILES]

    def project(i, _):
        rows = tile_at(i)
        source = packed[rows, :]
        for p in range(3):
            cols = slice(p * width, (p + 1) * width)
            proj[rows, cols] = mm(source, wide[:, cols]).astype(LOW)
        return 0

    lax.fori_loop(0, tiles, project, 0)
    proj[pl.ds(pl.multiple_of(tiles * TILE, TILE), length), :] = jnp.zeros(
        (length, 3 * width), LOW
    )

    def attend(s, _):
        rows = rows_of(table, s)
        n = table[LENS + s]
        for p in range(width // PAIR):
            at = p * PAIR
            queries = proj[rows, at : at + PAIR]
            keys = split_heads(proj[rows, width + at : width + at + PAIR])
            values = split_heads(proj[rows, 2 * width + at : 2 * width + at + PAIR])
            probs = jnp.concatenate(softmax_pair(queries, keys, n), axis=1).astype(LOW)
            ctx[rows, at : at + PAIR] = mm(probs, values).astype(LOW)
        return 0

    lax.fori_loop(0, sents, attend, 0)

    def finish(i, _):
        rows = tile_at(i)
        attended = mm(ctx[rows, :], wide[:, 3 * width :], NT)
        z, root = normalize(packed[rows, :].astype(F32) + attended)
        z1[rows, :] = z
        root1[rows, :] = jnp.broadcast_to(root, (TILE, 128))
        return 0

    lax.fori_loop(0, tiles, finish, 0)


def gelu_parts(pre):
    a = jnp.abs(pre) * SQRT_HALF
    t = pl.reciprocal(1.0 + 0.3275911 * a)
    poly = 1.061405429
    for c in (-1.453152027, 1.421413741, -0.284496736, 0.254829592):
        poly = poly * t + c
    e = jnp.exp(-a * a)
    tail = 0.5 * poly * t * e
    cdf = jnp.where(pre >= 0.0, 1.0 - tail, tail)
    return pre * cdf, cdf + pre * (e * INV_SQRT_2PI)


def ffn_forward(
    table, z1, gain1, bias1, up, down, bias, gain2, bias2, active, slope, z2, root2, pooled, first, total
):
    k = pl.program_id(0)
    tiles = table[TILES]

    @pl.when(k == 0)
    def _():
        def start(i, _):
            rows = tile_at(i)
            value = z1[rows, :] * gain1[...] + bias1[...]
            first[rows, :] = value.astype(LOW)
            total[rows, :] = value
            return 0

        lax.fori_loop(0, tiles, start, 0)

    def work(i, _):
        rows = tile_at(i)
        pre = mm(first[rows, :], up[0]) + bias[0]
        act, slp = gelu_parts(pre)
        act = act.astype(LOW)
        active[0, rows, :] = act
        slope[0, rows, :] = slp.astype(LOW)
        total[rows, :] += mm(act, down[0], NT)
        return 0

    lax.fori_loop(0, tiles, work, 0)

    @pl.when(k == pl.num_programs(0) - 1)
    def _():
        z2[pl.ds(pl.multiple_of(tiles * TILE, TILE), 128), :] = jnp.zeros((128, z2.shape[1]), F32)

        def finish(i, _):
            rows = tile_at(i)
            z, root = normalize(total[rows, :])
            z2[rows, :] = z
            root2[rows, :] = jnp.broadcast_to(root, (TILE, 128))
            return 0

        lax.fori_loop(0, tiles, finish, 0)
        for s in range(pooled.shape[0]):
            n = table[LENS + s]
            valid = lax.broadcasted_iota(jnp.int32, (128, z2.shape[1]), 0) < n
            rows = jnp.where(valid, z2[rows_of(table, s), :], 0.0)
            mean = jnp.sum(rows, axis=0, keepdims=True) / n.astype(F32)
            pooled[s : s + 1, :] = mean * gain2[...] + bias2[...]


def send_rows(table, acc, source, mine, other, columns):
    chips, slab = mine.shape[0], mine.shape[1]
    core = table[CORE]
    for m in range(chips):
        base = (table[MASKS + m] * 2) * slab
        here = pl.multiple_of(base + core * slab, 8)
        there = pl.multiple_of(base + (1 - core) * slab, 8)
        mine[m, :, columns] = acc[pl.ds(here, slab), source].astype(LOW)
        other[m, :, columns] = acc[pl.ds(there, slab), source].astype(LOW)


def ffn_backward(
    table, pool, z2, root2, gain2, z1, root1, gain1, bias1, up, down, active, slope,
    mine, other, attn_grad, sums, bias_sum,
    first_t, branch, branch_t, total, hidden, acc,
):
    k = pl.program_id(0)
    tiles = table[TILES]
    width = z2.shape[1]

    @pl.when(k == 0)
    def _():
        total[...] = jnp.zeros_like(total)
        for s in range(pool.shape[0]):
            n = table[LENS + s]
            valid = lax.broadcasted_iota(jnp.int32, (128, width), 0) < n
            row = pool[s : s + 1, :] / n.astype(F32)
            total[rows_of(table, s), :] = jnp.where(valid, row, 0.0)
        sums[...] = jnp.zeros_like(sums)

        def start(i, _):
            rows = tile_at(i)
            grad = total[rows, :]
            z = z2[rows, :]
            sums[0:1, :] += jnp.sum(grad * z, axis=0, keepdims=True)
            sums[1:2, :] += jnp.sum(grad, axis=0, keepdims=True)
            back = normalize_back(z, root2[rows, 0:1], grad * gain2[...])
            low = back.astype(LOW)
            total[rows, :] = back
            branch[rows, :] = low
            branch_t[:, rows] = low.T
            first = (z1[rows, :] * gain1[...] + bias1[...]).astype(LOW)
            first_t[:, rows] = first.T
            return 0

        lax.fori_loop(0, tiles, start, 0)

    bias_sum[...] = jnp.zeros_like(bias_sum)

    def work(i, _):
        rows = tile_at(i)
        grad = mm(branch[rows, :], down[0])
        hid = (slope[0, rows, :].astype(F32) * grad).astype(LOW)
        hidden[rows, :] = hid
        bias_sum[0] += jnp.sum(hid.astype(F32), axis=0, keepdims=True)
        total[rows, :] += mm(hid, up[0], NT)
        return 0

    lax.fori_loop(0, tiles, work, 0)

    def weight_grad(left, right, columns):
        acc[...] = jnp.zeros_like(acc)

        def step(i, _):
            rows = tile_at(i)
            acc[...] += mm(left[:, rows], right(rows))
            return 0

        lax.fori_loop(0, tiles, step, 0)
        send_rows(table, acc, slice(None), mine.at[0], other.at[0], columns)

    units = hidden.shape[1]
    weight_grad(first_t, lambda rows: hidden[rows, :], slice(0, units))
    weight_grad(branch_t, lambda rows: active[0, rows, :], slice(units, 2 * units))

    @pl.when(k == pl.num_programs(0) - 1)
    def _():
        def finish(i, _):
            rows = tile_at(i)
            grad = total[rows, :]
            z = z1[rows, :]
            sums[2:3, :] += jnp.sum(grad * z, axis=0, keepdims=True)
            sums[3:4, :] += jnp.sum(grad, axis=0, keepdims=True)
            attn_grad[rows, :] = normalize_back(z, root1[rows, 0:1], grad * gain1[...])
            return 0

        lax.fori_loop(0, tiles, finish, 0)


def attention_backward(
    table, attn_grad, proj, ctx, x, wide, mine, other, out,
    packed_t, attn_t, ctx_grad, proj_grad, acc,
):
    sents, length, width = x.shape
    tiles = table[TILES]
    packed = ctx_grad

    packed[...] = jnp.zeros_like(packed)

    def place(s, _):
        packed[rows_of(table, s), :] = x[s]
        return 0

    lax.fori_loop(0, sents, place, 0)

    def flip(i, _):
        rows = tile_at(i)
        packed_t[:, rows] = packed[rows, :].T
        return 0

    lax.fori_loop(0, tiles, flip, 0)
    ctx_grad[...] = jnp.zeros_like(ctx_grad)
    proj_grad[...] = jnp.zeros_like(proj_grad)

    def start(i, _):
        rows = tile_at(i)
        low = attn_grad[rows, :].astype(LOW)
        attn_t[:, rows] = low.T
        ctx_grad[rows, :] = mm(low, wide[:, 3 * width :]).astype(LOW)
        return 0

    lax.fori_loop(0, tiles, start, 0)

    scale = HD**-0.5

    def attend(s, _):
        rows = rows_of(table, s)
        n = table[LENS + s]
        live = lax.broadcasted_iota(jnp.int32, (length, PAIR), 0) < n
        for p in range(width // PAIR):
            at = p * PAIR
            queries = proj[rows, at : at + PAIR]
            keys = split_heads(proj[rows, width + at : width + at + PAIR])
            values = split_heads(proj[rows, 2 * width + at : 2 * width + at + PAIR])
            grad = ctx_grad[rows, at : at + PAIR]
            grad = jnp.where(live, grad, jnp.zeros_like(grad))
            probs = softmax_pair(queries, keys, n)
            prob_grad = mm(grad, values, NT)
            score_grad = []
            for h in range(2):
                part = prob_grad[:, h * length : (h + 1) * length]
                inner = jnp.sum(probs[h] * part, axis=-1, keepdims=True)
                score_grad.append((probs[h] * (part - inner)).astype(LOW))
            probs_t = jnp.concatenate([q.astype(LOW).T for q in probs], axis=0)
            score_t = jnp.concatenate([q.T for q in score_grad], axis=0)
            score_grad = jnp.concatenate(score_grad, axis=1)
            proj_grad[rows, at : at + PAIR] = (mm(score_grad, keys) * scale).astype(LOW)
            proj_grad[rows, width + at : width + at + PAIR] = (
                join_heads(mm(score_t, queries)) * scale
            ).astype(LOW)
            proj_grad[rows, 2 * width + at : 2 * width + at + PAIR] = join_heads(
                mm(probs_t, grad)
            ).astype(LOW)
        return 0

    lax.fori_loop(0, sents, attend, 0)

    count = mine.shape[0]
    part = width // count

    def weight_grad(left, right, p):
        acc[...] = jnp.zeros_like(acc)

        def step(i, _):
            rows = tile_at(i)
            acc[...] += mm(left[:, rows], right(rows))
            return 0

        lax.fori_loop(0, tiles, step, 0)
        for k in range(count):
            send_rows(
                table,
                acc,
                slice(k * part, (k + 1) * part),
                mine.at[k],
                other.at[k],
                slice(p * part, (p + 1) * part),
            )

    weight_grad(attn_t, lambda rows: ctx[rows, :], 3)
    for p in range(3):
        weight_grad(packed_t, lambda rows: proj_grad[rows, p * width : (p + 1) * width], p)

    def finish(i, _):
        rows = tile_at(i)
        ctx_grad[rows, :] = (
            attn_grad[rows, :] + mm(proj_grad[rows, :], wide[:, : 3 * width], NT)
        ).astype(LOW)
        return 0

    lax.fori_loop(0, tiles, finish, 0)
    for s in range(sents):
        n = table[LENS + s]
        live = lax.broadcasted_iota(jnp.int32, (length, width), 0) < n
        value = ctx_grad[rows_of(table, s), :]
        out[s] = jnp.where(live, value, jnp.zeros_like(value))


SMEM = pl.BlockSpec(memory_space=pltpu.SMEM)
VMEM = pl.BlockSpec(memory_space=pltpu.VMEM)


def shape(dims, dtype):
    return jax.ShapeDtypeStruct(dims, dtype)


def params():
    return pltpu.CompilerParams(vmem_limit_bytes=VMEM_BYTES)


def cost(flops, nbytes):
    return pl.CostEstimate(flops=flops, bytes_accessed=nbytes, transcendentals=0)


def sum_low(*terms):
    return sum(term.astype(F32) for term in terms)


def swap(value, mask):
    return lax.ppermute(value, "dp", [(i, i ^ mask) for i in range(lax.axis_size("dp"))])


def shift(value, k):
    n = lax.axis_size("tensor")
    return lax.ppermute(value, "tensor", [(i, (i + k) % n) for i in range(n)])


def reduce_weight(mine, other):
    n, chips = mine.shape[0], mine.shape[1]
    t_me = lax.axis_index("tensor")
    got = swap(other, 1)
    parts = [sum_low(mine[:, m], got[:, m]).astype(LOW) for m in range(chips)]
    landed = [swap(parts[m], 2 * m) for m in range(1, chips)]
    whole = sum_low(parts[0], *landed).astype(LOW)
    pieces = [lax.dynamic_index_in_dim(whole, (t_me + k) % n, 0, False) for k in range(n)]
    landed = [shift(pieces[k], k) for k in range(1, n)]
    total = sum_low(pieces[0], *landed).astype(LOW)
    return lax.all_gather(total, "dp", axis=0, tiled=True)


def shards(
    tokens,
    lengths,
    partner,
    w_qkv,
    w_out,
    ln1_gain,
    ln1_bias,
    up_weight,
    up_projection_bias,
    down_weight,
    ln2_gain,
    ln2_bias,
    cot_pooled,
    cot_paired,
):
    dp_count = lax.axis_size("dp")
    t_count = lax.axis_size("tensor")
    dp_me = lax.axis_index("dp")
    t_me = lax.axis_index("tensor")
    length, sentences, width = tokens.shape
    mine = sentences // t_count
    rows = mine * length
    pad = rows + length
    slab = width // dp_count
    chips = dp_count // 2
    heads = w_qkv.shape[1] // (3 * HD)
    units = up_weight.shape[1]
    ctx_cols = w_out.shape[0]
    block = 4 * ctx_cols

    def cut(weight):
        return lax.dynamic_slice_in_dim(weight, dp_me * slab, slab, 0)

    def cut_columns(weight):
        return lax.dynamic_slice_in_dim(weight, dp_me * slab, slab, 1).T

    qkv_piece = cut(w_qkv).reshape(slab, heads, 3, HD).transpose(0, 2, 1, 3).reshape(slab, -1)
    attn_piece = jnp.concatenate([qkv_piece, cut_columns(w_out)], axis=1)
    ffn_piece = jnp.concatenate([cut(up_weight), cut_columns(down_weight)], axis=1)
    attn_all = lax.all_gather(attn_piece, ("tensor", "dp"), axis=0, tiled=True)
    attn_all = attn_all.reshape(t_count, width, block)
    ffn_all = lax.all_gather(ffn_piece, ("tensor", "dp"), axis=0, tiled=True)
    ffn_all = ffn_all.reshape(t_count, width, 2 * units)
    bias_all = lax.all_gather(up_projection_bias.reshape(1, units), "tensor", axis=0, tiled=False)

    x = lax.dynamic_slice_in_dim(tokens, t_me * mine, mine, 1).transpose(1, 0, 2)
    counts = lax.dynamic_slice_in_dim(lengths, t_me * mine, mine, 0)
    taken = (counts + 15) // 16 * 16
    ends = jnp.cumsum(taken)
    chip = dp_me // 2
    table = jnp.concatenate(
        [
            ends - taken,
            jnp.zeros(LENS - mine, jnp.int32),
            counts,
            jnp.zeros(TILES - LENS - mine, jnp.int32),
            ((ends[-1:] + TILE - 1) // TILE),
            (dp_me % 2).reshape(1),
            jnp.arange(chips, dtype=jnp.int32) ^ chip,
        ]
    ).astype(jnp.int32)

    proj, ctx, z1, root1, wide = pl.pallas_call(
        attention_forward,
        out_shape=(
            shape((pad, 3 * width), LOW),
            shape((pad, width), LOW),
            shape((rows, width), F32),
            shape((rows, 128), F32),
            shape((width, 4 * width), LOW),
        ),
        in_specs=[SMEM, VMEM, VMEM],
        out_specs=(VMEM,) * 5,
        scratch_shapes=[pltpu.VMEM((pad, width), LOW)],
        compiler_params=params(),
        cost_estimate=cost(8 * rows * width * width, 30 * rows * width),
    )(table, x, attn_all)

    gain1, bias1 = ln1_gain.reshape(1, width), ln1_bias.reshape(1, width)
    gain2, bias2 = ln2_gain.reshape(1, width), ln2_bias.reshape(1, width)

    def whole(*dims):
        return pl.BlockSpec(dims, lambda k, table: (0,) * len(dims))

    act_spec = pl.BlockSpec((1, rows, units), lambda k, table: (k, 0, 0))
    up_spec = pl.BlockSpec((1, width, units), lambda k, table: (k, 0, 0))
    down_spec = pl.BlockSpec((1, width, units), lambda k, table: (k, 0, 1))
    bias_spec = pl.BlockSpec((1, 1, units), lambda k, table: (k, 0, 0))
    active, slope, z2, root2, pooled = pl.pallas_call(
        ffn_forward,
        out_shape=(
            shape((t_count, rows, units), LOW),
            shape((t_count, rows, units), LOW),
            shape((pad, width), F32),
            shape((rows, 128), F32),
            shape((mine, width), F32),
        ),
        grid_spec=pltpu.PrefetchScalarGridSpec(
            num_scalar_prefetch=1,
            grid=(t_count,),
            in_specs=[
                whole(rows, width),
                whole(1, width),
                whole(1, width),
                up_spec,
                down_spec,
                bias_spec,
                whole(1, width),
                whole(1, width),
            ],
            out_specs=(
                act_spec,
                act_spec,
                whole(pad, width),
                whole(rows, 128),
                whole(mine, width),
            ),
            scratch_shapes=[pltpu.VMEM((rows, width), LOW), pltpu.VMEM((rows, width), F32)],
        ),
        compiler_params=params(),
        cost_estimate=cost(4 * rows * width * units * t_count, 40 * rows * width),
    )(table, z1, gain1, bias1, ffn_all, ffn_all, bias_all, gain2, bias2)

    pooled = pooled.astype(LOW)
    returned = lax.all_gather(pooled, "tensor", axis=0, tiled=True)
    everyone = lax.all_gather(jnp.concatenate([returned, cot_paired], 1), "dp", axis=0, tiled=True)
    partner_rows = everyone[partner]
    partner_pooled = partner_rows[:, :width].astype(F32)
    paired = (returned.astype(F32) * partner_pooled).astype(LOW)
    pool_grad = cot_pooled.astype(F32) + partner_pooled * (
        cot_paired.astype(F32) + partner_rows[:, width:].astype(F32)
    )
    pool_grad = lax.dynamic_slice_in_dim(pool_grad.astype(LOW).astype(F32), t_me * mine, mine, 0)

    send_spec = pl.BlockSpec((1, chips, slab, 2 * units), lambda k, table: (k, 0, 0, 0))
    ffn_mine, ffn_other, attn_grad, sums, bias_sum = pl.pallas_call(
        ffn_backward,
        out_shape=(
            shape((t_count, chips, slab, 2 * units), LOW),
            shape((t_count, chips, slab, 2 * units), LOW),
            shape((rows, width), F32),
            shape((8, width), F32),
            shape((t_count, 1, units), F32),
        ),
        grid_spec=pltpu.PrefetchScalarGridSpec(
            num_scalar_prefetch=1,
            grid=(t_count,),
            in_specs=[
                whole(mine, width),
                whole(pad, width),
                whole(rows, 128),
                whole(1, width),
                whole(rows, width),
                whole(rows, 128),
                whole(1, width),
                whole(1, width),
                up_spec,
                down_spec,
                act_spec,
                act_spec,
            ],
            out_specs=(
                send_spec,
                send_spec,
                whole(rows, width),
                whole(8, width),
                bias_spec,
            ),
            scratch_shapes=[
                pltpu.VMEM((width, rows), LOW),
                pltpu.VMEM((rows, width), LOW),
                pltpu.VMEM((width, rows), LOW),
                pltpu.VMEM((pad, width), F32),
                pltpu.VMEM((rows, units), LOW),
                pltpu.VMEM((width, units), F32),
            ],
        ),
        compiler_params=params(),
        cost_estimate=cost(8 * rows * width * units * t_count, 60 * rows * width),
    )(table, pool_grad, z2, root2, gain2, z1, root1, gain1, bias1, ffn_all, ffn_all, active, slope)
    ffn_grad = reduce_weight(ffn_mine, ffn_other)

    attn_mine, attn_other, input_grad = pl.pallas_call(
        attention_backward,
        out_shape=(
            shape((t_count, chips, slab, block), LOW),
            shape((t_count, chips, slab, block), LOW),
            shape((mine, length, width), LOW),
        ),
        in_specs=[SMEM] + [VMEM] * 5,
        out_specs=(VMEM,) * 3,
        scratch_shapes=[
            pltpu.VMEM((width, rows), LOW),
            pltpu.VMEM((width, rows), LOW),
            pltpu.VMEM((pad, width), LOW),
            pltpu.VMEM((pad, 3 * width), LOW),
            pltpu.VMEM((width, width), F32),
        ],
        compiler_params=params(),
        cost_estimate=cost(16 * rows * width * width, 60 * rows * width),
    )(table, attn_grad, proj, ctx, x, wide)
    attn_w_grad = reduce_weight(attn_mine, attn_other)

    share = length // t_count
    blocks = [lax.dynamic_slice_in_dim(input_grad, t_me * share, share, 1)]
    for k in range(1, t_count):
        piece = lax.dynamic_slice_in_dim(input_grad, (t_me + k) % t_count * share, share, 1)
        blocks.append(shift(piece, k))
    home = jnp.zeros((t_count, mine, share, width), LOW)
    for k in range(t_count):
        home = lax.dynamic_update_index_in_dim(home, blocks[k], (t_me - k) % t_count, 0)
    home = home.reshape(sentences, share, width).transpose(1, 0, 2)

    up_bias_sum, norm_sums = lax.psum((bias_sum, sums[:4]), ("dp", "tensor"))
    up_bias_sum = lax.dynamic_index_in_dim(up_bias_sum, t_me, 0, False).reshape(units)
    qkv_grad = attn_w_grad[:, : 3 * ctx_cols].astype(F32)
    qkv_grad = qkv_grad.reshape(width, 3, heads, HD).transpose(0, 2, 1, 3).reshape(width, -1)
    return (
        returned,
        paired,
        home,
        qkv_grad,
        attn_w_grad[:, 3 * ctx_cols :].astype(F32).T,
        norm_sums[2],
        norm_sums[3],
        ffn_grad[:, :units].astype(F32),
        up_bias_sum,
        ffn_grad[:, units:].astype(F32).T,
        norm_sums[0],
        norm_sums[1],
    )


def solution(mesh):
    placed = (
        P(None, "dp", None),
        P("dp"),
        P("dp"),
        P(None, "tensor"),
        P("tensor", None),
        P(),
        P(),
        P(None, "tensor"),
        P("tensor"),
        P("tensor", None),
        P(),
        P(),
        P("dp", None),
        P("dp", None),
    )
    return jax.shard_map(
        shards,
        mesh=mesh,
        in_specs=placed,
        out_specs=(
            P("dp", None),
            P("dp", None),
            P("tensor", "dp", None),
            P(None, "tensor"),
            P("tensor", None),
            P(),
            P(),
            P(None, "tensor"),
            P("tensor"),
            P("tensor", None),
            P(),
            P(),
        ),
        check_vma=False,
    )
```

```python
import functools

import jax
import jax.numpy as jnp
from jax import lax
from jax.experimental import pallas as pl
from jax.experimental.pallas import tpu as pltpu
from jax.sharding import PartitionSpec as P

HD = 64
EPSILON = 1e-06
LOW = jnp.bfloat16
F32 = jnp.float32
INV_SQRT_2PI = 0.3989422804014327
SQRT_HALF = 0.7071067811865476
TILE = 256
MASKED = -1000000000.0
VMEM_BYTES = 60 * 2**20
NN = (((1,), (0,)), ((), ()))
NT = (((1,), (1,)), ((), ()))
PAIR = 2 * HD
LENS, TILES, CORE, MASKS, PLACE = 16, 32, 33, 34, 64


def mm(a, b, dims=NN):
    return lax.dot_general(a, b, dims, preferred_element_type=F32)


def rows_of(table, s):
    return pl.ds(pl.multiple_of(table[s], 16), 128)


def tile_at(i):
    return pl.ds(pl.multiple_of(i * TILE, TILE), TILE)


def normalize(values):
    center = values - jnp.mean(values, axis=-1, keepdims=True)
    spread = jnp.mean(center * center, axis=-1, keepdims=True)
    root = lax.rsqrt(spread + EPSILON)
    return center * root, root


def normalize_back(z, root, dz):
    return root * (
        dz - jnp.mean(dz, -1, keepdims=True) - z * jnp.mean(dz * z, -1, keepdims=True)
    )


def split_heads(pair):
    first = lax.broadcasted_iota(jnp.int32, pair.shape, 1) < HD
    zero = jnp.zeros_like(pair)
    return jnp.concatenate([jnp.where(first, pair, zero), jnp.where(first, zero, pair)], axis=0)


def join_heads(split):
    n = split.shape[0] // 2
    first = lax.broadcasted_iota(jnp.int32, (n, PAIR), 1) < HD
    return jnp.where(first, split[:n], split[n:])


def softmax_pair(queries, keys_split, count):
    length = queries.shape[0]
    scores = mm(queries, keys_split, NT) * (HD**-0.5)
    valid = lax.broadcasted_iota(jnp.int32, (length, length), 1) < count
    out = []
    for h in range(2):
        part = jnp.where(valid, scores[:, h * length : (h + 1) * length], MASKED)
        part = jnp.exp(part - jnp.max(part, axis=-1, keepdims=True))
        out.append(part * (1.0 / jnp.sum(part, axis=-1, keepdims=True)))
    return out


def place_pieces(table, pieces, slabs, sems):
    copies = []
    for i, piece in enumerate(pieces):
        copies.append(pltpu.make_async_copy(piece, slabs.at[table[PLACE + i]], sems.at[i]))
    return copies


def attention_forward(table, x, own, *refs):
    pieces, (proj, ctx, z1, root1, wide, packed, slabs, sems) = refs[:-8], refs[-8:]
    sents, length, width = x.shape
    block = own.shape[1]
    part = block // 4
    copies = place_pieces(table, pieces, slabs, sems)
    for copy in copies:
        copy.start()
    count, slab = slabs.shape[0], slabs.shape[1]

    def widen(k, rows, source, base):
        for p in range(4):
            wide[rows, p * width + k * part : p * width + (k + 1) * part] = source[
                :, base + p * part : base + (p + 1) * part
            ]

    widen(0, slice(None), own[...], 0)
    packed[...] = jnp.zeros_like(packed)
    ctx[...] = jnp.zeros_like(ctx)

    def place(s, _):
        packed[rows_of(table, s), :] = x[s]
        return 0

    lax.fori_loop(0, sents, place, 0)
    for copy in copies:
        copy.wait()
    for j in range(count):
        for k in range(1, width // part):
            widen(k, slice(j * slab, (j + 1) * slab), slabs[j], (k - 1) * block)
    tiles = table[TILES]

    def project(i, _):
        rows = tile_at(i)
        source = packed[rows, :]
        for p in range(3):
            cols = slice(p * width, (p + 1) * width)
            proj[rows, cols] = mm(source, wide[:, cols]).astype(LOW)
        return 0

    lax.fori_loop(0, tiles, project, 0)
    proj[pl.ds(pl.multiple_of(tiles * TILE, TILE), length), :] = jnp.zeros(
        (length, 3 * width), LOW
    )

    def attend(s, _):
        rows = rows_of(table, s)
        n = table[LENS + s]
        for p in range(width // PAIR):
            at = p * PAIR
            queries = proj[rows, at : at + PAIR]
            keys = split_heads(proj[rows, width + at : width + at + PAIR])
            values = split_heads(proj[rows, 2 * width + at : 2 * width + at + PAIR])
            probs = jnp.concatenate(softmax_pair(queries, keys, n), axis=1).astype(LOW)
            ctx[rows, at : at + PAIR] = mm(probs, values).astype(LOW)
        return 0

    lax.fori_loop(0, sents, attend, 0)

    def finish(i, _):
        rows = tile_at(i)
        attended = mm(ctx[rows, :], wide[:, 3 * width :], NT)
        z, root = normalize(packed[rows, :].astype(F32) + attended)
        z1[rows, :] = z
        root1[rows, :] = jnp.broadcast_to(root, (TILE, 128))
        return 0

    lax.fori_loop(0, tiles, finish, 0)


def gelu_parts(pre):
    a = jnp.abs(pre) * SQRT_HALF
    t = pl.reciprocal(1.0 + 0.3275911 * a)
    poly = 1.061405429
    for c in (-1.453152027, 1.421413741, -0.284496736, 0.254829592):
        poly = poly * t + c
    e = jnp.exp(-a * a)
    tail = 0.5 * poly * t * e
    cdf = jnp.where(pre >= 0.0, 1.0 - tail, tail)
    return pre * cdf, cdf + pre * (e * INV_SQRT_2PI)


def ffn_forward(table, z1, gain1, bias1, own, bias, gain2, bias2, *refs):
    pieces, refs = refs[:-10], refs[-10:]
    active, slope, z2, root2, pooled, weight, first, total, slabs, sems = refs
    k = pl.program_id(0)
    tiles = table[TILES]
    count, slab = slabs.shape[0], slabs.shape[1]
    units = active.shape[2]

    @pl.when(k == 0)
    def _():
        for copy in place_pieces(table, pieces, slabs, sems):
            copy.start()
        weight[0] = own[...]

    @pl.when(k == 1)
    def _():
        for copy in place_pieces(table, pieces, slabs, sems):
            copy.wait()

    for t in range(1, pl.num_programs(0)):

        @pl.when(k == t)
        def _():
            for j in range(count):
                weight[0, j * slab : (j + 1) * slab, :] = slabs[
                    j, :, (t - 1) * 2 * units : t * 2 * units
                ]

    @pl.when(k == 0)
    def _():
        def start(i, _):
            rows = tile_at(i)
            value = z1[rows, :] * gain1[...] + bias1[...]
            first[rows, :] = value.astype(LOW)
            total[rows, :] = value
            return 0

        lax.fori_loop(0, tiles, start, 0)

    def work(i, _):
        rows = tile_at(i)
        pre = mm(first[rows, :], weight[0, :, :units]) + bias[0]
        act, slp = gelu_parts(pre)
        act = act.astype(LOW)
        active[0, rows, :] = act
        slope[0, rows, :] = slp.astype(LOW)
        total[rows, :] += mm(act, weight[0, :, units:], NT)
        return 0

    lax.fori_loop(0, tiles, work, 0)

    @pl.when(k == pl.num_programs(0) - 1)
    def _():
        z2[pl.ds(pl.multiple_of(tiles * TILE, TILE), 128), :] = jnp.zeros((128, z2.shape[1]), F32)

        def finish(i, _):
            rows = tile_at(i)
            z, root = normalize(total[rows, :])
            z2[rows, :] = z
            root2[rows, :] = jnp.broadcast_to(root, (TILE, 128))
            return 0

        lax.fori_loop(0, tiles, finish, 0)
        for s in range(pooled.shape[0]):
            n = table[LENS + s]
            valid = lax.broadcasted_iota(jnp.int32, (128, z2.shape[1]), 0) < n
            rows = jnp.where(valid, z2[rows_of(table, s), :], 0.0)
            mean = jnp.sum(rows, axis=0, keepdims=True) / n.astype(F32)
            pooled[s : s + 1, :] = mean * gain2[...] + bias2[...]


def send_rows(table, acc, source, mine, other, columns):
    chips, slab = mine.shape[0], mine.shape[2]
    core = table[CORE]
    for m in range(chips):
        base = (table[MASKS + m] * 2) * slab
        here = pl.multiple_of(base + core * slab, 8)
        there = pl.multiple_of(base + (1 - core) * slab, 8)
        mine[m, 0, :, columns] = acc[pl.ds(here, slab), source].astype(LOW)
        other[m, 0, :, columns] = acc[pl.ds(there, slab), source].astype(LOW)


def weight_grad(tiles, acc, left, right):
    acc[...] = jnp.zeros_like(acc)

    def step(i, _):
        rows = tile_at(i)
        acc[...] += mm(left[:, rows], right(rows))
        return 0

    lax.fori_loop(0, tiles, step, 0)


def down_backward(
    table, pool, z2, root2, gain2, active, mine, other, back, branch, sums, branch_t, acc
):
    tiles = table[TILES]
    width = z2.shape[1]

    @pl.when(pl.program_id(0) == 0)
    def _():
        back[...] = jnp.zeros_like(back)
        for s in range(pool.shape[0]):
            n = table[LENS + s]
            valid = lax.broadcasted_iota(jnp.int32, (128, width), 0) < n
            row = pool[s : s + 1, :] / n.astype(F32)
            back[rows_of(table, s), :] = jnp.where(valid, row, 0.0)
        sums[...] = jnp.zeros_like(sums)

        def start(i, _):
            rows = tile_at(i)
            grad = back[rows, :]
            z = z2[rows, :]
            sums[0:1, :] += jnp.sum(grad * z, axis=0, keepdims=True)
            sums[1:2, :] += jnp.sum(grad, axis=0, keepdims=True)
            value = normalize_back(z, root2[rows, 0:1], grad * gain2[...])
            low = value.astype(LOW)
            back[rows, :] = value
            branch[rows, :] = low
            branch_t[:, rows] = low.T
            return 0

        lax.fori_loop(0, tiles, start, 0)

    weight_grad(tiles, acc, branch_t, lambda rows: active[0, rows, :])
    send_rows(table, acc, slice(None), mine, other, slice(None))


def up_backward(
    table, back, branch, z1, root1, gain1, bias1, up, down, slope,
    mine, other, attn_grad, sums, bias_sum, first_t, hidden, total, acc,
):
    k = pl.program_id(0)
    tiles = table[TILES]

    @pl.when(k == 0)
    def _():
        sums[...] = jnp.zeros_like(sums)

        def start(i, _):
            rows = tile_at(i)
            first = (z1[rows, :] * gain1[...] + bias1[...]).astype(LOW)
            first_t[:, rows] = first.T
            total[rows, :] = back[rows, :]
            return 0

        lax.fori_loop(0, tiles, start, 0)

    bias_sum[...] = jnp.zeros_like(bias_sum)

    def work(i, _):
        rows = tile_at(i)
        grad = mm(branch[rows, :], down[0])
        hid = (slope[0, rows, :].astype(F32) * grad).astype(LOW)
        hidden[rows, :] = hid
        bias_sum[0] += jnp.sum(hid.astype(F32), axis=0, keepdims=True)
        total[rows, :] += mm(hid, up[0], NT)
        return 0

    lax.fori_loop(0, tiles, work, 0)
    weight_grad(tiles, acc, first_t, lambda rows: hidden[rows, :])
    send_rows(table, acc, slice(None), mine, other, slice(None))

    @pl.when(k == pl.num_programs(0) - 1)
    def _():
        def finish(i, _):
            rows = tile_at(i)
            grad = total[rows, :]
            z = z1[rows, :]
            sums[0:1, :] += jnp.sum(grad * z, axis=0, keepdims=True)
            sums[1:2, :] += jnp.sum(grad, axis=0, keepdims=True)
            attn_grad[rows, :] = normalize_back(z, root1[rows, 0:1], grad * gain1[...])
            return 0

        lax.fori_loop(0, tiles, finish, 0)


def attention_backward(table, attn_grad, proj, wide, proj_grad, attn_low, ctx_grad):
    length = proj.shape[0] - attn_grad.shape[0]
    sents = attn_grad.shape[0] // length
    tiles = table[TILES]
    width = attn_grad.shape[1]
    ctx_grad[...] = jnp.zeros_like(ctx_grad)
    proj_grad[...] = jnp.zeros_like(proj_grad)

    def start(i, _):
        rows = tile_at(i)
        low = attn_grad[rows, :].astype(LOW)
        attn_low[rows, :] = low
        ctx_grad[rows, :] = mm(low, wide[:, 3 * width :]).astype(LOW)
        return 0

    lax.fori_loop(0, tiles, start, 0)

    scale = HD**-0.5

    def attend(s, _):
        rows = rows_of(table, s)
        n = table[LENS + s]
        live = lax.broadcasted_iota(jnp.int32, (length, PAIR), 0) < n
        for p in range(width // PAIR):
            at = p * PAIR
            queries = proj[rows, at : at + PAIR]
            keys = split_heads(proj[rows, width + at : width + at + PAIR])
            values = split_heads(proj[rows, 2 * width + at : 2 * width + at + PAIR])
            grad = ctx_grad[rows, at : at + PAIR]
            grad = jnp.where(live, grad, jnp.zeros_like(grad))
            probs = softmax_pair(queries, keys, n)
            prob_grad = mm(grad, values, NT)
            score_grad = []
            for h in range(2):
                part = prob_grad[:, h * length : (h + 1) * length]
                inner = jnp.sum(probs[h] * part, axis=-1, keepdims=True)
                score_grad.append((probs[h] * (part - inner)).astype(LOW))
            probs_t = jnp.concatenate([q.astype(LOW).T for q in probs], axis=0)
            score_t = jnp.concatenate([q.T for q in score_grad], axis=0)
            score_grad = jnp.concatenate(score_grad, axis=1)
            proj_grad[rows, at : at + PAIR] = (mm(score_grad, keys) * scale).astype(LOW)
            proj_grad[rows, width + at : width + at + PAIR] = (
                join_heads(mm(score_t, queries)) * scale
            ).astype(LOW)
            proj_grad[rows, 2 * width + at : 2 * width + at + PAIR] = join_heads(
                mm(probs_t, grad)
            ).astype(LOW)
        return 0

    lax.fori_loop(0, sents, attend, 0)


def attention_weights(table, x, attn_low, ctx, proj_grad, mine, other, packed, packed_t, attn_t, acc):
    sents, length, width = x.shape
    tiles = table[TILES]
    packed[...] = jnp.zeros_like(packed)

    def place(s, _):
        packed[rows_of(table, s), :] = x[s]
        return 0

    lax.fori_loop(0, sents, place, 0)

    def flip(i, _):
        rows = tile_at(i)
        packed_t[:, rows] = packed[rows, :].T
        attn_t[:, rows] = attn_low[rows, :].T
        return 0

    lax.fori_loop(0, tiles, flip, 0)
    count = mine.shape[1]
    part = width // count
    for p in range(4):
        if p == 3:
            weight_grad(tiles, acc, attn_t, lambda rows: ctx[rows, :])
        else:
            cols = slice(p * width, (p + 1) * width)
            weight_grad(tiles, acc, packed_t, lambda rows: proj_grad[rows, cols])
        for k in range(count):
            send_rows(
                table,
                acc,
                slice(k * part, (k + 1) * part),
                mine.at[:, k : k + 1],
                other.at[:, k : k + 1],
                slice(p * part, (p + 1) * part),
            )


def input_backward(table, attn_grad, proj_grad, wide, out, total):
    sents, length, width = out.shape
    tiles = table[TILES]

    def finish(i, _):
        rows = tile_at(i)
        total[rows, :] = (
            attn_grad[rows, :] + mm(proj_grad[rows, :], wide[:, : 3 * width], NT)
        ).astype(LOW)
        return 0

    lax.fori_loop(0, tiles, finish, 0)
    total[pl.ds(pl.multiple_of(tiles * TILE, TILE), length), :] = jnp.zeros((length, width), LOW)
    for s in range(sents):
        n = table[LENS + s]
        live = lax.broadcasted_iota(jnp.int32, (length, width), 0) < n
        value = total[rows_of(table, s), :]
        out[s] = jnp.where(live, value, jnp.zeros_like(value))


SMEM = pl.BlockSpec(memory_space=pltpu.SMEM)
VMEM = pl.BlockSpec(memory_space=pltpu.VMEM)
ANY = pl.BlockSpec(memory_space=pl.ANY)


def shape(dims, dtype):
    return jax.ShapeDtypeStruct(dims, dtype)


def params():
    return pltpu.CompilerParams(vmem_limit_bytes=VMEM_BYTES)


def cost(flops, nbytes):
    return pl.CostEstimate(flops=flops, bytes_accessed=nbytes, transcendentals=0)


def add(*terms):
    return sum(term.astype(F32) for term in terms)


def swap(value, mask, axis="dp"):
    return lax.ppermute(value, axis, [(i, i ^ mask) for i in range(lax.axis_size(axis))])


def bits_of(count):
    return [1 << i for i in range(count.bit_length() - 1)]


def gather_line(piece):
    n = lax.axis_size("tensor")
    return jnp.concatenate([swap(piece, k, "tensor") for k in range(1, n)], axis=1)


def gather_plane(value):
    chips = lax.axis_size("dp") // 2
    near = [value] + [swap(value, 2 * m) for m in range(1, chips)]
    return near + [swap(item, 1) for item in near]


def halve(terms, bit, mask, axis):
    def pick(term, side):
        dims = term.shape
        low = 1 if bit is None else bit
        view = term.reshape((dims[0] // (2 * low), 2, low) + dims[1:])[:, side]
        return view.reshape((dims[0] // 2,) + dims[1:])

    sent = add(*[pick(term, 1) for term in terms]).astype(LOW)
    return [pick(term, 0) for term in terms] + [swap(sent, mask, axis)]


def reduce_line(total):
    terms = [total]
    for bit in bits_of(lax.axis_size("tensor")):
        terms = halve(terms, 1, bit, "tensor")
    return add(*terms)[0].astype(LOW)


def reduce_halving(mine, other, falling):
    terms = [mine, swap(other, 1)]
    bits = bits_of(mine.shape[0])
    if falling:
        for bit in bits[::-1]:
            terms = halve(terms, bit, 2 * bit, "dp")
    else:
        for bit in bits:
            terms = halve(terms, 1, 2 * bit, "dp")
    return reduce_line(add(*terms)[0].astype(LOW))


def reduce_direct(mine, other):
    got = swap(other, 1)
    chips = mine.shape[0]
    landed = [swap(add(mine[m], got[m]).astype(LOW), 2 * m) for m in range(1, chips)]
    return reduce_line(add(mine[0], got[0], *landed).astype(LOW))


def place_plane(pieces, spots):
    out = jnp.zeros((len(pieces),) + pieces[0].shape, pieces[0].dtype)
    for i, piece in enumerate(pieces):
        out = lax.dynamic_update_index_in_dim(out, piece, spots[i], 0)
    return out.reshape((-1,) + pieces[0].shape[1:])


def shards(
    tokens,
    lengths,
    partner,
    w_qkv,
    w_out,
    ln1_gain,
    ln1_bias,
    up_weight,
    up_projection_bias,
    down_weight,
    ln2_gain,
    ln2_bias,
    cot_pooled,
    cot_paired,
):
    dp_count = lax.axis_size("dp")
    t_count = lax.axis_size("tensor")
    dp_me = lax.axis_index("dp")
    t_me = lax.axis_index("tensor")
    length, sentences, width = tokens.shape
    mine = sentences // t_count
    rows = mine * length
    pad = rows + length
    slab = width // dp_count
    chips = dp_count // 2
    heads = w_qkv.shape[1] // (3 * HD)
    units = up_weight.shape[1]
    ctx_cols = w_out.shape[0]
    block = 4 * ctx_cols

    def cut(weight):
        return lax.dynamic_slice_in_dim(weight, dp_me * slab, slab, 0)

    def by_part(weight):
        return weight.reshape(-1, heads, 3, HD).transpose(0, 2, 1, 3).reshape(weight.shape)

    def cut_columns(weight):
        return lax.dynamic_slice_in_dim(weight, dp_me * slab, slab, 1).T

    attn_piece = jnp.concatenate([by_part(cut(w_qkv)), cut_columns(w_out)], axis=1)
    ffn_piece = jnp.concatenate([cut(up_weight), cut_columns(down_weight)], axis=1)
    attn_line = gather_line(attn_piece)
    ffn_line = gather_line(ffn_piece)
    attn_pieces = gather_plane(attn_line)
    attn_own = jnp.concatenate([by_part(w_qkv), w_out.T], axis=1)
    ffn_own = jnp.concatenate([up_weight, down_weight.T], axis=1)
    bias_own = up_projection_bias.reshape(1, units)
    bias_all = jnp.stack([bias_own] + [swap(bias_own, k, "tensor") for k in range(1, t_count)])
    cot_pieces = gather_plane(cot_paired)

    x = lax.dynamic_slice_in_dim(tokens, t_me * mine, mine, 1).transpose(1, 0, 2)
    counts = lax.dynamic_slice_in_dim(lengths, t_me * mine, mine, 0)
    taken = (counts + 15) // 16 * 16
    ends = jnp.cumsum(taken)
    chip = dp_me // 2
    near = dp_me ^ (2 * jnp.arange(chips, dtype=jnp.int32))
    spots = jnp.concatenate([near, near ^ 1])
    table = jnp.concatenate(
        [
            ends - taken,
            jnp.zeros(LENS - mine, jnp.int32),
            counts,
            jnp.zeros(TILES - LENS - mine, jnp.int32),
            ((ends[-1:] + TILE - 1) // TILE),
            (dp_me % 2).reshape(1),
            jnp.arange(chips, dtype=jnp.int32) ^ chip,
            jnp.zeros(PLACE - MASKS - chips, jnp.int32),
            spots,
        ]
    ).astype(jnp.int32)

    attn_pieces, ffn_line = lax.optimization_barrier((attn_pieces, ffn_line))
    ffn_pieces = gather_plane(ffn_line)
    proj, ctx, z1, root1, wide = pl.pallas_call(
        attention_forward,
        out_shape=(
            shape((pad, 3 * width), LOW),
            shape((pad, width), LOW),
            shape((rows, width), F32),
            shape((rows, 128), F32),
            shape((width, 4 * width), LOW),
        ),
        in_specs=[SMEM, VMEM, VMEM] + [ANY] * dp_count,
        out_specs=(VMEM,) * 5,
        scratch_shapes=[
            pltpu.VMEM((pad, width), LOW),
            pltpu.VMEM((dp_count, slab, (t_count - 1) * block), LOW),
            pltpu.SemaphoreType.DMA((dp_count,)),
        ],
        compiler_params=params(),
        cost_estimate=cost(8 * rows * width * width, 30 * rows * width),
        name="attention_forward",
    )(table, x, attn_own, *attn_pieces)

    gain1, bias1 = ln1_gain.reshape(1, width), ln1_bias.reshape(1, width)
    gain2, bias2 = ln2_gain.reshape(1, width), ln2_bias.reshape(1, width)

    def whole(*dims):
        return pl.BlockSpec(dims, lambda k, table: (0,) * len(dims))

    def call(kernel, outs, ins, out_specs, scratch, flops, nbytes):
        return pl.pallas_call(
            kernel,
            out_shape=outs,
            grid_spec=pltpu.PrefetchScalarGridSpec(
                num_scalar_prefetch=1,
                grid=(t_count,),
                in_specs=ins,
                out_specs=out_specs,
                scratch_shapes=scratch,
            ),
            compiler_params=params(),
            cost_estimate=cost(flops, nbytes),
            name=kernel.__name__,
        )

    act_spec = pl.BlockSpec((1, rows, units), lambda k, table: (k, 0, 0))
    up_spec = pl.BlockSpec((1, width, units), lambda k, table: (k, 0, 0))
    down_spec = pl.BlockSpec((1, width, units), lambda k, table: (k, 0, 1))
    bias_spec = pl.BlockSpec((1, 1, units), lambda k, table: (k, 0, 0))
    line = whole(1, width)
    full = whole(rows, width)
    full_pad = whole(pad, width)
    root_spec = whole(rows, 128)
    act_shape = shape((t_count, rows, units), LOW)
    active, slope, z2, root2, pooled, ffn_all = call(
        ffn_forward,
        (
            act_shape,
            act_shape,
            shape((pad, width), F32),
            shape((rows, 128), F32),
            shape((mine, width), F32),
            shape((t_count, width, 2 * units), LOW),
        ),
        [full, line, line, whole(width, 2 * units), bias_spec, line, line] + [ANY] * dp_count,
        (
            act_spec,
            act_spec,
            full_pad,
            root_spec,
            whole(mine, width),
            pl.BlockSpec((1, width, 2 * units), lambda k, table: (k, 0, 0)),
        ),
        [
            pltpu.VMEM((rows, width), LOW),
            pltpu.VMEM((rows, width), F32),
            pltpu.VMEM((dp_count, slab, (t_count - 1) * 2 * units), LOW),
            pltpu.SemaphoreType.DMA((dp_count,)),
        ],
        4 * rows * width * units * t_count,
        40 * rows * width,
    )(table, z1, gain1, bias1, ffn_own, bias_all, gain2, bias2, *ffn_pieces)

    pooled = pooled.astype(LOW)
    line_pooled = jnp.stack([pooled] + [swap(pooled, k, "tensor") for k in range(1, t_count)])
    everyone = jnp.stack(gather_plane(line_pooled)).reshape(-1, width)
    cot_all = jnp.stack(cot_pieces).reshape(-1, width)
    home_device = partner // sentences
    apart = home_device ^ dp_me
    where_device = apart % 2 * chips + apart // 2
    inside = partner % sentences
    partner_pooled = everyone[
        (where_device * t_count + (inside // mine ^ t_me)) * mine + inside % mine
    ].astype(F32)
    partner_cot = cot_all[where_device * sentences + inside].astype(F32)
    returned = line_pooled[jnp.arange(t_count) ^ t_me].reshape(sentences, width)
    paired = (returned.astype(F32) * partner_pooled).astype(LOW)
    pool_grad = cot_pooled.astype(F32) + partner_pooled * (cot_paired.astype(F32) + partner_cot)
    pool_grad = lax.dynamic_slice_in_dim(pool_grad.astype(LOW).astype(F32), t_me * mine, mine, 0)

    send_spec = pl.BlockSpec((chips, 1, slab, units), lambda k, table: (0, k, 0, 0))
    send_shape = shape((chips, t_count, slab, units), LOW)
    down_mine, down_other, back, branch, sums_two = call(
        down_backward,
        (
            send_shape,
            send_shape,
            shape((pad, width), F32),
            shape((rows, width), LOW),
            shape((2, width), F32),
        ),
        [whole(mine, width), full_pad, root_spec, line, act_spec],
        (send_spec, send_spec, full_pad, full, whole(2, width)),
        [pltpu.VMEM((width, rows), LOW), pltpu.VMEM((width, units), F32)],
        2 * rows * width * units * t_count,
        40 * rows * width,
    )(table, pool_grad, z2, root2, gain2, active)

    up_mine, up_other, attn_grad, sums_one, bias_sum = call(
        up_backward,
        (
            send_shape,
            send_shape,
            shape((rows, width), F32),
            shape((2, width), F32),
            shape((t_count, 1, units), F32),
        ),
        [full_pad, full, full, root_spec, line, line, up_spec, down_spec, act_spec],
        (send_spec, send_spec, full, whole(2, width), bias_spec),
        [
            pltpu.VMEM((width, rows), LOW),
            pltpu.VMEM((rows, units), LOW),
            pltpu.VMEM((rows, width), F32),
            pltpu.VMEM((width, units), F32),
        ],
        6 * rows * width * units * t_count,
        40 * rows * width,
    )(table, back, branch, z1, root1, gain1, bias1, ffn_all, ffn_all, slope)

    proj_grad, attn_low = pl.pallas_call(
        attention_backward,
        out_shape=(shape((pad, 3 * width), LOW), shape((rows, width), LOW)),
        in_specs=[SMEM] + [VMEM] * 3,
        out_specs=(VMEM,) * 2,
        scratch_shapes=[pltpu.VMEM((pad, width), LOW)],
        compiler_params=params(),
        cost_estimate=cost(6 * rows * width * width, 30 * rows * width),
        name="attention_backward",
    )(table, attn_grad, proj, wide)
    attn_mine, attn_other = pl.pallas_call(
        attention_weights,
        out_shape=(shape((chips, t_count, slab, block), LOW),) * 2,
        in_specs=[SMEM] + [VMEM] * 4,
        out_specs=(VMEM,) * 2,
        scratch_shapes=[
            pltpu.VMEM((pad, width), LOW),
            pltpu.VMEM((width, rows), LOW),
            pltpu.VMEM((width, rows), LOW),
            pltpu.VMEM((width, width), F32),
        ],
        compiler_params=params(),
        cost_estimate=cost(8 * rows * width * width, 30 * rows * width),
        name="attention_weights",
    )(table, x, attn_low, ctx, proj_grad)
    input_grad = pl.pallas_call(
        input_backward,
        out_shape=shape((mine, length, width), LOW),
        in_specs=[SMEM] + [VMEM] * 3,
        out_specs=VMEM,
        scratch_shapes=[pltpu.VMEM((pad, width), LOW)],
        compiler_params=params(),
        cost_estimate=cost(6 * rows * width * width, 20 * rows * width),
        name="input_backward",
    )(table, attn_grad, proj_grad, wide)

    down_sum = reduce_halving(down_mine, down_other, False)
    up_sum = reduce_halving(up_mine, up_other, True)
    ffn_grad = place_plane(gather_plane(jnp.concatenate([up_sum, down_sum], 1)), spots)
    attn_w_grad = place_plane(gather_plane(reduce_direct(attn_mine, attn_other)), spots)

    share = length // t_count
    pieces = input_grad.reshape(mine, t_count, share, width)
    blocks = []
    for k in range(t_count):
        piece = lax.dynamic_index_in_dim(pieces, t_me ^ k, 1, False)
        blocks.append(swap(piece, k, "tensor") if k else piece)
    home = jnp.zeros((t_count, mine, share, width), LOW)
    for k in range(t_count):
        home = lax.dynamic_update_index_in_dim(home, blocks[k], t_me ^ k, 0)
    home = home.reshape(sentences, share, width).transpose(1, 0, 2)

    small = jnp.concatenate([bias_sum.reshape(t_count, units), sums_one, sums_two])
    for mask in bits_of(dp_count):
        small = small + swap(small, mask)
    norms, bias_part = small[t_count:], small[:t_count]
    for mask in bits_of(t_count):
        half = bias_part.shape[0] // 2
        split = bias_part.reshape(half, 2, units)
        got = swap(jnp.concatenate([split[:, 1], norms]), mask, "tensor")
        bias_part = split[:, 0] + got[:half]
        norms = norms + got[half:]

    qkv_grad = attn_w_grad[:, : 3 * ctx_cols].astype(F32)
    qkv_grad = qkv_grad.reshape(width, 3, heads, HD).transpose(0, 2, 1, 3).reshape(width, -1)
    return (
        returned,
        paired,
        home,
        qkv_grad,
        attn_w_grad[:, 3 * ctx_cols :].astype(F32).T,
        norms[0],
        norms[1],
        ffn_grad[:, :units].astype(F32),
        bias_part[0],
        ffn_grad[:, units:].astype(F32).T,
        norms[2],
        norms[3],
    )


def solution(mesh):
    placed = (
        P(None, "dp", None),
        P("dp"),
        P("dp"),
        P(None, "tensor"),
        P("tensor", None),
        P(),
        P(),
        P(None, "tensor"),
        P("tensor"),
        P("tensor", None),
        P(),
        P(),
        P("dp", None),
        P("dp", None),
    )
    return jax.shard_map(
        shards,
        mesh=mesh,
        in_specs=placed,
        out_specs=(
            P("dp", None),
            P("dp", None),
            P("tensor", "dp", None),
            P(None, "tensor"),
            P("tensor", None),
            P(),
            P(),
            P(None, "tensor"),
            P("tensor"),
            P("tensor", None),
            P(),
            P(),
        ),
        check_vma=False,
    )
```

```python
import functools

import jax
import jax.numpy as jnp
import numpy as np
from jax import lax
from jax.experimental import pallas as pl
from jax.experimental.pallas import tpu as pltpu
from jax.sharding import PartitionSpec as P

HD = 64
EPSILON = 1e-06
LOW = jnp.bfloat16
F32 = jnp.float32
INV_SQRT_2PI = 0.3989422804014327
SQRT_HALF = 0.7071067811865476
TILE = 256
MASKED = -1000000000.0
VMEM_BYTES = 60 * 2**20
NN = (((1,), (0,)), ((), ()))
NT = (((1,), (1,)), ((), ()))
PAIR = 2 * HD
LENS, TILES, CORE, LINE, MASKS, PLACE = 16, 32, 33, 34, 48, 64


def mm(a, b, dims=NN):
    return lax.dot_general(a, b, dims, preferred_element_type=F32)


def rows_of(table, s):
    return pl.ds(pl.multiple_of(table[s], 16), 128)


def tile_at(i):
    return pl.ds(pl.multiple_of(i * TILE, TILE), TILE)


def normalize(values):
    center = values - jnp.mean(values, axis=-1, keepdims=True)
    spread = jnp.mean(center * center, axis=-1, keepdims=True)
    root = lax.rsqrt(spread + EPSILON)
    return center * root, root


def normalize_back(z, root, dz):
    return root * (
        dz - jnp.mean(dz, -1, keepdims=True) - z * jnp.mean(dz * z, -1, keepdims=True)
    )


def split_heads(pair):
    first = lax.broadcasted_iota(jnp.int32, pair.shape, 1) < HD
    zero = jnp.zeros_like(pair)
    return jnp.concatenate([jnp.where(first, pair, zero), jnp.where(first, zero, pair)], axis=0)


def join_heads(split):
    n = split.shape[0] // 2
    first = lax.broadcasted_iota(jnp.int32, (n, PAIR), 1) < HD
    return jnp.where(first, split[:n], split[n:])


def softmax_pair(queries, keys_split, count):
    length = queries.shape[0]
    scores = mm(queries, keys_split, NT) * (HD**-0.5)
    valid = lax.broadcasted_iota(jnp.int32, (length, length), 1) < count
    out = []
    for h in range(2):
        part = jnp.where(valid, scores[:, h * length : (h + 1) * length], MASKED)
        part = jnp.exp(part - jnp.max(part, axis=-1, keepdims=True))
        out.append(part * (1.0 / jnp.sum(part, axis=-1, keepdims=True)))
    return out


def place_pieces(table, pieces, slabs, sems):
    copies = []
    for i, piece in enumerate(pieces):
        copies.append(pltpu.make_async_copy(piece, slabs.at[table[PLACE + i]], sems.at[i]))
    return copies


def attention_forward(table, x, own, *refs):
    pieces, (proj, ctx, z1, root1, wide, packed, slabs, sems) = refs[:-8], refs[-8:]
    sents, length, width = x.shape
    block = own.shape[1]
    part = block // 4
    copies = place_pieces(table, pieces, slabs, sems)
    for copy in copies:
        copy.start()
    count, slab = slabs.shape[0], slabs.shape[1]

    def widen(k, rows, source, base):
        for p in range(4):
            wide[rows, p * width + k * part : p * width + (k + 1) * part] = source[
                :, base + p * part : base + (p + 1) * part
            ]

    widen(0, slice(None), own[...], 0)
    packed[...] = jnp.zeros_like(packed)
    ctx[...] = jnp.zeros_like(ctx)

    def place(s, _):
        packed[rows_of(table, s), :] = x[s]
        return 0

    lax.fori_loop(0, sents, place, 0)
    for copy in copies:
        copy.wait()
    for j in range(count):
        for k in range(1, width // part):
            widen(k, slice(j * slab, (j + 1) * slab), slabs[j], (k - 1) * block)
    tiles = table[TILES]

    def project(i, _):
        rows = tile_at(i)
        source = packed[rows, :]
        for p in range(3):
            cols = slice(p * width, (p + 1) * width)
            proj[rows, cols] = mm(source, wide[:, cols]).astype(LOW)
        return 0

    lax.fori_loop(0, tiles, project, 0)
    proj[pl.ds(pl.multiple_of(tiles * TILE, TILE), length), :] = jnp.zeros(
        (length, 3 * width), LOW
    )

    def attend(s, _):
        rows = rows_of(table, s)
        n = table[LENS + s]
        for p in range(width // PAIR):
            at = p * PAIR
            queries = proj[rows, at : at + PAIR]
            keys = split_heads(proj[rows, width + at : width + at + PAIR])
            values = split_heads(proj[rows, 2 * width + at : 2 * width + at + PAIR])
            probs = jnp.concatenate(softmax_pair(queries, keys, n), axis=1).astype(LOW)
            ctx[rows, at : at + PAIR] = mm(probs, values).astype(LOW)
        return 0

    lax.fori_loop(0, sents, attend, 0)

    def finish(i, _):
        rows = tile_at(i)
        attended = mm(ctx[rows, :], wide[:, 3 * width :], NT)
        z, root = normalize(packed[rows, :].astype(F32) + attended)
        z1[rows, :] = z
        root1[rows, :] = jnp.broadcast_to(root, (TILE, 128))
        return 0

    lax.fori_loop(0, tiles, finish, 0)


def gelu_parts(pre):
    a = jnp.abs(pre) * SQRT_HALF
    t = pl.reciprocal(1.0 + 0.3275911 * a)
    poly = 1.061405429
    for c in (-1.453152027, 1.421413741, -0.284496736, 0.254829592):
        poly = poly * t + c
    e = jnp.exp(-a * a)
    tail = 0.5 * poly * t * e
    cdf = jnp.where(pre >= 0.0, 1.0 - tail, tail)
    return pre * cdf, cdf + pre * (e * INV_SQRT_2PI)


def ffn_forward(table, z1, gain1, bias1, own, bias, gain2, bias2, *refs):
    pieces, refs = refs[:-10], refs[-10:]
    active, slope, z2, root2, pooled, weight, first, total, slabs, sems = refs
    k = pl.program_id(0)
    tiles = table[TILES]
    count, slab = slabs.shape[0], slabs.shape[1]
    units = active.shape[2]

    @pl.when(k == 0)
    def _():
        for copy in place_pieces(table, pieces, slabs, sems):
            copy.start()
        weight[0] = own[...]

    @pl.when(k == 1)
    def _():
        for copy in place_pieces(table, pieces, slabs, sems):
            copy.wait()

    for t in range(1, pl.num_programs(0)):

        @pl.when(k == t)
        def _():
            for j in range(count):
                weight[0, j * slab : (j + 1) * slab, :] = slabs[
                    j, :, (t - 1) * 2 * units : t * 2 * units
                ]

    @pl.when(k == 0)
    def _():
        def start(i, _):
            rows = tile_at(i)
            value = z1[rows, :] * gain1[...] + bias1[...]
            first[rows, :] = value.astype(LOW)
            total[rows, :] = value
            return 0

        lax.fori_loop(0, tiles, start, 0)

    def work(i, _):
        rows = tile_at(i)
        pre = mm(first[rows, :], weight[0, :, :units]) + bias[0]
        act, slp = gelu_parts(pre)
        act = act.astype(LOW)
        active[0, rows, :] = act
        slope[0, rows, :] = slp.astype(LOW)
        total[rows, :] += mm(act, weight[0, :, units:], NT)
        return 0

    lax.fori_loop(0, tiles, work, 0)

    @pl.when(k == pl.num_programs(0) - 1)
    def _():
        z2[pl.ds(pl.multiple_of(tiles * TILE, TILE), 128), :] = jnp.zeros((128, z2.shape[1]), F32)

        def finish(i, _):
            rows = tile_at(i)
            z, root = normalize(total[rows, :])
            z2[rows, :] = z
            root2[rows, :] = jnp.broadcast_to(root, (TILE, 128))
            return 0

        lax.fori_loop(0, tiles, finish, 0)
        for s in range(pooled.shape[0]):
            n = table[LENS + s]
            valid = lax.broadcasted_iota(jnp.int32, (128, z2.shape[1]), 0) < n
            rows = jnp.where(valid, z2[rows_of(table, s), :], 0.0)
            mean = jnp.sum(rows, axis=0, keepdims=True) / n.astype(F32)
            pooled[s : s + 1, :] = mean * gain2[...] + bias2[...]


def send_rows(table, acc, source, mine, other, columns):
    chips, slab = mine.shape[0], mine.shape[2]
    core = table[CORE]
    for m in range(chips):
        base = (table[MASKS + m] * 2) * slab
        here = pl.multiple_of(base + core * slab, 8)
        there = pl.multiple_of(base + (1 - core) * slab, 8)
        mine[m, 0, :, columns] = acc[pl.ds(here, slab), source].astype(LOW)
        other[m, 0, :, columns] = acc[pl.ds(there, slab), source].astype(LOW)


def weight_grad(tiles, acc, left, right):
    acc[...] = jnp.zeros_like(acc)

    def step(i, _):
        rows = tile_at(i)
        acc[...] += mm(left[:, rows], right(rows))
        return 0

    lax.fori_loop(0, tiles, step, 0)


def down_backward(
    table, pool, z2, root2, gain2, active, mine, other, back, branch, sums, branch_t, acc
):
    tiles = table[TILES]
    width = z2.shape[1]

    @pl.when(pl.program_id(0) == 0)
    def _():
        back[...] = jnp.zeros_like(back)
        for s in range(pool.shape[0]):
            n = table[LENS + s]
            valid = lax.broadcasted_iota(jnp.int32, (128, width), 0) < n
            row = pool[s : s + 1, :] / n.astype(F32)
            back[rows_of(table, s), :] = jnp.where(valid, row, 0.0)
        sums[...] = jnp.zeros_like(sums)

        def start(i, _):
            rows = tile_at(i)
            grad = back[rows, :]
            z = z2[rows, :]
            sums[0:1, :] += jnp.sum(grad * z, axis=0, keepdims=True)
            sums[1:2, :] += jnp.sum(grad, axis=0, keepdims=True)
            value = normalize_back(z, root2[rows, 0:1], grad * gain2[...])
            low = value.astype(LOW)
            back[rows, :] = value
            branch[rows, :] = low
            branch_t[:, rows] = low.T
            return 0

        lax.fori_loop(0, tiles, start, 0)

    weight_grad(tiles, acc, branch_t, lambda rows: active[0, rows, :])
    send_rows(table, acc, slice(None), mine, other, slice(None))


def up_backward(
    table, back, branch, z1, root1, gain1, bias1, up, down, slope,
    mine, other, attn_grad, sums, bias_sum, first_t, hidden, total, acc,
):
    k = pl.program_id(0)
    tiles = table[TILES]

    @pl.when(k == 0)
    def _():
        sums[...] = jnp.zeros_like(sums)

        def start(i, _):
            rows = tile_at(i)
            first = (z1[rows, :] * gain1[...] + bias1[...]).astype(LOW)
            first_t[:, rows] = first.T
            total[rows, :] = back[rows, :]
            return 0

        lax.fori_loop(0, tiles, start, 0)

    bias_sum[...] = jnp.zeros_like(bias_sum)

    def work(i, _):
        rows = tile_at(i)
        grad = mm(branch[rows, :], down[0])
        hid = (slope[0, rows, :].astype(F32) * grad).astype(LOW)
        hidden[rows, :] = hid
        bias_sum[0] += jnp.sum(hid.astype(F32), axis=0, keepdims=True)
        total[rows, :] += mm(hid, up[0], NT)
        return 0

    lax.fori_loop(0, tiles, work, 0)
    weight_grad(tiles, acc, first_t, lambda rows: hidden[rows, :])
    send_rows(table, acc, slice(None), mine, other, slice(None))

    @pl.when(k == pl.num_programs(0) - 1)
    def _():
        def finish(i, _):
            rows = tile_at(i)
            grad = total[rows, :]
            z = z1[rows, :]
            sums[0:1, :] += jnp.sum(grad * z, axis=0, keepdims=True)
            sums[1:2, :] += jnp.sum(grad, axis=0, keepdims=True)
            attn_grad[rows, :] = normalize_back(z, root1[rows, 0:1], grad * gain1[...])
            return 0

        lax.fori_loop(0, tiles, finish, 0)


def attention_backward(table, attn_grad, proj, wide, proj_grad, attn_low, ctx_grad):
    length = proj.shape[0] - attn_grad.shape[0]
    sents = attn_grad.shape[0] // length
    tiles = table[TILES]
    width = attn_grad.shape[1]
    ctx_grad[...] = jnp.zeros_like(ctx_grad)
    proj_grad[...] = jnp.zeros_like(proj_grad)

    def start(i, _):
        rows = tile_at(i)
        low = attn_grad[rows, :].astype(LOW)
        attn_low[rows, :] = low
        ctx_grad[rows, :] = mm(low, wide[:, 3 * width :]).astype(LOW)
        return 0

    lax.fori_loop(0, tiles, start, 0)

    scale = HD**-0.5

    def attend(s, _):
        rows = rows_of(table, s)
        n = table[LENS + s]
        live = lax.broadcasted_iota(jnp.int32, (length, PAIR), 0) < n
        for p in range(width // PAIR):
            at = p * PAIR
            queries = proj[rows, at : at + PAIR]
            keys = split_heads(proj[rows, width + at : width + at + PAIR])
            values = split_heads(proj[rows, 2 * width + at : 2 * width + at + PAIR])
            grad = ctx_grad[rows, at : at + PAIR]
            grad = jnp.where(live, grad, jnp.zeros_like(grad))
            probs = softmax_pair(queries, keys, n)
            prob_grad = mm(grad, values, NT)
            score_grad = []
            for h in range(2):
                part = prob_grad[:, h * length : (h + 1) * length]
                inner = jnp.sum(probs[h] * part, axis=-1, keepdims=True)
                score_grad.append((probs[h] * (part - inner)).astype(LOW))
            probs_t = jnp.concatenate([q.astype(LOW).T for q in probs], axis=0)
            score_t = jnp.concatenate([q.T for q in score_grad], axis=0)
            score_grad = jnp.concatenate(score_grad, axis=1)
            proj_grad[rows, at : at + PAIR] = (mm(score_grad, keys) * scale).astype(LOW)
            proj_grad[rows, width + at : width + at + PAIR] = (
                join_heads(mm(score_t, queries)) * scale
            ).astype(LOW)
            proj_grad[rows, 2 * width + at : 2 * width + at + PAIR] = join_heads(
                mm(probs_t, grad)
            ).astype(LOW)
        return 0

    lax.fori_loop(0, sents, attend, 0)


def attention_weights(table, x, attn_low, ctx, proj_grad, mine, other, packed, packed_t, attn_t, acc):
    sents, length, width = x.shape
    tiles = table[TILES]
    packed[...] = jnp.zeros_like(packed)

    def place(s, _):
        packed[rows_of(table, s), :] = x[s]
        return 0

    lax.fori_loop(0, sents, place, 0)

    def flip(i, _):
        rows = tile_at(i)
        packed_t[:, rows] = packed[rows, :].T
        attn_t[:, rows] = attn_low[rows, :].T
        return 0

    lax.fori_loop(0, tiles, flip, 0)
    count = mine.shape[1]
    part = width // count
    for p in range(4):
        if p == 3:
            weight_grad(tiles, acc, attn_t, lambda rows: ctx[rows, :])
        else:
            cols = slice(p * width, (p + 1) * width)
            weight_grad(tiles, acc, packed_t, lambda rows: proj_grad[rows, cols])
        for k in range(count):
            send_rows(
                table,
                acc,
                slice(k * part, (k + 1) * part),
                mine.at[:, k : k + 1],
                other.at[:, k : k + 1],
                slice(p * part, (p + 1) * part),
            )


def input_backward(table, attn_grad, proj_grad, wide, *refs):
    outs, total = refs[:-1], refs[-1]
    sents, share, width = outs[0].shape
    length = share * len(outs)
    tiles = table[TILES]

    def finish(i, _):
        rows = tile_at(i)
        total[rows, :] = (
            attn_grad[rows, :] + mm(proj_grad[rows, :], wide[:, : 3 * width], NT)
        ).astype(LOW)
        return 0

    lax.fori_loop(0, tiles, finish, 0)
    total[pl.ds(pl.multiple_of(tiles * TILE, TILE), length), :] = jnp.zeros((length, width), LOW)
    for k, out in enumerate(outs):
        first = table[LINE + k] * share
        position = lax.broadcasted_iota(jnp.int32, (share, width), 0) + first
        for s in range(sents):
            value = total[pl.ds(pl.multiple_of(table[s] + first, 16), share), :]
            out[s] = jnp.where(position < table[LENS + s], value, jnp.zeros_like(value))


def place_grads(columns, table, *refs):
    pieces, (straight, turned, slabs, flat, sems) = refs[:-5], refs[-5:]
    count, slab = slabs.shape[0], slabs.shape[1]
    copies = place_pieces(table, pieces, slabs, sems)
    for copy in copies:
        copy.start()
    for copy in copies:
        copy.wait()
    width = straight.shape[1]
    for j in range(count):
        rows = slice(j * slab, (j + 1) * slab)
        for source, target, n in columns:
            straight[rows, target : target + n] = slabs[j, :, source : source + n].astype(F32)
        flat[rows, :] = slabs[j, :, width:].astype(F32)
    turned[...] = flat[...].T


SMEM = pl.BlockSpec(memory_space=pltpu.SMEM)
VMEM = pl.BlockSpec(memory_space=pltpu.VMEM)
ANY = pl.BlockSpec(memory_space=pl.ANY)


def shape(dims, dtype):
    return jax.ShapeDtypeStruct(dims, dtype)


def params():
    return pltpu.CompilerParams(vmem_limit_bytes=VMEM_BYTES)


def cost(flops, nbytes):
    return pl.CostEstimate(flops=flops, bytes_accessed=nbytes, transcendentals=0)


def add(*terms):
    return sum(term.astype(F32) for term in terms)


def swap(value, mask, axis="dp"):
    return lax.ppermute(value, axis, [(i, i ^ mask) for i in range(lax.axis_size(axis))])


def bits_of(count):
    return [1 << i for i in range(count.bit_length() - 1)]


def take(values, index, axis=0):
    return lax.dynamic_index_in_dim(values, index, axis, False, allow_negative_indices=False)


def cut(values, start, size, axis):
    return lax.dynamic_slice_in_dim(values, start, size, axis, allow_negative_indices=False)


def tie(*values):
    return lax.optimization_barrier(values)


def by_index(values, me):
    n = values.shape[0]
    for bit in bits_of(n):
        view = values.reshape((n // (2 * bit), 2, bit) + values.shape[1:])
        flipped = jnp.concatenate([view[:, 1:], view[:, :1]], axis=1)
        values = jnp.where((me & bit) != 0, flipped, view).reshape(values.shape)
    return values


def gather_line(piece):
    n = lax.axis_size("tensor")
    return jnp.concatenate([swap(piece, k, "tensor") for k in range(1, n)], axis=1)


def gather_chips(value):
    return [value] + [swap(value, 2 * m) for m in range(1, lax.axis_size("dp") // 2)]


def gather_cores(near):
    return near + [swap(item, 1) for item in near]


def gather_plane(value):
    return gather_cores(gather_chips(value))


def pick(term, side, bit):
    dims = term.shape
    view = term.reshape((dims[0] // (2 * bit), 2, bit) + dims[1:])[:, side]
    return view.reshape((dims[0] // 2,) + dims[1:])


def sent(terms, bit):
    return add(*[pick(term, 1, bit) for term in terms]).astype(LOW)


def kept(terms, bit, landed):
    return [pick(term, 0, bit) for term in terms] + [landed]


def reduce_line(terms):
    for bit in bits_of(lax.axis_size("tensor")):
        terms = kept(terms, 1, swap(sent(terms, 1), bit, "tensor"))
    return add(*terms)[0].astype(LOW)


def reduce_chips(terms, bits, falling):
    for bit in bits:
        at = bit if falling else 1
        terms = kept(terms, at, swap(sent(terms, at), 2 * bit))
    return terms


def shards(
    tokens,
    lengths,
    partner,
    w_qkv,
    w_out,
    ln1_gain,
    ln1_bias,
    up_weight,
    up_projection_bias,
    down_weight,
    ln2_gain,
    ln2_bias,
    cot_pooled,
    cot_paired,
):
    dp_count = lax.axis_size("dp")
    t_count = lax.axis_size("tensor")
    dp_me = lax.axis_index("dp")
    t_me = lax.axis_index("tensor")
    length, sentences, width = tokens.shape
    mine = sentences // t_count
    rows = mine * length
    pad = rows + length
    slab = width // dp_count
    chips = dp_count // 2
    heads = w_qkv.shape[1] // (3 * HD)
    units = up_weight.shape[1]
    ctx_cols = w_out.shape[0]
    block = 4 * ctx_cols

    def by_part(weight):
        return weight.reshape(-1, heads, 3, HD).transpose(0, 2, 1, 3).reshape(weight.shape)

    def rows_piece(weight):
        return cut(weight, dp_me * slab, slab, 0)

    def columns_piece(weight):
        return cut(weight, dp_me * slab, slab, 1).T

    attn_piece = jnp.concatenate([by_part(rows_piece(w_qkv)), columns_piece(w_out)], axis=1)
    ffn_piece = jnp.concatenate([rows_piece(up_weight), columns_piece(down_weight)], axis=1)
    attn_piece, ffn_piece, tokens, w_qkv, up_weight, up_projection_bias, cot_paired = tie(
        attn_piece, ffn_piece, tokens, w_qkv, up_weight, up_projection_bias, cot_paired
    )
    attn_line = gather_line(attn_piece)
    ffn_line = gather_line(ffn_piece)
    attn_line, ffn_piece, cot_paired, up_projection_bias = tie(
        attn_line, ffn_piece, cot_paired, up_projection_bias
    )
    attn_pieces = gather_plane(attn_line)
    attn_own = jnp.concatenate([by_part(w_qkv), w_out.T], axis=1)
    ffn_own = jnp.concatenate([up_weight, down_weight.T], axis=1)
    bias_own = up_projection_bias.reshape(1, units)
    bias_all = jnp.stack([bias_own] + [swap(bias_own, k, "tensor") for k in range(1, t_count)])

    x = cut(tokens, t_me * mine, mine, 1).transpose(1, 0, 2)
    counts = cut(lengths, t_me * mine, mine, 0)
    taken = (counts + 15) & ~15
    ends = jnp.sum(jnp.where(np.tri(mine, dtype=bool), taken[None, :], 0), axis=1)
    devices = np.arange(dp_count)
    distance = 2 * np.arange(chips)
    near = devices[:, None] ^ distance[None, :]
    spots = np.concatenate([near, near ^ 1], axis=1)
    lines = np.arange(t_count)[:, None] ^ np.arange(t_count)[None, :]
    fixed = np.zeros((dp_count, PLACE - MASKS + dp_count), np.int32)
    fixed[:, :chips] = near // 2
    fixed[:, PLACE - MASKS :] = spots
    line_fixed = np.zeros((t_count, MASKS - LINE), np.int32)
    line_fixed[:, :t_count] = lines
    table = jnp.concatenate(
        [
            ends - taken,
            np.zeros(LENS - mine, np.int32),
            counts,
            np.zeros(TILES - LENS - mine, np.int32),
            (ends[-1:] + (TILE - 1)) >> (TILE.bit_length() - 1),
            (dp_me & 1).reshape(1),
            take(jnp.asarray(line_fixed), t_me),
            take(jnp.asarray(fixed), dp_me),
        ]
    ).astype(jnp.int32)

    ffn_chips = gather_chips(ffn_line)
    attn_pieces[0], ffn_chips[0] = tie(attn_pieces[0], ffn_chips[0])
    proj, ctx, z1, root1, wide = pl.pallas_call(
        attention_forward,
        out_shape=(
            shape((pad, 3 * width), LOW),
            shape((pad, width), LOW),
            shape((rows, width), F32),
            shape((rows, 128), F32),
            shape((width, 4 * width), LOW),
        ),
        in_specs=[SMEM, VMEM, VMEM] + [ANY] * dp_count,
        out_specs=(VMEM,) * 5,
        scratch_shapes=[
            pltpu.VMEM((pad, width), LOW),
            pltpu.VMEM((dp_count, slab, (t_count - 1) * block), LOW),
            pltpu.SemaphoreType.DMA((dp_count,)),
        ],
        compiler_params=params(),
        cost_estimate=cost(8 * rows * width * width, 30 * rows * width),
        name="attention_forward",
    )(table, x, attn_own, *attn_pieces)
    *ffn_chips, z1 = tie(*ffn_chips, z1)
    ffn_pieces = gather_cores(ffn_chips)
    cot_pieces = gather_plane(cot_paired)

    gain1, bias1 = ln1_gain.reshape(1, width), ln1_bias.reshape(1, width)
    gain2, bias2 = ln2_gain.reshape(1, width), ln2_bias.reshape(1, width)

    def whole(*dims):
        return pl.BlockSpec(dims, lambda k, table: (0,) * len(dims))

    def call(kernel, outs, ins, out_specs, scratch, flops, nbytes):
        return pl.pallas_call(
            kernel,
            out_shape=outs,
            grid_spec=pltpu.PrefetchScalarGridSpec(
                num_scalar_prefetch=1,
                grid=(t_count,),
                in_specs=ins,
                out_specs=out_specs,
                scratch_shapes=scratch,
            ),
            compiler_params=params(),
            cost_estimate=cost(flops, nbytes),
            name=kernel.__name__,
        )

    act_spec = pl.BlockSpec((1, rows, units), lambda k, table: (k, 0, 0))
    up_spec = pl.BlockSpec((1, width, units), lambda k, table: (k, 0, 0))
    down_spec = pl.BlockSpec((1, width, units), lambda k, table: (k, 0, 1))
    bias_spec = pl.BlockSpec((1, 1, units), lambda k, table: (k, 0, 0))
    line = whole(1, width)
    full = whole(rows, width)
    full_pad = whole(pad, width)
    root_spec = whole(rows, 128)
    act_shape = shape((t_count, rows, units), LOW)
    active, slope, z2, root2, pooled, ffn_all = call(
        ffn_forward,
        (
            act_shape,
            act_shape,
            shape((pad, width), F32),
            shape((rows, 128), F32),
            shape((mine, width), F32),
            shape((t_count, width, 2 * units), LOW),
        ),
        [full, line, line, whole(width, 2 * units), bias_spec, line, line] + [ANY] * dp_count,
        (
            act_spec,
            act_spec,
            full_pad,
            root_spec,
            whole(mine, width),
            pl.BlockSpec((1, width, 2 * units), lambda k, table: (k, 0, 0)),
        ),
        [
            pltpu.VMEM((rows, width), LOW),
            pltpu.VMEM((rows, width), F32),
            pltpu.VMEM((dp_count, slab, (t_count - 1) * 2 * units), LOW),
            pltpu.SemaphoreType.DMA((dp_count,)),
        ],
        4 * rows * width * units * t_count,
        40 * rows * width,
    )(table, z1, gain1, bias1, ffn_own, bias_all, gain2, bias2, *ffn_pieces)

    pooled = pooled.astype(LOW)
    line_pooled = jnp.stack([pooled] + [swap(pooled, k, "tensor") for k in range(1, t_count)])
    everyone = jnp.stack(gather_plane(line_pooled)).reshape(-1, width)
    cot_all = jnp.stack(cot_pieces).reshape(-1, width)
    home_device = partner // sentences
    apart = home_device ^ dp_me
    where_device = apart % 2 * chips + apart // 2
    inside = partner % sentences
    partner_pooled = everyone[
        (where_device * t_count + (inside // mine ^ t_me)) * mine + inside % mine
    ].astype(F32)
    partner_cot = cot_all[where_device * sentences + inside].astype(F32)
    returned = by_index(line_pooled, t_me).reshape(sentences, width)
    paired = (returned.astype(F32) * partner_pooled).astype(LOW)
    pool_grad = cot_pooled.astype(F32) + partner_pooled * (cot_paired.astype(F32) + partner_cot)
    pool_grad = cut(pool_grad.astype(LOW).astype(F32), t_me * mine, mine, 0)

    send_spec = pl.BlockSpec((chips, 1, slab, units), lambda k, table: (0, k, 0, 0))
    send_shape = shape((chips, t_count, slab, units), LOW)
    down_mine, down_other, back, branch, sums_two = call(
        down_backward,
        (
            send_shape,
            send_shape,
            shape((pad, width), F32),
            shape((rows, width), LOW),
            shape((2, width), F32),
        ),
        [whole(mine, width), full_pad, root_spec, line, act_spec],
        (send_spec, send_spec, full_pad, full, whole(2, width)),
        [pltpu.VMEM((width, rows), LOW), pltpu.VMEM((width, units), F32)],
        2 * rows * width * units * t_count,
        40 * rows * width,
    )(table, pool_grad, z2, root2, gain2, active)

    chip_bits = bits_of(chips)
    first_bits, last_bits = chip_bits[:1], chip_bits[1:]
    down_terms = [down_mine, swap(down_other, 1)]
    down_sent, branch = tie(sent(down_terms, 1), branch)
    down_got = swap(down_sent, 2)

    up_mine, up_other, attn_grad, sums_one, bias_sum = call(
        up_backward,
        (
            send_shape,
            send_shape,
            shape((rows, width), F32),
            shape((2, width), F32),
            shape((t_count, 1, units), F32),
        ),
        [full_pad, full, full, root_spec, line, line, up_spec, down_spec, act_spec],
        (send_spec, send_spec, full, whole(2, width), bias_spec),
        [
            pltpu.VMEM((width, rows), LOW),
            pltpu.VMEM((rows, units), LOW),
            pltpu.VMEM((rows, width), F32),
            pltpu.VMEM((width, units), F32),
        ],
        6 * rows * width * units * t_count,
        40 * rows * width,
    )(table, back, branch, z1, root1, gain1, bias1, ffn_all, ffn_all, slope)

    down_got, up_other = tie(down_got, up_other)
    up_terms = [up_mine, swap(up_other, 1)]
    down_terms = kept(down_terms, 1, down_got)
    top = chip_bits[-1]
    down_sent, up_sent, attn_grad = tie(sent(down_terms, 1), sent(up_terms, top), attn_grad)
    down_got, up_got = swap(down_sent, 2 * chip_bits[1]), swap(up_sent, 2 * top)

    proj_grad, attn_low = pl.pallas_call(
        attention_backward,
        out_shape=(shape((pad, 3 * width), LOW), shape((rows, width), LOW)),
        in_specs=[SMEM] + [VMEM] * 3,
        out_specs=(VMEM,) * 2,
        scratch_shapes=[pltpu.VMEM((pad, width), LOW)],
        compiler_params=params(),
        cost_estimate=cost(6 * rows * width * width, 30 * rows * width),
        name="attention_backward",
    )(table, attn_grad, proj, wide)
    down_got, up_got, proj_grad = tie(down_got, up_got, proj_grad)
    down_terms = reduce_chips(kept(down_terms, 1, down_got), chip_bits[2:], False)
    up_terms = kept(up_terms, top, up_got)
    at = chip_bits[-2]
    down_line = [add(*down_terms)[0].astype(LOW)]
    down_sent, up_sent, proj_grad = tie(sent(down_line, 1), sent(up_terms, at), proj_grad)
    down_got, up_got = swap(down_sent, 1, "tensor"), swap(up_sent, 2 * at)

    attn_mine, attn_other = pl.pallas_call(
        attention_weights,
        out_shape=(shape((chips, t_count, slab, block), LOW),) * 2,
        in_specs=[SMEM] + [VMEM] * 4,
        out_specs=(VMEM,) * 2,
        scratch_shapes=[
            pltpu.VMEM((pad, width), LOW),
            pltpu.VMEM((width, rows), LOW),
            pltpu.VMEM((width, rows), LOW),
            pltpu.VMEM((width, width), F32),
        ],
        compiler_params=params(),
        cost_estimate=cost(8 * rows * width * width, 30 * rows * width),
        name="attention_weights",
    )(table, x, attn_low, ctx, proj_grad)
    down_got, up_got, attn_other = tie(down_got, up_got, attn_other)
    attn_got = swap(attn_other, 1)
    attn_sent = [add(attn_mine[m], attn_got[m]).astype(LOW) for m in range(1, chips)]
    down_line = kept(down_line, 1, down_got)
    down_sent = sent(down_line, 1)
    up_terms = reduce_chips(kept(up_terms, at, up_got), chip_bits[:-2][::-1], True)
    up_line = [add(*up_terms)[0].astype(LOW)]
    *attn_sent, down_sent, up_sent, attn_grad = tie(*attn_sent, down_sent, sent(up_line, 1), attn_grad)
    attn_got = [attn_got[0]] + [swap(item, 2 * m) for m, item in zip(range(1, chips), attn_sent)]
    down_got, up_got = swap(down_sent, 2, "tensor"), swap(up_sent, 1, "tensor")

    share = length // t_count
    input_blocks = pl.pallas_call(
        input_backward,
        out_shape=(shape((mine, share, width), LOW),) * t_count,
        in_specs=[SMEM] + [VMEM] * 3,
        out_specs=(VMEM,) * t_count,
        scratch_shapes=[pltpu.VMEM((pad, width), LOW)],
        compiler_params=params(),
        cost_estimate=cost(6 * rows * width * width, 20 * rows * width),
        name="input_backward",
    )(table, attn_grad, proj_grad, wide)

    input_landed = [input_blocks[0]]
    input_landed += [swap(input_blocks[k], k, "tensor") for k in range(1, t_count)]

    def finish(pieces, columns, straight, turned):
        piece = pieces[0].shape
        return pl.pallas_call(
            functools.partial(place_grads, columns),
            out_shape=(shape((width, straight), F32), shape((turned, width), F32)),
            in_specs=[SMEM] + [ANY] * dp_count,
            out_specs=(VMEM,) * 2,
            scratch_shapes=[
                pltpu.VMEM((dp_count,) + piece, LOW),
                pltpu.VMEM((width, turned), F32),
                pltpu.SemaphoreType.DMA((dp_count,)),
            ],
            compiler_params=params(),
            cost_estimate=cost(0, 8 * width * (straight + turned)),
            name="place_grads",
        )(table, *pieces)

    def rest(line, done):
        for bit in bits_of(t_count)[done:]:
            line = kept(line, 1, swap(sent(line, 1), bit, "tensor"))
        return add(*line)[0].astype(LOW)

    down_sum = rest(kept(down_line, 1, down_got), 2)
    up_sum = rest(kept(up_line, 1, up_got), 1)
    up_grad, down_grad = finish(
        gather_plane(jnp.concatenate([up_sum, down_sum], 1)), [(0, 0, units)], units, units
    )
    attn_line = [add(attn_mine[0], *attn_got).astype(LOW)]
    qkv_columns = [
        ((p * heads + h) * HD, (h * 3 + p) * HD, HD) for h in range(heads) for p in range(3)
    ]
    qkv_grad, out_grad = finish(
        gather_plane(rest(attn_line, 0)), qkv_columns, 3 * ctx_cols, ctx_cols
    )
    home = by_index(jnp.stack(input_landed), t_me)
    home = home.reshape(sentences, share, width).transpose(1, 0, 2)

    small = jnp.concatenate([bias_sum.reshape(t_count, units), sums_one, sums_two])
    for mask in bits_of(dp_count):
        small = small + swap(small, mask)
    norms, bias_part = small[t_count:], small[:t_count]
    for mask in bits_of(t_count):
        half = bias_part.shape[0] // 2
        split = bias_part.reshape(half, 2, units)
        got = swap(jnp.concatenate([split[:, 1], norms]), mask, "tensor")
        bias_part = split[:, 0] + got[:half]
        norms = norms + got[half:]

    return (
        returned,
        paired,
        home,
        qkv_grad,
        out_grad,
        norms[0],
        norms[1],
        up_grad,
        bias_part[0],
        down_grad,
        norms[2],
        norms[3],
    )


def solution(mesh):
    placed = (
        P(None, "dp", None),
        P("dp"),
        P("dp"),
        P(None, "tensor"),
        P("tensor", None),
        P(),
        P(),
        P(None, "tensor"),
        P("tensor"),
        P("tensor", None),
        P(),
        P(),
        P("dp", None),
        P("dp", None),
    )
    return jax.shard_map(
        shards,
        mesh=mesh,
        in_specs=placed,
        out_specs=(
            P("dp", None),
            P("dp", None),
            P("tensor", "dp", None),
            P(None, "tensor"),
            P("tensor", None),
            P(),
            P(),
            P(None, "tensor"),
            P("tensor"),
            P("tensor", None),
            P(),
            P(),
        ),
        check_vma=False,
    )
```

```python
import functools

import jax
import jax.numpy as jnp
import numpy as np
from jax import lax
from jax.experimental import pallas as pl
from jax.experimental.pallas import tpu as pltpu
from jax.sharding import PartitionSpec as P

HD = 64
EPSILON = 1e-06
LOW = jnp.bfloat16
F32 = jnp.float32
INV_SQRT_2PI = 0.3989422804014327
SQRT_HALF = 0.7071067811865476
TILE = 256
CHUNK = 256
MASKED = -1000000000.0
LOG2_E = 1.4426950408889634
VMEM_BYTES = 60 * 2**20
NN = (((1,), (0,)), ((), ()))
NT = (((1,), (1,)), ((), ()))
PAIR = 2 * HD
LENS, TILES, LINE, PLACE, DEST = 16, 32, 33, 48, 80


def mm(a, b, dims=NN):
    return lax.dot_general(a, b, dims, preferred_element_type=F32)


def rows_of(table, s):
    return pl.ds(pl.multiple_of(table[s], 16), 128)


def tile_at(i):
    return pl.ds(pl.multiple_of(i * TILE, TILE), TILE)


def normalize(values):
    center = values - jnp.mean(values, axis=-1, keepdims=True)
    spread = jnp.mean(center * center, axis=-1, keepdims=True)
    root = lax.rsqrt(spread + EPSILON)
    return center * root, root


def normalize_back(z, root, dz):
    return root * (
        dz - jnp.mean(dz, -1, keepdims=True) - z * jnp.mean(dz * z, -1, keepdims=True)
    )


def split_heads(pair):
    first = lax.broadcasted_iota(jnp.int32, pair.shape, 1) < HD
    zero = jnp.zeros_like(pair)
    return jnp.concatenate([jnp.where(first, pair, zero), jnp.where(first, zero, pair)], axis=0)


def join_heads(split):
    n = split.shape[0] // 2
    first = lax.broadcasted_iota(jnp.int32, (n, PAIR), 1) < HD
    return jnp.where(first, split[:n], split[n:])


def place_pieces(table, pieces, slabs, sems):
    copies = []
    for i, piece in enumerate(pieces):
        copies.append(pltpu.make_async_copy(piece, slabs.at[table[PLACE + i]], sems.at[i]))
    return copies


def turn(table, turned, rows, value):
    flat = value.T
    count, slab = turned.shape[0], turned.shape[1]
    for j in range(count):
        turned[table[DEST + j], :, rows] = flat[j * slab : (j + 1) * slab, :]


def pack(table, x, packed, packed_t):
    packed[...] = jnp.zeros_like(packed)

    def place(s, _):
        packed[rows_of(table, s), :] = x[s]
        return 0

    lax.fori_loop(0, x.shape[0], place, 0)

    def flip(i, _):
        rows = tile_at(i)
        turn(table, packed_t, rows, packed[rows, :])
        return 0

    lax.fori_loop(0, table[TILES], flip, 0)


def start_all(copies):
    for copy in copies:
        copy.start()


def wait_all(copies):
    for copy in copies:
        copy.wait()


def attention_forward(table, packed, own_qkv, own_out, *refs):
    pieces, refs = refs[:-16], refs[-16:]
    proj_out, ctx_out, probs_out, qkv_out, wo_out, z1, root1 = refs[:7]
    proj, ctx, probs, qkv, wo, slabs, sems, out_sems, wide_sems = refs[7:]
    sents, pairs = probs.shape[0], probs.shape[1]
    width = packed.shape[1]
    length = probs.shape[3]
    part = own_out.shape[0]
    block = 4 * part
    heads = part // HD
    arrivals = place_pieces(table, pieces, slabs, sems)
    start_all(arrivals)
    count, slab = slabs.shape[0], slabs.shape[1]
    for h in range(heads):
        for p in range(3):
            source = (h * 3 + p) * HD
            qkv[:, p * width + h * HD : p * width + (h + 1) * HD] = own_qkv[
                source : source + HD, :
            ].T
    wo[:, :part] = own_out[...].T
    ctx[...] = jnp.zeros_like(ctx)
    tiles = table[TILES]
    end = pl.ds(pl.multiple_of(tiles * TILE, TILE), length)
    proj[end, :] = jnp.zeros((length, 3 * width), LOW)
    wait_all(arrivals)
    for j in range(count):
        rows = slice(j * slab, (j + 1) * slab)
        for k in range(1, width // part):
            base = (k - 1) * block
            for p in range(3):
                qkv[rows, p * width + k * part : p * width + (k + 1) * part] = slabs[
                    j, :, base + p * part : base + (p + 1) * part
                ]
            wo[rows, k * part : (k + 1) * part] = slabs[j, :, base + 3 * part : base + block]
    wide_copies = [
        pltpu.make_async_copy(qkv, qkv_out, wide_sems.at[0]),
        pltpu.make_async_copy(wo, wo_out, wide_sems.at[1]),
    ]
    start_all(wide_copies)

    def project(i, _):
        rows = tile_at(i)
        source = packed[rows, :]
        for p in range(3):
            cols = slice(p * width, (p + 1) * width)
            proj[rows, cols] = mm(source, qkv[:, cols]).astype(LOW)
        return 0

    lax.fori_loop(0, tiles, project, 0)
    proj_copy = pltpu.make_async_copy(proj, proj_out, out_sems.at[0])
    proj_copy.start()

    def attend(s, _):
        rows = rows_of(table, s)
        valid = lax.broadcasted_iota(jnp.int32, (length, length), 0) < table[LENS + s]
        for p in range(pairs):
            at = p * PAIR
            queries = proj[rows, at : at + PAIR]
            keys = split_heads(proj[rows, width + at : width + at + PAIR])
            values = split_heads(proj[rows, 2 * width + at : 2 * width + at + PAIR])
            scores = mm(keys, queries, NT)
            for h in range(2):
                half = slice(h * length, (h + 1) * length)
                score = jnp.where(valid, scores[half], MASKED)
                top = jnp.max(score, axis=0, keepdims=True)
                score = jnp.exp2((score - top) * (HD**-0.5 * LOG2_E))
                total = jnp.sum(score, axis=0, keepdims=True)
                probs[s, p, half, :] = (score * (1.0 / total)).astype(LOW)
            ctx[rows, at : at + PAIR] = mm(probs[s, p].T, values).astype(LOW)
        return 0

    lax.fori_loop(0, sents, attend, 0)
    ctx_copies = [
        pltpu.make_async_copy(ctx, ctx_out, out_sems.at[1]),
        pltpu.make_async_copy(probs, probs_out, out_sems.at[2]),
    ]
    start_all(ctx_copies)

    def finish(i, _):
        rows = tile_at(i)
        attended = mm(ctx[rows, :], wo[...], NT)
        z, root = normalize(packed[rows, :].astype(F32) + attended)
        z1[rows, :] = z
        root1[rows, :] = jnp.broadcast_to(root, (TILE, 128))
        return 0

    lax.fori_loop(0, tiles, finish, 0)
    wait_all(wide_copies + [proj_copy] + ctx_copies)


def gelu_parts(pre):
    t = pl.reciprocal(1.0 + jnp.abs(pre) * (0.3275911 * SQRT_HALF))
    poly = 0.5 * 1.061405429
    for c in (-1.453152027, 1.421413741, -0.284496736, 0.254829592):
        poly = poly * t + 0.5 * c
    e = jnp.exp2(pre * pre * (-0.5 * LOG2_E))
    tail = poly * t * e
    cdf = jnp.where(pre >= 0.0, 1.0 - tail, tail)
    return pre * cdf, cdf + pre * (e * INV_SQRT_2PI)


def ffn_forward(table, z1, gain1, bias1, own_up, own_down, bias, gain2, bias2, *refs):
    pieces, refs = refs[:-10], refs[-10:]
    active, slope, z2, root2, pooled, weight, first, total, slabs, sems = refs
    k = pl.program_id(0)
    tiles = table[TILES]
    count, slab = slabs.shape[0], slabs.shape[1]
    units = active.shape[2]

    @pl.when(k == 0)
    def _():
        for copy in place_pieces(table, pieces, slabs, sems):
            copy.start()
        weight[0, :, :units] = own_up[...]
        weight[0, :, units:] = own_down[...].T

    @pl.when(k == 1)
    def _():
        for copy in place_pieces(table, pieces, slabs, sems):
            copy.wait()

    for t in range(1, pl.num_programs(0)):

        @pl.when(k == t)
        def _():
            for j in range(count):
                weight[0, j * slab : (j + 1) * slab, :] = slabs[
                    j, :, (t - 1) * 2 * units : t * 2 * units
                ]

    @pl.when(k == 0)
    def _():
        def start(i, _):
            rows = tile_at(i)
            value = z1[rows, :] * gain1[...] + bias1[...]
            first[rows, :] = value.astype(LOW)
            total[rows, :] = value
            return 0

        lax.fori_loop(0, tiles, start, 0)

    def work(i, _):
        rows = tile_at(i)
        source = first[rows, :]
        for c in range(0, units, CHUNK):
            cols = slice(c, c + CHUNK)
            act, slp = gelu_parts(mm(source, weight[0, :, cols]) + bias[0, :, cols])
            active[0, rows, cols] = act.astype(LOW)
            slope[0, rows, cols] = slp.astype(LOW)
        total[rows, :] += mm(active[0, rows, :], weight[0, :, units:], NT)
        return 0

    lax.fori_loop(0, tiles, work, 0)

    @pl.when(k == pl.num_programs(0) - 1)
    def _():
        z2[pl.ds(pl.multiple_of(tiles * TILE, TILE), 128), :] = jnp.zeros((128, z2.shape[1]), F32)

        def finish(i, _):
            rows = tile_at(i)
            z, root = normalize(total[rows, :])
            z2[rows, :] = z
            root2[rows, :] = jnp.broadcast_to(root, (TILE, 128))
            return 0

        lax.fori_loop(0, tiles, finish, 0)
        for s in range(pooled.shape[0]):
            n = table[LENS + s]
            valid = lax.broadcasted_iota(jnp.int32, (128, z2.shape[1]), 0) < n
            rows = jnp.where(valid, z2[rows_of(table, s), :], 0.0)
            mean = jnp.sum(rows, axis=0, keepdims=True) / n.astype(F32)
            pooled[s : s + 1, :] = mean * gain2[...] + bias2[...]


def weight_grad(tiles, turned, right, store):
    count, slab, rows = turned.shape
    for n in range(1, rows // TILE + 1):

        @pl.when(tiles == n)
        def _():
            if slab % 16 == 0:
                left = turned[:, :, : n * TILE].reshape(count * slab, n * TILE)
            else:
                left = jnp.concatenate([turned[j, :, : n * TILE] for j in range(count)], axis=0)
            store(lambda columns: mm(left, right(n * TILE, columns)))


def split_send(mine, other, value, k, columns):
    chips, slab = mine.shape[0], mine.shape[2]
    for m in range(chips):
        mine[m, k, :, columns] = value[m * slab : (m + 1) * slab].astype(LOW)
        other[m, k, :, columns] = value[(chips + m) * slab : (chips + m + 1) * slab].astype(LOW)


def send_chunks(mine, other, product):
    for c in range(0, mine.shape[3], CHUNK):
        cols = slice(c, c + CHUNK)
        split_send(mine, other, product(cols), 0, cols)


def down_backward(
    table, pool, z2, root2, gain2, active, mine, other, back, branch, sums, branch_t
):
    tiles = table[TILES]
    width = z2.shape[1]

    @pl.when(pl.program_id(0) == 0)
    def _():
        back[...] = jnp.zeros_like(back)
        for s in range(pool.shape[0]):
            n = table[LENS + s]
            valid = lax.broadcasted_iota(jnp.int32, (128, width), 0) < n
            row = pool[s : s + 1, :] / n.astype(F32)
            back[rows_of(table, s), :] = jnp.where(valid, row, 0.0)
        sums[...] = jnp.zeros_like(sums)

        def start(i, _):
            rows = tile_at(i)
            grad = back[rows, :]
            z = z2[rows, :]
            sums[0:1, :] += jnp.sum(grad * z, axis=0, keepdims=True)
            sums[1:2, :] += jnp.sum(grad, axis=0, keepdims=True)
            value = normalize_back(z, root2[rows, 0:1], grad * gain2[...])
            low = value.astype(LOW)
            back[rows, :] = value
            branch[rows, :] = low
            turn(table, branch_t, rows, low)
            return 0

        lax.fori_loop(0, tiles, start, 0)

    weight_grad(
        tiles,
        branch_t,
        lambda n, cols: active[0, :n, cols],
        lambda product: send_chunks(mine, other, product),
    )


def up_backward(
    table, back, branch, z1, root1, gain1, bias1, up, down, slope,
    mine, other, attn_grad, attn_low, attn_t, sums, bias_sum, first_t, hidden, total,
):
    k = pl.program_id(0)
    tiles = table[TILES]

    @pl.when(k == 0)
    def _():
        sums[...] = jnp.zeros_like(sums)

        def start(i, _):
            rows = tile_at(i)
            first = (z1[rows, :] * gain1[...] + bias1[...]).astype(LOW)
            turn(table, first_t, rows, first)
            total[rows, :] = back[rows, :]
            return 0

        lax.fori_loop(0, tiles, start, 0)

    bias_sum[...] = jnp.zeros_like(bias_sum)

    def work(i, _):
        rows = tile_at(i)
        source = branch[rows, :]
        for c in range(0, hidden.shape[1], CHUNK):
            cols = slice(c, c + CHUNK)
            grad = mm(source, down[0, :, cols])
            hid = (slope[0, rows, cols].astype(F32) * grad).astype(LOW)
            hidden[rows, cols] = hid
            bias_sum[0, :, cols] += jnp.sum(hid.astype(F32), axis=0, keepdims=True)
        total[rows, :] += mm(hidden[rows, :], up[0], NT)
        return 0

    lax.fori_loop(0, tiles, work, 0)
    weight_grad(
        tiles,
        first_t,
        lambda n, cols: hidden[:n, cols],
        lambda product: send_chunks(mine, other, product),
    )

    @pl.when(k == pl.num_programs(0) - 1)
    def _():
        def finish(i, _):
            rows = tile_at(i)
            grad = total[rows, :]
            z = z1[rows, :]
            sums[0:1, :] += jnp.sum(grad * z, axis=0, keepdims=True)
            sums[1:2, :] += jnp.sum(grad, axis=0, keepdims=True)
            value = normalize_back(z, root1[rows, 0:1], grad * gain1[...])
            low = value.astype(LOW)
            attn_grad[rows, :] = value
            attn_low[rows, :] = low
            turn(table, attn_t, rows, low)
            return 0

        lax.fori_loop(0, tiles, finish, 0)


def attention_backward(
    table, attn_low, wo, proj_in, probs_in, proj_grad, ctx_grad, proj, probs, sems
):
    sents, pairs = probs.shape[0], probs.shape[1]
    length = probs.shape[3]
    width = attn_low.shape[1]
    tiles = table[TILES]
    arrivals = [
        pltpu.make_async_copy(proj_in, proj, sems.at[0]),
        pltpu.make_async_copy(probs_in, probs, sems.at[1]),
    ]
    start_all(arrivals)
    ctx_grad[...] = jnp.zeros_like(ctx_grad)
    proj_grad[...] = jnp.zeros_like(proj_grad)

    def start(i, _):
        rows = tile_at(i)
        ctx_grad[rows, :] = mm(attn_low[rows, :], wo[...]).astype(LOW)
        return 0

    lax.fori_loop(0, tiles, start, 0)
    wait_all(arrivals)
    scale = HD**-0.5

    def attend(s, _):
        rows = rows_of(table, s)
        live = lax.broadcasted_iota(jnp.int32, (length, PAIR), 0) < table[LENS + s]
        for p in range(pairs):
            at = p * PAIR
            queries = proj[rows, at : at + PAIR]
            keys = split_heads(proj[rows, width + at : width + at + PAIR])
            values = split_heads(proj[rows, 2 * width + at : 2 * width + at + PAIR])
            grad = ctx_grad[rows, at : at + PAIR]
            grad = jnp.where(live, grad, jnp.zeros_like(grad))
            prob_grad = mm(values, grad, NT)
            score_grad = []
            for h in range(2):
                half = slice(h * length, (h + 1) * length)
                prob = probs[s, p, half, :].astype(F32)
                part = prob_grad[half]
                inner = jnp.sum(prob * part, axis=0, keepdims=True)
                score_grad.append((prob * (part - inner)).astype(LOW))
            score_grad = jnp.concatenate(score_grad, axis=0)
            proj_grad[rows, at : at + PAIR] = (mm(score_grad.T, keys) * scale).astype(LOW)
            proj_grad[rows, width + at : width + at + PAIR] = (
                join_heads(mm(score_grad, queries)) * scale
            ).astype(LOW)
            proj_grad[rows, 2 * width + at : 2 * width + at + PAIR] = join_heads(
                mm(probs[s, p], grad)
            ).astype(LOW)
        return 0

    lax.fori_loop(0, sents, attend, 0)


def attention_weights(table, packed_t, attn_t, ctx, proj_grad, mine, other):
    tiles = table[TILES]
    width = ctx.shape[1]
    count = mine.shape[1]
    part = width // count

    def store(p, product):
        value = product(slice(p * width, (p + 1) * width) if p < 3 else slice(None))
        for k in range(count):
            split_send(
                mine,
                other,
                value[:, k * part : (k + 1) * part],
                k,
                slice(p * part, (p + 1) * part),
            )

    weight_grad(
        tiles, attn_t, lambda n, cols: ctx[:n, cols], lambda product: store(3, product)
    )
    for p in range(3):
        weight_grad(
            tiles,
            packed_t,
            lambda n, cols: proj_grad[:n, cols],
            lambda product: store(p, product),
        )


def input_backward(table, attn_grad, proj_grad, qkv, *refs):
    outs, total = refs[:-1], refs[-1]
    sents, share, width = outs[0].shape
    length = share * len(outs)
    tiles = table[TILES]

    def finish(i, _):
        rows = tile_at(i)
        total[rows, :] = (
            attn_grad[rows, :] + mm(proj_grad[rows, :], qkv[...], NT)
        ).astype(LOW)
        return 0

    lax.fori_loop(0, tiles, finish, 0)
    total[pl.ds(pl.multiple_of(tiles * TILE, TILE), length), :] = jnp.zeros((length, width), LOW)
    for k, out in enumerate(outs):
        first = table[LINE + k] * share
        position = lax.broadcasted_iota(jnp.int32, (share, width), 0) + first
        for s in range(sents):
            value = total[pl.ds(pl.multiple_of(table[s] + first, 16), share), :]
            out[s] = jnp.where(position < table[LENS + s], value, jnp.zeros_like(value))


def place_grads(table, *refs):
    pieces, (straight, turned, slabs, flat, sems) = refs[:-5], refs[-5:]
    count, slab = slabs.shape[0], slabs.shape[1]
    arrivals = place_pieces(table, pieces, slabs, sems)
    start_all(arrivals)
    wait_all(arrivals)
    width = straight.shape[1]
    for j in range(count):
        rows = slice(j * slab, (j + 1) * slab)
        straight[rows, :] = slabs[j, :, :width].astype(F32)
        flat[rows, :] = slabs[j, :, width:].astype(F32)
    turned[...] = flat[...].T


def place_attention_grads(table, *refs):
    pieces, (qkv, wo, slabs, flat, sems) = refs[:-5], refs[-5:]
    count, slab = slabs.shape[0], slabs.shape[1]
    arrivals = place_pieces(table, pieces, slabs, sems)
    start_all(arrivals)
    wait_all(arrivals)
    for j in range(count):
        flat[j * slab : (j + 1) * slab, :] = slabs[j].astype(F32)
    part = wo.shape[0]
    heads = part // HD
    for p in range(3):
        piece = flat[:, p * part : (p + 1) * part].T
        for h in range(heads):
            target = (h * 3 + p) * HD
            qkv[target : target + HD, :] = piece[h * HD : (h + 1) * HD, :]
    wo[...] = flat[:, 3 * part :].T


SMEM = pl.BlockSpec(memory_space=pltpu.SMEM)
VMEM = pl.BlockSpec(memory_space=pltpu.VMEM)
ANY = pl.BlockSpec(memory_space=pl.ANY)


def shape(dims, dtype):
    return jax.ShapeDtypeStruct(dims, dtype)


def params():
    return pltpu.CompilerParams(vmem_limit_bytes=VMEM_BYTES)


def cost(flops, nbytes):
    return pl.CostEstimate(flops=flops, bytes_accessed=nbytes, transcendentals=0)


def add(*terms):
    return sum(term.astype(F32) for term in terms)


def swap(value, mask, axis="dp"):
    return lax.ppermute(value, axis, [(i, i ^ mask) for i in range(lax.axis_size(axis))])


def bits_of(count):
    return [1 << i for i in range(count.bit_length() - 1)]


def take(values, index, axis=0):
    return lax.dynamic_index_in_dim(values, index, axis, False, allow_negative_indices=False)


def cut(values, start, size, axis):
    return lax.dynamic_slice_in_dim(values, start, size, axis, allow_negative_indices=False)


def tie(*values):
    return lax.optimization_barrier(values)


def by_index(values, me):
    n = values.shape[0]
    for bit in bits_of(n):
        view = values.reshape((n // (2 * bit), 2, bit) + values.shape[1:])
        flipped = jnp.concatenate([view[:, 1:], view[:, :1]], axis=1)
        values = jnp.where((me & bit) != 0, flipped, view).reshape(values.shape)
    return values


def gather_line(piece):
    n = lax.axis_size("tensor")
    return jnp.concatenate([swap(piece, k, "tensor") for k in range(1, n)], axis=1)


def gather_chips(value):
    return [value] + [swap(value, 2 * m) for m in range(1, lax.axis_size("dp") // 2)]


def gather_cores(near):
    return near + [swap(item, 1) for item in near]


def gather_plane(value):
    return gather_cores(gather_chips(value))


def pick(term, side, bit):
    dims = term.shape
    view = term.reshape((dims[0] // (2 * bit), 2, bit) + dims[1:])[:, side]
    return view.reshape((dims[0] // 2,) + dims[1:])


def sent(terms, bit):
    return add(*[pick(term, 1, bit) for term in terms]).astype(LOW)


def kept(terms, bit, landed):
    return [pick(term, 0, bit) for term in terms] + [landed]


def reduce_line(terms):
    for bit in bits_of(lax.axis_size("tensor")):
        terms = kept(terms, 1, swap(sent(terms, 1), bit, "tensor"))
    return add(*terms)[0].astype(LOW)


def reduce_chips(terms, bits, falling):
    for bit in bits:
        at = bit if falling else 1
        terms = kept(terms, at, swap(sent(terms, at), 2 * bit))
    return terms


def shards(
    tokens,
    lengths,
    partner,
    w_qkv,
    w_out,
    ln1_gain,
    ln1_bias,
    up_weight,
    up_projection_bias,
    down_weight,
    ln2_gain,
    ln2_bias,
    cot_pooled,
    cot_paired,
):
    dp_count = lax.axis_size("dp")
    t_count = lax.axis_size("tensor")
    dp_me = lax.axis_index("dp")
    t_me = lax.axis_index("tensor")
    length, sentences, width = tokens.shape
    mine = sentences // t_count
    rows = mine * length
    pad = rows + length
    slab = width // dp_count
    chips = dp_count // 2
    heads = w_qkv.shape[1] // (3 * HD)
    units = up_weight.shape[1]
    ctx_cols = w_out.shape[0]
    block = 4 * ctx_cols

    def by_part(weight):
        return weight.reshape(-1, heads, 3, HD).transpose(0, 2, 1, 3).reshape(weight.shape)

    def rows_piece(weight):
        return cut(weight, dp_me * slab, slab, 0)

    def columns_piece(weight):
        return cut(weight, dp_me * slab, slab, 1).T

    attn_piece = jnp.concatenate([by_part(rows_piece(w_qkv)), columns_piece(w_out)], axis=1)
    attn_piece, up_early, down_early = tie(attn_piece, up_weight, down_weight)
    attn_line = gather_line(attn_piece)
    ffn_piece = jnp.concatenate([rows_piece(up_early), columns_piece(down_early)], axis=1)
    ffn_line = gather_line(ffn_piece)
    attn_line, cot_paired, up_projection_bias = tie(attn_line, cot_paired, up_projection_bias)
    attn_pieces = gather_plane(attn_line)
    bias_own = up_projection_bias.reshape(1, units)
    bias_all = jnp.stack([bias_own] + [swap(bias_own, k, "tensor") for k in range(1, t_count)])

    x = cut(tokens, t_me * mine, mine, 1).transpose(1, 0, 2)
    counts = cut(lengths, t_me * mine, mine, 0)
    taken = (counts + 15) & ~15
    ends = jnp.sum(jnp.where(np.tri(mine, dtype=bool), taken[None, :], 0), axis=1)
    devices = np.arange(dp_count)
    distance = 2 * np.arange(chips)
    near = devices[:, None] ^ distance[None, :]
    spots = np.concatenate([near, near ^ 1], axis=1)
    lines = np.arange(t_count)[:, None] ^ np.arange(t_count)[None, :]
    apart = devices[:, None] ^ devices[None, :]
    fixed = np.zeros((dp_count, DEST - PLACE + dp_count), np.int32)
    fixed[:, :dp_count] = spots
    fixed[:, DEST - PLACE :] = apart % 2 * chips + apart // 2
    line_fixed = np.zeros((t_count, PLACE - LINE), np.int32)
    line_fixed[:, :t_count] = lines
    table = jnp.concatenate(
        [
            ends - taken,
            np.zeros(LENS - mine, np.int32),
            counts,
            np.zeros(TILES - LENS - mine, np.int32),
            (ends[-1:] + (TILE - 1)) >> (TILE.bit_length() - 1),
            take(jnp.asarray(line_fixed), t_me),
            take(jnp.asarray(fixed), dp_me),
        ]
    ).astype(jnp.int32)
    turn_shape = shape((dp_count, slab, rows), LOW)
    packed, packed_t = pl.pallas_call(
        pack,
        out_shape=(shape((pad, width), LOW), turn_shape),
        in_specs=[SMEM, VMEM],
        out_specs=(VMEM,) * 2,
        compiler_params=params(),
        cost_estimate=cost(0, 8 * rows * width),
        name="pack",
    )(table, x)

    ffn_chips = gather_chips(ffn_line)
    attn_pieces[0], ffn_chips[0] = tie(attn_pieces[0], ffn_chips[0])
    pairs = width // PAIR
    probs_shape = (mine, pairs, 2 * length, length)
    proj, ctx, probs, qkv, wo, z1, root1 = pl.pallas_call(
        attention_forward,
        out_shape=(
            shape((pad, 3 * width), LOW),
            shape((pad, width), LOW),
            shape(probs_shape, LOW),
            shape((width, 3 * width), LOW),
            shape((width, width), LOW),
            shape((rows, width), F32),
            shape((rows, 128), F32),
        ),
        in_specs=[SMEM, VMEM, VMEM, VMEM] + [ANY] * dp_count,
        out_specs=(ANY,) * 5 + (VMEM,) * 2,
        scratch_shapes=[
            pltpu.VMEM((pad, 3 * width), LOW),
            pltpu.VMEM((pad, width), LOW),
            pltpu.VMEM(probs_shape, LOW),
            pltpu.VMEM((width, 3 * width), LOW),
            pltpu.VMEM((width, width), LOW),
            pltpu.VMEM((dp_count, slab, (t_count - 1) * block), LOW),
            pltpu.SemaphoreType.DMA((dp_count,)),
            pltpu.SemaphoreType.DMA((3,)),
            pltpu.SemaphoreType.DMA((2,)),
        ],
        compiler_params=params(),
        cost_estimate=cost(8 * rows * width * width, 30 * rows * width),
        name="attention_forward",
    )(table, packed, w_qkv.T, w_out, *attn_pieces)
    *ffn_chips, z1 = tie(*ffn_chips, z1)
    ffn_pieces = gather_cores(ffn_chips)
    cot_pieces = gather_plane(cot_paired)

    gain1, bias1 = ln1_gain.reshape(1, width), ln1_bias.reshape(1, width)
    gain2, bias2 = ln2_gain.reshape(1, width), ln2_bias.reshape(1, width)

    def whole(*dims):
        return pl.BlockSpec(dims, lambda k, table: (0,) * len(dims))

    def call(kernel, outs, ins, out_specs, scratch, flops, nbytes):
        return pl.pallas_call(
            kernel,
            out_shape=outs,
            grid_spec=pltpu.PrefetchScalarGridSpec(
                num_scalar_prefetch=1,
                grid=(t_count,),
                in_specs=ins,
                out_specs=out_specs,
                scratch_shapes=scratch,
            ),
            compiler_params=params(),
            cost_estimate=cost(flops, nbytes),
            name=kernel.__name__,
        )

    act_spec = pl.BlockSpec((1, rows, units), lambda k, table: (k, 0, 0))
    up_spec = pl.BlockSpec((1, width, units), lambda k, table: (k, 0, 0))
    down_spec = pl.BlockSpec((1, width, units), lambda k, table: (k, 0, 1))
    bias_spec = pl.BlockSpec((1, 1, units), lambda k, table: (k, 0, 0))
    line = whole(1, width)
    full = whole(rows, width)
    full_pad = whole(pad, width)
    root_spec = whole(rows, 128)
    act_shape = shape((t_count, rows, units), LOW)
    active, slope, z2, root2, pooled, ffn_all = call(
        ffn_forward,
        (
            act_shape,
            act_shape,
            shape((pad, width), F32),
            shape((rows, 128), F32),
            shape((mine, width), F32),
            shape((t_count, width, 2 * units), LOW),
        ),
        [full, line, line, whole(width, units), whole(units, width), bias_spec, line, line]
        + [ANY] * dp_count,
        (
            act_spec,
            act_spec,
            full_pad,
            root_spec,
            whole(mine, width),
            pl.BlockSpec((1, width, 2 * units), lambda k, table: (k, 0, 0)),
        ),
        [
            pltpu.VMEM((rows, width), LOW),
            pltpu.VMEM((rows, width), F32),
            pltpu.VMEM((dp_count, slab, (t_count - 1) * 2 * units), LOW),
            pltpu.SemaphoreType.DMA((dp_count,)),
        ],
        4 * rows * width * units * t_count,
        40 * rows * width,
    )(table, z1, gain1, bias1, up_weight, down_weight, bias_all, gain2, bias2, *ffn_pieces)

    pooled = pooled.astype(LOW)
    line_pooled = jnp.stack([pooled] + [swap(pooled, k, "tensor") for k in range(1, t_count)])
    everyone = jnp.stack(gather_plane(line_pooled)).reshape(-1, width)
    cot_all = jnp.stack(cot_pieces).reshape(-1, width)
    home_device = partner // sentences
    apart = home_device ^ dp_me
    where_device = apart % 2 * chips + apart // 2
    inside = partner % sentences
    partner_pooled = everyone[
        (where_device * t_count + (inside // mine ^ t_me)) * mine + inside % mine
    ].astype(F32)
    partner_cot = cot_all[where_device * sentences + inside].astype(F32)
    returned = by_index(line_pooled, t_me).reshape(sentences, width)
    paired = (returned.astype(F32) * partner_pooled).astype(LOW)
    pool_grad = cot_pooled.astype(F32) + partner_pooled * (cot_paired.astype(F32) + partner_cot)
    pool_grad = cut(pool_grad.astype(LOW).astype(F32), t_me * mine, mine, 0)

    send_spec = pl.BlockSpec((chips, 1, slab, units), lambda k, table: (0, k, 0, 0))
    send_shape = shape((chips, t_count, slab, units), LOW)
    down_mine, down_other, back, branch, sums_two = call(
        down_backward,
        (
            send_shape,
            send_shape,
            shape((pad, width), F32),
            shape((rows, width), LOW),
            shape((2, width), F32),
        ),
        [whole(mine, width), full_pad, root_spec, line, act_spec],
        (send_spec, send_spec, full_pad, full, whole(2, width)),
        [pltpu.VMEM((dp_count, slab, rows), LOW)],
        2 * rows * width * units * t_count,
        40 * rows * width,
    )(table, pool_grad, z2, root2, gain2, active)

    chip_bits = bits_of(chips)
    first_bits, last_bits = chip_bits[:1], chip_bits[1:]
    down_terms = [down_mine, swap(down_other, 1)]
    down_sent, branch = tie(sent(down_terms, 1), branch)
    down_got = swap(down_sent, 2)

    up_mine, up_other, attn_grad, attn_low, attn_t, sums_one, bias_sum = call(
        up_backward,
        (
            send_shape,
            send_shape,
            shape((rows, width), F32),
            shape((rows, width), LOW),
            turn_shape,
            shape((2, width), F32),
            shape((t_count, 1, units), F32),
        ),
        [full_pad, full, full, root_spec, line, line, up_spec, down_spec, act_spec],
        (send_spec, send_spec, full, full, whole(dp_count, slab, rows), whole(2, width), bias_spec),
        [
            pltpu.VMEM((dp_count, slab, rows), LOW),
            pltpu.VMEM((rows, units), LOW),
            pltpu.VMEM((rows, width), F32),
        ],
        6 * rows * width * units * t_count,
        40 * rows * width,
    )(table, back, branch, z1, root1, gain1, bias1, ffn_all, ffn_all, slope)

    down_got, up_other, bias_sum = tie(down_got, up_other, bias_sum)
    small = jnp.concatenate([bias_sum.reshape(t_count, units), sums_one, sums_two])
    small = small + swap(small, 1)
    up_terms = [up_mine, swap(up_other, 1)]
    down_terms = kept(down_terms, 1, down_got)
    top = chip_bits[-1]
    down_sent, up_sent, small, attn_low = tie(
        sent(down_terms, 1), sent(up_terms, top), small, attn_low
    )
    small_got = swap(small, 2)
    down_got, up_got = swap(down_sent, 2 * chip_bits[1]), swap(up_sent, 2 * top)

    proj_grad = pl.pallas_call(
        attention_backward,
        out_shape=shape((pad, 3 * width), LOW),
        in_specs=[SMEM, VMEM, VMEM, ANY, ANY],
        out_specs=VMEM,
        scratch_shapes=[
            pltpu.VMEM((pad, width), LOW),
            pltpu.VMEM((pad, 3 * width), LOW),
            pltpu.VMEM(probs_shape, LOW),
            pltpu.SemaphoreType.DMA((2,)),
        ],
        compiler_params=params(),
        cost_estimate=cost(6 * rows * width * width, 30 * rows * width),
        name="attention_backward",
    )(table, attn_low, wo, proj, probs)
    down_got, up_got, small_got, proj_grad = tie(down_got, up_got, small_got, proj_grad)
    small = small + small_got
    down_terms = reduce_chips(kept(down_terms, 1, down_got), chip_bits[2:], False)
    up_terms = kept(up_terms, top, up_got)
    at = chip_bits[-2]
    down_line = [add(*down_terms)[0].astype(LOW)]
    down_sent, up_sent, small, proj_grad = tie(
        sent(down_line, 1), sent(up_terms, at), small, proj_grad
    )
    small_got = swap(small, 4)
    down_got, up_got = swap(down_sent, 1, "tensor"), swap(up_sent, 2 * at)

    attn_mine, attn_other = pl.pallas_call(
        attention_weights,
        out_shape=(shape((chips, t_count, slab, block), LOW),) * 2,
        in_specs=[SMEM] + [VMEM] * 4,
        out_specs=(VMEM,) * 2,
        compiler_params=params(),
        cost_estimate=cost(8 * rows * width * width, 30 * rows * width),
        name="attention_weights",
    )(table, packed_t, attn_t, ctx, proj_grad)
    down_got, up_got, small_got, attn_other = tie(down_got, up_got, small_got, attn_other)
    small = small + small_got
    for mask in bits_of(dp_count)[3:]:
        small = small + swap(small, mask)
    attn_got = swap(attn_other, 1)
    attn_sent = [add(attn_mine[m], attn_got[m]).astype(LOW) for m in range(1, chips)]
    down_line = kept(down_line, 1, down_got)
    down_sent = sent(down_line, 1)
    up_terms = reduce_chips(kept(up_terms, at, up_got), chip_bits[:-2][::-1], True)
    up_line = [add(*up_terms)[0].astype(LOW)]
    *attn_sent, down_sent, up_sent, attn_grad = tie(*attn_sent, down_sent, sent(up_line, 1), attn_grad)
    attn_got = [attn_got[0]] + [swap(item, 2 * m) for m, item in zip(range(1, chips), attn_sent)]
    down_got, up_got = swap(down_sent, 2, "tensor"), swap(up_sent, 1, "tensor")

    share = length // t_count
    input_blocks = pl.pallas_call(
        input_backward,
        out_shape=(shape((mine, share, width), LOW),) * t_count,
        in_specs=[SMEM] + [VMEM] * 3,
        out_specs=(VMEM,) * t_count,
        scratch_shapes=[pltpu.VMEM((pad, width), LOW)],
        compiler_params=params(),
        cost_estimate=cost(6 * rows * width * width, 20 * rows * width),
        name="input_backward",
    )(table, attn_grad, proj_grad, qkv)

    input_landed = [input_blocks[0]]
    input_landed += [swap(input_blocks[k], k, "tensor") for k in range(1, t_count)]

    def finish(kernel, pieces, outs, flat):
        return pl.pallas_call(
            kernel,
            out_shape=tuple(shape(dims, F32) for dims in outs),
            in_specs=[SMEM] + [ANY] * dp_count,
            out_specs=(VMEM,) * 2,
            scratch_shapes=[
                pltpu.VMEM((dp_count,) + pieces[0].shape, LOW),
                pltpu.VMEM((width, flat), F32),
                pltpu.SemaphoreType.DMA((dp_count,)),
            ],
            compiler_params=params(),
            cost_estimate=cost(0, 8 * width * pieces[0].shape[1]),
            name=kernel.__name__,
        )(table, *pieces)

    def rest(line, done):
        for bit in bits_of(t_count)[done:]:
            line = kept(line, 1, swap(sent(line, 1), bit, "tensor"))
        return add(*line)[0].astype(LOW)

    down_sum = rest(kept(down_line, 1, down_got), 2)
    up_sum = rest(kept(up_line, 1, up_got), 1)
    up_grad, down_grad = finish(
        place_grads,
        gather_plane(jnp.concatenate([up_sum, down_sum], 1)),
        ((width, units), (units, width)),
        units,
    )
    attn_line = [add(attn_mine[0], *attn_got).astype(LOW)]
    qkv_grad, out_grad = finish(
        place_attention_grads,
        gather_plane(rest(attn_line, 0)),
        ((3 * ctx_cols, width), (ctx_cols, width)),
        block,
    )
    home = by_index(jnp.stack(input_landed), t_me)
    home = home.reshape(sentences, share, width).transpose(1, 0, 2)

    norms, bias_part = small[t_count:], small[:t_count]
    for mask in bits_of(t_count):
        half = bias_part.shape[0] // 2
        split = bias_part.reshape(half, 2, units)
        got = swap(jnp.concatenate([split[:, 1], norms]), mask, "tensor")
        bias_part = split[:, 0] + got[:half]
        norms = norms + got[half:]

    return (
        returned,
        paired,
        home,
        qkv_grad.T,
        out_grad,
        norms[0],
        norms[1],
        up_grad,
        bias_part[0],
        down_grad,
        norms[2],
        norms[3],
    )


def solution(mesh):
    placed = (
        P(None, "dp", None),
        P("dp"),
        P("dp"),
        P(None, "tensor"),
        P("tensor", None),
        P(),
        P(),
        P(None, "tensor"),
        P("tensor"),
        P("tensor", None),
        P(),
        P(),
        P("dp", None),
        P("dp", None),
    )
    return jax.shard_map(
        shards,
        mesh=mesh,
        in_specs=placed,
        out_specs=(
            P("dp", None),
            P("dp", None),
            P("tensor", "dp", None),
            P(None, "tensor"),
            P("tensor", None),
            P(),
            P(),
            P(None, "tensor"),
            P("tensor"),
            P("tensor", None),
            P(),
            P(),
        ),
        check_vma=False,
    )
```

```python
import functools

import jax
import jax.numpy as jnp
import numpy as np
from jax import lax
from jax.experimental import pallas as pl
from jax.experimental.pallas import tpu as pltpu
from jax.sharding import PartitionSpec as P

HD = 64
EPSILON = 1e-06
LOW = jnp.bfloat16
F32 = jnp.float32
INV_SQRT_2PI = 0.3989422804014327
SQRT_HALF = 0.7071067811865476
TILE = 256
CHUNK = 256
STEP = 16
MASKED = -1000000000.0
LOG2_E = 1.4426950408889634
VMEM_BYTES = 60 * 2**20
NN = (((1,), (0,)), ((), ()))
NT = (((1,), (1,)), ((), ()))
PAIR = 2 * HD
LENS, TILES, LINE, PLACE, DEST = 16, 32, 33, 48, 80


def mm(a, b, dims=NN):
    return lax.dot_general(a, b, dims, preferred_element_type=F32)


def rows_of(table, s):
    return pl.ds(pl.multiple_of(table[s], 16), 128)


def tile_at(i):
    return pl.ds(pl.multiple_of(i * TILE, TILE), TILE)


def normalize(values):
    center = values - jnp.mean(values, axis=-1, keepdims=True)
    spread = jnp.mean(center * center, axis=-1, keepdims=True)
    root = lax.rsqrt(spread + EPSILON)
    return center * root, root


def normalize_back(z, root, dz):
    return root * (
        dz - jnp.mean(dz, -1, keepdims=True) - z * jnp.mean(dz * z, -1, keepdims=True)
    )


def split_heads(pair):
    first = lax.broadcasted_iota(jnp.int32, pair.shape, 1) < HD
    zero = jnp.zeros_like(pair)
    return jnp.concatenate([jnp.where(first, pair, zero), jnp.where(first, zero, pair)], axis=0)


def join_heads(split):
    n = split.shape[0] // 2
    first = lax.broadcasted_iota(jnp.int32, (n, PAIR), 1) < HD
    return jnp.where(first, split[:n], split[n:])


def place_pieces(table, pieces, slabs, sems):
    copies = []
    for i, piece in enumerate(pieces):
        copies.append(pltpu.make_async_copy(piece, slabs.at[table[PLACE + i]], sems.at[i]))
    return copies


def turn(table, turned, rows, value):
    flat = value.T
    count, slab = turned.shape[0], turned.shape[1]
    for j in range(count):
        turned[table[DEST + j], :, rows] = flat[j * slab : (j + 1) * slab, :]


def pack(table, chosen, tokens, packed, packed_t, x):
    sents, length, width = x.shape
    total = tokens.shape[1]
    depth = total * STEP
    column = lax.broadcasted_iota(jnp.int32, (STEP, depth), 1)
    position = lax.broadcasted_iota(jnp.int32, (STEP, depth), 0)
    here = (column // total) == position
    pick = [here & ((column % total) == chosen[s]) for s in range(sents)]
    pick = jnp.concatenate([jnp.where(item, 1.0, 0.0).astype(LOW) for item in pick], axis=0)
    for block in range(length // STEP):
        rows = slice(block * STEP, (block + 1) * STEP)
        found = mm(pick, tokens[rows].reshape(depth, width)).astype(LOW)
        for s in range(sents):
            x[s, rows, :] = found[s * STEP : (s + 1) * STEP]
    packed[...] = jnp.zeros_like(packed)

    def place(s, _):
        packed[rows_of(table, s), :] = x[s]
        return 0

    lax.fori_loop(0, sents, place, 0)

    def flip(i, _):
        rows = tile_at(i)
        turn(table, packed_t, rows, packed[rows, :])
        return 0

    lax.fori_loop(0, table[TILES], flip, 0)


def send_home(source, *refs):
    blocks, home = refs[:-1], refs[-1]
    share, total, width = home.shape
    depth = total * STEP
    column = lax.broadcasted_iota(jnp.int32, (depth, depth), 1)
    row = lax.broadcasted_iota(jnp.int32, (depth, depth), 0)
    pick = ((column % STEP) == (row // total)) & ((column // STEP) == source[...])
    pick = jnp.where(pick, 1.0, 0.0).astype(LOW)
    for block in range(share // STEP):
        rows = slice(block * STEP, (block + 1) * STEP)
        values = [item[:, rows, :].reshape(-1, width) for item in blocks]
        found = mm(pick, jnp.concatenate(values, axis=0)).astype(LOW)
        home[rows] = found.reshape(STEP, total, width)


def start_all(copies):
    for copy in copies:
        copy.start()


def wait_all(copies):
    for copy in copies:
        copy.wait()


def attention_forward(table, packed, own_qkv, own_out, *refs):
    pieces, refs = refs[:-16], refs[-16:]
    proj_out, ctx_out, probs_out, qkv_out, wo_out, z1, root1 = refs[:7]
    proj, ctx, probs, qkv, wo, slabs, sems, out_sems, wide_sems = refs[7:]
    sents, pairs = probs.shape[0], probs.shape[1]
    width = packed.shape[1]
    length = probs.shape[3]
    part = own_out.shape[0]
    block = 4 * part
    heads = part // HD
    arrivals = place_pieces(table, pieces, slabs, sems)
    start_all(arrivals)
    count, slab = slabs.shape[0], slabs.shape[1]
    for h in range(heads):
        for p in range(3):
            source = (h * 3 + p) * HD
            qkv[:, p * width + h * HD : p * width + (h + 1) * HD] = own_qkv[
                source : source + HD, :
            ].T
    wo[:, :part] = own_out[...].T
    ctx[...] = jnp.zeros_like(ctx)
    tiles = table[TILES]
    end = pl.ds(pl.multiple_of(tiles * TILE, TILE), length)
    proj[end, :] = jnp.zeros((length, 3 * width), LOW)
    wait_all(arrivals)
    for j in range(count):
        rows = slice(j * slab, (j + 1) * slab)
        for k in range(1, width // part):
            base = (k - 1) * block
            for p in range(3):
                qkv[rows, p * width + k * part : p * width + (k + 1) * part] = slabs[
                    j, :, base + p * part : base + (p + 1) * part
                ]
            wo[rows, k * part : (k + 1) * part] = slabs[j, :, base + 3 * part : base + block]
    wide_copies = [
        pltpu.make_async_copy(qkv, qkv_out, wide_sems.at[0]),
        pltpu.make_async_copy(wo, wo_out, wide_sems.at[1]),
    ]
    start_all(wide_copies)

    def project(i, _):
        rows = tile_at(i)
        source = packed[rows, :]
        for p in range(3):
            cols = slice(p * width, (p + 1) * width)
            proj[rows, cols] = mm(source, qkv[:, cols]).astype(LOW)
        return 0

    lax.fori_loop(0, tiles, project, 0)
    proj_copy = pltpu.make_async_copy(proj, proj_out, out_sems.at[0])
    proj_copy.start()

    def attend(s, _):
        rows = rows_of(table, s)
        valid = lax.broadcasted_iota(jnp.int32, (length, length), 0) < table[LENS + s]
        for p in range(pairs):
            at = p * PAIR
            queries = proj[rows, at : at + PAIR]
            keys = split_heads(proj[rows, width + at : width + at + PAIR])
            values = split_heads(proj[rows, 2 * width + at : 2 * width + at + PAIR])
            scores = mm(keys, queries, NT)
            for h in range(2):
                half = slice(h * length, (h + 1) * length)
                score = jnp.where(valid, scores[half], MASKED)
                top = jnp.max(score, axis=0, keepdims=True)
                score = jnp.exp2((score - top) * (HD**-0.5 * LOG2_E))
                total = jnp.sum(score, axis=0, keepdims=True)
                probs[s, p, half, :] = (score * (1.0 / total)).astype(LOW)
            ctx[rows, at : at + PAIR] = mm(probs[s, p].T, values).astype(LOW)
        return 0

    lax.fori_loop(0, sents, attend, 0)
    ctx_copies = [
        pltpu.make_async_copy(ctx, ctx_out, out_sems.at[1]),
        pltpu.make_async_copy(probs, probs_out, out_sems.at[2]),
    ]
    start_all(ctx_copies)

    def finish(i, _):
        rows = tile_at(i)
        attended = mm(ctx[rows, :], wo[...], NT)
        z, root = normalize(packed[rows, :].astype(F32) + attended)
        z1[rows, :] = z
        root1[rows, :] = jnp.broadcast_to(root, (TILE, 128))
        return 0

    lax.fori_loop(0, tiles, finish, 0)
    wait_all(wide_copies + [proj_copy] + ctx_copies)


def gelu_parts(pre):
    t = pl.reciprocal(1.0 + jnp.abs(pre) * (0.3275911 * SQRT_HALF))
    poly = 0.5 * 1.061405429
    for c in (-1.453152027, 1.421413741, -0.284496736, 0.254829592):
        poly = poly * t + 0.5 * c
    e = jnp.exp2(pre * pre * (-0.5 * LOG2_E))
    tail = poly * t * e
    cdf = jnp.where(pre >= 0.0, 1.0 - tail, tail)
    return pre * cdf, cdf + pre * (e * INV_SQRT_2PI)


def ffn_forward(table, z1, gain1, bias1, own_up, own_down, bias, gain2, bias2, *refs):
    pieces, refs = refs[:-10], refs[-10:]
    active, slope, z2, root2, pooled, weight, first, total, slabs, sems = refs
    k = pl.program_id(0)
    tiles = table[TILES]
    count, slab = slabs.shape[0], slabs.shape[1]
    units = active.shape[2]

    @pl.when(k == 0)
    def _():
        for copy in place_pieces(table, pieces, slabs, sems):
            copy.start()
        weight[0, :, :units] = own_up[...]
        weight[0, :, units:] = own_down[...].T

    @pl.when(k == 1)
    def _():
        for copy in place_pieces(table, pieces, slabs, sems):
            copy.wait()

    for t in range(1, pl.num_programs(0)):

        @pl.when(k == t)
        def _():
            for j in range(count):
                weight[0, j * slab : (j + 1) * slab, :] = slabs[
                    j, :, (t - 1) * 2 * units : t * 2 * units
                ]

    @pl.when(k == 0)
    def _():
        def start(i, _):
            rows = tile_at(i)
            value = z1[rows, :] * gain1[...] + bias1[...]
            first[rows, :] = value.astype(LOW)
            total[rows, :] = value
            return 0

        lax.fori_loop(0, tiles, start, 0)

    def work(i, _):
        rows = tile_at(i)
        source = first[rows, :]
        for c in range(0, units, CHUNK):
            cols = slice(c, c + CHUNK)
            act, slp = gelu_parts(mm(source, weight[0, :, cols]) + bias[0, :, cols])
            active[0, rows, cols] = act.astype(LOW)
            slope[0, rows, cols] = slp.astype(LOW)
        total[rows, :] += mm(active[0, rows, :], weight[0, :, units:], NT)
        return 0

    lax.fori_loop(0, tiles, work, 0)

    @pl.when(k == pl.num_programs(0) - 1)
    def _():
        z2[pl.ds(pl.multiple_of(tiles * TILE, TILE), 128), :] = jnp.zeros((128, z2.shape[1]), F32)

        def finish(i, _):
            rows = tile_at(i)
            z, root = normalize(total[rows, :])
            z2[rows, :] = z
            root2[rows, :] = jnp.broadcast_to(root, (TILE, 128))
            return 0

        lax.fori_loop(0, tiles, finish, 0)
        for s in range(pooled.shape[0]):
            n = table[LENS + s]
            valid = lax.broadcasted_iota(jnp.int32, (128, z2.shape[1]), 0) < n
            rows = jnp.where(valid, z2[rows_of(table, s), :], 0.0)
            mean = jnp.sum(rows, axis=0, keepdims=True) / n.astype(F32)
            pooled[s : s + 1, :] = mean * gain2[...] + bias2[...]


def weight_grad(tiles, turned, right, store):
    count, slab, rows = turned.shape
    for n in range(1, rows // TILE + 1):

        @pl.when(tiles == n)
        def _():
            if slab % 16 == 0:
                left = turned[:, :, : n * TILE].reshape(count * slab, n * TILE)
            else:
                left = jnp.concatenate([turned[j, :, : n * TILE] for j in range(count)], axis=0)
            store(lambda columns: mm(left, right(n * TILE, columns)))


def split_send(mine, other, value, k, columns):
    chips, slab = mine.shape[0], mine.shape[2]
    for m in range(chips):
        mine[m, k, :, columns] = value[m * slab : (m + 1) * slab].astype(LOW)
        other[m, k, :, columns] = value[(chips + m) * slab : (chips + m + 1) * slab].astype(LOW)


def send_chunks(mine, other, product):
    for c in range(0, mine.shape[3], CHUNK):
        cols = slice(c, c + CHUNK)
        split_send(mine, other, product(cols), 0, cols)


def down_backward(
    table, pool, z2, root2, gain2, active, mine, other, back, branch, sums, branch_t
):
    tiles = table[TILES]
    width = z2.shape[1]

    @pl.when(pl.program_id(0) == 0)
    def _():
        back[...] = jnp.zeros_like(back)
        for s in range(pool.shape[0]):
            n = table[LENS + s]
            valid = lax.broadcasted_iota(jnp.int32, (128, width), 0) < n
            row = pool[s : s + 1, :] / n.astype(F32)
            back[rows_of(table, s), :] = jnp.where(valid, row, 0.0)
        sums[...] = jnp.zeros_like(sums)

        def start(i, _):
            rows = tile_at(i)
            grad = back[rows, :]
            z = z2[rows, :]
            sums[0:1, :] += jnp.sum(grad * z, axis=0, keepdims=True)
            sums[1:2, :] += jnp.sum(grad, axis=0, keepdims=True)
            value = normalize_back(z, root2[rows, 0:1], grad * gain2[...])
            low = value.astype(LOW)
            back[rows, :] = value
            branch[rows, :] = low
            turn(table, branch_t, rows, low)
            return 0

        lax.fori_loop(0, tiles, start, 0)

    weight_grad(
        tiles,
        branch_t,
        lambda n, cols: active[0, :n, cols],
        lambda product: send_chunks(mine, other, product),
    )


def up_backward(
    table, back, branch, z1, root1, gain1, bias1, up, down, slope,
    mine, other, attn_grad, attn_low, attn_t, sums, bias_sum, first_t, hidden, total,
):
    k = pl.program_id(0)
    tiles = table[TILES]

    @pl.when(k == 0)
    def _():
        sums[...] = jnp.zeros_like(sums)

        def start(i, _):
            rows = tile_at(i)
            first = (z1[rows, :] * gain1[...] + bias1[...]).astype(LOW)
            turn(table, first_t, rows, first)
            total[rows, :] = back[rows, :]
            return 0

        lax.fori_loop(0, tiles, start, 0)

    bias_sum[...] = jnp.zeros_like(bias_sum)

    def work(i, _):
        rows = tile_at(i)
        source = branch[rows, :]
        for c in range(0, hidden.shape[1], CHUNK):
            cols = slice(c, c + CHUNK)
            grad = mm(source, down[0, :, cols])
            hid = (slope[0, rows, cols].astype(F32) * grad).astype(LOW)
            hidden[rows, cols] = hid
            bias_sum[0, :, cols] += jnp.sum(hid.astype(F32), axis=0, keepdims=True)
        total[rows, :] += mm(hidden[rows, :], up[0], NT)
        return 0

    lax.fori_loop(0, tiles, work, 0)
    weight_grad(
        tiles,
        first_t,
        lambda n, cols: hidden[:n, cols],
        lambda product: send_chunks(mine, other, product),
    )

    @pl.when(k == pl.num_programs(0) - 1)
    def _():
        def finish(i, _):
            rows = tile_at(i)
            grad = total[rows, :]
            z = z1[rows, :]
            sums[0:1, :] += jnp.sum(grad * z, axis=0, keepdims=True)
            sums[1:2, :] += jnp.sum(grad, axis=0, keepdims=True)
            value = normalize_back(z, root1[rows, 0:1], grad * gain1[...])
            low = value.astype(LOW)
            attn_grad[rows, :] = value
            attn_low[rows, :] = low
            turn(table, attn_t, rows, low)
            return 0

        lax.fori_loop(0, tiles, finish, 0)


def attention_backward(
    table, attn_low, wo, proj_in, probs_in, proj_grad, ctx_grad, proj, probs, sems
):
    sents, pairs = probs.shape[0], probs.shape[1]
    length = probs.shape[3]
    width = attn_low.shape[1]
    tiles = table[TILES]
    arrivals = [
        pltpu.make_async_copy(proj_in, proj, sems.at[0]),
        pltpu.make_async_copy(probs_in, probs, sems.at[1]),
    ]
    start_all(arrivals)
    ctx_grad[...] = jnp.zeros_like(ctx_grad)
    proj_grad[...] = jnp.zeros_like(proj_grad)

    def start(i, _):
        rows = tile_at(i)
        ctx_grad[rows, :] = mm(attn_low[rows, :], wo[...]).astype(LOW)
        return 0

    lax.fori_loop(0, tiles, start, 0)
    wait_all(arrivals)
    scale = HD**-0.5

    def attend(s, _):
        rows = rows_of(table, s)
        live = lax.broadcasted_iota(jnp.int32, (length, PAIR), 0) < table[LENS + s]
        for p in range(pairs):
            at = p * PAIR
            queries = proj[rows, at : at + PAIR]
            keys = split_heads(proj[rows, width + at : width + at + PAIR])
            values = split_heads(proj[rows, 2 * width + at : 2 * width + at + PAIR])
            grad = ctx_grad[rows, at : at + PAIR]
            grad = jnp.where(live, grad, jnp.zeros_like(grad))
            prob_grad = mm(values, grad, NT)
            score_grad = []
            for h in range(2):
                half = slice(h * length, (h + 1) * length)
                prob = probs[s, p, half, :].astype(F32)
                part = prob_grad[half]
                inner = jnp.sum(prob * part, axis=0, keepdims=True)
                score_grad.append((prob * (part - inner)).astype(LOW))
            score_grad = jnp.concatenate(score_grad, axis=0)
            proj_grad[rows, at : at + PAIR] = (mm(score_grad.T, keys) * scale).astype(LOW)
            proj_grad[rows, width + at : width + at + PAIR] = (
                join_heads(mm(score_grad, queries)) * scale
            ).astype(LOW)
            proj_grad[rows, 2 * width + at : 2 * width + at + PAIR] = join_heads(
                mm(probs[s, p], grad)
            ).astype(LOW)
        return 0

    lax.fori_loop(0, sents, attend, 0)


def attention_weights(table, packed_t, attn_t, ctx, proj_grad, mine, other):
    tiles = table[TILES]
    width = ctx.shape[1]
    count = mine.shape[1]
    part = width // count

    def store(p, product):
        value = product(slice(p * width, (p + 1) * width) if p < 3 else slice(None))
        for k in range(count):
            split_send(
                mine,
                other,
                value[:, k * part : (k + 1) * part],
                k,
                slice(p * part, (p + 1) * part),
            )

    weight_grad(
        tiles, attn_t, lambda n, cols: ctx[:n, cols], lambda product: store(3, product)
    )
    for p in range(3):
        weight_grad(
            tiles,
            packed_t,
            lambda n, cols: proj_grad[:n, cols],
            lambda product: store(p, product),
        )


def input_backward(table, attn_grad, proj_grad, qkv, *refs):
    outs, total = refs[:-1], refs[-1]
    sents, share, width = outs[0].shape
    length = share * len(outs)
    tiles = table[TILES]

    def finish(i, _):
        rows = tile_at(i)
        total[rows, :] = (
            attn_grad[rows, :] + mm(proj_grad[rows, :], qkv[...], NT)
        ).astype(LOW)
        return 0

    lax.fori_loop(0, tiles, finish, 0)
    total[pl.ds(pl.multiple_of(tiles * TILE, TILE), length), :] = jnp.zeros((length, width), LOW)
    for k, out in enumerate(outs):
        first = table[LINE + k] * share
        position = lax.broadcasted_iota(jnp.int32, (share, width), 0) + first
        for s in range(sents):
            value = total[pl.ds(pl.multiple_of(table[s] + first, 16), share), :]
            out[s] = jnp.where(position < table[LENS + s], value, jnp.zeros_like(value))


def place_grads(table, *refs):
    pieces, (straight, turned, slabs, flat, sems) = refs[:-5], refs[-5:]
    count, slab = slabs.shape[0], slabs.shape[1]
    arrivals = place_pieces(table, pieces, slabs, sems)
    start_all(arrivals)
    wait_all(arrivals)
    width = straight.shape[1]
    for j in range(count):
        rows = slice(j * slab, (j + 1) * slab)
        straight[rows, :] = slabs[j, :, :width].astype(F32)
        flat[rows, :] = slabs[j, :, width:].astype(F32)
    turned[...] = flat[...].T


def place_attention_grads(table, *refs):
    pieces, (qkv, wo, slabs, flat, sems) = refs[:-5], refs[-5:]
    count, slab = slabs.shape[0], slabs.shape[1]
    arrivals = place_pieces(table, pieces, slabs, sems)
    start_all(arrivals)
    wait_all(arrivals)
    for j in range(count):
        flat[j * slab : (j + 1) * slab, :] = slabs[j].astype(F32)
    part = wo.shape[0]
    heads = part // HD
    for p in range(3):
        piece = flat[:, p * part : (p + 1) * part].T
        for h in range(heads):
            target = (h * 3 + p) * HD
            qkv[target : target + HD, :] = piece[h * HD : (h + 1) * HD, :]
    wo[...] = flat[:, 3 * part :].T


COST = 1000000
SMEM = pl.BlockSpec(memory_space=pltpu.SMEM)
VMEM = pl.BlockSpec(memory_space=pltpu.VMEM)
ANY = pl.BlockSpec(memory_space=pl.ANY)


def shape(dims, dtype):
    return jax.ShapeDtypeStruct(dims, dtype)


def params():
    return pltpu.CompilerParams(vmem_limit_bytes=VMEM_BYTES)


def cost(flops, nbytes):
    return pl.CostEstimate(flops=flops // COST, bytes_accessed=nbytes // COST, transcendentals=0)


def add(*terms):
    return sum(term.astype(F32) for term in terms)


def swap(value, mask, axis="dp"):
    return lax.ppermute(value, axis, [(i, i ^ mask) for i in range(lax.axis_size(axis))])


def bits_of(count):
    return [1 << i for i in range(count.bit_length() - 1)]


def take(values, index, axis=0):
    return lax.dynamic_index_in_dim(values, index, axis, False, allow_negative_indices=False)


def cut(values, start, size, axis):
    return lax.dynamic_slice_in_dim(values, start, size, axis, allow_negative_indices=False)


def tie(*values):
    return lax.optimization_barrier(values)


def gather_line(piece):
    n = lax.axis_size("tensor")
    return jnp.concatenate([swap(piece, k, "tensor") for k in range(1, n)], axis=1)


def gather_chips(value):
    return [value] + [swap(value, 2 * m) for m in range(1, lax.axis_size("dp") // 2)]


def gather_cores(near):
    return near + [swap(item, 1) for item in near]


def gather_plane(value):
    return gather_cores(gather_chips(value))


def pick(term, side, bit):
    dims = term.shape
    view = term.reshape((dims[0] // (2 * bit), 2, bit) + dims[1:])[:, side]
    return view.reshape((dims[0] // 2,) + dims[1:])


def sent(terms, bit):
    return add(*[pick(term, 1, bit) for term in terms]).astype(LOW)


def kept(terms, bit, landed):
    return [pick(term, 0, bit) for term in terms] + [landed]


def reduce_line(terms):
    for bit in bits_of(lax.axis_size("tensor")):
        terms = kept(terms, 1, swap(sent(terms, 1), bit, "tensor"))
    return add(*terms)[0].astype(LOW)


def reduce_chips(terms, bits):
    for bit in bits:
        terms = kept(terms, 1, swap(sent(terms, 1), 2 * bit))
    return terms


def shards(
    tokens,
    lengths,
    partner,
    w_qkv,
    w_out,
    ln1_gain,
    ln1_bias,
    up_weight,
    up_projection_bias,
    down_weight,
    ln2_gain,
    ln2_bias,
    cot_pooled,
    cot_paired,
):
    dp_count = lax.axis_size("dp")
    t_count = lax.axis_size("tensor")
    dp_me = lax.axis_index("dp")
    t_me = lax.axis_index("tensor")
    length, sentences, width = tokens.shape
    mine = sentences // t_count
    rows = mine * length
    pad = rows + length
    slab = width // dp_count
    chips = dp_count // 2
    heads = w_qkv.shape[1] // (3 * HD)
    units = up_weight.shape[1]
    ctx_cols = w_out.shape[0]
    block = 4 * ctx_cols

    def by_part(weight):
        return weight.reshape(-1, heads, 3, HD).transpose(0, 2, 1, 3).reshape(weight.shape)

    def rows_piece(weight):
        return cut(weight, dp_me * slab, slab, 0)

    def columns_piece(weight):
        return cut(weight, dp_me * slab, slab, 1).T

    attn_piece = jnp.concatenate([by_part(rows_piece(w_qkv)), columns_piece(w_out)], axis=1)
    attn_piece, up_early, down_early = tie(attn_piece, up_weight, down_weight)
    attn_line = gather_line(attn_piece)
    ffn_piece = jnp.concatenate([rows_piece(up_early), columns_piece(down_early)], axis=1)
    ffn_parts, bias_parts = [ffn_piece], [up_projection_bias.reshape(1, units)]

    def widen_line(parts, bit):
        return parts + [swap(jnp.concatenate(parts, axis=1), bit, "tensor")]

    ffn_parts = widen_line(ffn_parts, 1)
    bias_parts = widen_line(bias_parts, 1)

    order = np.arange(sentences)
    ahead = (lengths[None, :] > lengths[:, None]) | (
        (lengths[None, :] == lengths[:, None]) & (order[None, :] < order[:, None])
    )
    rank = jnp.sum(ahead.astype(jnp.int32), axis=1)
    row = rank // t_count
    column = rank % t_count
    column = jnp.where(row % 2 == 0, column, t_count - 1 - column)
    mine_here = (column == t_me)[None, :] & (row[None, :] == order[:mine, None])
    chosen = jnp.sum(jnp.where(mine_here, order[None, :], 0), axis=1)
    counts = jnp.sum(jnp.where(mine_here, lengths[None, :], 0), axis=1)
    source = (column ^ t_me) * mine + row
    taken = (counts + 15) & ~15
    ends = jnp.sum(jnp.where(np.tri(mine, dtype=bool), taken[None, :], 0), axis=1)
    devices = np.arange(dp_count)
    distance = 2 * np.arange(chips)
    near = devices[:, None] ^ distance[None, :]
    spots = np.concatenate([near, near ^ 1], axis=1)
    lines = np.arange(t_count)[:, None] ^ np.arange(t_count)[None, :]
    apart = devices[:, None] ^ devices[None, :]
    fixed = np.zeros((dp_count, DEST - PLACE + dp_count), np.int32)
    fixed[:, :dp_count] = spots
    fixed[:, DEST - PLACE :] = apart % 2 * chips + apart // 2
    line_fixed = np.zeros((t_count, PLACE - LINE), np.int32)
    line_fixed[:, :t_count] = lines
    table = jnp.concatenate(
        [
            ends - taken,
            np.zeros(LENS - mine, np.int32),
            counts,
            np.zeros(TILES - LENS - mine, np.int32),
            (ends[-1:] + (TILE - 1)) >> (TILE.bit_length() - 1),
            take(jnp.asarray(line_fixed), t_me),
            take(jnp.asarray(fixed), dp_me),
        ]
    ).astype(jnp.int32)
    turn_shape = shape((dp_count, slab, rows), LOW)
    packed, packed_t = pl.pallas_call(
        pack,
        out_shape=(shape((pad, width), LOW), turn_shape),
        in_specs=[SMEM, SMEM, VMEM],
        out_specs=(VMEM,) * 2,
        scratch_shapes=[pltpu.VMEM((mine, length, width), LOW)],
        compiler_params=params(),
        cost_estimate=cost(0, 8 * rows * width),
        name="pack",
    )(table, chosen, tokens)

    attn_line, ffn_parts[1], bias_parts[1], packed = tie(
        attn_line, ffn_parts[1], bias_parts[1], packed
    )
    attn_chips = gather_chips(attn_line)
    for bit in bits_of(t_count)[1:]:
        ffn_parts = widen_line(ffn_parts, bit)
        bias_parts = widen_line(bias_parts, bit)
    bias_all = jnp.concatenate(bias_parts, axis=1).reshape(t_count, 1, units)
    attn_pieces = gather_cores(list(tie(*attn_chips)))
    ffn_chips = gather_chips(jnp.concatenate(ffn_parts[1:], axis=1))
    attn_pieces[0], ffn_chips[0], bias_all = tie(attn_pieces[0], ffn_chips[0], bias_all)
    pairs = width // PAIR
    probs_shape = (mine, pairs, 2 * length, length)
    proj, ctx, probs, qkv, wo, z1, root1 = pl.pallas_call(
        attention_forward,
        out_shape=(
            shape((pad, 3 * width), LOW),
            shape((pad, width), LOW),
            shape(probs_shape, LOW),
            shape((width, 3 * width), LOW),
            shape((width, width), LOW),
            shape((rows, width), F32),
            shape((rows, 128), F32),
        ),
        in_specs=[SMEM, VMEM, VMEM, VMEM] + [ANY] * dp_count,
        out_specs=(ANY,) * 5 + (VMEM,) * 2,
        scratch_shapes=[
            pltpu.VMEM((pad, 3 * width), LOW),
            pltpu.VMEM((pad, width), LOW),
            pltpu.VMEM(probs_shape, LOW),
            pltpu.VMEM((width, 3 * width), LOW),
            pltpu.VMEM((width, width), LOW),
            pltpu.VMEM((dp_count, slab, (t_count - 1) * block), LOW),
            pltpu.SemaphoreType.DMA((dp_count,)),
            pltpu.SemaphoreType.DMA((3,)),
            pltpu.SemaphoreType.DMA((2,)),
        ],
        compiler_params=params(),
        cost_estimate=cost(8 * rows * width * width, 30 * rows * width),
        name="attention_forward",
    )(table, packed, w_qkv.T, w_out, *attn_pieces)
    *ffn_chips, z1 = tie(*ffn_chips, z1)
    ffn_pieces = gather_cores(ffn_chips)

    gain1, bias1 = ln1_gain.reshape(1, width), ln1_bias.reshape(1, width)
    gain2, bias2 = ln2_gain.reshape(1, width), ln2_bias.reshape(1, width)

    def whole(*dims):
        return pl.BlockSpec(dims, lambda k, table: (0,) * len(dims))

    def call(kernel, outs, ins, out_specs, scratch, flops, nbytes):
        return pl.pallas_call(
            kernel,
            out_shape=outs,
            grid_spec=pltpu.PrefetchScalarGridSpec(
                num_scalar_prefetch=1,
                grid=(t_count,),
                in_specs=ins,
                out_specs=out_specs,
                scratch_shapes=scratch,
            ),
            compiler_params=params(),
            cost_estimate=cost(flops, nbytes),
            name=kernel.__name__,
        )

    act_spec = pl.BlockSpec((1, rows, units), lambda k, table: (k, 0, 0))
    up_spec = pl.BlockSpec((1, width, units), lambda k, table: (k, 0, 0))
    down_spec = pl.BlockSpec((1, width, units), lambda k, table: (k, 0, 1))
    bias_spec = pl.BlockSpec((1, 1, units), lambda k, table: (k, 0, 0))
    line = whole(1, width)
    full = whole(rows, width)
    full_pad = whole(pad, width)
    root_spec = whole(rows, 128)
    act_shape = shape((t_count, rows, units), LOW)
    active, slope, z2, root2, pooled, ffn_all = call(
        ffn_forward,
        (
            act_shape,
            act_shape,
            shape((pad, width), F32),
            shape((rows, 128), F32),
            shape((mine, width), F32),
            shape((t_count, width, 2 * units), LOW),
        ),
        [full, line, line, whole(width, units), whole(units, width), bias_spec, line, line]
        + [ANY] * dp_count,
        (
            act_spec,
            act_spec,
            full_pad,
            root_spec,
            whole(mine, width),
            pl.BlockSpec((1, width, 2 * units), lambda k, table: (k, 0, 0)),
        ),
        [
            pltpu.VMEM((rows, width), LOW),
            pltpu.VMEM((rows, width), F32),
            pltpu.VMEM((dp_count, slab, (t_count - 1) * 2 * units), LOW),
            pltpu.SemaphoreType.DMA((dp_count,)),
        ],
        4 * rows * width * units * t_count,
        40 * rows * width,
    )(table, z1, gain1, bias1, up_weight, down_weight, bias_all, gain2, bias2, *ffn_pieces)

    pooled = pooled.astype(LOW)
    line_pooled = jnp.stack([pooled] + [swap(pooled, k, "tensor") for k in range(1, t_count)])
    returned = line_pooled.reshape(sentences, width)[source]
    both = jnp.concatenate([returned, cot_paired])
    everyone = jnp.stack(gather_plane(both)).reshape(-1, width)
    apart = (partner // sentences) ^ dp_me
    base = ((apart & 1) * chips + (apart >> 1)) * (2 * sentences) + partner % sentences
    partner_pooled = everyone[base].astype(F32)
    partner_cot = everyone[base + sentences].astype(F32)
    paired = (returned.astype(F32) * partner_pooled).astype(LOW)
    pool_grad = cot_pooled.astype(F32) + partner_pooled * (cot_paired.astype(F32) + partner_cot)
    pool_grad = pool_grad.astype(LOW).astype(F32)[chosen]

    send_spec = pl.BlockSpec((chips, 1, slab, units), lambda k, table: (0, k, 0, 0))
    send_shape = shape((chips, t_count, slab, units), LOW)
    down_mine, down_other, back, branch, sums_two = call(
        down_backward,
        (
            send_shape,
            send_shape,
            shape((pad, width), F32),
            shape((rows, width), LOW),
            shape((2, width), F32),
        ),
        [whole(mine, width), full_pad, root_spec, line, act_spec],
        (send_spec, send_spec, full_pad, full, whole(2, width)),
        [pltpu.VMEM((dp_count, slab, rows), LOW)],
        2 * rows * width * units * t_count,
        40 * rows * width,
    )(table, pool_grad, z2, root2, gain2, active)

    chip_bits = bits_of(chips)
    down_got = swap(down_other, 1)
    up_mine, up_other, attn_grad, attn_low, attn_t, sums_one, bias_sum = call(
        up_backward,
        (
            send_shape,
            send_shape,
            shape((rows, width), F32),
            shape((rows, width), LOW),
            turn_shape,
            shape((2, width), F32),
            shape((t_count, 1, units), F32),
        ),
        [full_pad, full, full, root_spec, line, line, up_spec, down_spec, act_spec],
        (send_spec, send_spec, full, full, whole(dp_count, slab, rows), whole(2, width), bias_spec),
        [
            pltpu.VMEM((dp_count, slab, rows), LOW),
            pltpu.VMEM((rows, units), LOW),
            pltpu.VMEM((rows, width), F32),
        ],
        6 * rows * width * units * t_count,
        40 * rows * width,
    )(table, back, branch, z1, root1, gain1, bias1, ffn_all, ffn_all, slope)

    down_got, up_other, bias_sum = tie(down_got, up_other, bias_sum)
    down_terms, up_terms = [down_mine, down_got], [up_mine, swap(up_other, 1)]
    small = jnp.concatenate([bias_sum.reshape(t_count, units), sums_one, sums_two])
    small = small + swap(small, 1)
    high = chip_bits[-1]
    down_sent, up_sent, small, attn_low = tie(
        sent(down_terms, 1), sent(up_terms, high), small, attn_low
    )
    small_got = swap(small, 2)
    down_got, up_got = swap(down_sent, 2), swap(up_sent, 2 * high)

    proj_grad = pl.pallas_call(
        attention_backward,
        out_shape=shape((pad, 3 * width), LOW),
        in_specs=[SMEM, VMEM, VMEM, ANY, ANY],
        out_specs=VMEM,
        scratch_shapes=[
            pltpu.VMEM((pad, width), LOW),
            pltpu.VMEM((pad, 3 * width), LOW),
            pltpu.VMEM(probs_shape, LOW),
            pltpu.SemaphoreType.DMA((2,)),
        ],
        compiler_params=params(),
        cost_estimate=cost(6 * rows * width * width, 30 * rows * width),
        name="attention_backward",
    )(table, attn_low, wo, proj, probs)
    share = length // t_count
    input_blocks = pl.pallas_call(
        input_backward,
        out_shape=(shape((mine, share, width), LOW),) * t_count,
        in_specs=[SMEM] + [VMEM] * 3,
        out_specs=(VMEM,) * t_count,
        scratch_shapes=[pltpu.VMEM((pad, width), LOW)],
        compiler_params=params(),
        cost_estimate=cost(6 * rows * width * width, 20 * rows * width),
        name="input_backward",
    )(table, attn_grad, proj_grad, qkv)

    down_got, up_got, small_got, proj_grad, *input_blocks = tie(
        down_got, up_got, small_got, proj_grad, *input_blocks
    )
    small = small + small_got
    down_terms, up_terms = kept(down_terms, 1, down_got), kept(up_terms, high, up_got)
    for low, top in zip(chip_bits[1:-1], chip_bits[1:-1][::-1]):
        down_terms = kept(down_terms, 1, swap(sent(down_terms, 1), 2 * low))
        up_terms = kept(up_terms, top, swap(sent(up_terms, top), 2 * top))
    down_sent, up_sent, small, proj_grad, *input_blocks = tie(
        sent(down_terms, 1), sent(up_terms, 1), small, proj_grad, *input_blocks
    )
    small_got = swap(small, 4)
    down_got, up_got = swap(down_sent, 2 * high), swap(up_sent, 2)
    input_landed = [input_blocks[0]] + [None] * (t_count - 1)
    input_landed[2] = swap(input_blocks[2], 2, "tensor")

    attn_mine, attn_other = pl.pallas_call(
        attention_weights,
        out_shape=(shape((chips, t_count, slab, block), LOW),) * 2,
        in_specs=[SMEM] + [VMEM] * 4,
        out_specs=(VMEM,) * 2,
        compiler_params=params(),
        cost_estimate=cost(8 * rows * width * width, 30 * rows * width),
        name="attention_weights",
    )(table, packed_t, attn_t, ctx, proj_grad)
    def finish(kernel, pieces, outs, flat):
        return pl.pallas_call(
            kernel,
            out_shape=tuple(shape(dims, F32) for dims in outs),
            in_specs=[SMEM] + [ANY] * dp_count,
            out_specs=(VMEM,) * 2,
            scratch_shapes=[
                pltpu.VMEM((dp_count,) + pieces[0].shape, LOW),
                pltpu.VMEM((width, flat), F32),
                pltpu.SemaphoreType.DMA((dp_count,)),
            ],
            compiler_params=params(),
            cost_estimate=cost(0, 8 * width * pieces[0].shape[1]),
            name=kernel.__name__,
        )(table, *pieces)

    attn_other, small_got, down_got, up_got, input_landed[2] = tie(
        attn_other, small_got, down_got, up_got, input_landed[2]
    )
    small = small + small_got
    for mask in bits_of(dp_count)[3:]:
        small = small + swap(small, mask)
    attn_got = swap(attn_other, 1)
    attn_sent = [add(attn_mine[m], attn_got[m]).astype(LOW) for m in range(1, chips)]
    ffn_line = jnp.concatenate(
        [add(*kept(up_terms, 1, up_got))[0], add(*kept(down_terms, 1, down_got))[0]], axis=2
    )
    ffn_line = [ffn_line.astype(LOW)]
    ffn_sent, input_blocks[3], small, *attn_sent = tie(
        sent(ffn_line, 1), input_blocks[3], small, *attn_sent
    )
    attn_got = [attn_got[0]] + [swap(item, 2 * m) for m, item in zip(range(1, chips), attn_sent)]
    ffn_got = swap(ffn_sent, 1, "tensor")
    input_landed[3] = swap(input_blocks[3], 3, "tensor")
    norms, bias_part = small[t_count:], small[:t_count]

    def small_step(norms, bias_part, mask):
        half = bias_part.shape[0] // 2
        split = bias_part.reshape(half, 2, units)
        got = swap(jnp.concatenate([split[:, 1], norms]), mask, "tensor")
        return norms, got, split[:, 0]

    def small_sum(norms, got, bias_part):
        half = bias_part.shape[0]
        return norms + got[half:], bias_part + got[:half]

    *attn_got, ffn_got, norms, input_blocks[1], input_landed[3] = tie(
        *attn_got, ffn_got, norms, input_blocks[1], input_landed[3]
    )
    attn_line = [add(attn_mine[0], *attn_got).astype(LOW)]
    ffn_line = kept(ffn_line, 1, ffn_got)
    attn_sent, ffn_sent, norms, input_blocks[1] = tie(
        sent(attn_line, 1), sent(ffn_line, 1), norms, input_blocks[1]
    )
    attn_got = swap(attn_sent, 1, "tensor")
    ffn_got = swap(ffn_sent, 2, "tensor")
    input_landed[1] = swap(input_blocks[1], 1, "tensor")
    norms, small_got, bias_part = small_step(norms, bias_part, 1)
    attn_got, ffn_got, small_got, input_landed[1] = tie(
        attn_got, ffn_got, small_got, input_landed[1]
    )
    norms, bias_part = small_sum(norms, small_got, bias_part)
    attn_line = kept(attn_line, 1, attn_got)
    ffn_sum = add(*kept(ffn_line, 1, ffn_got))[0].astype(LOW)
    attn_sent, ffn_sum, norms = tie(sent(attn_line, 1), ffn_sum, norms)
    attn_got = swap(attn_sent, 2, "tensor")
    ffn_chips = gather_chips(ffn_sum)
    norms, small_got, bias_part = small_step(norms, bias_part, 2)
    attn_got, small_got, *ffn_chips = tie(attn_got, small_got, *ffn_chips)
    norms, bias_part = small_sum(norms, small_got, bias_part)
    attn_sum = add(*kept(attn_line, 1, attn_got))[0].astype(LOW)
    attn_sum, ffn_chips[0], input_landed[0] = tie(attn_sum, ffn_chips[0], input_landed[0])
    attn_chips = gather_chips(attn_sum)
    home = pl.pallas_call(
        send_home,
        out_shape=shape((share, sentences, width), LOW),
        in_specs=[VMEM] * (1 + t_count),
        out_specs=VMEM,
        compiler_params=params(),
        cost_estimate=cost(0, 4 * share * sentences * width),
        name="send_home",
    )(jnp.tile(source, STEP).reshape(-1, 1), *input_landed)
    up_grad, down_grad = finish(
        place_grads, gather_cores(ffn_chips), ((width, units), (units, width)), units
    )
    attn_chips[0], up_grad, home = tie(attn_chips[0], up_grad, home)
    qkv_grad, out_grad = finish(
        place_attention_grads,
        gather_cores(attn_chips),
        ((3 * ctx_cols, width), (ctx_cols, width)),
        block,
    )

    return (
        returned,
        paired,
        home,
        qkv_grad.T,
        out_grad,
        norms[0],
        norms[1],
        up_grad,
        bias_part[0],
        down_grad,
        norms[2],
        norms[3],
    )


def solution(mesh):
    placed = (
        P(None, "dp", None),
        P("dp"),
        P("dp"),
        P(None, "tensor"),
        P("tensor", None),
        P(),
        P(),
        P(None, "tensor"),
        P("tensor"),
        P("tensor", None),
        P(),
        P(),
        P("dp", None),
        P("dp", None),
    )
    return jax.shard_map(
        shards,
        mesh=mesh,
        in_specs=placed,
        out_specs=(
            P("dp", None),
            P("dp", None),
            P("tensor", "dp", None),
            P(None, "tensor"),
            P("tensor", None),
            P(),
            P(),
            P(None, "tensor"),
            P("tensor"),
            P("tensor", None),
            P(),
            P(),
        ),
        check_vma=False,
    )
```

```python
import functools

import jax
import jax.numpy as jnp
import numpy as np
from jax import lax
from jax.experimental import pallas as pl
from jax.experimental.pallas import tpu as pltpu
from jax.sharding import PartitionSpec as P

HD = 64
EPSILON = 1e-06
LOW = jnp.bfloat16
F32 = jnp.float32
INV_SQRT_2PI = 0.3989422804014327
SQRT_HALF = 0.7071067811865476
TILE = 256
CHUNK = 256
STEP = 16
MASKED = -1000000000.0
LOG2_E = 1.4426950408889634
VMEM_BYTES = 60 * 2**20
NN = (((1,), (0,)), ((), ()))
NT = (((1,), (1,)), ((), ()))
PAIR = 2 * HD
LENS, TILES, LINE, PLACE, DEST = 16, 32, 33, 48, 80


def mm(a, b, dims=NN):
    return lax.dot_general(a, b, dims, preferred_element_type=F32)


def rows_of(table, s):
    return pl.ds(pl.multiple_of(table[s], 16), 128)


def tile_at(i):
    return pl.ds(pl.multiple_of(i * TILE, TILE), TILE)


def normalize(values):
    center = values - jnp.mean(values, axis=-1, keepdims=True)
    spread = jnp.mean(center * center, axis=-1, keepdims=True)
    root = lax.rsqrt(spread + EPSILON)
    return center * root, root


def normalize_back(z, root, dz):
    return root * (
        dz - jnp.mean(dz, -1, keepdims=True) - z * jnp.mean(dz * z, -1, keepdims=True)
    )


def split_heads(pair):
    first = lax.broadcasted_iota(jnp.int32, pair.shape, 1) < HD
    zero = jnp.zeros_like(pair)
    return jnp.concatenate([jnp.where(first, pair, zero), jnp.where(first, zero, pair)], axis=0)


def join_heads(split):
    n = split.shape[0] // 2
    first = lax.broadcasted_iota(jnp.int32, (n, PAIR), 1) < HD
    return jnp.where(first, split[:n], split[n:])


def place_pieces(table, pieces, slabs, sems):
    copies = []
    for i, piece in enumerate(pieces):
        copies.append(pltpu.make_async_copy(piece, slabs.at[table[PLACE + i]], sems.at[i]))
    return copies


def turn(table, turned, rows, value):
    flat = value.T
    count, slab = turned.shape[0], turned.shape[1]
    for j in range(count):
        turned[table[DEST + j], :, rows] = flat[j * slab : (j + 1) * slab, :]


def pack(table, chosen, tokens, packed, packed_t, x):
    sents, length, width = x.shape
    total = tokens.shape[1]
    depth = total * STEP
    column = lax.broadcasted_iota(jnp.int32, (STEP, depth), 1)
    position = lax.broadcasted_iota(jnp.int32, (STEP, depth), 0)
    here = (column // total) == position
    pick = [here & ((column % total) == chosen[s]) for s in range(sents)]
    pick = jnp.concatenate([jnp.where(item, 1.0, 0.0).astype(LOW) for item in pick], axis=0)
    for block in range(length // STEP):
        rows = slice(block * STEP, (block + 1) * STEP)
        found = mm(pick, tokens[rows].reshape(depth, width)).astype(LOW)
        for s in range(sents):
            x[s, rows, :] = found[s * STEP : (s + 1) * STEP]
    packed[...] = jnp.zeros_like(packed)

    def place(s, _):
        packed[rows_of(table, s), :] = x[s]
        return 0

    lax.fori_loop(0, sents, place, 0)

    def flip(i, _):
        rows = tile_at(i)
        turn(table, packed_t, rows, packed[rows, :])
        return 0

    lax.fori_loop(0, table[TILES], flip, 0)


def send_home(source, *refs):
    blocks, home = refs[:-1], refs[-1]
    share, total, width = home.shape
    depth = total * STEP
    column = lax.broadcasted_iota(jnp.int32, (depth, depth), 1)
    row = lax.broadcasted_iota(jnp.int32, (depth, depth), 0)
    pick = ((column % STEP) == (row // total)) & ((column // STEP) == source[...])
    pick = jnp.where(pick, 1.0, 0.0).astype(LOW)
    for block in range(share // STEP):
        rows = slice(block * STEP, (block + 1) * STEP)
        values = [item[:, rows, :].reshape(-1, width) for item in blocks]
        found = mm(pick, jnp.concatenate(values, axis=0)).astype(LOW)
        home[rows] = found.reshape(STEP, total, width)


def start_all(copies):
    for copy in copies:
        copy.start()


def wait_all(copies):
    for copy in copies:
        copy.wait()


def by_tiles(table, rows, body):
    for n in range(1, rows // TILE + 1):

        @pl.when(table[TILES] == n)
        def _():
            body(n * TILE)


def tile_copies(table, source, target, sems):
    def at(i):
        rows = slice(i * TILE, (i + 1) * TILE)
        return pltpu.make_async_copy(source.at[rows], target.at[rows], sems.at[i])

    def each(act):
        for i in range(sems.shape[0]):

            @pl.when(i < table[TILES])
            def _():
                act(at(i))

    return each


def place_weight(k, steps, weight, own_down, slabs):
    count, slab = slabs.shape[0], slabs.shape[1]
    columns = weight.shape[1]

    @pl.when(k == 0)
    def _():
        weight[:, columns // 2 :] = own_down[...].T

    for t in range(1, steps):

        @pl.when(k == t)
        def _():
            for j in range(count):
                weight[j * slab : (j + 1) * slab, :] = slabs[
                    j, :, (t - 1) * columns : t * columns
                ]


def attention_forward(table, packed, own_qkv, own_out, *refs):
    pieces, refs = refs[:-18], refs[-18:]
    proj_out, ctx_out, probs_out, qkv_out, wo_out, z1_out, root1 = refs[:7]
    proj, ctx, probs, qkv, wo, z1, slabs, sems, out_sems, wide_sems, z1_sems = refs[7:]
    sents, pairs = probs.shape[0], probs.shape[1]
    width = packed.shape[1]
    length = probs.shape[3]
    part = own_out.shape[0]
    block = 4 * part
    heads = part // HD
    arrivals = place_pieces(table, pieces, slabs, sems)
    start_all(arrivals)
    count, slab = slabs.shape[0], slabs.shape[1]
    for h in range(heads):
        for p in range(3):
            source = (h * 3 + p) * HD
            qkv[:, p * width + h * HD : p * width + (h + 1) * HD] = own_qkv[
                source : source + HD, :
            ].T
    wo[:, :part] = own_out[...].T
    ctx[...] = jnp.zeros_like(ctx)
    tiles = table[TILES]
    end = pl.ds(pl.multiple_of(tiles * TILE, TILE), length)
    proj[end, :] = jnp.zeros((length, 3 * width), LOW)
    wait_all(arrivals)
    for j in range(count):
        rows = slice(j * slab, (j + 1) * slab)
        for k in range(1, width // part):
            base = (k - 1) * block
            for p in range(3):
                qkv[rows, p * width + k * part : p * width + (k + 1) * part] = slabs[
                    j, :, base + p * part : base + (p + 1) * part
                ]
            wo[rows, k * part : (k + 1) * part] = slabs[j, :, base + 3 * part : base + block]
    wide_copies = [
        pltpu.make_async_copy(qkv, qkv_out, wide_sems.at[0]),
        pltpu.make_async_copy(wo, wo_out, wide_sems.at[1]),
    ]
    start_all(wide_copies)

    def project(n):
        source = packed[:n, :]
        for c in range(0, 3 * width, CHUNK):
            cols = slice(c, c + CHUNK)
            proj[:n, cols] = mm(source, qkv[:, cols]).astype(LOW)

    by_tiles(table, z1.shape[0], project)
    proj_copy = pltpu.make_async_copy(proj, proj_out, out_sems.at[0])
    proj_copy.start()

    def attend(s, _):
        rows = rows_of(table, s)
        valid = lax.broadcasted_iota(jnp.int32, (length, length), 0) < table[LENS + s]
        for p in range(pairs):
            at = p * PAIR
            queries = proj[rows, at : at + PAIR]
            keys = split_heads(proj[rows, width + at : width + at + PAIR])
            values = split_heads(proj[rows, 2 * width + at : 2 * width + at + PAIR])
            scores = mm(keys, queries, NT)
            for h in range(2):
                half = slice(h * length, (h + 1) * length)
                score = jnp.where(valid, scores[half], MASKED)
                top = jnp.max(score, axis=0, keepdims=True)
                score = jnp.exp2((score - top) * (HD**-0.5 * LOG2_E))
                total = jnp.sum(score, axis=0, keepdims=True)
                probs[s, p, half, :] = (score * (1.0 / total)).astype(LOW)
            ctx[rows, at : at + PAIR] = mm(probs[s, p].T, values).astype(LOW)
        return 0

    lax.fori_loop(0, sents, attend, 0)
    ctx_copies = [
        pltpu.make_async_copy(ctx, ctx_out, out_sems.at[1]),
        pltpu.make_async_copy(probs, probs_out, out_sems.at[2]),
    ]
    start_all(ctx_copies)

    for i in range(z1_sems.shape[0]):
        rows = slice(i * TILE, (i + 1) * TILE)

        @pl.when(i < tiles)
        def _():
            attended = mm(ctx[rows, :], wo[...], NT)
            z, root = normalize(packed[rows, :].astype(F32) + attended)
            z1[rows, :] = z
            root1[rows, :] = jnp.broadcast_to(root, (TILE, 128))
            pltpu.make_async_copy(z1.at[rows], z1_out.at[rows], z1_sems.at[i]).start()

    tile_copies(table, z1, z1_out, z1_sems)(lambda copy: copy.wait())
    wait_all(wide_copies + [proj_copy] + ctx_copies)


def gelu_parts(pre):
    t = pl.reciprocal(1.0 + jnp.abs(pre) * (0.3275911 * SQRT_HALF))
    poly = 0.5 * 1.061405429
    for c in (-1.453152027, 1.421413741, -0.284496736, 0.254829592):
        poly = poly * t + 0.5 * c
    e = jnp.exp2(pre * pre * (-0.5 * LOG2_E))
    tail = poly * t * e
    cdf = jnp.where(pre >= 0.0, 1.0 - tail, tail)
    return pre * cdf, cdf + pre * (e * INV_SQRT_2PI)


def ffn_forward(parts, table, z1_in, gain1, bias1, own_up, own_down_in, bias, gain2, bias2, *refs):
    pieces, refs = refs[:-16], refs[-16:]
    active, slope, z2_out, root2, pooled = refs[:5]
    weight, first, total, z1, z2, own_down, slabs, sems, own_sems, z1_sems, z2_sems = refs[5:]
    k = pl.program_id(0)
    steps = pl.num_programs(0)
    tiles = table[TILES]
    units = active.shape[2]
    arrivals = place_pieces(table, pieces, slabs, sems)
    own = [
        pltpu.make_async_copy(own_up, weight.at[:, :units], own_sems.at[0]),
        pltpu.make_async_copy(own_down_in, own_down, own_sems.at[1]),
    ]
    z1_copies = tile_copies(table, z1_in, z1, z1_sems)

    @pl.when(k == 0)
    def _():
        z1_copies(lambda copy: copy.start())
        start_all(own)
        start_all(arrivals)
        z1_copies(lambda copy: copy.wait())

        def start(i, _):
            rows = tile_at(i)
            value = z1[rows, :] * gain1[...] + bias1[...]
            first[rows, :] = value.astype(LOW)
            total[rows, :] = value
            return 0

        lax.fori_loop(0, tiles, start, 0)
        wait_all(own)

    @pl.when(k == 1)
    def _():
        wait_all(arrivals)

    place_weight(k, parts, weight, own_down, slabs)

    def work(n):
        source = first[:n, :]
        for c in range(0, units, CHUNK):
            cols = slice(c, c + CHUNK)
            act, slp = gelu_parts(mm(source, weight[:, cols]) + bias[0, :, cols])
            active[0, :n, cols] = act.astype(LOW)
            slope[0, :n, cols] = slp.astype(LOW)
        total[:n, :] += mm(active[0, :n, :], weight[:, units:], NT)

    by_tiles(table, first.shape[0], work)

    @pl.when(k == steps - 1)
    def _():
        z2[pl.ds(pl.multiple_of(tiles * TILE, TILE), 128), :] = jnp.zeros((128, z2.shape[1]), F32)

        def finish(i, _):
            rows = tile_at(i)
            z, root = normalize(total[rows, :])
            z2[rows, :] = z
            root2[rows, :] = jnp.broadcast_to(root, (TILE, 128))
            return 0

        lax.fori_loop(0, tiles, finish, 0)
        z2_copies = tile_copies(table, z2, z2_out, z2_sems)
        z2_copies(lambda copy: copy.start())
        for s in range(pooled.shape[0]):
            n = table[LENS + s]
            valid = lax.broadcasted_iota(jnp.int32, (128, z2.shape[1]), 0) < n
            rows = jnp.where(valid, z2[rows_of(table, s), :], 0.0)
            mean = jnp.sum(rows, axis=0, keepdims=True) / n.astype(F32)
            pooled[s : s + 1, :] = mean * gain2[...] + bias2[...]
        z2_copies(lambda copy: copy.wait())


def weight_grad(table, turned, right, store):
    count, slab, rows = turned.shape

    def body(n):
        if slab % 16 == 0:
            left = turned[:, :, :n].reshape(count * slab, n)
        else:
            left = jnp.concatenate([turned[j, :, :n] for j in range(count)], axis=0)
        store(lambda columns: mm(left, right(n, columns)))

    by_tiles(table, rows, body)


def split_send(mine, other, value, k, columns):
    chips, slab = mine.shape[0], mine.shape[2]
    for m in range(chips):
        mine[m, k, :, columns] = value[m * slab : (m + 1) * slab].astype(LOW)
        other[m, k, :, columns] = value[(chips + m) * slab : (chips + m + 1) * slab].astype(LOW)


def send_chunks(mine, other, product):
    for c in range(0, mine.shape[3], CHUNK):
        cols = slice(c, c + CHUNK)
        split_send(mine, other, product(cols), 0, cols)


def ffn_backward(
    parts, table, pool, z2_in, root2, gain2, z1_in, root1, gain1, bias1, own_up, own_down_in,
    active, slope, *refs
):
    pieces, refs = refs[:-22], refs[-22:]
    down_mine, down_other, up_mine, up_other, attn_low, attn_t, sums, bias_sum = refs[:8]
    weight, z1, z2, total, branch, branch_t, first_t, hidden, own_down, slabs = refs[8:18]
    sems, own_sems, z1_sems, z2_sems = refs[18:]
    k = pl.program_id(0)
    tiles = table[TILES]
    width, units = own_up.shape
    arrivals = place_pieces(table, pieces, slabs, sems)
    own = [
        pltpu.make_async_copy(own_up, weight.at[:, :units], own_sems.at[0]),
        pltpu.make_async_copy(own_down_in, own_down, own_sems.at[1]),
    ]
    z1_copies = tile_copies(table, z1_in, z1, z1_sems)
    z2_copies = tile_copies(table, z2_in, z2, z2_sems)

    @pl.when(k == 0)
    def _():
        z2_copies(lambda copy: copy.start())
        z1_copies(lambda copy: copy.start())
        start_all(own)
        start_all(arrivals)
        total[...] = jnp.zeros_like(total)
        for s in range(pool.shape[0]):
            n = table[LENS + s]
            valid = lax.broadcasted_iota(jnp.int32, (128, width), 0) < n
            row = pool[s : s + 1, :] / n.astype(F32)
            total[rows_of(table, s), :] = jnp.where(valid, row, 0.0)
        sums[...] = jnp.zeros_like(sums)
        z2_copies(lambda copy: copy.wait())
        z1_copies(lambda copy: copy.wait())

        def start(i, _):
            rows = tile_at(i)
            grad = total[rows, :]
            z = z2[rows, :]
            sums[0:1, :] += jnp.sum(grad * z, axis=0, keepdims=True)
            sums[1:2, :] += jnp.sum(grad, axis=0, keepdims=True)
            value = normalize_back(z, root2[rows, 0:1], grad * gain2[...])
            low = value.astype(LOW)
            total[rows, :] = value
            branch[rows, :] = low
            turn(table, branch_t, rows, low)
            turn(table, first_t, rows, (z1[rows, :] * gain1[...] + bias1[...]).astype(LOW))
            return 0

        lax.fori_loop(0, tiles, start, 0)
        wait_all(own)

    @pl.when(k == 1)
    def _():
        wait_all(arrivals)

    place_weight(k, parts, weight, own_down, slabs)
    weight_grad(
        table,
        branch_t,
        lambda n, cols: active[0, :n, cols],
        lambda product: send_chunks(down_mine, down_other, product),
    )
    bias_sum[...] = jnp.zeros_like(bias_sum)

    def work(n):
        source = branch[:n, :]
        for c in range(0, units, CHUNK):
            cols = slice(c, c + CHUNK)
            grad = mm(source, weight[:, units + c : units + c + CHUNK])
            hid = (slope[0, :n, cols].astype(F32) * grad).astype(LOW)
            hidden[:n, cols] = hid
            bias_sum[0, :, cols] += jnp.sum(hid.astype(F32), axis=0, keepdims=True)
        total[:n, :] += mm(hidden[:n, :], weight[:, :units], NT)

    by_tiles(table, hidden.shape[0], work)
    weight_grad(
        table,
        first_t,
        lambda n, cols: hidden[:n, cols],
        lambda product: send_chunks(up_mine, up_other, product),
    )

    @pl.when(k == pl.num_programs(0) - 1)
    def _():
        def finish(i, _):
            rows = tile_at(i)
            grad = total[rows, :]
            z = z1[rows, :]
            sums[2:3, :] += jnp.sum(grad * z, axis=0, keepdims=True)
            sums[3:4, :] += jnp.sum(grad, axis=0, keepdims=True)
            value = normalize_back(z, root1[rows, 0:1], grad * gain1[...])
            low = value.astype(LOW)
            attn_low[rows, :] = low
            turn(table, attn_t, rows, low)
            return 0

        lax.fori_loop(0, tiles, finish, 0)


def attention_backward(table, attn_low, wo, proj_in, probs_in, qkv_in, proj_grad_out, *refs):
    outs, refs = refs[:-7], refs[-7:]
    ctx_grad, proj, probs, qkv, proj_grad, sems, out_sem = refs
    sents, pairs = probs.shape[0], probs.shape[1]
    length = probs.shape[3]
    width = attn_low.shape[1]
    tiles = table[TILES]
    arrivals = [
        pltpu.make_async_copy(proj_in, proj, sems.at[0]),
        pltpu.make_async_copy(probs_in, probs, sems.at[1]),
        pltpu.make_async_copy(qkv_in, qkv, sems.at[2]),
    ]
    start_all(arrivals)
    ctx_grad[...] = jnp.zeros_like(ctx_grad)
    proj_grad[...] = jnp.zeros_like(proj_grad)

    def start(n):
        ctx_grad[:n, :] = mm(attn_low[:n, :], wo[...]).astype(LOW)

    by_tiles(table, attn_low.shape[0], start)
    wait_all(arrivals[:2])
    scale = HD**-0.5

    def attend(s, _):
        rows = rows_of(table, s)
        live = lax.broadcasted_iota(jnp.int32, (length, PAIR), 0) < table[LENS + s]
        for p in range(pairs):
            at = p * PAIR
            queries = proj[rows, at : at + PAIR]
            keys = split_heads(proj[rows, width + at : width + at + PAIR])
            values = split_heads(proj[rows, 2 * width + at : 2 * width + at + PAIR])
            grad = ctx_grad[rows, at : at + PAIR]
            grad = jnp.where(live, grad, jnp.zeros_like(grad))
            prob_grad = mm(values, grad, NT)
            score_grad = []
            for h in range(2):
                half = slice(h * length, (h + 1) * length)
                prob = probs[s, p, half, :].astype(F32)
                part = prob_grad[half]
                inner = jnp.sum(prob * part, axis=0, keepdims=True)
                score_grad.append((prob * (part - inner)).astype(LOW))
            score_grad = jnp.concatenate(score_grad, axis=0)
            proj_grad[rows, at : at + PAIR] = (mm(score_grad.T, keys) * scale).astype(LOW)
            proj_grad[rows, width + at : width + at + PAIR] = (
                join_heads(mm(score_grad, queries)) * scale
            ).astype(LOW)
            proj_grad[rows, 2 * width + at : 2 * width + at + PAIR] = join_heads(
                mm(probs[s, p], grad)
            ).astype(LOW)
        return 0

    lax.fori_loop(0, sents, attend, 0)
    proj_copy = pltpu.make_async_copy(proj_grad, proj_grad_out, out_sem.at[0])
    proj_copy.start()
    arrivals[2].wait()

    def finish(n):
        total = mm(proj_grad[:n, :], qkv[...], NT)
        ctx_grad[:n, :] = (attn_low[:n, :].astype(F32) + total).astype(LOW)

    by_tiles(table, attn_low.shape[0], finish)
    ctx_grad[pl.ds(pl.multiple_of(tiles * TILE, TILE), length), :] = jnp.zeros(
        (length, width), LOW
    )
    share = outs[0].shape[1]
    for k, out in enumerate(outs):
        first = table[LINE + k] * share
        position = lax.broadcasted_iota(jnp.int32, (share, width), 0) + first
        for s in range(sents):
            value = ctx_grad[pl.ds(pl.multiple_of(table[s] + first, 16), share), :]
            out[s] = jnp.where(position < table[LENS + s], value, jnp.zeros_like(value))
    proj_copy.wait()


def attention_weights(table, *refs):
    sources, (mine, other), (packed_t, attn_t, ctx, proj_grad, sems) = refs[:4], refs[4:6], refs[6:]
    width = ctx.shape[1]
    count = mine.shape[1]
    part = width // count
    copies = [
        pltpu.make_async_copy(source, target, sems.at[i])
        for i, (source, target) in enumerate(zip(sources[:3], (packed_t, attn_t, ctx)))
    ]
    for p in range(3):
        cols = slice(p * width, (p + 1) * width)
        copies.append(
            pltpu.make_async_copy(sources[3].at[:, cols], proj_grad.at[:, cols], sems.at[3 + p])
        )
    order = [copies[1], copies[2], copies[0]] + copies[3:]
    start_all(order)

    def store(p, product):
        value = product(slice(p * width, (p + 1) * width) if p < 3 else slice(None))
        for k in range(count):
            split_send(
                mine,
                other,
                value[:, k * part : (k + 1) * part],
                k,
                slice(p * part, (p + 1) * part),
            )

    wait_all(order[:2])
    weight_grad(
        table, attn_t, lambda n, cols: ctx[:n, cols], lambda product: store(3, product)
    )
    order[2].wait()
    for p in range(3):
        order[3 + p].wait()
        weight_grad(
            table,
            packed_t,
            lambda n, cols: proj_grad[:n, cols],
            lambda product: store(p, product),
        )


def place_grads(table, *refs):
    pieces, (straight, turned, slabs, flat, sems) = refs[:-5], refs[-5:]
    count, slab = slabs.shape[0], slabs.shape[1]
    arrivals = place_pieces(table, pieces, slabs, sems)
    start_all(arrivals)
    wait_all(arrivals)
    width = straight.shape[1]
    for j in range(count):
        rows = slice(j * slab, (j + 1) * slab)
        straight[rows, :] = slabs[j, :, :width].astype(F32)
        flat[rows, :] = slabs[j, :, width:].astype(F32)
    turned[...] = flat[...].T


def place_attention_grads(table, *refs):
    pieces, (qkv, wo, slabs, flat, sems) = refs[:-5], refs[-5:]
    count, slab = slabs.shape[0], slabs.shape[1]
    arrivals = place_pieces(table, pieces, slabs, sems)
    start_all(arrivals)
    wait_all(arrivals)
    for j in range(count):
        flat[j * slab : (j + 1) * slab, :] = slabs[j].astype(F32)
    part = wo.shape[0]
    heads = part // HD
    for p in range(3):
        piece = flat[:, p * part : (p + 1) * part].T
        for h in range(heads):
            target = (h * 3 + p) * HD
            qkv[target : target + HD, :] = piece[h * HD : (h + 1) * HD, :]
    wo[...] = flat[:, 3 * part :].T


COST = 1000000
SMEM = pl.BlockSpec(memory_space=pltpu.SMEM)
VMEM = pl.BlockSpec(memory_space=pltpu.VMEM)
ANY = pl.BlockSpec(memory_space=pl.ANY)


def shape(dims, dtype):
    return jax.ShapeDtypeStruct(dims, dtype)


def params():
    return pltpu.CompilerParams(vmem_limit_bytes=VMEM_BYTES)


def cost(flops, nbytes):
    return pl.CostEstimate(flops=flops // COST, bytes_accessed=nbytes // COST, transcendentals=0)


def add(*terms):
    return sum(term.astype(F32) for term in terms)


def swap(value, mask, axis="dp"):
    return lax.ppermute(value, axis, [(i, i ^ mask) for i in range(lax.axis_size(axis))])


def bits_of(count):
    return [1 << i for i in range(count.bit_length() - 1)]


def take(values, index, axis=0):
    return lax.dynamic_index_in_dim(values, index, axis, False, allow_negative_indices=False)


def cut(values, start, size, axis):
    return lax.dynamic_slice_in_dim(values, start, size, axis, allow_negative_indices=False)


def tie(*values):
    return lax.optimization_barrier(values)


def gather_line(piece):
    n = lax.axis_size("tensor")
    return jnp.concatenate([swap(piece, k, "tensor") for k in range(1, n)], axis=1)


def gather_chips(value):
    return [value] + [swap(value, 2 * m) for m in range(1, lax.axis_size("dp") // 2)]


def gather_cores(near):
    return near + [swap(item, 1) for item in near]


def gather_plane(value):
    return gather_cores(gather_chips(value))


def pick(term, side, bit):
    dims = term.shape
    view = term.reshape((dims[0] // (2 * bit), 2, bit) + dims[1:])[:, side]
    return view.reshape((dims[0] // 2,) + dims[1:])


def sent(terms, bit):
    return add(*[pick(term, 1, bit) for term in terms]).astype(LOW)


def kept(terms, bit, landed):
    return [pick(term, 0, bit) for term in terms] + [landed]


def reduce_line(terms):
    for bit in bits_of(lax.axis_size("tensor")):
        terms = kept(terms, 1, swap(sent(terms, 1), bit, "tensor"))
    return add(*terms)[0].astype(LOW)


def reduce_chips(terms, bits):
    for bit in bits:
        terms = kept(terms, 1, swap(sent(terms, 1), 2 * bit))
    return terms


def shards(
    tokens,
    lengths,
    partner,
    w_qkv,
    w_out,
    ln1_gain,
    ln1_bias,
    up_weight,
    up_projection_bias,
    down_weight,
    ln2_gain,
    ln2_bias,
    cot_pooled,
    cot_paired,
):
    dp_count = lax.axis_size("dp")
    t_count = lax.axis_size("tensor")
    dp_me = lax.axis_index("dp")
    t_me = lax.axis_index("tensor")
    length, sentences, width = tokens.shape
    mine = sentences // t_count
    rows = mine * length
    pad = rows + length
    slab = width // dp_count
    chips = dp_count // 2
    heads = w_qkv.shape[1] // (3 * HD)
    units = up_weight.shape[1]
    ctx_cols = w_out.shape[0]
    block = 4 * ctx_cols

    def by_part(weight):
        return weight.reshape(-1, heads, 3, HD).transpose(0, 2, 1, 3).reshape(weight.shape)

    def rows_piece(weight):
        return cut(weight, dp_me * slab, slab, 0)

    def columns_piece(weight):
        return cut(weight, dp_me * slab, slab, 1).T

    attn_piece = jnp.concatenate([by_part(rows_piece(w_qkv)), columns_piece(w_out)], axis=1)
    attn_piece, up_early, down_early = tie(attn_piece, up_weight, down_weight)
    attn_line = gather_line(attn_piece)
    ffn_piece = jnp.concatenate([rows_piece(up_early), columns_piece(down_early)], axis=1)
    ffn_parts, bias_parts = [ffn_piece], [up_projection_bias.reshape(1, units)]

    def widen_line(parts, bit):
        return parts + [swap(jnp.concatenate(parts, axis=1), bit, "tensor")]

    ffn_parts = widen_line(ffn_parts, 1)
    bias_parts = widen_line(bias_parts, 1)

    order = np.arange(sentences)
    ahead = (lengths[None, :] > lengths[:, None]) | (
        (lengths[None, :] == lengths[:, None]) & (order[None, :] < order[:, None])
    )
    rank = jnp.sum(ahead.astype(jnp.int32), axis=1)
    row = rank // t_count
    column = rank % t_count
    column = jnp.where(row % 2 == 0, column, t_count - 1 - column)
    mine_here = (column == t_me)[None, :] & (row[None, :] == order[:mine, None])
    chosen = jnp.sum(jnp.where(mine_here, order[None, :], 0), axis=1)
    counts = jnp.sum(jnp.where(mine_here, lengths[None, :], 0), axis=1)
    source = (column ^ t_me) * mine + row
    taken = (counts + 15) & ~15
    ends = jnp.sum(jnp.where(np.tri(mine, dtype=bool), taken[None, :], 0), axis=1)
    devices = np.arange(dp_count)
    distance = 2 * np.arange(chips)
    near = devices[:, None] ^ distance[None, :]
    spots = np.concatenate([near, near ^ 1], axis=1)
    lines = np.arange(t_count)[:, None] ^ np.arange(t_count)[None, :]
    apart = devices[:, None] ^ devices[None, :]
    fixed = np.zeros((dp_count, DEST - PLACE + dp_count), np.int32)
    fixed[:, :dp_count] = spots
    fixed[:, DEST - PLACE :] = apart % 2 * chips + apart // 2
    line_fixed = np.zeros((t_count, PLACE - LINE), np.int32)
    line_fixed[:, :t_count] = lines
    table = jnp.concatenate(
        [
            ends - taken,
            np.zeros(LENS - mine, np.int32),
            counts,
            np.zeros(TILES - LENS - mine, np.int32),
            (ends[-1:] + (TILE - 1)) >> (TILE.bit_length() - 1),
            take(jnp.asarray(line_fixed), t_me),
            take(jnp.asarray(fixed), dp_me),
        ]
    ).astype(jnp.int32)
    turn_shape = shape((dp_count, slab, rows), LOW)
    packed, packed_t = pl.pallas_call(
        pack,
        out_shape=(shape((pad, width), LOW), turn_shape),
        in_specs=[SMEM, SMEM, VMEM],
        out_specs=(VMEM,) * 2,
        scratch_shapes=[pltpu.VMEM((mine, length, width), LOW)],
        compiler_params=params(),
        cost_estimate=cost(0, 8 * rows * width),
        name="pack",
    )(table, chosen, tokens)

    attn_line, ffn_parts[1], bias_parts[1], packed = tie(
        attn_line, ffn_parts[1], bias_parts[1], packed
    )
    attn_chips = gather_chips(attn_line)
    for bit in bits_of(t_count)[1:]:
        ffn_parts = widen_line(ffn_parts, bit)
        bias_parts = widen_line(bias_parts, bit)
    bias_all = jnp.concatenate(bias_parts, axis=1).reshape(t_count, 1, units)
    attn_pieces = gather_cores(list(tie(*attn_chips)))
    ffn_chips = gather_chips(jnp.concatenate(ffn_parts[1:], axis=1))
    attn_pieces[0], ffn_chips[0], bias_all = tie(attn_pieces[0], ffn_chips[0], bias_all)
    pairs = width // PAIR
    probs_shape = (mine, pairs, 2 * length, length)
    proj, ctx, probs, qkv, wo, z1, root1 = pl.pallas_call(
        attention_forward,
        out_shape=(
            shape((pad, 3 * width), LOW),
            shape((pad, width), LOW),
            shape(probs_shape, LOW),
            shape((width, 3 * width), LOW),
            shape((width, width), LOW),
            shape((rows, width), F32),
            shape((rows, 128), F32),
        ),
        in_specs=[SMEM, VMEM, VMEM, VMEM] + [ANY] * dp_count,
        out_specs=(ANY,) * 6 + (VMEM,),
        scratch_shapes=[
            pltpu.VMEM((pad, 3 * width), LOW),
            pltpu.VMEM((pad, width), LOW),
            pltpu.VMEM(probs_shape, LOW),
            pltpu.VMEM((width, 3 * width), LOW),
            pltpu.VMEM((width, width), LOW),
            pltpu.VMEM((rows, width), F32),
            pltpu.VMEM((dp_count, slab, (t_count - 1) * block), LOW),
            pltpu.SemaphoreType.DMA((dp_count,)),
            pltpu.SemaphoreType.DMA((3,)),
            pltpu.SemaphoreType.DMA((2,)),
            pltpu.SemaphoreType.DMA((rows // TILE,)),
        ],
        compiler_params=params(),
        cost_estimate=cost(8 * rows * width * width, 30 * rows * width),
        name="attention_forward",
    )(table, packed, w_qkv.T, w_out, *attn_pieces)
    *ffn_chips, z1 = tie(*ffn_chips, z1)
    ffn_pieces = gather_cores(ffn_chips)

    gain1, bias1 = ln1_gain.reshape(1, width), ln1_bias.reshape(1, width)
    gain2, bias2 = ln2_gain.reshape(1, width), ln2_bias.reshape(1, width)

    def whole(*dims):
        return pl.BlockSpec(dims, lambda k, table: (0,) * len(dims))

    def call(kernel, outs, ins, out_specs, scratch, flops, nbytes):
        return pl.pallas_call(
            functools.partial(kernel, t_count),
            out_shape=outs,
            grid_spec=pltpu.PrefetchScalarGridSpec(
                num_scalar_prefetch=1,
                grid=(t_count,),
                in_specs=ins,
                out_specs=out_specs,
                scratch_shapes=scratch,
            ),
            compiler_params=params(),
            cost_estimate=cost(flops, nbytes),
            name=kernel.__name__,
        )

    act_spec = pl.BlockSpec((1, rows, units), lambda k, table: (k, 0, 0))
    bias_spec = pl.BlockSpec((1, 1, units), lambda k, table: (k, 0, 0))
    line = whole(1, width)
    full = whole(rows, width)
    root_spec = whole(rows, 128)
    act_shape = shape((t_count, rows, units), LOW)
    weight_scratch = [
        pltpu.VMEM((units, width), LOW),
        pltpu.VMEM((dp_count, slab, (t_count - 1) * 2 * units), LOW),
        pltpu.SemaphoreType.DMA((dp_count,)),
        pltpu.SemaphoreType.DMA((2,)),
        pltpu.SemaphoreType.DMA((rows // TILE,)),
        pltpu.SemaphoreType.DMA((rows // TILE,)),
    ]
    active, slope, z2, root2, pooled = call(
        ffn_forward,
        (
            act_shape,
            act_shape,
            shape((rows, width), F32),
            shape((rows, 128), F32),
            shape((mine, width), F32),
        ),
        [ANY, line, line, ANY, ANY, bias_spec, line, line] + [ANY] * dp_count,
        (act_spec, act_spec, ANY, root_spec, whole(mine, width)),
        [
            pltpu.VMEM((width, 2 * units), LOW),
            pltpu.VMEM((rows, width), LOW),
            pltpu.VMEM((rows, width), F32),
            pltpu.VMEM((rows, width), F32),
            pltpu.VMEM((pad, width), F32),
        ]
        + weight_scratch,
        4 * rows * width * units * t_count,
        40 * rows * width,
    )(table, z1, gain1, bias1, up_weight, down_weight, bias_all, gain2, bias2, *ffn_pieces)

    pooled = pooled.astype(LOW)
    line_pooled = jnp.stack([pooled] + [swap(pooled, k, "tensor") for k in range(1, t_count)])
    returned = line_pooled.reshape(sentences, width)[source]
    both = jnp.concatenate([returned, cot_paired])
    everyone = jnp.stack(gather_plane(both)).reshape(-1, width)
    apart = (partner // sentences) ^ dp_me
    base = ((apart & 1) * chips + (apart >> 1)) * (2 * sentences) + partner % sentences
    partner_pooled = everyone[base].astype(F32)
    partner_cot = everyone[base + sentences].astype(F32)
    paired = (returned.astype(F32) * partner_pooled).astype(LOW)
    pool_grad = cot_pooled.astype(F32) + partner_pooled * (cot_paired.astype(F32) + partner_cot)
    pool_grad = pool_grad.astype(LOW).astype(F32)[chosen]

    send_spec = pl.BlockSpec((chips, 1, slab, units), lambda k, table: (0, k, 0, 0))
    send_shape = shape((chips, t_count, slab, units), LOW)
    down_mine, down_other, up_mine, up_other, attn_low, attn_t, sums, bias_sum = call(
        ffn_backward,
        (send_shape,) * 4
        + (
            shape((rows, width), LOW),
            turn_shape,
            shape((4, width), F32),
            shape((t_count, 1, units), F32),
        ),
        [whole(mine, width), ANY, root_spec, line, ANY, root_spec, line, line, ANY, ANY]
        + [act_spec, act_spec]
        + [ANY] * dp_count,
        (send_spec,) * 4 + (full, whole(dp_count, slab, rows), whole(4, width), bias_spec),
        [
            pltpu.VMEM((width, 2 * units), LOW),
            pltpu.VMEM((rows, width), F32),
            pltpu.VMEM((rows, width), F32),
            pltpu.VMEM((pad, width), F32),
            pltpu.VMEM((rows, width), LOW),
            pltpu.VMEM((dp_count, slab, rows), LOW),
            pltpu.VMEM((dp_count, slab, rows), LOW),
            pltpu.VMEM((rows, units), LOW),
        ]
        + weight_scratch,
        8 * rows * width * units * t_count,
        60 * rows * width,
    )(
        table, pool_grad, z2, root2, gain2, z1, root1, gain1, bias1, up_weight, down_weight,
        active, slope, *ffn_pieces
    )

    chip_bits = bits_of(chips)
    high = chip_bits[-1]
    down_terms, up_terms = [down_mine, swap(down_other, 1)], [up_mine, swap(up_other, 1)]
    small = jnp.concatenate([bias_sum.reshape(t_count, units), sums])
    small = small + swap(small, 1)
    down_sent, up_sent, small, attn_low = tie(
        sent(down_terms, 1), sent(up_terms, high), small, attn_low
    )
    small_got = swap(small, 2)
    down_got, up_got = swap(down_sent, 2), swap(up_sent, 2 * high)

    share = length // t_count
    proj_grad, *input_blocks = pl.pallas_call(
        attention_backward,
        out_shape=(shape((pad, 3 * width), LOW),)
        + (shape((mine, share, width), LOW),) * t_count,
        in_specs=[SMEM, VMEM, VMEM, ANY, ANY, ANY],
        out_specs=(ANY,) + (VMEM,) * t_count,
        scratch_shapes=[
            pltpu.VMEM((pad, width), LOW),
            pltpu.VMEM((pad, 3 * width), LOW),
            pltpu.VMEM(probs_shape, LOW),
            pltpu.VMEM((width, 3 * width), LOW),
            pltpu.VMEM((pad, 3 * width), LOW),
            pltpu.SemaphoreType.DMA((3,)),
            pltpu.SemaphoreType.DMA((1,)),
        ],
        compiler_params=params(),
        cost_estimate=cost(12 * rows * width * width, 30 * rows * width),
        name="attention_backward",
    )(table, attn_low, wo, proj, probs, qkv)

    down_got, up_got, small_got, proj_grad, *input_blocks = tie(
        down_got, up_got, small_got, proj_grad, *input_blocks
    )
    small = small + small_got
    down_terms, up_terms = kept(down_terms, 1, down_got), kept(up_terms, high, up_got)
    for low, top in zip(chip_bits[1:-1], chip_bits[1:-1][::-1]):
        down_terms = kept(down_terms, 1, swap(sent(down_terms, 1), 2 * low))
        up_terms = kept(up_terms, top, swap(sent(up_terms, top), 2 * top))
    down_sent, up_sent, small, proj_grad, *input_blocks = tie(
        sent(down_terms, 1), sent(up_terms, 1), small, proj_grad, *input_blocks
    )
    small_got = swap(small, 4)
    down_got, up_got = swap(down_sent, 2 * high), swap(up_sent, 2)
    input_landed = [input_blocks[0]] + [None] * (t_count - 1)
    input_landed[2] = swap(input_blocks[2], 2, "tensor")
    input_landed[1] = swap(input_blocks[1], 1, "tensor")

    attn_mine, attn_other = pl.pallas_call(
        attention_weights,
        out_shape=(shape((chips, t_count, slab, block), LOW),) * 2,
        in_specs=[SMEM] + [ANY] * 4,
        out_specs=(VMEM,) * 2,
        scratch_shapes=[
            pltpu.VMEM((dp_count, slab, rows), LOW),
            pltpu.VMEM((dp_count, slab, rows), LOW),
            pltpu.VMEM((pad, width), LOW),
            pltpu.VMEM((pad, 3 * width), LOW),
            pltpu.SemaphoreType.DMA((6,)),
        ],
        compiler_params=params(),
        cost_estimate=cost(8 * rows * width * width, 30 * rows * width),
        name="attention_weights",
    )(table, packed_t, attn_t, ctx, proj_grad)

    def finish(kernel, pieces, outs, flat):
        return pl.pallas_call(
            kernel,
            out_shape=tuple(shape(dims, F32) for dims in outs),
            in_specs=[SMEM] + [ANY] * dp_count,
            out_specs=(VMEM,) * 2,
            scratch_shapes=[
                pltpu.VMEM((dp_count,) + pieces[0].shape, LOW),
                pltpu.VMEM((width, flat), F32),
                pltpu.SemaphoreType.DMA((dp_count,)),
            ],
            compiler_params=params(),
            cost_estimate=cost(0, 8 * width * pieces[0].shape[1]),
            name=kernel.__name__,
        )(table, *pieces)

    attn_other, small_got, down_got, up_got, input_landed[1], input_landed[2] = tie(
        attn_other, small_got, down_got, up_got, input_landed[1], input_landed[2]
    )
    small = small + small_got
    for mask in bits_of(dp_count)[3:]:
        small = small + swap(small, mask)
    attn_got = swap(attn_other, 1)
    attn_sent = [add(attn_mine[m], attn_got[m]).astype(LOW) for m in range(1, chips)]
    ffn_line = jnp.concatenate(
        [add(*kept(up_terms, 1, up_got))[0], add(*kept(down_terms, 1, down_got))[0]], axis=2
    )
    ffn_line = [ffn_line.astype(LOW)]
    ffn_sent, input_blocks[3], small, *attn_sent = tie(
        sent(ffn_line, 1), input_blocks[3], small, *attn_sent
    )
    attn_got = [attn_got[0]] + [swap(item, 2 * m) for m, item in zip(range(1, chips), attn_sent)]
    ffn_got = swap(ffn_sent, 1, "tensor")
    input_landed[3] = swap(input_blocks[3], 3, "tensor")
    norms, bias_part = small[t_count:], small[:t_count]

    def small_step(norms, bias_part, mask):
        half = bias_part.shape[0] // 2
        split = bias_part.reshape(half, 2, units)
        got = swap(jnp.concatenate([split[:, 1], norms]), mask, "tensor")
        return norms, got, split[:, 0]

    def small_sum(norms, got, bias_part):
        half = bias_part.shape[0]
        return norms + got[half:], bias_part + got[:half]

    ffn_line = kept(ffn_line, 1, ffn_got)
    ffn_got = swap(sent(ffn_line, 1), 2, "tensor")
    *attn_got, ffn_got, norms, input_landed[3] = tie(
        *attn_got, ffn_got, norms, input_landed[3]
    )
    attn_line = [add(attn_mine[0], *attn_got).astype(LOW)]
    ffn_sum = add(*kept(ffn_line, 1, ffn_got))[0].astype(LOW)
    attn_sent, ffn_sum, norms = tie(sent(attn_line, 1), ffn_sum, norms)
    attn_got = swap(attn_sent, 1, "tensor")
    ffn_chips = gather_chips(ffn_sum)
    norms, small_got, bias_part = small_step(norms, bias_part, 1)
    attn_got, small_got, *ffn_chips = tie(attn_got, small_got, *ffn_chips)
    norms, bias_part = small_sum(norms, small_got, bias_part)
    attn_line = kept(attn_line, 1, attn_got)
    attn_sent, norms, ffn_chips[0] = tie(sent(attn_line, 1), norms, ffn_chips[0])
    attn_got = swap(attn_sent, 2, "tensor")
    norms, small_got, bias_part = small_step(norms, bias_part, 2)
    norms, bias_part = small_sum(norms, small_got, bias_part)
    attn_sum = add(*kept(attn_line, 1, attn_got))[0].astype(LOW)
    attn_sum, ffn_chips[0], input_landed[0] = tie(attn_sum, ffn_chips[0], input_landed[0])
    attn_chips = gather_chips(attn_sum)
    home = pl.pallas_call(
        send_home,
        out_shape=shape((share, sentences, width), LOW),
        in_specs=[VMEM] * (1 + t_count),
        out_specs=VMEM,
        compiler_params=params(),
        cost_estimate=cost(0, 4 * share * sentences * width),
        name="send_home",
    )(jnp.tile(source, STEP).reshape(-1, 1), *input_landed)
    up_grad, down_grad = finish(
        place_grads, gather_cores(ffn_chips), ((width, units), (units, width)), units
    )
    attn_chips[0], up_grad, home = tie(attn_chips[0], up_grad, home)
    qkv_grad, out_grad = finish(
        place_attention_grads,
        gather_cores(attn_chips),
        ((3 * ctx_cols, width), (ctx_cols, width)),
        block,
    )

    return (
        returned,
        paired,
        home,
        qkv_grad.T,
        out_grad,
        norms[2],
        norms[3],
        up_grad,
        bias_part[0],
        down_grad,
        norms[0],
        norms[1],
    )


def solution(mesh):
    placed = (
        P(None, "dp", None),
        P("dp"),
        P("dp"),
        P(None, "tensor"),
        P("tensor", None),
        P(),
        P(),
        P(None, "tensor"),
        P("tensor"),
        P("tensor", None),
        P(),
        P(),
        P("dp", None),
        P("dp", None),
    )
    return jax.shard_map(
        shards,
        mesh=mesh,
        in_specs=placed,
        out_specs=(
            P("dp", None),
            P("dp", None),
            P("tensor", "dp", None),
            P(None, "tensor"),
            P("tensor", None),
            P(),
            P(),
            P(None, "tensor"),
            P("tensor"),
            P("tensor", None),
            P(),
            P(),
        ),
        check_vma=False,
    )
```

```python
import functools

import jax
import jax.numpy as jnp
import numpy as np
from jax import lax
from jax.experimental import pallas as pl
from jax.experimental.pallas import tpu as pltpu
from jax.sharding import PartitionSpec as P

HD = 64
EPSILON = 1e-06
LOW = jnp.bfloat16
F32 = jnp.float32
INV_SQRT_2PI = 0.3989422804014327
SQRT_HALF = 0.7071067811865476
TILE = 256
CHUNK = 256
STEP = 16
MASKED = -1000000000.0
LOG2_E = 1.4426950408889634
VMEM_BYTES = 60 * 2**20
NN = (((1,), (0,)), ((), ()))
NT = (((1,), (1,)), ((), ()))
PAIR = 2 * HD
LENS, TILES, LINE, PLACE, DEST = 16, 32, 33, 48, 80


def mm(a, b, dims=NN):
    return lax.dot_general(a, b, dims, preferred_element_type=F32)


def rows_of(table, s):
    return pl.ds(pl.multiple_of(table[s], 16), 128)


def tile_at(i):
    return pl.ds(pl.multiple_of(i * TILE, TILE), TILE)


def normalize(values):
    center = values - jnp.mean(values, axis=-1, keepdims=True)
    spread = jnp.mean(center * center, axis=-1, keepdims=True)
    root = lax.rsqrt(spread + EPSILON)
    return center * root, root


def normalize_back(z, root, dz):
    return root * (
        dz - jnp.mean(dz, -1, keepdims=True) - z * jnp.mean(dz * z, -1, keepdims=True)
    )


def split_heads(pair):
    first = lax.broadcasted_iota(jnp.int32, pair.shape, 1) < HD
    zero = jnp.zeros_like(pair)
    return jnp.concatenate([jnp.where(first, pair, zero), jnp.where(first, zero, pair)], axis=0)


def join_heads(split):
    n = split.shape[0] // 2
    first = lax.broadcasted_iota(jnp.int32, (n, PAIR), 1) < HD
    return jnp.where(first, split[:n], split[n:])


def place_pieces(table, pieces, slabs, sems):
    copies = []
    for i, piece in enumerate(pieces):
        copies.append(pltpu.make_async_copy(piece, slabs.at[table[PLACE + i]], sems.at[i]))
    return copies


def turn(table, turned, rows, value):
    flat = value.T
    count, slab = turned.shape[0], turned.shape[1]
    for j in range(count):
        turned[table[DEST + j], :, rows] = flat[j * slab : (j + 1) * slab, :]


def pack(table, chosen, tokens, packed, packed_t, x):
    sents, length, width = x.shape
    total = tokens.shape[1]
    depth = total * STEP
    column = lax.broadcasted_iota(jnp.int32, (STEP, depth), 1)
    position = lax.broadcasted_iota(jnp.int32, (STEP, depth), 0)
    here = (column // total) == position
    pick = [here & ((column % total) == chosen[s]) for s in range(sents)]
    pick = jnp.concatenate([jnp.where(item, 1.0, 0.0).astype(LOW) for item in pick], axis=0)
    for block in range(length // STEP):
        rows = slice(block * STEP, (block + 1) * STEP)
        found = mm(pick, tokens[rows].reshape(depth, width)).astype(LOW)
        for s in range(sents):
            x[s, rows, :] = found[s * STEP : (s + 1) * STEP]
    packed[...] = jnp.zeros_like(packed)

    def place(s, _):
        packed[rows_of(table, s), :] = x[s]
        return 0

    lax.fori_loop(0, sents, place, 0)

    def flip(i, _):
        rows = tile_at(i)
        turn(table, packed_t, rows, packed[rows, :])
        return 0

    lax.fori_loop(0, table[TILES], flip, 0)


def send_home(source, *refs):
    blocks, home = refs[:-1], refs[-1]
    share, total, width = home.shape
    depth = total * STEP
    column = lax.broadcasted_iota(jnp.int32, (depth, depth), 1)
    row = lax.broadcasted_iota(jnp.int32, (depth, depth), 0)
    pick = ((column % STEP) == (row // total)) & ((column // STEP) == source[...])
    pick = jnp.where(pick, 1.0, 0.0).astype(LOW)
    for block in range(share // STEP):
        rows = slice(block * STEP, (block + 1) * STEP)
        values = [item[:, rows, :].reshape(-1, width) for item in blocks]
        found = mm(pick, jnp.concatenate(values, axis=0)).astype(LOW)
        home[rows] = found.reshape(STEP, total, width)


def start_all(copies):
    for copy in copies:
        copy.start()


def wait_all(copies):
    for copy in copies:
        copy.wait()


def by_tiles(table, rows, body):
    for n in range(1, rows // TILE + 1):

        @pl.when(table[TILES] == n)
        def _():
            body(n * TILE)


def tile_copies(table, source, target, sems):
    def at(i):
        rows = slice(i * TILE, (i + 1) * TILE)
        return pltpu.make_async_copy(source.at[rows], target.at[rows], sems.at[i])

    def each(act):
        for i in range(sems.shape[0]):

            @pl.when(i < table[TILES])
            def _():
                act(at(i))

    return each


def place_weight(k, steps, weight, own_down, slabs):
    count, slab = slabs.shape[0], slabs.shape[1]
    columns = weight.shape[1]

    @pl.when(k == 0)
    def _():
        weight[:, columns // 2 :] = own_down[...].T

    for t in range(1, steps):

        @pl.when(k == t)
        def _():
            for j in range(count):
                weight[j * slab : (j + 1) * slab, :] = slabs[
                    j, :, (t - 1) * columns : t * columns
                ]


def attention_forward(table, packed, own_qkv, own_out, *refs):
    pieces, refs = refs[:-18], refs[-18:]
    proj_out, ctx_out, probs_out, qkv_out, wo_out, z1_out, root1 = refs[:7]
    proj, ctx, probs, qkv, wo, z1, slabs, sems, out_sems, wide_sems, z1_sems = refs[7:]
    sents, pairs = probs.shape[0], probs.shape[1]
    width = packed.shape[1]
    length = probs.shape[3]
    part = own_out.shape[0]
    block = 4 * part
    heads = part // HD
    arrivals = place_pieces(table, pieces, slabs, sems)
    start_all(arrivals)
    count, slab = slabs.shape[0], slabs.shape[1]
    for h in range(heads):
        for p in range(3):
            source = (h * 3 + p) * HD
            qkv[:, p * width + h * HD : p * width + (h + 1) * HD] = own_qkv[
                source : source + HD, :
            ].T
    wo[:, :part] = own_out[...].T
    ctx[...] = jnp.zeros_like(ctx)
    tiles = table[TILES]
    end = pl.ds(pl.multiple_of(tiles * TILE, TILE), length)
    proj[end, :] = jnp.zeros((length, 3 * width), LOW)
    wait_all(arrivals)
    for j in range(count):
        rows = slice(j * slab, (j + 1) * slab)
        for k in range(1, width // part):
            base = (k - 1) * block
            for p in range(3):
                qkv[rows, p * width + k * part : p * width + (k + 1) * part] = slabs[
                    j, :, base + p * part : base + (p + 1) * part
                ]
            wo[rows, k * part : (k + 1) * part] = slabs[j, :, base + 3 * part : base + block]
    wide_copies = [
        pltpu.make_async_copy(qkv, qkv_out, wide_sems.at[0]),
        pltpu.make_async_copy(wo, wo_out, wide_sems.at[1]),
    ]
    start_all(wide_copies)

    def project(n):
        source = packed[:n, :]
        for c in range(0, 3 * width, CHUNK):
            cols = slice(c, c + CHUNK)
            proj[:n, cols] = mm(source, qkv[:, cols]).astype(LOW)

    by_tiles(table, z1.shape[0], project)
    proj_copy = pltpu.make_async_copy(proj, proj_out, out_sems.at[0])
    proj_copy.start()

    def attend(s, _):
        rows = rows_of(table, s)
        valid = lax.broadcasted_iota(jnp.int32, (length, length), 0) < table[LENS + s]
        for p in range(pairs):
            at = p * PAIR
            queries = proj[rows, at : at + PAIR]
            keys = split_heads(proj[rows, width + at : width + at + PAIR])
            values = split_heads(proj[rows, 2 * width + at : 2 * width + at + PAIR])
            scores = mm(keys, queries, NT)
            for h in range(2):
                half = slice(h * length, (h + 1) * length)
                score = jnp.where(valid, scores[half], MASKED)
                top = jnp.max(score, axis=0, keepdims=True)
                score = jnp.exp2((score - top) * (HD**-0.5 * LOG2_E))
                total = jnp.sum(score, axis=0, keepdims=True)
                probs[s, p, half, :] = (score * (1.0 / total)).astype(LOW)
            ctx[rows, at : at + PAIR] = mm(probs[s, p].T, values).astype(LOW)
        return 0

    lax.fori_loop(0, sents, attend, 0)
    ctx_copies = [
        pltpu.make_async_copy(ctx, ctx_out, out_sems.at[1]),
        pltpu.make_async_copy(probs, probs_out, out_sems.at[2]),
    ]
    start_all(ctx_copies)

    for i in range(z1_sems.shape[0]):
        rows = slice(i * TILE, (i + 1) * TILE)

        @pl.when(i < tiles)
        def _():
            attended = mm(ctx[rows, :], wo[...], NT)
            z, root = normalize(packed[rows, :].astype(F32) + attended)
            z1[rows, :] = z
            root1[rows, :] = jnp.broadcast_to(root, (TILE, 128))
            pltpu.make_async_copy(z1.at[rows], z1_out.at[rows], z1_sems.at[i]).start()

    tile_copies(table, z1, z1_out, z1_sems)(lambda copy: copy.wait())
    wait_all(wide_copies + [proj_copy] + ctx_copies)


def gelu_parts(pre):
    t = pl.reciprocal(1.0 + jnp.abs(pre) * (0.3275911 * SQRT_HALF))
    poly = 0.5 * 1.061405429
    for c in (-1.453152027, 1.421413741, -0.284496736, 0.254829592):
        poly = poly * t + 0.5 * c
    e = jnp.exp2(pre * pre * (-0.5 * LOG2_E))
    tail = poly * t * e
    cdf = jnp.where(pre >= 0.0, 1.0 - tail, tail)
    return pre * cdf, cdf + pre * (e * INV_SQRT_2PI)


def ffn_forward(parts, table, z1_in, gain1, bias1, own_up, own_down_in, bias, gain2, bias2, *refs):
    pieces, refs = refs[:-16], refs[-16:]
    active, slope, z2_out, root2, pooled = refs[:5]
    weight, first, total, z1, z2, own_down, slabs, sems, own_sems, z1_sems, z2_sems = refs[5:]
    k = pl.program_id(0)
    steps = pl.num_programs(0)
    tiles = table[TILES]
    units = active.shape[2]
    arrivals = place_pieces(table, pieces, slabs, sems)
    own = [
        pltpu.make_async_copy(own_up, weight.at[:, :units], own_sems.at[0]),
        pltpu.make_async_copy(own_down_in, own_down, own_sems.at[1]),
    ]
    z1_copies = tile_copies(table, z1_in, z1, z1_sems)

    @pl.when(k == 0)
    def _():
        z1_copies(lambda copy: copy.start())
        start_all(own)
        start_all(arrivals)
        z1_copies(lambda copy: copy.wait())

        def start(i, _):
            rows = tile_at(i)
            value = z1[rows, :] * gain1[...] + bias1[...]
            first[rows, :] = value.astype(LOW)
            total[rows, :] = value
            return 0

        lax.fori_loop(0, tiles, start, 0)
        wait_all(own)

    @pl.when(k == 1)
    def _():
        wait_all(arrivals)

    place_weight(k, parts, weight, own_down, slabs)

    def work(n):
        source = first[:n, :]
        for c in range(0, units, CHUNK):
            cols = slice(c, c + CHUNK)
            act, slp = gelu_parts(mm(source, weight[:, cols]) + bias[0, :, cols])
            active[0, :n, cols] = act.astype(LOW)
            slope[0, :n, cols] = slp.astype(LOW)
        total[:n, :] += mm(active[0, :n, :], weight[:, units:], NT)

    by_tiles(table, first.shape[0], work)

    @pl.when(k == steps - 1)
    def _():
        z2[pl.ds(pl.multiple_of(tiles * TILE, TILE), 128), :] = jnp.zeros((128, z2.shape[1]), F32)

        def finish(i, _):
            rows = tile_at(i)
            z, root = normalize(total[rows, :])
            z2[rows, :] = z
            root2[rows, :] = jnp.broadcast_to(root, (TILE, 128))
            return 0

        lax.fori_loop(0, tiles, finish, 0)
        z2_copies = tile_copies(table, z2, z2_out, z2_sems)
        z2_copies(lambda copy: copy.start())
        for s in range(pooled.shape[0]):
            n = table[LENS + s]
            valid = lax.broadcasted_iota(jnp.int32, (128, z2.shape[1]), 0) < n
            rows = jnp.where(valid, z2[rows_of(table, s), :], 0.0)
            mean = jnp.sum(rows, axis=0, keepdims=True) / n.astype(F32)
            pooled[s : s + 1, :] = mean * gain2[...] + bias2[...]
        z2_copies(lambda copy: copy.wait())


def weight_grad(table, turned, right, store):
    count, slab, rows = turned.shape

    def body(n):
        if slab % 16 == 0:
            left = turned[:, :, :n].reshape(count * slab, n)
        else:
            left = jnp.concatenate([turned[j, :, :n] for j in range(count)], axis=0)
        store(lambda columns: mm(left, right(n, columns)))

    by_tiles(table, rows, body)


def split_send(mine, other, value, k, columns):
    chips, slab = mine.shape[0], mine.shape[2]
    for m in range(chips):
        mine[m, k, :, columns] = value[m * slab : (m + 1) * slab].astype(LOW)
        other[m, k, :, columns] = value[(chips + m) * slab : (chips + m + 1) * slab].astype(LOW)


def send_chunks(mine, other, product):
    for c in range(0, mine.shape[3], CHUNK):
        cols = slice(c, c + CHUNK)
        split_send(mine, other, product(cols), 0, cols)


def ffn_backward(
    parts, table, pool, z2_in, root2, gain2, z1_in, root1, gain1, bias1, own_up, own_down_in,
    active, slope, *refs
):
    pieces, refs = refs[:-22], refs[-22:]
    down_mine, down_other, up_mine, up_other, attn_low, attn_t, sums, bias_sum = refs[:8]
    weight, z1, z2, total, branch, branch_t, first_t, hidden, own_down, slabs = refs[8:18]
    sems, own_sems, z1_sems, z2_sems = refs[18:]
    k = pl.program_id(0)
    tiles = table[TILES]
    width, units = own_up.shape
    arrivals = place_pieces(table, pieces, slabs, sems)
    own = [
        pltpu.make_async_copy(own_up, weight.at[:, :units], own_sems.at[0]),
        pltpu.make_async_copy(own_down_in, own_down, own_sems.at[1]),
    ]
    z1_copies = tile_copies(table, z1_in, z1, z1_sems)
    z2_copies = tile_copies(table, z2_in, z2, z2_sems)

    @pl.when(k == 0)
    def _():
        z2_copies(lambda copy: copy.start())
        z1_copies(lambda copy: copy.start())
        start_all(own)
        start_all(arrivals)
        total[...] = jnp.zeros_like(total)
        for s in range(pool.shape[0]):
            n = table[LENS + s]
            valid = lax.broadcasted_iota(jnp.int32, (128, width), 0) < n
            row = pool[s : s + 1, :] / n.astype(F32)
            total[rows_of(table, s), :] = jnp.where(valid, row, 0.0)
        sums[...] = jnp.zeros_like(sums)
        z2_copies(lambda copy: copy.wait())
        z1_copies(lambda copy: copy.wait())

        def start(i, _):
            rows = tile_at(i)
            grad = total[rows, :]
            z = z2[rows, :]
            sums[0:1, :] += jnp.sum(grad * z, axis=0, keepdims=True)
            sums[1:2, :] += jnp.sum(grad, axis=0, keepdims=True)
            value = normalize_back(z, root2[rows, 0:1], grad * gain2[...])
            low = value.astype(LOW)
            total[rows, :] = value
            branch[rows, :] = low
            turn(table, branch_t, rows, low)
            turn(table, first_t, rows, (z1[rows, :] * gain1[...] + bias1[...]).astype(LOW))
            return 0

        lax.fori_loop(0, tiles, start, 0)
        wait_all(own)

    @pl.when(k == 1)
    def _():
        wait_all(arrivals)

    place_weight(k, parts, weight, own_down, slabs)
    weight_grad(
        table,
        branch_t,
        lambda n, cols: active[0, :n, cols],
        lambda product: send_chunks(down_mine, down_other, product),
    )
    bias_sum[...] = jnp.zeros_like(bias_sum)

    def work(n):
        source = branch[:n, :]
        for c in range(0, units, CHUNK):
            cols = slice(c, c + CHUNK)
            grad = mm(source, weight[:, units + c : units + c + CHUNK])
            hid = (slope[0, :n, cols].astype(F32) * grad).astype(LOW)
            hidden[:n, cols] = hid
            bias_sum[0, :, cols] += jnp.sum(hid.astype(F32), axis=0, keepdims=True)
        total[:n, :] += mm(hidden[:n, :], weight[:, :units], NT)

    by_tiles(table, hidden.shape[0], work)
    weight_grad(
        table,
        first_t,
        lambda n, cols: hidden[:n, cols],
        lambda product: send_chunks(up_mine, up_other, product),
    )

    @pl.when(k == pl.num_programs(0) - 1)
    def _():
        def finish(i, _):
            rows = tile_at(i)
            grad = total[rows, :]
            z = z1[rows, :]
            sums[2:3, :] += jnp.sum(grad * z, axis=0, keepdims=True)
            sums[3:4, :] += jnp.sum(grad, axis=0, keepdims=True)
            value = normalize_back(z, root1[rows, 0:1], grad * gain1[...])
            low = value.astype(LOW)
            attn_low[rows, :] = low
            turn(table, attn_t, rows, low)
            return 0

        lax.fori_loop(0, tiles, finish, 0)


def attention_backward(table, attn_low, wo, proj_in, probs_in, qkv_in, proj_grad_out, *refs):
    outs, refs = refs[:-7], refs[-7:]
    ctx_grad, proj, probs, qkv, proj_grad, sems, out_sem = refs
    sents, pairs = probs.shape[0], probs.shape[1]
    length = probs.shape[3]
    width = attn_low.shape[1]
    tiles = table[TILES]
    arrivals = [
        pltpu.make_async_copy(proj_in, proj, sems.at[0]),
        pltpu.make_async_copy(probs_in, probs, sems.at[1]),
        pltpu.make_async_copy(qkv_in, qkv, sems.at[2]),
    ]
    start_all(arrivals)
    ctx_grad[...] = jnp.zeros_like(ctx_grad)
    proj_grad[...] = jnp.zeros_like(proj_grad)

    def start(n):
        ctx_grad[:n, :] = mm(attn_low[:n, :], wo[...]).astype(LOW)

    by_tiles(table, attn_low.shape[0], start)
    wait_all(arrivals[:2])
    scale = HD**-0.5

    def attend(s, _):
        rows = rows_of(table, s)
        live = lax.broadcasted_iota(jnp.int32, (length, PAIR), 0) < table[LENS + s]
        for p in range(pairs):
            at = p * PAIR
            queries = proj[rows, at : at + PAIR]
            keys = split_heads(proj[rows, width + at : width + at + PAIR])
            values = split_heads(proj[rows, 2 * width + at : 2 * width + at + PAIR])
            grad = ctx_grad[rows, at : at + PAIR]
            grad = jnp.where(live, grad, jnp.zeros_like(grad))
            prob_grad = mm(values, grad, NT)
            score_grad = []
            for h in range(2):
                half = slice(h * length, (h + 1) * length)
                prob = probs[s, p, half, :].astype(F32)
                part = prob_grad[half]
                inner = jnp.sum(prob * part, axis=0, keepdims=True)
                score_grad.append((prob * (part - inner)).astype(LOW))
            score_grad = jnp.concatenate(score_grad, axis=0)
            proj_grad[rows, at : at + PAIR] = (mm(score_grad.T, keys) * scale).astype(LOW)
            proj_grad[rows, width + at : width + at + PAIR] = (
                join_heads(mm(score_grad, queries)) * scale
            ).astype(LOW)
            proj_grad[rows, 2 * width + at : 2 * width + at + PAIR] = join_heads(
                mm(probs[s, p], grad)
            ).astype(LOW)
        return 0

    lax.fori_loop(0, sents, attend, 0)
    proj_copy = pltpu.make_async_copy(proj_grad, proj_grad_out, out_sem.at[0])
    proj_copy.start()
    arrivals[2].wait()

    def finish(n):
        total = mm(proj_grad[:n, :], qkv[...], NT)
        ctx_grad[:n, :] = (attn_low[:n, :].astype(F32) + total).astype(LOW)

    by_tiles(table, attn_low.shape[0], finish)
    ctx_grad[pl.ds(pl.multiple_of(tiles * TILE, TILE), length), :] = jnp.zeros(
        (length, width), LOW
    )
    share = outs[0].shape[1]
    for k, out in enumerate(outs):
        first = table[LINE + k] * share
        position = lax.broadcasted_iota(jnp.int32, (share, width), 0) + first
        for s in range(sents):
            value = ctx_grad[pl.ds(pl.multiple_of(table[s] + first, 16), share), :]
            out[s] = jnp.where(position < table[LENS + s], value, jnp.zeros_like(value))
    proj_copy.wait()


def attention_weights(table, *refs):
    sources, (mine, other), (packed_t, attn_t, ctx, proj_grad, sems) = refs[:4], refs[4:6], refs[6:]
    width = ctx.shape[1]
    count = mine.shape[1]
    part = width // count
    copies = [
        pltpu.make_async_copy(source, target, sems.at[i])
        for i, (source, target) in enumerate(zip(sources[:3], (packed_t, attn_t, ctx)))
    ]
    for p in range(3):
        cols = slice(p * width, (p + 1) * width)
        copies.append(
            pltpu.make_async_copy(sources[3].at[:, cols], proj_grad.at[:, cols], sems.at[3 + p])
        )
    order = [copies[1], copies[2], copies[0]] + copies[3:]
    start_all(order)

    def store(p, product):
        value = product(slice(p * width, (p + 1) * width) if p < 3 else slice(None))
        for k in range(count):
            split_send(
                mine,
                other,
                value[:, k * part : (k + 1) * part],
                k,
                slice(p * part, (p + 1) * part),
            )

    wait_all(order[:2])
    weight_grad(
        table, attn_t, lambda n, cols: ctx[:n, cols], lambda product: store(3, product)
    )
    order[2].wait()
    for p in range(3):
        order[3 + p].wait()
        weight_grad(
            table,
            packed_t,
            lambda n, cols: proj_grad[:n, cols],
            lambda product: store(p, product),
        )


def stacked_pieces(stacks):
    return [stack.at[i] for stack in stacks for i in range(stack.shape[0])]


def place_grads(table, near, far, straight, turned, slabs, flat, sems):
    count, slab = slabs.shape[0], slabs.shape[1]
    arrivals = place_pieces(table, stacked_pieces((near, far)), slabs, sems)
    start_all(arrivals)
    wait_all(arrivals)
    width = straight.shape[1]
    for j in range(count):
        rows = slice(j * slab, (j + 1) * slab)
        straight[rows, :] = slabs[j, :, :width].astype(F32)
        flat[rows, :] = slabs[j, :, width:].astype(F32)
    turned[...] = flat[...].T


def place_attention_grads(table, near, far, qkv, wo, slabs, flat, sems):
    count, slab = slabs.shape[0], slabs.shape[1]
    arrivals = place_pieces(table, stacked_pieces((near, far)), slabs, sems)
    start_all(arrivals)
    wait_all(arrivals)
    for j in range(count):
        flat[j * slab : (j + 1) * slab, :] = slabs[j].astype(F32)
    part = wo.shape[0]
    heads = part // HD
    for p in range(3):
        piece = flat[:, p * part : (p + 1) * part].T
        for h in range(heads):
            target = (h * 3 + p) * HD
            qkv[target : target + HD, :] = piece[h * HD : (h + 1) * HD, :]
    wo[...] = flat[:, 3 * part :].T


COST = 1000000
SMEM = pl.BlockSpec(memory_space=pltpu.SMEM)
VMEM = pl.BlockSpec(memory_space=pltpu.VMEM)
ANY = pl.BlockSpec(memory_space=pl.ANY)


def shape(dims, dtype):
    return jax.ShapeDtypeStruct(dims, dtype)


def params():
    return pltpu.CompilerParams(vmem_limit_bytes=VMEM_BYTES)


def cost(flops, nbytes):
    return pl.CostEstimate(flops=flops // COST, bytes_accessed=nbytes // COST, transcendentals=0)


def add(*terms):
    return sum(term.astype(F32) for term in terms)


def swap(value, mask, axis="dp"):
    return lax.ppermute(value, axis, [(i, i ^ mask) for i in range(lax.axis_size(axis))])


def bits_of(count):
    return [1 << i for i in range(count.bit_length() - 1)]


def take(values, index, axis=0):
    return lax.dynamic_index_in_dim(values, index, axis, False, allow_negative_indices=False)


def cut(values, start, size, axis):
    return lax.dynamic_slice_in_dim(values, start, size, axis, allow_negative_indices=False)


def tie(*values):
    return lax.optimization_barrier(values)


def gather_line(piece):
    n = lax.axis_size("tensor")
    return jnp.concatenate([swap(piece, k, "tensor") for k in range(1, n)], axis=1)


def gather_chips(value):
    return [value] + [swap(value, 2 * m) for m in range(1, lax.axis_size("dp") // 2)]


def gather_cores(near):
    return near + [swap(item, 1) for item in near]


def gather_plane(value):
    return gather_cores(gather_chips(value))


def pick(term, side, bit):
    dims = term.shape
    view = term.reshape((dims[0] // (2 * bit), 2, bit) + dims[1:])[:, side]
    return view.reshape((dims[0] // 2,) + dims[1:])


def sent(terms, bit):
    return add(*[pick(term, 1, bit) for term in terms]).astype(LOW)


def kept(terms, bit, landed):
    return [pick(term, 0, bit) for term in terms] + [landed]


def reduce_line(terms):
    for bit in bits_of(lax.axis_size("tensor")):
        terms = kept(terms, 1, swap(sent(terms, 1), bit, "tensor"))
    return add(*terms)[0].astype(LOW)


def reduce_chips(terms, bits):
    for bit in bits:
        terms = kept(terms, 1, swap(sent(terms, 1), 2 * bit))
    return terms


def shards(
    tokens,
    lengths,
    partner,
    w_qkv,
    w_out,
    ln1_gain,
    ln1_bias,
    up_weight,
    up_projection_bias,
    down_weight,
    ln2_gain,
    ln2_bias,
    cot_pooled,
    cot_paired,
):
    dp_count = lax.axis_size("dp")
    t_count = lax.axis_size("tensor")
    dp_me = lax.axis_index("dp")
    t_me = lax.axis_index("tensor")
    length, sentences, width = tokens.shape
    mine = sentences // t_count
    rows = mine * length
    pad = rows + length
    slab = width // dp_count
    chips = dp_count // 2
    heads = w_qkv.shape[1] // (3 * HD)
    units = up_weight.shape[1]
    ctx_cols = w_out.shape[0]
    block = 4 * ctx_cols

    def by_part(weight):
        return weight.reshape(-1, heads, 3, HD).transpose(0, 2, 1, 3).reshape(weight.shape)

    def rows_piece(weight):
        return cut(weight, dp_me * slab, slab, 0)

    def columns_piece(weight):
        return cut(weight, dp_me * slab, slab, 1).T

    attn_piece = jnp.concatenate([by_part(rows_piece(w_qkv)), columns_piece(w_out)], axis=1)
    attn_piece, up_early, down_early = tie(attn_piece, up_weight, down_weight)
    line_bits = bits_of(t_count)[::-1]

    def widen_line(parts, bit):
        return parts + [swap(jnp.concatenate(parts, axis=1), bit, "tensor")]

    def line_order():
        order = [0]
        for bit in line_bits:
            order += [item ^ bit for item in order]
        return order

    def by_distance(parts, columns):
        wide = jnp.concatenate(parts, axis=1)
        order = line_order()
        return [wide[:, order.index(d) * columns : (order.index(d) + 1) * columns] for d in range(t_count)]

    attn_parts = widen_line([attn_piece], line_bits[0])
    ffn_piece = jnp.concatenate([rows_piece(up_early), columns_piece(down_early)], axis=1)
    attn_parts[1], ffn_piece, up_projection_bias = tie(attn_parts[1], ffn_piece, up_projection_bias)
    for bit in line_bits[1:]:
        attn_parts = widen_line(attn_parts, bit)
    ffn_parts = widen_line([ffn_piece], line_bits[0])
    bias_parts = widen_line([up_projection_bias.reshape(1, units)], line_bits[0])
    attn_line = jnp.concatenate(by_distance(attn_parts, block)[1:], axis=1)

    order = np.arange(sentences)
    ahead = (lengths[None, :] > lengths[:, None]) | (
        (lengths[None, :] == lengths[:, None]) & (order[None, :] < order[:, None])
    )
    rank = jnp.sum(ahead.astype(jnp.int32), axis=1)
    row = rank // t_count
    column = rank % t_count
    column = jnp.where(row % 2 == 0, column, t_count - 1 - column)
    mine_here = (column == t_me)[None, :] & (row[None, :] == order[:mine, None])
    chosen = jnp.sum(jnp.where(mine_here, order[None, :], 0), axis=1)
    counts = jnp.sum(jnp.where(mine_here, lengths[None, :], 0), axis=1)
    source = (column ^ t_me) * mine + row
    taken = (counts + 15) & ~15
    ends = jnp.sum(jnp.where(np.tri(mine, dtype=bool), taken[None, :], 0), axis=1)
    devices = np.arange(dp_count)
    distance = 2 * np.arange(chips)
    near = devices[:, None] ^ distance[None, :]
    spots = np.concatenate([near, near ^ 1], axis=1)
    lines = np.arange(t_count)[:, None] ^ np.arange(t_count)[None, :]
    apart = devices[:, None] ^ devices[None, :]
    fixed = np.zeros((dp_count, DEST - PLACE + dp_count), np.int32)
    fixed[:, :dp_count] = spots
    fixed[:, DEST - PLACE :] = apart % 2 * chips + apart // 2
    line_fixed = np.zeros((t_count, PLACE - LINE), np.int32)
    line_fixed[:, :t_count] = lines
    table = jnp.concatenate(
        [
            ends - taken,
            np.zeros(LENS - mine, np.int32),
            counts,
            np.zeros(TILES - LENS - mine, np.int32),
            (ends[-1:] + (TILE - 1)) >> (TILE.bit_length() - 1),
            take(jnp.asarray(line_fixed), t_me),
            take(jnp.asarray(fixed), dp_me),
        ]
    ).astype(jnp.int32)
    attn_line, chosen = tie(attn_line, chosen)
    turn_shape = shape((dp_count, slab, rows), LOW)
    packed, packed_t = pl.pallas_call(
        pack,
        out_shape=(shape((pad, width), LOW), turn_shape),
        in_specs=[SMEM, SMEM, VMEM],
        out_specs=(VMEM,) * 2,
        scratch_shapes=[pltpu.VMEM((mine, length, width), LOW)],
        compiler_params=params(),
        cost_estimate=cost(0, 8 * rows * width),
        name="pack",
    )(table, chosen, tokens)

    attn_chips = gather_chips(attn_line)
    for bit in line_bits[1:]:
        ffn_parts = widen_line(ffn_parts, bit)
        bias_parts = widen_line(bias_parts, bit)
    bias_all = jnp.stack(by_distance(bias_parts, units))
    *attn_chips, packed = tie(*attn_chips, packed)
    attn_pieces = gather_cores(attn_chips)
    ffn_chips = gather_chips(jnp.concatenate(by_distance(ffn_parts, 2 * units)[1:], axis=1))
    attn_pieces[0], ffn_chips[0], bias_all = tie(attn_pieces[0], ffn_chips[0], bias_all)
    pairs = width // PAIR
    probs_shape = (mine, pairs, 2 * length, length)
    proj, ctx, probs, qkv, wo, z1, root1 = pl.pallas_call(
        attention_forward,
        out_shape=(
            shape((pad, 3 * width), LOW),
            shape((pad, width), LOW),
            shape(probs_shape, LOW),
            shape((width, 3 * width), LOW),
            shape((width, width), LOW),
            shape((rows, width), F32),
            shape((rows, 128), F32),
        ),
        in_specs=[SMEM, VMEM, VMEM, VMEM] + [ANY] * dp_count,
        out_specs=(ANY,) * 6 + (VMEM,),
        scratch_shapes=[
            pltpu.VMEM((pad, 3 * width), LOW),
            pltpu.VMEM((pad, width), LOW),
            pltpu.VMEM(probs_shape, LOW),
            pltpu.VMEM((width, 3 * width), LOW),
            pltpu.VMEM((width, width), LOW),
            pltpu.VMEM((rows, width), F32),
            pltpu.VMEM((dp_count, slab, (t_count - 1) * block), LOW),
            pltpu.SemaphoreType.DMA((dp_count,)),
            pltpu.SemaphoreType.DMA((3,)),
            pltpu.SemaphoreType.DMA((2,)),
            pltpu.SemaphoreType.DMA((rows // TILE,)),
        ],
        compiler_params=params(),
        cost_estimate=cost(8 * rows * width * width, 30 * rows * width),
        name="attention_forward",
    )(table, packed, w_qkv.T, w_out, *attn_pieces)
    *ffn_chips, z1 = tie(*ffn_chips, z1)
    ffn_pieces = gather_cores(ffn_chips)

    gain1, bias1 = ln1_gain.reshape(1, width), ln1_bias.reshape(1, width)
    gain2, bias2 = ln2_gain.reshape(1, width), ln2_bias.reshape(1, width)

    def whole(*dims):
        return pl.BlockSpec(dims, lambda k, table: (0,) * len(dims))

    def call(kernel, outs, ins, out_specs, scratch, flops, nbytes):
        return pl.pallas_call(
            functools.partial(kernel, t_count),
            out_shape=outs,
            grid_spec=pltpu.PrefetchScalarGridSpec(
                num_scalar_prefetch=1,
                grid=(t_count,),
                in_specs=ins,
                out_specs=out_specs,
                scratch_shapes=scratch,
            ),
            compiler_params=params(),
            cost_estimate=cost(flops, nbytes),
            name=kernel.__name__,
        )

    act_spec = pl.BlockSpec((1, rows, units), lambda k, table: (k, 0, 0))
    bias_spec = pl.BlockSpec((1, 1, units), lambda k, table: (k, 0, 0))
    line = whole(1, width)
    full = whole(rows, width)
    root_spec = whole(rows, 128)
    act_shape = shape((t_count, rows, units), LOW)
    weight_scratch = [
        pltpu.VMEM((units, width), LOW),
        pltpu.VMEM((dp_count, slab, (t_count - 1) * 2 * units), LOW),
        pltpu.SemaphoreType.DMA((dp_count,)),
        pltpu.SemaphoreType.DMA((2,)),
        pltpu.SemaphoreType.DMA((rows // TILE,)),
        pltpu.SemaphoreType.DMA((rows // TILE,)),
    ]
    active, slope, z2, root2, pooled = call(
        ffn_forward,
        (
            act_shape,
            act_shape,
            shape((rows, width), F32),
            shape((rows, 128), F32),
            shape((mine, width), F32),
        ),
        [ANY, line, line, ANY, ANY, bias_spec, line, line] + [ANY] * dp_count,
        (act_spec, act_spec, ANY, root_spec, whole(mine, width)),
        [
            pltpu.VMEM((width, 2 * units), LOW),
            pltpu.VMEM((rows, width), LOW),
            pltpu.VMEM((rows, width), F32),
            pltpu.VMEM((rows, width), F32),
            pltpu.VMEM((pad, width), F32),
        ]
        + weight_scratch,
        4 * rows * width * units * t_count,
        40 * rows * width,
    )(table, z1, gain1, bias1, up_weight, down_weight, bias_all, gain2, bias2, *ffn_pieces)

    pooled = pooled.astype(LOW)
    line_pooled = jnp.stack([pooled] + [swap(pooled, k, "tensor") for k in range(1, t_count)])
    returned = line_pooled.reshape(sentences, width)[source]
    both = jnp.concatenate([returned, cot_paired])
    everyone = jnp.stack(gather_plane(both)).reshape(-1, width)
    apart = (partner // sentences) ^ dp_me
    base = ((apart & 1) * chips + (apart >> 1)) * (2 * sentences) + partner % sentences
    partner_pooled = everyone[base].astype(F32)
    partner_cot = everyone[base + sentences].astype(F32)
    paired = (returned.astype(F32) * partner_pooled).astype(LOW)
    pool_grad = cot_pooled.astype(F32) + partner_pooled * (cot_paired.astype(F32) + partner_cot)
    pool_grad = pool_grad.astype(LOW).astype(F32)[chosen]

    send_spec = pl.BlockSpec((chips, 1, slab, units), lambda k, table: (0, k, 0, 0))
    send_shape = shape((chips, t_count, slab, units), LOW)
    down_mine, down_other, up_mine, up_other, attn_low, attn_t, sums, bias_sum = call(
        ffn_backward,
        (send_shape,) * 4
        + (
            shape((rows, width), LOW),
            turn_shape,
            shape((4, width), F32),
            shape((t_count, 1, units), F32),
        ),
        [whole(mine, width), ANY, root_spec, line, ANY, root_spec, line, line, ANY, ANY]
        + [act_spec, act_spec]
        + [ANY] * dp_count,
        (send_spec,) * 4 + (full, whole(dp_count, slab, rows), whole(4, width), bias_spec),
        [
            pltpu.VMEM((width, 2 * units), LOW),
            pltpu.VMEM((rows, width), F32),
            pltpu.VMEM((rows, width), F32),
            pltpu.VMEM((pad, width), F32),
            pltpu.VMEM((rows, width), LOW),
            pltpu.VMEM((dp_count, slab, rows), LOW),
            pltpu.VMEM((dp_count, slab, rows), LOW),
            pltpu.VMEM((rows, units), LOW),
        ]
        + weight_scratch,
        8 * rows * width * units * t_count,
        60 * rows * width,
    )(
        table, pool_grad, z2, root2, gain2, z1, root1, gain1, bias1, up_weight, down_weight,
        active, slope, *ffn_pieces
    )

    chip_bits = bits_of(chips)
    high = chip_bits[-1]
    down_terms, up_terms = [down_mine, swap(down_other, 1)], [up_mine, swap(up_other, 1)]
    small = jnp.concatenate([bias_sum.reshape(t_count, units), sums])
    small = small + swap(small, 1)
    down_sent, up_sent, small, attn_low = tie(
        sent(down_terms, 1), sent(up_terms, high), small, attn_low
    )
    small_got = swap(small, 2)
    down_got, up_got = swap(down_sent, 2), swap(up_sent, 2 * high)

    share = length // t_count
    proj_grad, *input_blocks = pl.pallas_call(
        attention_backward,
        out_shape=(shape((pad, 3 * width), LOW),)
        + (shape((mine, share, width), LOW),) * t_count,
        in_specs=[SMEM, VMEM, VMEM, ANY, ANY, ANY],
        out_specs=(ANY,) + (VMEM,) * t_count,
        scratch_shapes=[
            pltpu.VMEM((pad, width), LOW),
            pltpu.VMEM((pad, 3 * width), LOW),
            pltpu.VMEM(probs_shape, LOW),
            pltpu.VMEM((width, 3 * width), LOW),
            pltpu.VMEM((pad, 3 * width), LOW),
            pltpu.SemaphoreType.DMA((3,)),
            pltpu.SemaphoreType.DMA((1,)),
        ],
        compiler_params=params(),
        cost_estimate=cost(12 * rows * width * width, 30 * rows * width),
        name="attention_backward",
    )(table, attn_low, wo, proj, probs, qkv)

    down_got, up_got, small_got, proj_grad, *input_blocks = tie(
        down_got, up_got, small_got, proj_grad, *input_blocks
    )
    small = small + small_got
    down_terms, up_terms = kept(down_terms, 1, down_got), kept(up_terms, high, up_got)
    for low, top in zip(chip_bits[1:-1], chip_bits[1:-1][::-1]):
        down_terms = kept(down_terms, 1, swap(sent(down_terms, 1), 2 * low))
        up_terms = kept(up_terms, top, swap(sent(up_terms, top), 2 * top))
    down_sent, up_sent, small, proj_grad, *input_blocks = tie(
        sent(down_terms, 1), sent(up_terms, 1), small, proj_grad, *input_blocks
    )
    small_got = swap(small, 4)
    down_got, up_got = swap(down_sent, 2 * high), swap(up_sent, 2)
    input_landed = [input_blocks[0]] + [None] * (t_count - 1)
    input_landed[2] = swap(input_blocks[2], 2, "tensor")

    attn_mine, attn_other = pl.pallas_call(
        attention_weights,
        out_shape=(shape((chips, t_count, slab, block), LOW),) * 2,
        in_specs=[SMEM] + [ANY] * 4,
        out_specs=(VMEM,) * 2,
        scratch_shapes=[
            pltpu.VMEM((dp_count, slab, rows), LOW),
            pltpu.VMEM((dp_count, slab, rows), LOW),
            pltpu.VMEM((pad, width), LOW),
            pltpu.VMEM((pad, 3 * width), LOW),
            pltpu.SemaphoreType.DMA((6,)),
        ],
        compiler_params=params(),
        cost_estimate=cost(8 * rows * width * width, 30 * rows * width),
        name="attention_weights",
    )(table, packed_t, attn_t, ctx, proj_grad)

    def finish(kernel, near, outs, flat):
        near = jnp.stack(near)
        far = swap(near, 1)
        return pl.pallas_call(
            kernel,
            out_shape=tuple(shape(dims, F32) for dims in outs),
            in_specs=[SMEM, ANY, ANY],
            out_specs=(VMEM,) * 2,
            scratch_shapes=[
                pltpu.VMEM((dp_count,) + near.shape[1:], LOW),
                pltpu.VMEM((width, flat), F32),
                pltpu.SemaphoreType.DMA((dp_count,)),
            ],
            compiler_params=params(),
            cost_estimate=cost(0, 8 * width * near.shape[2]),
            name=kernel.__name__,
        )(table, near, far)

    attn_other, small_got, down_got, up_got, input_landed[2] = tie(
        attn_other, small_got, down_got, up_got, input_landed[2]
    )
    small = small + small_got
    for mask in bits_of(dp_count)[3:]:
        small = small + swap(small, mask)
    attn_got = swap(attn_other, 1)
    attn_sent = [add(attn_mine[m], attn_got[m]).astype(LOW) for m in range(1, chips)]
    ffn_line = jnp.concatenate(
        [add(*kept(up_terms, 1, up_got))[0], add(*kept(down_terms, 1, down_got))[0]], axis=2
    )
    ffn_line = [ffn_line.astype(LOW)]
    ffn_sent, input_blocks[3], small, *attn_sent = tie(
        sent(ffn_line, 1), input_blocks[3], small, *attn_sent
    )
    attn_got = [attn_got[0]] + [swap(item, 2 * m) for m, item in zip(range(1, chips), attn_sent)]
    ffn_got = swap(ffn_sent, 1, "tensor")
    input_landed[3] = swap(input_blocks[3], 3, "tensor")
    norms, bias_part = small[t_count:], small[:t_count]

    def small_step(norms, bias_part, mask):
        half = bias_part.shape[0] // 2
        split = bias_part.reshape(half, 2, units)
        got = swap(jnp.concatenate([split[:, 1], norms]), mask, "tensor")
        return norms, got, split[:, 0]

    def small_sum(norms, got, bias_part):
        half = bias_part.shape[0]
        return norms + got[half:], bias_part + got[:half]

    ffn_line = kept(ffn_line, 1, ffn_got)
    ffn_got = swap(sent(ffn_line, 1), 2, "tensor")
    *attn_got, ffn_got, norms, input_landed[3] = tie(
        *attn_got, ffn_got, norms, input_landed[3]
    )
    attn_line = [add(attn_mine[0], *attn_got).astype(LOW)]
    ffn_sum = add(*kept(ffn_line, 1, ffn_got))[0].astype(LOW)
    attn_sent, ffn_sum, input_blocks[1] = tie(sent(attn_line, 1), ffn_sum, input_blocks[1])
    attn_got = swap(attn_sent, 1, "tensor")
    ffn_chips = gather_chips(ffn_sum)
    input_landed[1] = swap(input_blocks[1], 1, "tensor")
    attn_got, input_landed[1], norms, *ffn_chips = tie(
        attn_got, input_landed[1], norms, *ffn_chips
    )
    attn_line = kept(attn_line, 1, attn_got)
    attn_sent, norms, ffn_chips[0] = tie(sent(attn_line, 1), norms, ffn_chips[0])
    attn_got = swap(attn_sent, 2, "tensor")
    norms, small_got, bias_part = small_step(norms, bias_part, 1)
    norms, bias_part = small_sum(norms, small_got, bias_part)
    up_grad, down_grad = finish(place_grads, ffn_chips, ((width, units), (units, width)), units)
    attn_got, norms, up_grad = tie(attn_got, norms, up_grad)
    attn_sum = add(*kept(attn_line, 1, attn_got))[0].astype(LOW)
    attn_sum, input_landed[0] = tie(attn_sum, input_landed[0])
    norms, small_got, bias_part = small_step(norms, bias_part, 2)
    norms, bias_part = small_sum(norms, small_got, bias_part)
    attn_chips = gather_chips(attn_sum)
    home = pl.pallas_call(
        send_home,
        out_shape=shape((share, sentences, width), LOW),
        in_specs=[VMEM] * (1 + t_count),
        out_specs=VMEM,
        compiler_params=params(),
        cost_estimate=cost(0, 4 * share * sentences * width),
        name="send_home",
    )(jnp.tile(source, STEP).reshape(-1, 1), *input_landed)
    attn_chips[0], home = tie(attn_chips[0], home)
    qkv_grad, out_grad = finish(
        place_attention_grads, attn_chips, ((3 * ctx_cols, width), (ctx_cols, width)), block
    )

    return (
        returned,
        paired,
        home,
        qkv_grad.T,
        out_grad,
        norms[2],
        norms[3],
        up_grad,
        bias_part[0],
        down_grad,
        norms[0],
        norms[1],
    )


def solution(mesh):
    placed = (
        P(None, "dp", None),
        P("dp"),
        P("dp"),
        P(None, "tensor"),
        P("tensor", None),
        P(),
        P(),
        P(None, "tensor"),
        P("tensor"),
        P("tensor", None),
        P(),
        P(),
        P("dp", None),
        P("dp", None),
    )
    return jax.shard_map(
        shards,
        mesh=mesh,
        in_specs=placed,
        out_specs=(
            P("dp", None),
            P("dp", None),
            P("tensor", "dp", None),
            P(None, "tensor"),
            P("tensor", None),
            P(),
            P(),
            P(None, "tensor"),
            P("tensor"),
            P("tensor", None),
            P(),
            P(),
        ),
        check_vma=False,
    )
```

```python
import functools

import jax
import jax.numpy as jnp
import numpy as np
from jax import lax
from jax.experimental import pallas as pl
from jax.experimental.pallas import tpu as pltpu
from jax.sharding import PartitionSpec as P

HD = 64
EPSILON = 1e-06
LOW = jnp.bfloat16
F32 = jnp.float32
INV_SQRT_2PI = 0.3989422804014327
SQRT_HALF = 0.7071067811865476
TILE = 256
CHUNK = 256
STEP = 16
MASKED = -1000000000.0
LOG2_E = 1.4426950408889634
VMEM_BYTES = 60 * 2**20
NN = (((1,), (0,)), ((), ()))
NT = (((1,), (1,)), ((), ()))
PAIR = 2 * HD
LENS, TILES, LINE, PLACE, DEST = 16, 32, 33, 48, 80


def mm(a, b, dims=NN):
    return lax.dot_general(a, b, dims, preferred_element_type=F32)


def rows_of(table, s):
    return pl.ds(pl.multiple_of(table[s], 16), 128)


def tile_at(i):
    return pl.ds(pl.multiple_of(i * TILE, TILE), TILE)


def normalize(values):
    center = values - jnp.mean(values, axis=-1, keepdims=True)
    spread = jnp.mean(center * center, axis=-1, keepdims=True)
    root = lax.rsqrt(spread + EPSILON)
    return center * root, root


def normalize_back(z, root, dz):
    return root * (
        dz - jnp.mean(dz, -1, keepdims=True) - z * jnp.mean(dz * z, -1, keepdims=True)
    )


def split_heads(pair):
    first = lax.broadcasted_iota(jnp.int32, pair.shape, 1) < HD
    zero = jnp.zeros_like(pair)
    return jnp.concatenate([jnp.where(first, pair, zero), jnp.where(first, zero, pair)], axis=0)


def join_heads(split):
    n = split.shape[0] // 2
    first = lax.broadcasted_iota(jnp.int32, (n, PAIR), 1) < HD
    return jnp.where(first, split[:n], split[n:])


def place_pieces(table, pieces, slabs, sems):
    copies = []
    for i, piece in enumerate(pieces):
        copies.append(pltpu.make_async_copy(piece, slabs.at[table[PLACE + i]], sems.at[i]))
    return copies


def turn(table, turned, rows, value):
    flat = value.T
    count, slab = turned.shape[0], turned.shape[1]
    for j in range(count):
        turned[table[DEST + j], :, rows] = flat[j * slab : (j + 1) * slab, :]


def pack(table, chosen, tokens, packed, packed_t, x):
    sents, length, width = x.shape
    total = tokens.shape[1]
    depth = total * STEP
    column = lax.broadcasted_iota(jnp.int32, (STEP, depth), 1)
    position = lax.broadcasted_iota(jnp.int32, (STEP, depth), 0)
    here = (column // total) == position
    pick = [here & ((column % total) == chosen[s]) for s in range(sents)]
    pick = jnp.concatenate([jnp.where(item, 1.0, 0.0).astype(LOW) for item in pick], axis=0)
    for block in range(length // STEP):
        rows = slice(block * STEP, (block + 1) * STEP)
        found = mm(pick, tokens[rows].reshape(depth, width)).astype(LOW)
        for s in range(sents):
            x[s, rows, :] = found[s * STEP : (s + 1) * STEP]
    packed[...] = jnp.zeros_like(packed)

    def place(s, _):
        packed[rows_of(table, s), :] = x[s]
        return 0

    lax.fori_loop(0, sents, place, 0)

    def flip(i, _):
        rows = tile_at(i)
        turn(table, packed_t, rows, packed[rows, :])
        return 0

    lax.fori_loop(0, table[TILES], flip, 0)


def send_home(source, *refs):
    blocks, home = refs[:-1], refs[-1]
    share, total, width = home.shape
    depth = total * STEP
    column = lax.broadcasted_iota(jnp.int32, (depth, depth), 1)
    row = lax.broadcasted_iota(jnp.int32, (depth, depth), 0)
    pick = ((column % STEP) == (row // total)) & ((column // STEP) == source[...])
    pick = jnp.where(pick, 1.0, 0.0).astype(LOW)
    for block in range(share // STEP):
        rows = slice(block * STEP, (block + 1) * STEP)
        values = [item[:, rows, :].reshape(-1, width) for item in blocks]
        found = mm(pick, jnp.concatenate(values, axis=0)).astype(LOW)
        home[rows] = found.reshape(STEP, total, width)


def start_all(copies):
    for copy in copies:
        copy.start()


def wait_all(copies):
    for copy in copies:
        copy.wait()


def by_tiles(table, rows, body):
    for n in range(1, rows // TILE + 1):

        @pl.when(table[TILES] == n)
        def _():
            body(n * TILE)


def tile_copies(table, source, target, sems):
    def at(i):
        rows = slice(i * TILE, (i + 1) * TILE)
        return pltpu.make_async_copy(source.at[rows], target.at[rows], sems.at[i])

    def each(act):
        for i in range(sems.shape[0]):

            @pl.when(i < table[TILES])
            def _():
                act(at(i))

    return each


def place_weight(k, steps, weight, own_down, slabs):
    count, slab = slabs.shape[0], slabs.shape[1]
    columns = weight.shape[1]

    @pl.when(k == 0)
    def _():
        weight[:, columns // 2 :] = own_down[...].T

    for t in range(1, steps):

        @pl.when(k == t)
        def _():
            for j in range(count):
                weight[j * slab : (j + 1) * slab, :] = slabs[
                    j, :, (t - 1) * columns : t * columns
                ]


def attention_forward(table, packed, own_qkv, own_out, *refs):
    pieces, refs = refs[:-18], refs[-18:]
    proj_out, ctx_out, probs_out, qkv_out, wo_out, z1_out, root1 = refs[:7]
    proj, ctx, probs, qkv, wo, z1, slabs, sems, out_sems, wide_sems, z1_sems = refs[7:]
    sents, pairs = probs.shape[0], probs.shape[1]
    width = packed.shape[1]
    length = probs.shape[3]
    part = own_out.shape[0]
    block = 4 * part
    heads = part // HD
    arrivals = place_pieces(table, pieces, slabs, sems)
    start_all(arrivals)
    count, slab = slabs.shape[0], slabs.shape[1]
    for h in range(heads):
        for p in range(3):
            source = (h * 3 + p) * HD
            qkv[:, p * width + h * HD : p * width + (h + 1) * HD] = own_qkv[
                source : source + HD, :
            ].T
    wo[:, :part] = own_out[...].T
    ctx[...] = jnp.zeros_like(ctx)
    tiles = table[TILES]
    end = pl.ds(pl.multiple_of(tiles * TILE, TILE), length)
    proj[end, :] = jnp.zeros((length, 3 * width), LOW)
    wait_all(arrivals)
    for j in range(count):
        rows = slice(j * slab, (j + 1) * slab)
        for k in range(1, width // part):
            base = (k - 1) * block
            for p in range(3):
                qkv[rows, p * width + k * part : p * width + (k + 1) * part] = slabs[
                    j, :, base + p * part : base + (p + 1) * part
                ]
            wo[rows, k * part : (k + 1) * part] = slabs[j, :, base + 3 * part : base + block]
    wide_copies = [
        pltpu.make_async_copy(qkv, qkv_out, wide_sems.at[0]),
        pltpu.make_async_copy(wo, wo_out, wide_sems.at[1]),
    ]
    start_all(wide_copies)

    def project(n):
        source = packed[:n, :]
        for c in range(0, 3 * width, CHUNK):
            cols = slice(c, c + CHUNK)
            proj[:n, cols] = mm(source, qkv[:, cols]).astype(LOW)

    by_tiles(table, z1.shape[0], project)
    proj_copy = pltpu.make_async_copy(proj, proj_out, out_sems.at[0])
    proj_copy.start()

    def attend(s, _):
        rows = rows_of(table, s)
        valid = lax.broadcasted_iota(jnp.int32, (length, length), 0) < table[LENS + s]
        for p in range(pairs):
            at = p * PAIR
            queries = proj[rows, at : at + PAIR]
            keys = split_heads(proj[rows, width + at : width + at + PAIR])
            values = split_heads(proj[rows, 2 * width + at : 2 * width + at + PAIR])
            scores = mm(keys, queries, NT)
            for h in range(2):
                half = slice(h * length, (h + 1) * length)
                score = jnp.where(valid, scores[half], MASKED)
                top = jnp.max(score, axis=0, keepdims=True)
                score = jnp.exp2((score - top) * (HD**-0.5 * LOG2_E))
                total = jnp.sum(score, axis=0, keepdims=True)
                probs[s, p, half, :] = (score * (1.0 / total)).astype(LOW)
            ctx[rows, at : at + PAIR] = mm(probs[s, p].T, values).astype(LOW)
        return 0

    lax.fori_loop(0, sents, attend, 0)
    ctx_copies = [
        pltpu.make_async_copy(ctx, ctx_out, out_sems.at[1]),
        pltpu.make_async_copy(probs, probs_out, out_sems.at[2]),
    ]
    start_all(ctx_copies)

    for i in range(z1_sems.shape[0]):
        rows = slice(i * TILE, (i + 1) * TILE)

        @pl.when(i < tiles)
        def _():
            attended = mm(ctx[rows, :], wo[...], NT)
            z, root = normalize(packed[rows, :].astype(F32) + attended)
            z1[rows, :] = z
            root1[rows, :] = jnp.broadcast_to(root, (TILE, 128))
            pltpu.make_async_copy(z1.at[rows], z1_out.at[rows], z1_sems.at[i]).start()

    tile_copies(table, z1, z1_out, z1_sems)(lambda copy: copy.wait())
    wait_all(wide_copies + [proj_copy] + ctx_copies)


def gelu_parts(pre):
    t = pl.reciprocal(1.0 + jnp.abs(pre) * (0.3275911 * SQRT_HALF))
    poly = 0.5 * 1.061405429
    for c in (-1.453152027, 1.421413741, -0.284496736, 0.254829592):
        poly = poly * t + 0.5 * c
    e = jnp.exp2(pre * pre * (-0.5 * LOG2_E))
    tail = poly * t * e
    cdf = jnp.where(pre >= 0.0, 1.0 - tail, tail)
    return pre * cdf, cdf + pre * (e * INV_SQRT_2PI)


def ffn_forward(parts, table, z1_in, gain1, bias1, own_up, own_down_in, bias, gain2, bias2, *refs):
    pieces, refs = refs[:-16], refs[-16:]
    active, slope, z2_out, root2, pooled = refs[:5]
    weight, first, total, z1, z2, own_down, slabs, sems, own_sems, z1_sems, z2_sems = refs[5:]
    k = pl.program_id(0)
    steps = pl.num_programs(0)
    tiles = table[TILES]
    units = active.shape[2]
    arrivals = place_pieces(table, pieces, slabs, sems)
    own = [
        pltpu.make_async_copy(own_up, weight.at[:, :units], own_sems.at[0]),
        pltpu.make_async_copy(own_down_in, own_down, own_sems.at[1]),
    ]
    z1_copies = tile_copies(table, z1_in, z1, z1_sems)

    @pl.when(k == 0)
    def _():
        z1_copies(lambda copy: copy.start())
        start_all(own)
        z1_copies(lambda copy: copy.wait())

        def start(i, _):
            rows = tile_at(i)
            value = z1[rows, :] * gain1[...] + bias1[...]
            first[rows, :] = value.astype(LOW)
            total[rows, :] = value
            return 0

        lax.fori_loop(0, tiles, start, 0)
        wait_all(own)
        start_all(arrivals)

    @pl.when(k == 1)
    def _():
        wait_all(arrivals)

    place_weight(k, parts, weight, own_down, slabs)

    def work(n):
        for r in range(0, n, TILE):
            rows = slice(r, r + TILE)
            source = first[rows, :]
            for c in range(0, units, CHUNK):
                cols = slice(c, c + CHUNK)
                act, slp = gelu_parts(mm(source, weight[:, cols]) + bias[0, :, cols])
                active[0, rows, cols] = act.astype(LOW)
                slope[0, rows, cols] = slp.astype(LOW)
            total[rows, :] += mm(active[0, rows, :], weight[:, units:], NT)

    by_tiles(table, first.shape[0], work)

    @pl.when(k == steps - 1)
    def _():
        z2[pl.ds(pl.multiple_of(tiles * TILE, TILE), 128), :] = jnp.zeros((128, z2.shape[1]), F32)

        def finish(i, _):
            rows = tile_at(i)
            z, root = normalize(total[rows, :])
            z2[rows, :] = z
            root2[rows, :] = jnp.broadcast_to(root, (TILE, 128))
            return 0

        lax.fori_loop(0, tiles, finish, 0)
        z2_copies = tile_copies(table, z2, z2_out, z2_sems)
        z2_copies(lambda copy: copy.start())
        for s in range(pooled.shape[0]):
            n = table[LENS + s]
            valid = lax.broadcasted_iota(jnp.int32, (128, z2.shape[1]), 0) < n
            rows = jnp.where(valid, z2[rows_of(table, s), :], 0.0)
            mean = jnp.sum(rows, axis=0, keepdims=True) / n.astype(F32)
            pooled[s : s + 1, :] = mean * gain2[...] + bias2[...]
        z2_copies(lambda copy: copy.wait())


def weight_grad(table, turned, right, store):
    count, slab, rows = turned.shape

    def body(n):
        if slab % 16 == 0:
            left = turned[:, :, :n].reshape(count * slab, n)
        else:
            left = jnp.concatenate([turned[j, :, :n] for j in range(count)], axis=0)
        store(lambda columns: mm(left, right(n, columns)))

    by_tiles(table, rows, body)


def half_order(chips, bit):
    order = {}
    for m in range(chips):
        order[m] = sum(1 for other in range(m) if (other & bit) == (m & bit))
    return order


def split_send(mine, other, value, k, columns):
    chips, slab = mine.shape[0], mine.shape[2]
    for m in range(chips):
        mine[m, k, :, columns] = value[m * slab : (m + 1) * slab].astype(LOW)
        target, at = other(m)
        target[at, k, :, columns] = value[(chips + m) * slab : (chips + m + 1) * slab].astype(LOW)


def send_chunks(mine, early, late, bit, product):
    order = half_order(mine.shape[0], bit)

    def other(m):
        return (early if m & bit else late), order[m]

    for c in range(0, mine.shape[3], CHUNK):
        cols = slice(c, c + CHUNK)
        split_send(mine, other, product(cols), 0, cols)


def ffn_backward(
    parts, table, pool, z2_in, root2, gain2, z1_in, root1, gain1, bias1, own_up, own_down_in,
    active, slope, *refs
):
    pieces, refs = refs[:-24], refs[-24:]
    down_mine, down_early, down_late, up_mine, up_early, up_late = refs[:6]
    attn_low, attn_t, sums, bias_sum = refs[6:10]
    weight, z1, z2, total, branch, branch_t, first_t, hidden, own_down, slabs = refs[10:20]
    sems, own_sems, z1_sems, z2_sems = refs[20:]
    k = pl.program_id(0)
    tiles = table[TILES]
    width, units = own_up.shape
    arrivals = place_pieces(table, pieces, slabs, sems)
    own = [
        pltpu.make_async_copy(own_up, weight.at[:, :units], own_sems.at[0]),
        pltpu.make_async_copy(own_down_in, own_down, own_sems.at[1]),
    ]
    z1_copies = tile_copies(table, z1_in, z1, z1_sems)
    z2_copies = tile_copies(table, z2_in, z2, z2_sems)

    @pl.when(k == 0)
    def _():
        z2_copies(lambda copy: copy.start())
        z1_copies(lambda copy: copy.start())
        start_all(own)
        total[...] = jnp.zeros_like(total)
        for s in range(pool.shape[0]):
            n = table[LENS + s]
            valid = lax.broadcasted_iota(jnp.int32, (128, width), 0) < n
            row = pool[s : s + 1, :] / n.astype(F32)
            total[rows_of(table, s), :] = jnp.where(valid, row, 0.0)
        sums[...] = jnp.zeros_like(sums)
        z2_copies(lambda copy: copy.wait())

        def start(i, _):
            rows = tile_at(i)
            grad = total[rows, :]
            z = z2[rows, :]
            sums[0:1, :] += jnp.sum(grad * z, axis=0, keepdims=True)
            sums[1:2, :] += jnp.sum(grad, axis=0, keepdims=True)
            value = normalize_back(z, root2[rows, 0:1], grad * gain2[...])
            low = value.astype(LOW)
            total[rows, :] = value
            branch[rows, :] = low
            turn(table, branch_t, rows, low)
            return 0

        lax.fori_loop(0, tiles, start, 0)
        z1_copies(lambda copy: copy.wait())

        def flip(i, _):
            rows = tile_at(i)
            turn(table, first_t, rows, (z1[rows, :] * gain1[...] + bias1[...]).astype(LOW))
            return 0

        lax.fori_loop(0, tiles, flip, 0)
        wait_all(own)
        start_all(arrivals)

    @pl.when(k == 1)
    def _():
        wait_all(arrivals)

    place_weight(k, parts, weight, own_down, slabs)
    weight_grad(
        table,
        branch_t,
        lambda n, cols: active[0, :n, cols],
        lambda product: send_chunks(down_mine, down_early, down_late, 1, product),
    )
    bias_sum[...] = jnp.zeros_like(bias_sum)

    def work(n):
        source = branch[:n, :]
        for c in range(0, units, CHUNK):
            cols = slice(c, c + CHUNK)
            grad = mm(source, weight[:, units + c : units + c + CHUNK])
            hid = (slope[0, :n, cols].astype(F32) * grad).astype(LOW)
            hidden[:n, cols] = hid
            bias_sum[0, :, cols] += jnp.sum(hid.astype(F32), axis=0, keepdims=True)
        total[:n, :] += mm(hidden[:n, :], weight[:, :units], NT)

    by_tiles(table, hidden.shape[0], work)
    weight_grad(
        table,
        first_t,
        lambda n, cols: hidden[:n, cols],
        lambda product: send_chunks(
            up_mine, up_early, up_late, up_mine.shape[0] // 2, product
        ),
    )

    @pl.when(k == pl.num_programs(0) - 1)
    def _():
        def finish(i, _):
            rows = tile_at(i)
            grad = total[rows, :]
            z = z1[rows, :]
            sums[2:3, :] += jnp.sum(grad * z, axis=0, keepdims=True)
            sums[3:4, :] += jnp.sum(grad, axis=0, keepdims=True)
            value = normalize_back(z, root1[rows, 0:1], grad * gain1[...])
            low = value.astype(LOW)
            attn_low[rows, :] = low
            turn(table, attn_t, rows, low)
            return 0

        lax.fori_loop(0, tiles, finish, 0)


def attention_backward(table, attn_low, wo, proj_in, probs_in, qkv_in, proj_grad_out, *refs):
    outs, refs = refs[:-7], refs[-7:]
    ctx_grad, proj, probs, qkv, proj_grad, sems, out_sem = refs
    sents, pairs = probs.shape[0], probs.shape[1]
    length = probs.shape[3]
    width = attn_low.shape[1]
    tiles = table[TILES]
    arrivals = [
        pltpu.make_async_copy(proj_in, proj, sems.at[0]),
        pltpu.make_async_copy(probs_in, probs, sems.at[1]),
        pltpu.make_async_copy(qkv_in, qkv, sems.at[2]),
    ]
    start_all(arrivals)
    ctx_grad[...] = jnp.zeros_like(ctx_grad)
    proj_grad[...] = jnp.zeros_like(proj_grad)

    def start(n):
        ctx_grad[:n, :] = mm(attn_low[:n, :], wo[...]).astype(LOW)

    by_tiles(table, attn_low.shape[0], start)
    wait_all(arrivals[:2])
    scale = HD**-0.5

    def attend(s, _):
        rows = rows_of(table, s)
        live = lax.broadcasted_iota(jnp.int32, (length, PAIR), 0) < table[LENS + s]
        for p in range(pairs):
            at = p * PAIR
            queries = proj[rows, at : at + PAIR]
            keys = split_heads(proj[rows, width + at : width + at + PAIR])
            values = split_heads(proj[rows, 2 * width + at : 2 * width + at + PAIR])
            grad = ctx_grad[rows, at : at + PAIR]
            grad = jnp.where(live, grad, jnp.zeros_like(grad))
            prob_grad = mm(values, grad, NT)
            score_grad = []
            for h in range(2):
                half = slice(h * length, (h + 1) * length)
                prob = probs[s, p, half, :].astype(F32)
                part = prob_grad[half]
                inner = jnp.sum(prob * part, axis=0, keepdims=True)
                score_grad.append((prob * (part - inner)).astype(LOW))
            score_grad = jnp.concatenate(score_grad, axis=0)
            proj_grad[rows, at : at + PAIR] = (mm(score_grad.T, keys) * scale).astype(LOW)
            proj_grad[rows, width + at : width + at + PAIR] = (
                join_heads(mm(score_grad, queries)) * scale
            ).astype(LOW)
            proj_grad[rows, 2 * width + at : 2 * width + at + PAIR] = join_heads(
                mm(probs[s, p], grad)
            ).astype(LOW)
        return 0

    lax.fori_loop(0, sents, attend, 0)
    proj_copy = pltpu.make_async_copy(proj_grad, proj_grad_out, out_sem.at[0])
    proj_copy.start()
    arrivals[2].wait()

    def finish(n):
        total = mm(proj_grad[:n, :], qkv[...], NT)
        ctx_grad[:n, :] = (attn_low[:n, :].astype(F32) + total).astype(LOW)

    by_tiles(table, attn_low.shape[0], finish)
    ctx_grad[pl.ds(pl.multiple_of(tiles * TILE, TILE), length), :] = jnp.zeros(
        (length, width), LOW
    )
    share = outs[0].shape[1]
    for k, out in enumerate(outs):
        first = table[LINE + k] * share
        position = lax.broadcasted_iota(jnp.int32, (share, width), 0) + first
        for s in range(sents):
            value = ctx_grad[pl.ds(pl.multiple_of(table[s] + first, 16), share), :]
            out[s] = jnp.where(position < table[LENS + s], value, jnp.zeros_like(value))
    proj_copy.wait()


def attention_weights(table, *refs):
    sources, (mine, other), (packed_t, attn_t, ctx, proj_grad, sems) = refs[:4], refs[4:6], refs[6:]
    width = ctx.shape[1]
    count = mine.shape[1]
    part = width // count
    copies = [
        pltpu.make_async_copy(source, target, sems.at[i])
        for i, (source, target) in enumerate(zip(sources[:3], (packed_t, attn_t, ctx)))
    ]
    for p in range(3):
        cols = slice(p * width, (p + 1) * width)
        copies.append(
            pltpu.make_async_copy(sources[3].at[:, cols], proj_grad.at[:, cols], sems.at[3 + p])
        )
    order = [copies[1], copies[2], copies[0]] + copies[3:]
    start_all(order)

    def store(p, product):
        value = product(slice(p * width, (p + 1) * width) if p < 3 else slice(None))
        for k in range(count):
            split_send(
                mine,
                lambda m: (other, m),
                value[:, k * part : (k + 1) * part],
                k,
                slice(p * part, (p + 1) * part),
            )

    wait_all(order[:2])
    weight_grad(
        table, attn_t, lambda n, cols: ctx[:n, cols], lambda product: store(3, product)
    )
    order[2].wait()
    for p in range(3):
        order[3 + p].wait()
        weight_grad(
            table,
            packed_t,
            lambda n, cols: proj_grad[:n, cols],
            lambda product: store(p, product),
        )


def stacked_pieces(stacks):
    return [stack.at[i] for stack in stacks for i in range(stack.shape[0])]


def place_grads(table, near, far, straight, turned, slabs, flat, sems):
    count, slab = slabs.shape[0], slabs.shape[1]
    arrivals = place_pieces(table, stacked_pieces((near, far)), slabs, sems)
    start_all(arrivals)
    wait_all(arrivals)
    width = straight.shape[1]
    for j in range(count):
        rows = slice(j * slab, (j + 1) * slab)
        straight[rows, :] = slabs[j, :, :width].astype(F32)
        flat[rows, :] = slabs[j, :, width:].astype(F32)
    turned[...] = flat[...].T


def place_attention_grads(table, near, far, qkv, wo, slabs, flat, sems):
    count, slab = slabs.shape[0], slabs.shape[1]
    arrivals = place_pieces(table, stacked_pieces((near, far)), slabs, sems)
    start_all(arrivals)
    wait_all(arrivals)
    for j in range(count):
        flat[j * slab : (j + 1) * slab, :] = slabs[j].astype(F32)
    part = wo.shape[0]
    heads = part // HD
    for p in range(3):
        piece = flat[:, p * part : (p + 1) * part].T
        for h in range(heads):
            target = (h * 3 + p) * HD
            qkv[target : target + HD, :] = piece[h * HD : (h + 1) * HD, :]
    wo[...] = flat[:, 3 * part :].T


COST = 1000000
SMEM = pl.BlockSpec(memory_space=pltpu.SMEM)
VMEM = pl.BlockSpec(memory_space=pltpu.VMEM)
ANY = pl.BlockSpec(memory_space=pl.ANY)


def shape(dims, dtype):
    return jax.ShapeDtypeStruct(dims, dtype)


def params():
    return pltpu.CompilerParams(vmem_limit_bytes=VMEM_BYTES)


def cost(flops, nbytes):
    return pl.CostEstimate(flops=flops // COST, bytes_accessed=nbytes // COST, transcendentals=0)


def add(*terms):
    return sum(term.astype(F32) for term in terms)


def swap(value, mask, axis="dp"):
    return lax.ppermute(value, axis, [(i, i ^ mask) for i in range(lax.axis_size(axis))])


def bits_of(count):
    return [1 << i for i in range(count.bit_length() - 1)]


def take(values, index, axis=0):
    return lax.dynamic_index_in_dim(values, index, axis, False, allow_negative_indices=False)


def cut(values, start, size, axis):
    return lax.dynamic_slice_in_dim(values, start, size, axis, allow_negative_indices=False)


def tie(*values):
    return lax.optimization_barrier(values)


def gather_line(piece):
    n = lax.axis_size("tensor")
    return jnp.concatenate([swap(piece, k, "tensor") for k in range(1, n)], axis=1)


def gather_chips(value):
    return [value] + [swap(value, 2 * m) for m in range(1, lax.axis_size("dp") // 2)]


def gather_cores(near):
    return near + [swap(item, 1) for item in near]


def gather_plane(value):
    return gather_cores(gather_chips(value))


def pick(term, side, bit):
    dims = term.shape
    view = term.reshape((dims[0] // (2 * bit), 2, bit) + dims[1:])[:, side]
    return view.reshape((dims[0] // 2,) + dims[1:])


def sent(terms, bit):
    return add(*[pick(term, 1, bit) for term in terms]).astype(LOW)


def kept(terms, bit, landed):
    return [pick(term, 0, bit) for term in terms] + [landed]


def reduce_line(terms):
    for bit in bits_of(lax.axis_size("tensor")):
        terms = kept(terms, 1, swap(sent(terms, 1), bit, "tensor"))
    return add(*terms)[0].astype(LOW)


def reduce_chips(terms, bits):
    for bit in bits:
        terms = kept(terms, 1, swap(sent(terms, 1), 2 * bit))
    return terms


def shards(
    tokens,
    lengths,
    partner,
    w_qkv,
    w_out,
    ln1_gain,
    ln1_bias,
    up_weight,
    up_projection_bias,
    down_weight,
    ln2_gain,
    ln2_bias,
    cot_pooled,
    cot_paired,
):
    dp_count = lax.axis_size("dp")
    t_count = lax.axis_size("tensor")
    dp_me = lax.axis_index("dp")
    t_me = lax.axis_index("tensor")
    length, sentences, width = tokens.shape
    mine = sentences // t_count
    rows = mine * length
    pad = rows + length
    slab = width // dp_count
    chips = dp_count // 2
    heads = w_qkv.shape[1] // (3 * HD)
    units = up_weight.shape[1]
    ctx_cols = w_out.shape[0]
    block = 4 * ctx_cols

    def by_part(weight):
        return weight.reshape(-1, heads, 3, HD).transpose(0, 2, 1, 3).reshape(weight.shape)

    def rows_piece(weight):
        return cut(weight, dp_me * slab, slab, 0)

    def columns_piece(weight):
        return cut(weight, dp_me * slab, slab, 1).T

    attn_piece = jnp.concatenate([by_part(rows_piece(w_qkv)), columns_piece(w_out)], axis=1)
    attn_piece, up_early, down_early = tie(attn_piece, up_weight, down_weight)
    line_bits = bits_of(t_count)[::-1]

    def widen_line(parts, bit):
        return parts + [swap(jnp.concatenate(parts, axis=1), bit, "tensor")]

    def line_order():
        order = [0]
        for bit in line_bits:
            order += [item ^ bit for item in order]
        return order

    def by_distance(parts, columns):
        wide = jnp.concatenate(parts, axis=1)
        order = line_order()
        return [wide[:, order.index(d) * columns : (order.index(d) + 1) * columns] for d in range(t_count)]

    attn_parts = widen_line([attn_piece], line_bits[0])
    ffn_piece = jnp.concatenate([rows_piece(up_early), columns_piece(down_early)], axis=1)
    attn_parts[1], ffn_piece, up_projection_bias = tie(attn_parts[1], ffn_piece, up_projection_bias)
    for bit in line_bits[1:]:
        attn_parts = widen_line(attn_parts, bit)
    ffn_parts = widen_line([ffn_piece], line_bits[0])
    bias_parts = widen_line([up_projection_bias.reshape(1, units)], line_bits[0])
    attn_line = jnp.concatenate(by_distance(attn_parts, block)[1:], axis=1)

    order = np.arange(sentences)
    ahead = (lengths[None, :] > lengths[:, None]) | (
        (lengths[None, :] == lengths[:, None]) & (order[None, :] < order[:, None])
    )
    rank = jnp.sum(ahead.astype(jnp.int32), axis=1)
    row = rank // t_count
    column = rank % t_count
    column = jnp.where(row % 2 == 0, column, t_count - 1 - column)
    mine_here = (column == t_me)[None, :] & (row[None, :] == order[:mine, None])
    chosen = jnp.sum(jnp.where(mine_here, order[None, :], 0), axis=1)
    counts = jnp.sum(jnp.where(mine_here, lengths[None, :], 0), axis=1)
    source = (column ^ t_me) * mine + row
    taken = (counts + 15) & ~15
    ends = jnp.sum(jnp.where(np.tri(mine, dtype=bool), taken[None, :], 0), axis=1)
    devices = np.arange(dp_count)
    distance = 2 * np.arange(chips)
    near = devices[:, None] ^ distance[None, :]
    spots = np.concatenate([near, near ^ 1], axis=1)
    lines = np.arange(t_count)[:, None] ^ np.arange(t_count)[None, :]
    apart = devices[:, None] ^ devices[None, :]
    fixed = np.zeros((dp_count, DEST - PLACE + dp_count), np.int32)
    fixed[:, :dp_count] = spots
    fixed[:, DEST - PLACE :] = apart % 2 * chips + apart // 2
    line_fixed = np.zeros((t_count, PLACE - LINE), np.int32)
    line_fixed[:, :t_count] = lines
    table = jnp.concatenate(
        [
            ends - taken,
            np.zeros(LENS - mine, np.int32),
            counts,
            np.zeros(TILES - LENS - mine, np.int32),
            (ends[-1:] + (TILE - 1)) >> (TILE.bit_length() - 1),
            take(jnp.asarray(line_fixed), t_me),
            take(jnp.asarray(fixed), dp_me),
        ]
    ).astype(jnp.int32)
    attn_line, chosen = tie(attn_line, chosen)
    turn_shape = shape((dp_count, slab, rows), LOW)
    packed, packed_t = pl.pallas_call(
        pack,
        out_shape=(shape((pad, width), LOW), turn_shape),
        in_specs=[SMEM, SMEM, VMEM],
        out_specs=(VMEM,) * 2,
        scratch_shapes=[pltpu.VMEM((mine, length, width), LOW)],
        compiler_params=params(),
        cost_estimate=cost(0, 8 * rows * width),
        name="pack",
    )(table, chosen, tokens)

    attn_chips = gather_chips(attn_line)
    for bit in line_bits[1:]:
        ffn_parts = widen_line(ffn_parts, bit)
        bias_parts = widen_line(bias_parts, bit)
    bias_all = jnp.stack(by_distance(bias_parts, units))
    *attn_chips, packed = tie(*attn_chips, packed)
    attn_pieces = gather_cores(attn_chips)
    ffn_chips = gather_chips(jnp.concatenate(by_distance(ffn_parts, 2 * units)[1:], axis=1))
    attn_pieces[0], ffn_chips[0], bias_all = tie(attn_pieces[0], ffn_chips[0], bias_all)
    pairs = width // PAIR
    probs_shape = (mine, pairs, 2 * length, length)
    proj, ctx, probs, qkv, wo, z1, root1 = pl.pallas_call(
        attention_forward,
        out_shape=(
            shape((pad, 3 * width), LOW),
            shape((pad, width), LOW),
            shape(probs_shape, LOW),
            shape((width, 3 * width), LOW),
            shape((width, width), LOW),
            shape((rows, width), F32),
            shape((rows, 128), F32),
        ),
        in_specs=[SMEM, VMEM, VMEM, VMEM] + [ANY] * dp_count,
        out_specs=(ANY,) * 6 + (VMEM,),
        scratch_shapes=[
            pltpu.VMEM((pad, 3 * width), LOW),
            pltpu.VMEM((pad, width), LOW),
            pltpu.VMEM(probs_shape, LOW),
            pltpu.VMEM((width, 3 * width), LOW),
            pltpu.VMEM((width, width), LOW),
            pltpu.VMEM((rows, width), F32),
            pltpu.VMEM((dp_count, slab, (t_count - 1) * block), LOW),
            pltpu.SemaphoreType.DMA((dp_count,)),
            pltpu.SemaphoreType.DMA((3,)),
            pltpu.SemaphoreType.DMA((2,)),
            pltpu.SemaphoreType.DMA((rows // TILE,)),
        ],
        compiler_params=params(),
        cost_estimate=cost(8 * rows * width * width, 30 * rows * width),
        name="attention_forward",
    )(table, packed, w_qkv.T, w_out, *attn_pieces)
    *ffn_chips, z1 = tie(*ffn_chips, z1)
    ffn_pieces = gather_cores(ffn_chips)

    gain1, bias1 = ln1_gain.reshape(1, width), ln1_bias.reshape(1, width)
    gain2, bias2 = ln2_gain.reshape(1, width), ln2_bias.reshape(1, width)

    def whole(*dims):
        return pl.BlockSpec(dims, lambda k, table: (0,) * len(dims))

    def call(kernel, outs, ins, out_specs, scratch, flops, nbytes):
        return pl.pallas_call(
            functools.partial(kernel, t_count),
            out_shape=outs,
            grid_spec=pltpu.PrefetchScalarGridSpec(
                num_scalar_prefetch=1,
                grid=(t_count,),
                in_specs=ins,
                out_specs=out_specs,
                scratch_shapes=scratch,
            ),
            compiler_params=params(),
            cost_estimate=cost(flops, nbytes),
            name=kernel.__name__,
        )

    act_spec = pl.BlockSpec((1, rows, units), lambda k, table: (k, 0, 0))
    bias_spec = pl.BlockSpec((1, 1, units), lambda k, table: (k, 0, 0))
    line = whole(1, width)
    full = whole(rows, width)
    root_spec = whole(rows, 128)
    act_shape = shape((t_count, rows, units), LOW)
    weight_scratch = [
        pltpu.VMEM((units, width), LOW),
        pltpu.VMEM((dp_count, slab, (t_count - 1) * 2 * units), LOW),
        pltpu.SemaphoreType.DMA((dp_count,)),
        pltpu.SemaphoreType.DMA((2,)),
        pltpu.SemaphoreType.DMA((rows // TILE,)),
        pltpu.SemaphoreType.DMA((rows // TILE,)),
    ]
    active, slope, z2, root2, pooled = call(
        ffn_forward,
        (
            act_shape,
            act_shape,
            shape((rows, width), F32),
            shape((rows, 128), F32),
            shape((mine, width), F32),
        ),
        [ANY, line, line, ANY, ANY, bias_spec, line, line] + [ANY] * dp_count,
        (act_spec, act_spec, ANY, root_spec, whole(mine, width)),
        [
            pltpu.VMEM((width, 2 * units), LOW),
            pltpu.VMEM((rows, width), LOW),
            pltpu.VMEM((rows, width), F32),
            pltpu.VMEM((rows, width), F32),
            pltpu.VMEM((pad, width), F32),
        ]
        + weight_scratch,
        4 * rows * width * units * t_count,
        40 * rows * width,
    )(table, z1, gain1, bias1, up_weight, down_weight, bias_all, gain2, bias2, *ffn_pieces)

    pooled = pooled.astype(LOW)
    line_pooled = jnp.stack([pooled] + [swap(pooled, k, "tensor") for k in range(1, t_count)])
    returned = line_pooled.reshape(sentences, width)[source]
    both = jnp.concatenate([returned, cot_paired])
    everyone = jnp.stack(gather_plane(both)).reshape(-1, width)
    apart = (partner // sentences) ^ dp_me
    base = ((apart & 1) * chips + (apart >> 1)) * (2 * sentences) + partner % sentences
    partner_pooled = everyone[base].astype(F32)
    partner_cot = everyone[base + sentences].astype(F32)
    paired = (returned.astype(F32) * partner_pooled).astype(LOW)
    pool_grad = cot_pooled.astype(F32) + partner_pooled * (cot_paired.astype(F32) + partner_cot)
    pool_grad = pool_grad.astype(LOW).astype(F32)[chosen]

    send_spec = pl.BlockSpec((chips, 1, slab, units), lambda k, table: (0, k, 0, 0))
    send_shape = shape((chips, t_count, slab, units), LOW)
    half_spec = pl.BlockSpec((chips // 2, 1, slab, units), lambda k, table: (0, k, 0, 0))
    half_shape = shape((chips // 2, t_count, slab, units), LOW)
    down_mine, down_early, down_late, up_mine, up_early, up_late, *small_parts = call(
        ffn_backward,
        (send_shape, half_shape, half_shape) * 2
        + (
            shape((rows, width), LOW),
            turn_shape,
            shape((4, width), F32),
            shape((t_count, 1, units), F32),
        ),
        [whole(mine, width), ANY, root_spec, line, ANY, root_spec, line, line, ANY, ANY]
        + [act_spec, act_spec]
        + [ANY] * dp_count,
        (send_spec, half_spec, half_spec) * 2
        + (full, whole(dp_count, slab, rows), whole(4, width), bias_spec),
        [
            pltpu.VMEM((width, 2 * units), LOW),
            pltpu.VMEM((rows, width), F32),
            pltpu.VMEM((rows, width), F32),
            pltpu.VMEM((pad, width), F32),
            pltpu.VMEM((rows, width), LOW),
            pltpu.VMEM((dp_count, slab, rows), LOW),
            pltpu.VMEM((dp_count, slab, rows), LOW),
            pltpu.VMEM((rows, units), LOW),
        ]
        + weight_scratch,
        8 * rows * width * units * t_count,
        60 * rows * width,
    )(
        table, pool_grad, z2, root2, gain2, z1, root1, gain1, bias1, up_weight, down_weight,
        active, slope, *ffn_pieces
    )

    attn_low, attn_t, sums, bias_sum = small_parts

    chip_bits = bits_of(chips)
    high = chip_bits[-1]
    down_early, up_early = swap(down_early, 1), swap(up_early, 1)
    small = jnp.concatenate([bias_sum.reshape(t_count, units), sums])
    small = small + swap(small, 1)
    down_sent, up_sent, small, attn_low = tie(
        add(pick(down_mine, 1, 1), down_early).astype(LOW),
        add(pick(up_mine, 1, high), up_early).astype(LOW),
        small,
        attn_low,
    )
    down_got, up_got = swap(down_sent, 2), swap(up_sent, 2 * high)
    down_late, up_late, small, attn_t = tie(down_late, up_late, small, attn_t)
    small_got = swap(small, 2)
    down_late, up_late = swap(down_late, 1), swap(up_late, 1)

    share = length // t_count
    proj_grad, *input_blocks = pl.pallas_call(
        attention_backward,
        out_shape=(shape((pad, 3 * width), LOW),)
        + (shape((mine, share, width), LOW),) * t_count,
        in_specs=[SMEM, VMEM, VMEM, ANY, ANY, ANY],
        out_specs=(ANY,) + (VMEM,) * t_count,
        scratch_shapes=[
            pltpu.VMEM((pad, width), LOW),
            pltpu.VMEM((pad, 3 * width), LOW),
            pltpu.VMEM(probs_shape, LOW),
            pltpu.VMEM((width, 3 * width), LOW),
            pltpu.VMEM((pad, 3 * width), LOW),
            pltpu.SemaphoreType.DMA((3,)),
            pltpu.SemaphoreType.DMA((1,)),
        ],
        compiler_params=params(),
        cost_estimate=cost(12 * rows * width * width, 30 * rows * width),
        name="attention_backward",
    )(table, attn_low, wo, proj, probs, qkv)

    down_got, up_got, down_late, up_late, small_got, proj_grad, *input_blocks = tie(
        down_got, up_got, down_late, up_late, small_got, proj_grad, *input_blocks
    )
    small = small + small_got
    down_terms = [pick(down_mine, 0, 1), down_late, down_got]
    up_terms = [pick(up_mine, 0, high), up_late, up_got]
    for low, top in zip(chip_bits[1:-1], chip_bits[1:-1][::-1]):
        down_terms = kept(down_terms, 1, swap(sent(down_terms, 1), 2 * low))
        up_terms = kept(up_terms, top, swap(sent(up_terms, top), 2 * top))
    down_sent, up_sent, small, proj_grad, *input_blocks = tie(
        sent(down_terms, 1), sent(up_terms, 1), small, proj_grad, *input_blocks
    )
    small_got = swap(small, 4)
    down_got, up_got = swap(down_sent, 2 * high), swap(up_sent, 2)
    input_landed = [input_blocks[0]] + [None] * (t_count - 1)
    input_landed[2] = swap(input_blocks[2], 2, "tensor")

    attn_mine, attn_other = pl.pallas_call(
        attention_weights,
        out_shape=(shape((chips, t_count, slab, block), LOW),) * 2,
        in_specs=[SMEM] + [ANY] * 4,
        out_specs=(VMEM,) * 2,
        scratch_shapes=[
            pltpu.VMEM((dp_count, slab, rows), LOW),
            pltpu.VMEM((dp_count, slab, rows), LOW),
            pltpu.VMEM((pad, width), LOW),
            pltpu.VMEM((pad, 3 * width), LOW),
            pltpu.SemaphoreType.DMA((6,)),
        ],
        compiler_params=params(),
        cost_estimate=cost(8 * rows * width * width, 30 * rows * width),
        name="attention_weights",
    )(table, packed_t, attn_t, ctx, proj_grad)

    def finish(kernel, near, outs, flat):
        near = jnp.stack(near)
        far = swap(near, 1)
        return pl.pallas_call(
            kernel,
            out_shape=tuple(shape(dims, F32) for dims in outs),
            in_specs=[SMEM, ANY, ANY],
            out_specs=(VMEM,) * 2,
            scratch_shapes=[
                pltpu.VMEM((dp_count,) + near.shape[1:], LOW),
                pltpu.VMEM((width, flat), F32),
                pltpu.SemaphoreType.DMA((dp_count,)),
            ],
            compiler_params=params(),
            cost_estimate=cost(0, 8 * width * near.shape[2]),
            name=kernel.__name__,
        )(table, near, far)

    attn_other, small_got, down_got, up_got, input_landed[2] = tie(
        attn_other, small_got, down_got, up_got, input_landed[2]
    )
    small = small + small_got
    for mask in bits_of(dp_count)[3:]:
        small = small + swap(small, mask)
    attn_got = swap(attn_other, 1)
    attn_sent = [add(attn_mine[m], attn_got[m]).astype(LOW) for m in range(1, chips)]
    ffn_line = jnp.concatenate(
        [add(*kept(up_terms, 1, up_got))[0], add(*kept(down_terms, 1, down_got))[0]], axis=2
    )
    ffn_line = [ffn_line.astype(LOW)]
    ffn_sent, small, *attn_sent = tie(sent(ffn_line, 1), small, *attn_sent)
    attn_got = [attn_got[0]] + [swap(item, 2 * m) for m, item in zip(range(1, chips), attn_sent)]
    ffn_got = swap(ffn_sent, 1, "tensor")
    norms, bias_part = small[t_count:], small[:t_count]

    def small_step(norms, bias_part, mask):
        half = bias_part.shape[0] // 2
        split = bias_part.reshape(half, 2, units)
        got = swap(jnp.concatenate([split[:, 1], norms]), mask, "tensor")
        return norms, got, split[:, 0]

    def small_sum(norms, got, bias_part):
        half = bias_part.shape[0]
        return norms + got[half:], bias_part + got[:half]

    norms, small_got, bias_part = small_step(norms, bias_part, 1)
    ffn_line = kept(ffn_line, 1, ffn_got)
    ffn_got = swap(sent(ffn_line, 1), 2, "tensor")
    *attn_got, ffn_got, small_got, input_blocks[3] = tie(
        *attn_got, ffn_got, small_got, input_blocks[3]
    )
    norms, bias_part = small_sum(norms, small_got, bias_part)
    attn_line = [add(attn_mine[0], *attn_got).astype(LOW)]
    ffn_sum = add(*kept(ffn_line, 1, ffn_got))[0].astype(LOW)
    attn_sent, ffn_sum, input_blocks[3] = tie(sent(attn_line, 1), ffn_sum, input_blocks[3])
    attn_got = swap(attn_sent, 1, "tensor")
    ffn_chips = gather_chips(ffn_sum)
    input_landed[3] = swap(input_blocks[3], 3, "tensor")
    attn_got, input_landed[3], input_blocks[1], norms, *ffn_chips = tie(
        attn_got, input_landed[3], input_blocks[1], norms, *ffn_chips
    )
    attn_line = kept(attn_line, 1, attn_got)
    attn_sent, norms, input_blocks[1], ffn_chips[0] = tie(
        sent(attn_line, 1), norms, input_blocks[1], ffn_chips[0]
    )
    attn_got = swap(attn_sent, 2, "tensor")
    input_landed[1] = swap(input_blocks[1], 1, "tensor")
    norms, small_got, bias_part = small_step(norms, bias_part, 2)
    up_grad, down_grad = finish(place_grads, ffn_chips, ((width, units), (units, width)), units)
    attn_got, up_grad = tie(attn_got, up_grad)
    attn_sum = add(*kept(attn_line, 1, attn_got))[0].astype(LOW)
    attn_sum, input_landed[0] = tie(attn_sum, input_landed[0])
    attn_chips = gather_chips(attn_sum)
    input_landed[1], small_got, attn_chips[1] = tie(input_landed[1], small_got, attn_chips[1])
    norms, bias_part = small_sum(norms, small_got, bias_part)
    home = pl.pallas_call(
        send_home,
        out_shape=shape((share, sentences, width), LOW),
        in_specs=[VMEM] * (1 + t_count),
        out_specs=VMEM,
        compiler_params=params(),
        cost_estimate=cost(0, 4 * share * sentences * width),
        name="send_home",
    )(jnp.tile(source, STEP).reshape(-1, 1), *input_landed)
    attn_chips[0], home = tie(attn_chips[0], home)
    qkv_grad, out_grad = finish(
        place_attention_grads, attn_chips, ((3 * ctx_cols, width), (ctx_cols, width)), block
    )

    return (
        returned,
        paired,
        home,
        qkv_grad.T,
        out_grad,
        norms[2],
        norms[3],
        up_grad,
        bias_part[0],
        down_grad,
        norms[0],
        norms[1],
    )


def solution(mesh):
    placed = (
        P(None, "dp", None),
        P("dp"),
        P("dp"),
        P(None, "tensor"),
        P("tensor", None),
        P(),
        P(),
        P(None, "tensor"),
        P("tensor"),
        P("tensor", None),
        P(),
        P(),
        P("dp", None),
        P("dp", None),
    )
    return jax.shard_map(
        shards,
        mesh=mesh,
        in_specs=placed,
        out_specs=(
            P("dp", None),
            P("dp", None),
            P("tensor", "dp", None),
            P(None, "tensor"),
            P("tensor", None),
            P(),
            P(),
            P(None, "tensor"),
            P("tensor"),
            P("tensor", None),
            P(),
            P(),
        ),
        check_vma=False,
    )
```

```python
import functools

import jax
import jax.numpy as jnp
import numpy as np
from jax import lax
from jax.experimental import pallas as pl
from jax.experimental.pallas import tpu as pltpu
from jax.sharding import PartitionSpec as P

HD = 64
EPSILON = 1e-06
LOW = jnp.bfloat16
F32 = jnp.float32
INV_SQRT_2PI = 0.3989422804014327
SQRT_HALF = 0.7071067811865476
TILE = 256
CHUNK = 256
STEP = 16
MASKED = -1000000000.0
LOG2_E = 1.4426950408889634
VMEM_BYTES = 60 * 2**20
NN = (((1,), (0,)), ((), ()))
NT = (((1,), (1,)), ((), ()))
PAIR = 2 * HD
LENS, TILES, LINE, PLACE, DEST = 16, 32, 33, 48, 80


def mm(a, b, dims=NN):
    return lax.dot_general(a, b, dims, preferred_element_type=F32)


def rows_of(table, s):
    return pl.ds(pl.multiple_of(table[s], 16), 128)


def tile_at(i):
    return pl.ds(pl.multiple_of(i * TILE, TILE), TILE)


def normalize(values):
    center = values - jnp.mean(values, axis=-1, keepdims=True)
    spread = jnp.mean(center * center, axis=-1, keepdims=True)
    root = lax.rsqrt(spread + EPSILON)
    return center * root, root


def normalize_back(z, root, dz):
    return root * (
        dz - jnp.mean(dz, -1, keepdims=True) - z * jnp.mean(dz * z, -1, keepdims=True)
    )


def split_heads(pair):
    first = lax.broadcasted_iota(jnp.int32, pair.shape, 1) < HD
    zero = jnp.zeros_like(pair)
    return jnp.concatenate([jnp.where(first, pair, zero), jnp.where(first, zero, pair)], axis=0)


def join_heads(split):
    n = split.shape[0] // 2
    first = lax.broadcasted_iota(jnp.int32, (n, PAIR), 1) < HD
    return jnp.where(first, split[:n], split[n:])


def place_pieces(table, pieces, slabs, sems):
    copies = []
    for i, piece in enumerate(pieces):
        copies.append(pltpu.make_async_copy(piece, slabs.at[table[PLACE + i]], sems.at[i]))
    return copies


def turn(table, turned, rows, value):
    flat = value.T
    count, slab = turned.shape[0], turned.shape[1]
    for j in range(count):
        turned[table[DEST + j], :, rows] = flat[j * slab : (j + 1) * slab, :]


def pack(table, chosen, tokens, packed, packed_t, x):
    sents, length, width = x.shape
    total = tokens.shape[1]
    depth = total * STEP
    column = lax.broadcasted_iota(jnp.int32, (STEP, depth), 1)
    position = lax.broadcasted_iota(jnp.int32, (STEP, depth), 0)
    here = (column // total) == position
    pick = [here & ((column % total) == chosen[s]) for s in range(sents)]
    pick = jnp.concatenate([jnp.where(item, 1.0, 0.0).astype(LOW) for item in pick], axis=0)
    for block in range(length // STEP):
        rows = slice(block * STEP, (block + 1) * STEP)
        found = mm(pick, tokens[rows].reshape(depth, width)).astype(LOW)
        for s in range(sents):
            x[s, rows, :] = found[s * STEP : (s + 1) * STEP]
    packed[...] = jnp.zeros_like(packed)

    def place(s, _):
        packed[rows_of(table, s), :] = x[s]
        return 0

    lax.fori_loop(0, sents, place, 0)

    def flip(i, _):
        rows = tile_at(i)
        turn(table, packed_t, rows, packed[rows, :])
        return 0

    lax.fori_loop(0, table[TILES], flip, 0)


def send_home(source, *refs):
    blocks, home = refs[:-1], refs[-1]
    share, total, width = home.shape
    depth = total * STEP
    column = lax.broadcasted_iota(jnp.int32, (depth, depth), 1)
    row = lax.broadcasted_iota(jnp.int32, (depth, depth), 0)
    pick = ((column % STEP) == (row // total)) & ((column // STEP) == source[...])
    pick = jnp.where(pick, 1.0, 0.0).astype(LOW)
    for block in range(share // STEP):
        rows = slice(block * STEP, (block + 1) * STEP)
        values = [item[:, rows, :].reshape(-1, width) for item in blocks]
        found = mm(pick, jnp.concatenate(values, axis=0)).astype(LOW)
        home[rows] = found.reshape(STEP, total, width)


def start_all(copies):
    for copy in copies:
        copy.start()


def wait_all(copies):
    for copy in copies:
        copy.wait()


def by_tiles(table, rows, body):
    for n in range(1, rows // TILE + 1):

        @pl.when(table[TILES] == n)
        def _():
            body(n * TILE)


def tile_copies(table, source, target, sems):
    def at(i):
        rows = slice(i * TILE, (i + 1) * TILE)
        return pltpu.make_async_copy(source.at[rows], target.at[rows], sems.at[i])

    def each(act):
        for i in range(sems.shape[0]):

            @pl.when(i < table[TILES])
            def _():
                act(at(i))

    return each


def place_weight(k, steps, weight, own_down, slabs):
    count, slab = slabs.shape[0], slabs.shape[1]
    columns = weight.shape[1]

    @pl.when(k == 0)
    def _():
        weight[:, columns // 2 :] = own_down[...].T

    for t in range(1, steps):

        @pl.when(k == t)
        def _():
            for j in range(count):
                weight[j * slab : (j + 1) * slab, :] = slabs[
                    j, :, (t - 1) * columns : t * columns
                ]


def attention_forward(table, packed, own_qkv, own_out, *refs):
    pieces, refs = refs[:-18], refs[-18:]
    proj_out, ctx_out, probs_out, qkv_out, wo_out, z1_out, root1 = refs[:7]
    proj, ctx, probs, qkv, wo, z1, slabs, sems, out_sems, wide_sems, z1_sems = refs[7:]
    sents, pairs = probs.shape[0], probs.shape[1]
    width = packed.shape[1]
    length = probs.shape[3]
    part = own_out.shape[0]
    block = 4 * part
    heads = part // HD
    arrivals = place_pieces(table, pieces, slabs, sems)
    start_all(arrivals)
    count, slab = slabs.shape[0], slabs.shape[1]
    for h in range(heads):
        for p in range(3):
            source = (h * 3 + p) * HD
            qkv[:, p * width + h * HD : p * width + (h + 1) * HD] = own_qkv[
                source : source + HD, :
            ].T
    wo[:, :part] = own_out[...].T
    ctx[...] = jnp.zeros_like(ctx)
    tiles = table[TILES]
    end = pl.ds(pl.multiple_of(tiles * TILE, TILE), length)
    proj[end, :] = jnp.zeros((length, 3 * width), LOW)
    wait_all(arrivals)
    for j in range(count):
        rows = slice(j * slab, (j + 1) * slab)
        for k in range(1, width // part):
            base = (k - 1) * block
            for p in range(3):
                qkv[rows, p * width + k * part : p * width + (k + 1) * part] = slabs[
                    j, :, base + p * part : base + (p + 1) * part
                ]
            wo[rows, k * part : (k + 1) * part] = slabs[j, :, base + 3 * part : base + block]
    wide_copies = [
        pltpu.make_async_copy(qkv, qkv_out, wide_sems.at[0]),
        pltpu.make_async_copy(wo, wo_out, wide_sems.at[1]),
    ]
    start_all(wide_copies)

    def project(n):
        source = packed[:n, :]
        for c in range(0, 3 * width, CHUNK):
            cols = slice(c, c + CHUNK)
            proj[:n, cols] = mm(source, qkv[:, cols]).astype(LOW)

    by_tiles(table, z1.shape[0], project)
    proj_copy = pltpu.make_async_copy(proj, proj_out, out_sems.at[0])
    proj_copy.start()

    def attend(s, _):
        rows = rows_of(table, s)
        valid = lax.broadcasted_iota(jnp.int32, (length, length), 0) < table[LENS + s]
        for p in range(pairs):
            at = p * PAIR
            queries = proj[rows, at : at + PAIR]
            keys = split_heads(proj[rows, width + at : width + at + PAIR])
            values = split_heads(proj[rows, 2 * width + at : 2 * width + at + PAIR])
            scores = mm(keys, queries, NT)
            for h in range(2):
                half = slice(h * length, (h + 1) * length)
                score = jnp.where(valid, scores[half], MASKED)
                top = jnp.max(score, axis=0, keepdims=True)
                score = jnp.exp2((score - top) * (HD**-0.5 * LOG2_E))
                total = jnp.sum(score, axis=0, keepdims=True)
                probs[s, p, half, :] = (score * (1.0 / total)).astype(LOW)
            ctx[rows, at : at + PAIR] = mm(probs[s, p].T, values).astype(LOW)
        return 0

    lax.fori_loop(0, sents, attend, 0)
    ctx_copies = [
        pltpu.make_async_copy(ctx, ctx_out, out_sems.at[1]),
        pltpu.make_async_copy(probs, probs_out, out_sems.at[2]),
    ]
    start_all(ctx_copies)

    for i in range(z1_sems.shape[0]):
        rows = slice(i * TILE, (i + 1) * TILE)

        @pl.when(i < tiles)
        def _():
            attended = mm(ctx[rows, :], wo[...], NT)
            z, root = normalize(packed[rows, :].astype(F32) + attended)
            z1[rows, :] = z
            root1[rows, :] = jnp.broadcast_to(root, (TILE, 128))
            pltpu.make_async_copy(z1.at[rows], z1_out.at[rows], z1_sems.at[i]).start()

    tile_copies(table, z1, z1_out, z1_sems)(lambda copy: copy.wait())
    wait_all(wide_copies + [proj_copy] + ctx_copies)


def gelu_parts(pre):
    t = pl.reciprocal(1.0 + jnp.abs(pre) * (0.3275911 * SQRT_HALF))
    poly = 0.5 * 1.061405429
    for c in (-1.453152027, 1.421413741, -0.284496736, 0.254829592):
        poly = poly * t + 0.5 * c
    e = jnp.exp2(pre * pre * (-0.5 * LOG2_E))
    tail = poly * t * e
    cdf = jnp.where(pre >= 0.0, 1.0 - tail, tail)
    return pre * cdf, cdf + pre * (e * INV_SQRT_2PI)


def ffn_forward(parts, table, z1_in, gain1, bias1, own_up, own_down_in, bias, gain2, bias2, *refs):
    pieces, refs = refs[:-16], refs[-16:]
    active, slope, z2_out, root2, pooled = refs[:5]
    weight, first, total, z1, z2, own_down, slabs, sems, own_sems, z1_sems, z2_sems = refs[5:]
    k = pl.program_id(0)
    steps = pl.num_programs(0)
    tiles = table[TILES]
    units = active.shape[2]
    arrivals = place_pieces(table, pieces, slabs, sems)
    own = [
        pltpu.make_async_copy(own_up, weight.at[:, :units], own_sems.at[0]),
        pltpu.make_async_copy(own_down_in, own_down, own_sems.at[1]),
    ]
    z1_copies = tile_copies(table, z1_in, z1, z1_sems)

    @pl.when(k == 0)
    def _():
        z1_copies(lambda copy: copy.start())
        start_all(own)
        z1_copies(lambda copy: copy.wait())

        def start(i, _):
            rows = tile_at(i)
            value = z1[rows, :] * gain1[...] + bias1[...]
            first[rows, :] = value.astype(LOW)
            total[rows, :] = value
            return 0

        lax.fori_loop(0, tiles, start, 0)
        wait_all(own)
        start_all(arrivals)

    @pl.when(k == 1)
    def _():
        wait_all(arrivals)

    place_weight(k, parts, weight, own_down, slabs)

    def work(n):
        for r in range(0, n, TILE):
            rows = slice(r, r + TILE)
            source = first[rows, :]
            for c in range(0, units, CHUNK):
                cols = slice(c, c + CHUNK)
                act, slp = gelu_parts(mm(source, weight[:, cols]) + bias[0, :, cols])
                active[0, rows, cols] = act.astype(LOW)
                slope[0, rows, cols] = slp.astype(LOW)
            total[rows, :] += mm(active[0, rows, :], weight[:, units:], NT)

    by_tiles(table, first.shape[0], work)

    @pl.when(k == steps - 1)
    def _():
        z2[pl.ds(pl.multiple_of(tiles * TILE, TILE), 128), :] = jnp.zeros((128, z2.shape[1]), F32)

        def finish(i, _):
            rows = tile_at(i)
            z, root = normalize(total[rows, :])
            z2[rows, :] = z
            root2[rows, :] = jnp.broadcast_to(root, (TILE, 128))
            return 0

        lax.fori_loop(0, tiles, finish, 0)
        z2_copies = tile_copies(table, z2, z2_out, z2_sems)
        z2_copies(lambda copy: copy.start())
        for s in range(pooled.shape[0]):
            n = table[LENS + s]
            valid = lax.broadcasted_iota(jnp.int32, (128, z2.shape[1]), 0) < n
            rows = jnp.where(valid, z2[rows_of(table, s), :], 0.0)
            mean = jnp.sum(rows, axis=0, keepdims=True) / n.astype(F32)
            pooled[s : s + 1, :] = mean * gain2[...] + bias2[...]
        z2_copies(lambda copy: copy.wait())


def weight_grad(table, turned, right, store):
    count, slab, rows = turned.shape

    def body(n):
        if slab % 16 == 0:
            left = turned[:, :, :n].reshape(count * slab, n)
        else:
            left = jnp.concatenate([turned[j, :, :n] for j in range(count)], axis=0)
        store(lambda columns: mm(left, right(n, columns)))

    by_tiles(table, rows, body)


def half_order(chips, bit):
    order = {}
    for m in range(chips):
        order[m] = sum(1 for other in range(m) if (other & bit) == (m & bit))
    return order


def split_send(mine, other, value, k, columns):
    chips, slab = mine.shape[0], mine.shape[2]
    for m in range(chips):
        mine[m, k, :, columns] = value[m * slab : (m + 1) * slab].astype(LOW)
        target, at = other(m)
        target[at, k, :, columns] = value[(chips + m) * slab : (chips + m + 1) * slab].astype(LOW)


def send_chunks(mine, early, late, bit, product):
    order = half_order(mine.shape[0], bit)

    def other(m):
        return (early if m & bit else late), order[m]

    for c in range(0, mine.shape[3], CHUNK):
        cols = slice(c, c + CHUNK)
        split_send(mine, other, product(cols), 0, cols)


def ffn_backward(
    parts, table, pool, z2_in, root2, gain2, z1_in, root1, gain1, bias1, own_up, own_down_in,
    active, slope, *refs
):
    pieces, refs = refs[:-24], refs[-24:]
    down_mine, down_early, down_late, up_mine, up_early, up_late = refs[:6]
    attn_low, attn_t, sums, bias_sum = refs[6:10]
    weight, z1, z2, total, branch, branch_t, first_t, hidden, own_down, slabs = refs[10:20]
    sems, own_sems, z1_sems, z2_sems = refs[20:]
    k = pl.program_id(0)
    tiles = table[TILES]
    width, units = own_up.shape
    arrivals = place_pieces(table, pieces, slabs, sems)
    own = [
        pltpu.make_async_copy(own_up, weight.at[:, :units], own_sems.at[0]),
        pltpu.make_async_copy(own_down_in, own_down, own_sems.at[1]),
    ]
    z1_copies = tile_copies(table, z1_in, z1, z1_sems)
    z2_copies = tile_copies(table, z2_in, z2, z2_sems)

    @pl.when(k == 0)
    def _():
        z2_copies(lambda copy: copy.start())
        z1_copies(lambda copy: copy.start())
        start_all(own)
        total[...] = jnp.zeros_like(total)
        for s in range(pool.shape[0]):
            n = table[LENS + s]
            valid = lax.broadcasted_iota(jnp.int32, (128, width), 0) < n
            row = pool[s : s + 1, :] / n.astype(F32)
            total[rows_of(table, s), :] = jnp.where(valid, row, 0.0)
        sums[...] = jnp.zeros_like(sums)
        z2_copies(lambda copy: copy.wait())

        def start(i, _):
            rows = tile_at(i)
            grad = total[rows, :]
            z = z2[rows, :]
            sums[0:1, :] += jnp.sum(grad * z, axis=0, keepdims=True)
            sums[1:2, :] += jnp.sum(grad, axis=0, keepdims=True)
            value = normalize_back(z, root2[rows, 0:1], grad * gain2[...])
            low = value.astype(LOW)
            total[rows, :] = value
            branch[rows, :] = low
            turn(table, branch_t, rows, low)
            return 0

        lax.fori_loop(0, tiles, start, 0)
        z1_copies(lambda copy: copy.wait())

        def flip(i, _):
            rows = tile_at(i)
            turn(table, first_t, rows, (z1[rows, :] * gain1[...] + bias1[...]).astype(LOW))
            return 0

        lax.fori_loop(0, tiles, flip, 0)
        wait_all(own)
        start_all(arrivals)

    @pl.when(k == 1)
    def _():
        wait_all(arrivals)

    place_weight(k, parts, weight, own_down, slabs)
    weight_grad(
        table,
        branch_t,
        lambda n, cols: active[0, :n, cols],
        lambda product: send_chunks(down_mine, down_early, down_late, 1, product),
    )
    bias_sum[...] = jnp.zeros_like(bias_sum)

    def work(n):
        source = branch[:n, :]
        for c in range(0, units, CHUNK):
            cols = slice(c, c + CHUNK)
            grad = mm(source, weight[:, units + c : units + c + CHUNK])
            hid = (slope[0, :n, cols].astype(F32) * grad).astype(LOW)
            hidden[:n, cols] = hid
            bias_sum[0, :, cols] += jnp.sum(hid.astype(F32), axis=0, keepdims=True)
        total[:n, :] += mm(hidden[:n, :], weight[:, :units], NT)

    by_tiles(table, hidden.shape[0], work)
    weight_grad(
        table,
        first_t,
        lambda n, cols: hidden[:n, cols],
        lambda product: send_chunks(
            up_mine, up_early, up_late, up_mine.shape[0] // 2, product
        ),
    )

    @pl.when(k == pl.num_programs(0) - 1)
    def _():
        def finish(i, _):
            rows = tile_at(i)
            grad = total[rows, :]
            z = z1[rows, :]
            sums[2:3, :] += jnp.sum(grad * z, axis=0, keepdims=True)
            sums[3:4, :] += jnp.sum(grad, axis=0, keepdims=True)
            value = normalize_back(z, root1[rows, 0:1], grad * gain1[...])
            low = value.astype(LOW)
            attn_low[rows, :] = low
            turn(table, attn_t, rows, low)
            return 0

        lax.fori_loop(0, tiles, finish, 0)


def attention_backward(table, attn_low, wo, proj_in, probs_in, qkv_in, proj_grad_out, *refs):
    outs, refs = refs[:-7], refs[-7:]
    ctx_grad, proj, probs, qkv, proj_grad, sems, out_sem = refs
    sents, pairs = probs.shape[0], probs.shape[1]
    length = probs.shape[3]
    width = attn_low.shape[1]
    tiles = table[TILES]
    arrivals = [
        pltpu.make_async_copy(proj_in, proj, sems.at[0]),
        pltpu.make_async_copy(probs_in, probs, sems.at[1]),
        pltpu.make_async_copy(qkv_in, qkv, sems.at[2]),
    ]
    start_all(arrivals)
    ctx_grad[...] = jnp.zeros_like(ctx_grad)
    proj_grad[...] = jnp.zeros_like(proj_grad)

    def start(n):
        ctx_grad[:n, :] = mm(attn_low[:n, :], wo[...]).astype(LOW)

    by_tiles(table, attn_low.shape[0], start)
    wait_all(arrivals[:2])
    scale = HD**-0.5

    def attend(s, _):
        rows = rows_of(table, s)
        live = lax.broadcasted_iota(jnp.int32, (length, PAIR), 0) < table[LENS + s]
        for p in range(pairs):
            at = p * PAIR
            queries = proj[rows, at : at + PAIR]
            keys = split_heads(proj[rows, width + at : width + at + PAIR])
            values = split_heads(proj[rows, 2 * width + at : 2 * width + at + PAIR])
            grad = ctx_grad[rows, at : at + PAIR]
            grad = jnp.where(live, grad, jnp.zeros_like(grad))
            prob_grad = mm(values, grad, NT)
            score_grad = []
            for h in range(2):
                half = slice(h * length, (h + 1) * length)
                prob = probs[s, p, half, :].astype(F32)
                part = prob_grad[half]
                inner = jnp.sum(prob * part, axis=0, keepdims=True)
                score_grad.append((prob * (part - inner)).astype(LOW))
            score_grad = jnp.concatenate(score_grad, axis=0)
            proj_grad[rows, at : at + PAIR] = (mm(score_grad.T, keys) * scale).astype(LOW)
            proj_grad[rows, width + at : width + at + PAIR] = (
                join_heads(mm(score_grad, queries)) * scale
            ).astype(LOW)
            proj_grad[rows, 2 * width + at : 2 * width + at + PAIR] = join_heads(
                mm(probs[s, p], grad)
            ).astype(LOW)
        return 0

    lax.fori_loop(0, sents, attend, 0)
    proj_copy = pltpu.make_async_copy(proj_grad, proj_grad_out, out_sem.at[0])
    proj_copy.start()
    arrivals[2].wait()

    def finish(n):
        total = mm(proj_grad[:n, :], qkv[...], NT)
        ctx_grad[:n, :] = (attn_low[:n, :].astype(F32) + total).astype(LOW)

    by_tiles(table, attn_low.shape[0], finish)
    ctx_grad[pl.ds(pl.multiple_of(tiles * TILE, TILE), length), :] = jnp.zeros(
        (length, width), LOW
    )
    share = outs[0].shape[1]
    for k, out in enumerate(outs):
        first = table[LINE + k] * share
        position = lax.broadcasted_iota(jnp.int32, (share, width), 0) + first
        for s in range(sents):
            value = ctx_grad[pl.ds(pl.multiple_of(table[s] + first, 16), share), :]
            out[s] = jnp.where(position < table[LENS + s], value, jnp.zeros_like(value))
    proj_copy.wait()


def attention_weights(table, *refs):
    sources, (mine, other), (packed_t, attn_t, ctx, proj_grad, sems) = refs[:4], refs[4:6], refs[6:]
    width = ctx.shape[1]
    count = mine.shape[1]
    part = width // count
    copies = [
        pltpu.make_async_copy(source, target, sems.at[i])
        for i, (source, target) in enumerate(zip(sources[:3], (packed_t, attn_t, ctx)))
    ]
    for p in range(3):
        cols = slice(p * width, (p + 1) * width)
        copies.append(
            pltpu.make_async_copy(sources[3].at[:, cols], proj_grad.at[:, cols], sems.at[3 + p])
        )
    order = [copies[1], copies[2], copies[0]] + copies[3:]
    start_all(order)

    def store(p, product):
        value = product(slice(p * width, (p + 1) * width) if p < 3 else slice(None))
        for k in range(count):
            split_send(
                mine,
                lambda m: (other, m),
                value[:, k * part : (k + 1) * part],
                k,
                slice(p * part, (p + 1) * part),
            )

    wait_all(order[:2])
    weight_grad(
        table, attn_t, lambda n, cols: ctx[:n, cols], lambda product: store(3, product)
    )
    order[2].wait()
    for p in range(3):
        order[3 + p].wait()
        weight_grad(
            table,
            packed_t,
            lambda n, cols: proj_grad[:n, cols],
            lambda product: store(p, product),
        )


def stacked_pieces(stacks):
    return [stack.at[i] for stack in stacks for i in range(stack.shape[0])]


def place_grads(table, near, far, straight, turned, slabs, flat, sems):
    count, slab = slabs.shape[0], slabs.shape[1]
    arrivals = place_pieces(table, stacked_pieces((near, far)), slabs, sems)
    start_all(arrivals)
    wait_all(arrivals)
    width = straight.shape[1]
    for j in range(count):
        rows = slice(j * slab, (j + 1) * slab)
        straight[rows, :] = slabs[j, :, :width].astype(F32)
        flat[rows, :] = slabs[j, :, width:].astype(F32)
    turned[...] = flat[...].T


def place_attention_grads(table, near, far, qkv, wo, slabs, flat, sems):
    count, slab = slabs.shape[0], slabs.shape[1]
    arrivals = place_pieces(table, stacked_pieces((near, far)), slabs, sems)
    start_all(arrivals)
    wait_all(arrivals)
    for j in range(count):
        flat[j * slab : (j + 1) * slab, :] = slabs[j].astype(F32)
    part = wo.shape[0]
    heads = part // HD
    for p in range(3):
        piece = flat[:, p * part : (p + 1) * part].T
        for h in range(heads):
            target = (h * 3 + p) * HD
            qkv[target : target + HD, :] = piece[h * HD : (h + 1) * HD, :]
    wo[...] = flat[:, 3 * part :].T


COST = 1000000
SMEM = pl.BlockSpec(memory_space=pltpu.SMEM)
VMEM = pl.BlockSpec(memory_space=pltpu.VMEM)
ANY = pl.BlockSpec(memory_space=pl.ANY)


def shape(dims, dtype):
    return jax.ShapeDtypeStruct(dims, dtype)


def params():
    return pltpu.CompilerParams(vmem_limit_bytes=VMEM_BYTES)


def cost(flops, nbytes):
    return pl.CostEstimate(flops=flops // COST, bytes_accessed=nbytes // COST, transcendentals=0)


def add(*terms):
    return sum(term.astype(F32) for term in terms)


def swap(value, mask, axis="dp"):
    return lax.ppermute(value, axis, [(i, i ^ mask) for i in range(lax.axis_size(axis))])


def bits_of(count):
    return [1 << i for i in range(count.bit_length() - 1)]


def take(values, index, axis=0):
    return lax.dynamic_index_in_dim(values, index, axis, False, allow_negative_indices=False)


def cut(values, start, size, axis):
    return lax.dynamic_slice_in_dim(values, start, size, axis, allow_negative_indices=False)


def tie(*values):
    return lax.optimization_barrier(values)


def gather_line(piece):
    n = lax.axis_size("tensor")
    return jnp.concatenate([swap(piece, k, "tensor") for k in range(1, n)], axis=1)


def gather_chips(value):
    return [value] + [swap(value, 2 * m) for m in range(1, lax.axis_size("dp") // 2)]


def gather_cores(near):
    return near + [swap(item, 1) for item in near]


def gather_plane(value):
    return gather_cores(gather_chips(value))


def pick(term, side, bit):
    dims = term.shape
    view = term.reshape((dims[0] // (2 * bit), 2, bit) + dims[1:])[:, side]
    return view.reshape((dims[0] // 2,) + dims[1:])


def sent(terms, bit):
    return add(*[pick(term, 1, bit) for term in terms]).astype(LOW)


def kept(terms, bit, landed):
    return [pick(term, 0, bit) for term in terms] + [landed]


def reduce_line(terms):
    for bit in bits_of(lax.axis_size("tensor")):
        terms = kept(terms, 1, swap(sent(terms, 1), bit, "tensor"))
    return add(*terms)[0].astype(LOW)


def reduce_chips(terms, bits):
    for bit in bits:
        terms = kept(terms, 1, swap(sent(terms, 1), 2 * bit))
    return terms


def shards(
    tokens,
    lengths,
    partner,
    w_qkv,
    w_out,
    ln1_gain,
    ln1_bias,
    up_weight,
    up_projection_bias,
    down_weight,
    ln2_gain,
    ln2_bias,
    cot_pooled,
    cot_paired,
):
    dp_count = lax.axis_size("dp")
    t_count = lax.axis_size("tensor")
    dp_me = lax.axis_index("dp")
    t_me = lax.axis_index("tensor")
    length, sentences, width = tokens.shape
    mine = sentences // t_count
    rows = mine * length
    pad = rows + length
    slab = width // dp_count
    chips = dp_count // 2
    heads = w_qkv.shape[1] // (3 * HD)
    units = up_weight.shape[1]
    ctx_cols = w_out.shape[0]
    block = 4 * ctx_cols

    def by_part(weight):
        return weight.reshape(-1, heads, 3, HD).transpose(0, 2, 1, 3).reshape(weight.shape)

    def rows_piece(weight):
        return cut(weight, dp_me * slab, slab, 0)

    def columns_piece(weight):
        return cut(weight, dp_me * slab, slab, 1).T

    attn_piece = jnp.concatenate([by_part(rows_piece(w_qkv)), columns_piece(w_out)], axis=1)
    attn_piece, up_early, down_early = tie(attn_piece, up_weight, down_weight)
    line_bits = bits_of(t_count)[::-1]

    def widen_line(parts, bit):
        return parts + [swap(jnp.concatenate(parts, axis=1), bit, "tensor")]

    def line_order():
        order = [0]
        for bit in line_bits:
            order += [item ^ bit for item in order]
        return order

    def by_distance(parts, columns):
        wide = jnp.concatenate(parts, axis=1)
        order = line_order()
        return [wide[:, order.index(d) * columns : (order.index(d) + 1) * columns] for d in range(t_count)]

    attn_parts = widen_line([attn_piece], line_bits[0])
    ffn_piece = jnp.concatenate([rows_piece(up_early), columns_piece(down_early)], axis=1)
    attn_parts[1], ffn_piece, up_projection_bias = tie(attn_parts[1], ffn_piece, up_projection_bias)
    for bit in line_bits[1:]:
        attn_parts = widen_line(attn_parts, bit)
    ffn_parts = widen_line([ffn_piece], line_bits[0])
    bias_parts = widen_line([up_projection_bias.reshape(1, units)], line_bits[0])
    attn_line = jnp.concatenate(by_distance(attn_parts, block)[1:], axis=1)

    order = np.arange(sentences)
    ahead = (lengths[None, :] > lengths[:, None]) | (
        (lengths[None, :] == lengths[:, None]) & (order[None, :] < order[:, None])
    )
    rank = jnp.sum(ahead.astype(jnp.int32), axis=1)
    row = rank // t_count
    column = rank % t_count
    column = jnp.where(row % 2 == 0, column, t_count - 1 - column)
    mine_here = (column == t_me)[None, :] & (row[None, :] == order[:mine, None])
    chosen = jnp.sum(jnp.where(mine_here, order[None, :], 0), axis=1)
    counts = jnp.sum(jnp.where(mine_here, lengths[None, :], 0), axis=1)
    source = (column ^ t_me) * mine + row
    taken = (counts + 15) & ~15
    ends = jnp.sum(jnp.where(np.tri(mine, dtype=bool), taken[None, :], 0), axis=1)
    devices = np.arange(dp_count)
    distance = 2 * np.arange(chips)
    near = devices[:, None] ^ distance[None, :]
    spots = np.concatenate([near, near ^ 1], axis=1)
    lines = np.arange(t_count)[:, None] ^ np.arange(t_count)[None, :]
    apart = devices[:, None] ^ devices[None, :]
    fixed = np.zeros((dp_count, DEST - PLACE + dp_count), np.int32)
    fixed[:, :dp_count] = spots
    fixed[:, DEST - PLACE :] = apart % 2 * chips + apart // 2
    line_fixed = np.zeros((t_count, PLACE - LINE), np.int32)
    line_fixed[:, :t_count] = lines
    table = jnp.concatenate(
        [
            ends - taken,
            np.zeros(LENS - mine, np.int32),
            counts,
            np.zeros(TILES - LENS - mine, np.int32),
            (ends[-1:] + (TILE - 1)) >> (TILE.bit_length() - 1),
            take(jnp.asarray(line_fixed), t_me),
            take(jnp.asarray(fixed), dp_me),
        ]
    ).astype(jnp.int32)
    attn_line, chosen = tie(attn_line, chosen)
    turn_shape = shape((dp_count, slab, rows), LOW)
    packed, packed_t = pl.pallas_call(
        pack,
        out_shape=(shape((pad, width), LOW), turn_shape),
        in_specs=[SMEM, SMEM, VMEM],
        out_specs=(VMEM,) * 2,
        scratch_shapes=[pltpu.VMEM((mine, length, width), LOW)],
        compiler_params=params(),
        cost_estimate=cost(0, 8 * rows * width),
        name="pack",
    )(table, chosen, tokens)

    attn_chips = gather_chips(attn_line)
    for bit in line_bits[1:]:
        ffn_parts = widen_line(ffn_parts, bit)
        bias_parts = widen_line(bias_parts, bit)
    bias_all = jnp.stack(by_distance(bias_parts, units))
    *attn_chips, packed = tie(*attn_chips, packed)
    attn_pieces = gather_cores(attn_chips)
    ffn_chips = gather_chips(jnp.concatenate(by_distance(ffn_parts, 2 * units)[1:], axis=1))
    attn_pieces[0], ffn_chips[0], bias_all = tie(attn_pieces[0], ffn_chips[0], bias_all)
    pairs = width // PAIR
    probs_shape = (mine, pairs, 2 * length, length)
    proj, ctx, probs, qkv, wo, z1, root1 = pl.pallas_call(
        attention_forward,
        out_shape=(
            shape((pad, 3 * width), LOW),
            shape((pad, width), LOW),
            shape(probs_shape, LOW),
            shape((width, 3 * width), LOW),
            shape((width, width), LOW),
            shape((rows, width), F32),
            shape((rows, 128), F32),
        ),
        in_specs=[SMEM, VMEM, VMEM, VMEM] + [ANY] * dp_count,
        out_specs=(ANY,) * 6 + (VMEM,),
        scratch_shapes=[
            pltpu.VMEM((pad, 3 * width), LOW),
            pltpu.VMEM((pad, width), LOW),
            pltpu.VMEM(probs_shape, LOW),
            pltpu.VMEM((width, 3 * width), LOW),
            pltpu.VMEM((width, width), LOW),
            pltpu.VMEM((rows, width), F32),
            pltpu.VMEM((dp_count, slab, (t_count - 1) * block), LOW),
            pltpu.SemaphoreType.DMA((dp_count,)),
            pltpu.SemaphoreType.DMA((3,)),
            pltpu.SemaphoreType.DMA((2,)),
            pltpu.SemaphoreType.DMA((rows // TILE,)),
        ],
        compiler_params=params(),
        cost_estimate=cost(8 * rows * width * width, 30 * rows * width),
        name="attention_forward",
    )(table, packed, w_qkv.T, w_out, *attn_pieces)
    *ffn_chips, z1 = tie(*ffn_chips, z1)
    ffn_pieces = gather_cores(ffn_chips)

    gain1, bias1 = ln1_gain.reshape(1, width), ln1_bias.reshape(1, width)
    gain2, bias2 = ln2_gain.reshape(1, width), ln2_bias.reshape(1, width)

    def whole(*dims):
        return pl.BlockSpec(dims, lambda k, table: (0,) * len(dims))

    def call(kernel, outs, ins, out_specs, scratch, flops, nbytes):
        return pl.pallas_call(
            functools.partial(kernel, t_count),
            out_shape=outs,
            grid_spec=pltpu.PrefetchScalarGridSpec(
                num_scalar_prefetch=1,
                grid=(t_count,),
                in_specs=ins,
                out_specs=out_specs,
                scratch_shapes=scratch,
            ),
            compiler_params=params(),
            cost_estimate=cost(flops, nbytes),
            name=kernel.__name__,
        )

    act_spec = pl.BlockSpec((1, rows, units), lambda k, table: (k, 0, 0))
    bias_spec = pl.BlockSpec((1, 1, units), lambda k, table: (k, 0, 0))
    line = whole(1, width)
    full = whole(rows, width)
    root_spec = whole(rows, 128)
    act_shape = shape((t_count, rows, units), LOW)
    weight_scratch = [
        pltpu.VMEM((units, width), LOW),
        pltpu.VMEM((dp_count, slab, (t_count - 1) * 2 * units), LOW),
        pltpu.SemaphoreType.DMA((dp_count,)),
        pltpu.SemaphoreType.DMA((2,)),
        pltpu.SemaphoreType.DMA((rows // TILE,)),
        pltpu.SemaphoreType.DMA((rows // TILE,)),
    ]
    active, slope, z2, root2, pooled = call(
        ffn_forward,
        (
            act_shape,
            act_shape,
            shape((rows, width), F32),
            shape((rows, 128), F32),
            shape((mine, width), F32),
        ),
        [ANY, line, line, ANY, ANY, bias_spec, line, line] + [ANY] * dp_count,
        (act_spec, act_spec, ANY, root_spec, whole(mine, width)),
        [
            pltpu.VMEM((width, 2 * units), LOW),
            pltpu.VMEM((rows, width), LOW),
            pltpu.VMEM((rows, width), F32),
            pltpu.VMEM((rows, width), F32),
            pltpu.VMEM((pad, width), F32),
        ]
        + weight_scratch,
        4 * rows * width * units * t_count,
        40 * rows * width,
    )(table, z1, gain1, bias1, up_weight, down_weight, bias_all, gain2, bias2, *ffn_pieces)

    pooled = pooled.astype(LOW)
    line_pooled = jnp.stack([pooled] + [swap(pooled, k, "tensor") for k in range(1, t_count)])
    returned = line_pooled.reshape(sentences, width)[source]
    both = jnp.concatenate([returned, cot_paired])
    everyone = jnp.stack(gather_plane(both)).reshape(-1, width)
    apart = (partner // sentences) ^ dp_me
    base = ((apart & 1) * chips + (apart >> 1)) * (2 * sentences) + partner % sentences
    partner_pooled = everyone[base].astype(F32)
    partner_cot = everyone[base + sentences].astype(F32)
    paired = (returned.astype(F32) * partner_pooled).astype(LOW)
    pool_grad = cot_pooled.astype(F32) + partner_pooled * (cot_paired.astype(F32) + partner_cot)
    pool_grad = pool_grad.astype(LOW).astype(F32)[chosen]

    send_spec = pl.BlockSpec((chips, 1, slab, units), lambda k, table: (0, k, 0, 0))
    send_shape = shape((chips, t_count, slab, units), LOW)
    half_spec = pl.BlockSpec((chips // 2, 1, slab, units), lambda k, table: (0, k, 0, 0))
    half_shape = shape((chips // 2, t_count, slab, units), LOW)
    down_mine, down_early, down_late, up_mine, up_early, up_late, *small_parts = call(
        ffn_backward,
        (send_shape, half_shape, half_shape) * 2
        + (
            shape((rows, width), LOW),
            turn_shape,
            shape((4, width), F32),
            shape((t_count, 1, units), F32),
        ),
        [whole(mine, width), ANY, root_spec, line, ANY, root_spec, line, line, ANY, ANY]
        + [act_spec, act_spec]
        + [ANY] * dp_count,
        (send_spec, half_spec, half_spec) * 2
        + (full, whole(dp_count, slab, rows), whole(4, width), bias_spec),
        [
            pltpu.VMEM((width, 2 * units), LOW),
            pltpu.VMEM((rows, width), F32),
            pltpu.VMEM((rows, width), F32),
            pltpu.VMEM((pad, width), F32),
            pltpu.VMEM((rows, width), LOW),
            pltpu.VMEM((dp_count, slab, rows), LOW),
            pltpu.VMEM((dp_count, slab, rows), LOW),
            pltpu.VMEM((rows, units), LOW),
        ]
        + weight_scratch,
        8 * rows * width * units * t_count,
        60 * rows * width,
    )(
        table, pool_grad, z2, root2, gain2, z1, root1, gain1, bias1, up_weight, down_weight,
        active, slope, *ffn_pieces
    )

    attn_low, attn_t, sums, bias_sum = small_parts

    def small_step(norms, bias_part, mask):
        half = bias_part.shape[0] // 2
        split = bias_part.reshape(half, 2, units)
        got = swap(jnp.concatenate([split[:, 1], norms]), mask, "tensor")
        return norms, got, split[:, 0]

    def small_sum(norms, got, bias_part):
        half = bias_part.shape[0]
        return norms + got[half:], bias_part + got[:half]

    chip_bits = bits_of(chips)
    high = chip_bits[-1]
    down_early, up_early = swap(down_early, 1), swap(up_early, 1)
    small = jnp.concatenate([bias_sum.reshape(t_count, units), sums])
    small = small + swap(small, 1)
    down_sent, up_sent, small, attn_low = tie(
        add(pick(down_mine, 1, 1), down_early).astype(LOW),
        add(pick(up_mine, 1, high), up_early).astype(LOW),
        small,
        attn_low,
    )
    down_got, up_got = swap(down_sent, 2), swap(up_sent, 2 * high)
    down_late, up_late, small, attn_t = tie(down_late, up_late, small, attn_t)
    norms, small_got, bias_part = small_step(small[t_count:], small[:t_count], 1)
    down_late, up_late = swap(down_late, 1), swap(up_late, 1)

    share = length // t_count
    proj_grad, *input_blocks = pl.pallas_call(
        attention_backward,
        out_shape=(shape((pad, 3 * width), LOW),)
        + (shape((mine, share, width), LOW),) * t_count,
        in_specs=[SMEM, VMEM, VMEM, ANY, ANY, ANY],
        out_specs=(ANY,) + (VMEM,) * t_count,
        scratch_shapes=[
            pltpu.VMEM((pad, width), LOW),
            pltpu.VMEM((pad, 3 * width), LOW),
            pltpu.VMEM(probs_shape, LOW),
            pltpu.VMEM((width, 3 * width), LOW),
            pltpu.VMEM((pad, 3 * width), LOW),
            pltpu.SemaphoreType.DMA((3,)),
            pltpu.SemaphoreType.DMA((1,)),
        ],
        compiler_params=params(),
        cost_estimate=cost(12 * rows * width * width, 30 * rows * width),
        name="attention_backward",
    )(table, attn_low, wo, proj, probs, qkv)

    down_got, up_got, down_late, up_late, small_got, proj_grad, *input_blocks = tie(
        down_got, up_got, down_late, up_late, small_got, proj_grad, *input_blocks
    )
    norms, bias_part = small_sum(norms, small_got, bias_part)
    down_terms = [pick(down_mine, 0, 1), down_late, down_got]
    up_terms = [pick(up_mine, 0, high), up_late, up_got]
    for low, top in zip(chip_bits[1:-1], chip_bits[1:-1][::-1]):
        down_terms = kept(down_terms, 1, swap(sent(down_terms, 1), 2 * low))
        up_terms = kept(up_terms, top, swap(sent(up_terms, top), 2 * top))
    down_sent, up_sent, norms, proj_grad, *input_blocks = tie(
        sent(down_terms, 1), sent(up_terms, 1), norms, proj_grad, *input_blocks
    )
    norms, small_got, bias_part = small_step(norms, bias_part, 2)
    down_got, up_got = swap(down_sent, 2 * high), swap(up_sent, 2)
    input_landed = [input_blocks[0]] + [None] * (t_count - 1)
    input_landed[2] = swap(input_blocks[2], 2, "tensor")
    input_landed[1] = swap(input_blocks[1], 1, "tensor")

    attn_mine, attn_other = pl.pallas_call(
        attention_weights,
        out_shape=(shape((chips, t_count, slab, block), LOW),) * 2,
        in_specs=[SMEM] + [ANY] * 4,
        out_specs=(VMEM,) * 2,
        scratch_shapes=[
            pltpu.VMEM((dp_count, slab, rows), LOW),
            pltpu.VMEM((dp_count, slab, rows), LOW),
            pltpu.VMEM((pad, width), LOW),
            pltpu.VMEM((pad, 3 * width), LOW),
            pltpu.SemaphoreType.DMA((6,)),
        ],
        compiler_params=params(),
        cost_estimate=cost(8 * rows * width * width, 30 * rows * width),
        name="attention_weights",
    )(table, packed_t, attn_t, ctx, proj_grad)

    def finish(kernel, near, outs, flat):
        near = jnp.stack(near)
        far = swap(near, 1)
        return pl.pallas_call(
            kernel,
            out_shape=tuple(shape(dims, F32) for dims in outs),
            in_specs=[SMEM, ANY, ANY],
            out_specs=(VMEM,) * 2,
            scratch_shapes=[
                pltpu.VMEM((dp_count,) + near.shape[1:], LOW),
                pltpu.VMEM((width, flat), F32),
                pltpu.SemaphoreType.DMA((dp_count,)),
            ],
            compiler_params=params(),
            cost_estimate=cost(0, 8 * width * near.shape[2]),
            name=kernel.__name__,
        )(table, near, far)

    attn_other, small_got, down_got, up_got, input_landed[1], input_landed[2] = tie(
        attn_other, small_got, down_got, up_got, input_landed[1], input_landed[2]
    )
    norms, bias_part = small_sum(norms, small_got, bias_part)
    small = jnp.concatenate([bias_part, norms])
    attn_got = swap(attn_other, 1)
    attn_sent = [add(attn_mine[m], attn_got[m]).astype(LOW) for m in range(1, chips)]
    ffn_line = jnp.concatenate(
        [add(*kept(up_terms, 1, up_got))[0], add(*kept(down_terms, 1, down_got))[0]], axis=2
    )
    ffn_line = [ffn_line.astype(LOW)]
    ffn_sent, small, *attn_sent = tie(sent(ffn_line, 1), small, *attn_sent)
    attn_got = [attn_got[0]] + [swap(item, 2 * m) for m, item in zip(range(1, chips), attn_sent)]
    ffn_got = swap(ffn_sent, 1, "tensor")
    small_got = swap(small, 2)

    ffn_line = kept(ffn_line, 1, ffn_got)
    ffn_got = swap(sent(ffn_line, 1), 2, "tensor")
    *attn_got, ffn_got, small_got = tie(*attn_got, ffn_got, small_got)
    small = small + small_got
    attn_line = [add(attn_mine[0], *attn_got).astype(LOW)]
    ffn_sum = add(*kept(ffn_line, 1, ffn_got))[0].astype(LOW)
    attn_sent, ffn_sum, small = tie(sent(attn_line, 1), ffn_sum, small)
    small_got = swap(small, 4)
    attn_got = swap(attn_sent, 1, "tensor")
    ffn_chips = gather_chips(ffn_sum)
    attn_line = kept(attn_line, 1, attn_got)
    attn_got = swap(sent(attn_line, 1), 2, "tensor")
    attn_got, small_got, input_blocks[3], *ffn_chips = tie(
        attn_got, small_got, input_blocks[3], *ffn_chips
    )
    small = small + small_got
    for mask in bits_of(dp_count)[3:]:
        small = small + swap(small, mask)
    attn_sum = add(*kept(attn_line, 1, attn_got))[0].astype(LOW)
    attn_sum, input_blocks[3], ffn_chips[0] = tie(attn_sum, input_blocks[3], ffn_chips[0])
    attn_chips = gather_chips(attn_sum)
    input_landed[3] = swap(input_blocks[3], 3, "tensor")
    up_grad, down_grad = finish(place_grads, ffn_chips, ((width, units), (units, width)), units)
    attn_chips[0], up_grad, input_landed[3] = tie(attn_chips[0], up_grad, input_landed[3])
    qkv_grad, out_grad = finish(
        place_attention_grads, attn_chips, ((3 * ctx_cols, width), (ctx_cols, width)), block
    )
    home = pl.pallas_call(
        send_home,
        out_shape=shape((share, sentences, width), LOW),
        in_specs=[VMEM] * (1 + t_count),
        out_specs=VMEM,
        compiler_params=params(),
        cost_estimate=cost(0, 4 * share * sentences * width),
        name="send_home",
    )(jnp.tile(source, STEP).reshape(-1, 1), *input_landed)
    bias_sum, norms = small[0], small[1:]
    return (
        returned,
        paired,
        home,
        qkv_grad.T,
        out_grad,
        norms[2],
        norms[3],
        up_grad,
        bias_sum,
        down_grad,
        norms[0],
        norms[1],
    )


def solution(mesh):
    placed = (
        P(None, "dp", None),
        P("dp"),
        P("dp"),
        P(None, "tensor"),
        P("tensor", None),
        P(),
        P(),
        P(None, "tensor"),
        P("tensor"),
        P("tensor", None),
        P(),
        P(),
        P("dp", None),
        P("dp", None),
    )
    return jax.shard_map(
        shards,
        mesh=mesh,
        in_specs=placed,
        out_specs=(
            P("dp", None),
            P("dp", None),
            P("tensor", "dp", None),
            P(None, "tensor"),
            P("tensor", None),
            P(),
            P(),
            P(None, "tensor"),
            P("tensor"),
            P("tensor", None),
            P(),
            P(),
        ),
        check_vma=False,
    )
```

```python
import functools

import jax
import jax.numpy as jnp
import numpy as np
from jax import lax
from jax.experimental import pallas as pl
from jax.experimental.pallas import tpu as pltpu
from jax.sharding import PartitionSpec as P

HD = 64
EPSILON = 1e-06
LOW = jnp.bfloat16
F32 = jnp.float32
INV_SQRT_2PI = 0.3989422804014327
SQRT_HALF = 0.7071067811865476
TILE = 256
CHUNK = 256
STEP = 16
MASKED = -1000000000.0
LOG2_E = 1.4426950408889634
VMEM_BYTES = 60 * 2**20
NN = (((1,), (0,)), ((), ()))
NT = (((1,), (1,)), ((), ()))
PAIR = 2 * HD
LENS, TILES, LINE, CHOSEN, PLACE, DEST = 16, 32, 33, 40, 48, 80


def mm(a, b, dims=NN):
    return lax.dot_general(a, b, dims, preferred_element_type=F32)


def rows_of(table, s):
    return pl.ds(pl.multiple_of(table[s], 16), 128)


def tile_at(i):
    return pl.ds(pl.multiple_of(i * TILE, TILE), TILE)


def normalize(values):
    center = values - jnp.mean(values, axis=-1, keepdims=True)
    spread = jnp.mean(center * center, axis=-1, keepdims=True)
    root = lax.rsqrt(spread + EPSILON)
    return center * root, root


def normalize_back(z, root, dz):
    return root * (
        dz - jnp.mean(dz, -1, keepdims=True) - z * jnp.mean(dz * z, -1, keepdims=True)
    )


def split_heads(pair):
    first = lax.broadcasted_iota(jnp.int32, pair.shape, 1) < HD
    zero = jnp.zeros_like(pair)
    return jnp.concatenate([jnp.where(first, pair, zero), jnp.where(first, zero, pair)], axis=0)


def join_heads(split):
    n = split.shape[0] // 2
    first = lax.broadcasted_iota(jnp.int32, (n, PAIR), 1) < HD
    return jnp.where(first, split[:n], split[n:])


def place_pieces(table, pieces, slabs, sems):
    copies = []
    for i, piece in enumerate(pieces):
        copies.append(pltpu.make_async_copy(piece, slabs.at[table[PLACE + i]], sems.at[i]))
    return copies


def turn(table, turned, rows, value):
    flat = value.T
    count, slab = turned.shape[0], turned.shape[1]
    for j in range(count):
        turned[table[DEST + j], :, rows] = flat[j * slab : (j + 1) * slab, :]


def pack(table, chosen, tokens, packed, packed_t, x):
    sents, length, width = x.shape
    total = tokens.shape[1]
    depth = total * STEP
    column = lax.broadcasted_iota(jnp.int32, (STEP, depth), 1)
    position = lax.broadcasted_iota(jnp.int32, (STEP, depth), 0)
    here = (column // total) == position
    pick = [here & ((column % total) == chosen[s]) for s in range(sents)]
    pick = jnp.concatenate([jnp.where(item, 1.0, 0.0).astype(LOW) for item in pick], axis=0)
    for block in range(length // STEP):
        rows = slice(block * STEP, (block + 1) * STEP)
        found = mm(pick, tokens[rows].reshape(depth, width)).astype(LOW)
        for s in range(sents):
            x[s, rows, :] = found[s * STEP : (s + 1) * STEP]
    packed[...] = jnp.zeros_like(packed)

    def place(s, _):
        packed[rows_of(table, s), :] = x[s]
        return 0

    lax.fori_loop(0, sents, place, 0)

    def flip(i, _):
        rows = tile_at(i)
        turn(table, packed_t, rows, packed[rows, :])
        return 0

    lax.fori_loop(0, table[TILES], flip, 0)


def send_home(source, *refs):
    blocks, home = refs[:-1], refs[-1]
    share, total, width = home.shape
    depth = total * STEP
    column = lax.broadcasted_iota(jnp.int32, (depth, depth), 1)
    row = lax.broadcasted_iota(jnp.int32, (depth, depth), 0)
    pick = ((column % STEP) == (row // total)) & ((column // STEP) == source[...])
    pick = jnp.where(pick, 1.0, 0.0).astype(LOW)
    for block in range(share // STEP):
        rows = slice(block * STEP, (block + 1) * STEP)
        values = [item[:, rows, :].reshape(-1, width) for item in blocks]
        found = mm(pick, jnp.concatenate(values, axis=0)).astype(LOW)
        home[rows] = found.reshape(STEP, total, width)


def start_all(copies):
    for copy in copies:
        copy.start()


def wait_all(copies):
    for copy in copies:
        copy.wait()


def place_halves(table, orders, arrays, slabs, sems):
    chips, half = slabs.shape[0] // 2, slabs.shape[2] // 2
    copies = []
    for side in range(2):
        for group, order in enumerate(orders):
            columns = slice(0, half) if group < len(orders) // 2 else slice(half, 2 * half)
            source = arrays[side * len(orders) + group]
            for i, m in enumerate(order):
                target = slabs.at[table[PLACE + side * chips + m], :, columns]
                copies.append(
                    pltpu.make_async_copy(source.at[i], target, sems.at[len(copies)])
                )
    return copies


def by_tiles(table, rows, body):
    for n in range(1, rows // TILE + 1):

        @pl.when(table[TILES] == n)
        def _():
            body(n * TILE)


def tile_copies(table, source, target, sems):
    def at(i):
        rows = slice(i * TILE, (i + 1) * TILE)
        return pltpu.make_async_copy(source.at[rows], target.at[rows], sems.at[i])

    def each(act):
        for i in range(sems.shape[0]):

            @pl.when(i < table[TILES])
            def _():
                act(at(i))

    return each


def place_weight(k, steps, weight, own_down, slabs):
    count, slab = slabs.shape[0], slabs.shape[1]
    columns = weight.shape[1]

    @pl.when(k == 0)
    def _():
        weight[:, columns // 2 :] = own_down[...].T

    for t in range(1, steps):

        @pl.when(k == t)
        def _():
            for j in range(count):
                weight[j * slab : (j + 1) * slab, :] = slabs[
                    j, :, (t - 1) * columns : t * columns
                ]


def attention_forward(table, packed, own_qkv, own_out, *refs):
    pieces, refs = refs[:-18], refs[-18:]
    proj_out, ctx_out, probs_out, qkv_out, wo_out, z1_out, root1 = refs[:7]
    proj, ctx, probs, qkv, wo, z1, slabs, sems, out_sems, wide_sems, z1_sems = refs[7:]
    sents, pairs = probs.shape[0], probs.shape[1]
    width = packed.shape[1]
    length = probs.shape[3]
    part = own_out.shape[0]
    block = 4 * part
    heads = part // HD
    arrivals = place_pieces(table, pieces, slabs, sems)
    start_all(arrivals)
    count, slab = slabs.shape[0], slabs.shape[1]
    for h in range(heads):
        for p in range(3):
            source = (h * 3 + p) * HD
            qkv[:, p * width + h * HD : p * width + (h + 1) * HD] = own_qkv[
                source : source + HD, :
            ].T
    wo[:, :part] = own_out[...].T
    ctx[...] = jnp.zeros_like(ctx)
    tiles = table[TILES]
    end = pl.ds(pl.multiple_of(tiles * TILE, TILE), length)
    proj[end, :] = jnp.zeros((length, 3 * width), LOW)
    wait_all(arrivals)
    for j in range(count):
        rows = slice(j * slab, (j + 1) * slab)
        for k in range(1, width // part):
            base = (k - 1) * block
            for p in range(3):
                qkv[rows, p * width + k * part : p * width + (k + 1) * part] = slabs[
                    j, :, base + p * part : base + (p + 1) * part
                ]
            wo[rows, k * part : (k + 1) * part] = slabs[j, :, base + 3 * part : base + block]
    wide_copies = [
        pltpu.make_async_copy(qkv, qkv_out, wide_sems.at[0]),
        pltpu.make_async_copy(wo, wo_out, wide_sems.at[1]),
    ]
    start_all(wide_copies)

    def project(n):
        source = packed[:n, :]
        for c in range(0, 3 * width, CHUNK):
            cols = slice(c, c + CHUNK)
            proj[:n, cols] = mm(source, qkv[:, cols]).astype(LOW)

    by_tiles(table, z1.shape[0], project)
    proj_copy = pltpu.make_async_copy(proj, proj_out, out_sems.at[0])
    proj_copy.start()

    def attend(s, _):
        rows = rows_of(table, s)
        valid = lax.broadcasted_iota(jnp.int32, (length, length), 0) < table[LENS + s]
        for p in range(pairs):
            at = p * PAIR
            queries = proj[rows, at : at + PAIR]
            keys = split_heads(proj[rows, width + at : width + at + PAIR])
            values = split_heads(proj[rows, 2 * width + at : 2 * width + at + PAIR])
            scores = mm(keys, queries, NT)
            for h in range(2):
                half = slice(h * length, (h + 1) * length)
                score = jnp.where(valid, scores[half], MASKED)
                top = jnp.max(score, axis=0, keepdims=True)
                score = jnp.exp2((score - top) * (HD**-0.5 * LOG2_E))
                total = jnp.sum(score, axis=0, keepdims=True)
                probs[s, p, half, :] = (score * (1.0 / total)).astype(LOW)
            ctx[rows, at : at + PAIR] = mm(probs[s, p].T, values).astype(LOW)
        return 0

    lax.fori_loop(0, sents, attend, 0)
    ctx_copies = [
        pltpu.make_async_copy(ctx, ctx_out, out_sems.at[1]),
        pltpu.make_async_copy(probs, probs_out, out_sems.at[2]),
    ]
    start_all(ctx_copies)

    for i in range(z1_sems.shape[0]):
        rows = slice(i * TILE, (i + 1) * TILE)

        @pl.when(i < tiles)
        def _():
            attended = mm(ctx[rows, :], wo[...], NT)
            z, root = normalize(packed[rows, :].astype(F32) + attended)
            z1[rows, :] = z
            root1[rows, :] = jnp.broadcast_to(root, (TILE, 128))
            pltpu.make_async_copy(z1.at[rows], z1_out.at[rows], z1_sems.at[i]).start()

    tile_copies(table, z1, z1_out, z1_sems)(lambda copy: copy.wait())
    wait_all(wide_copies + [proj_copy] + ctx_copies)


def gelu_parts(pre):
    t = pl.reciprocal(1.0 + jnp.abs(pre) * (0.3275911 * SQRT_HALF))
    poly = 0.5 * 1.061405429
    for c in (-1.453152027, 1.421413741, -0.284496736, 0.254829592):
        poly = poly * t + 0.5 * c
    e = jnp.exp2(pre * pre * (-0.5 * LOG2_E))
    tail = poly * t * e
    cdf = jnp.where(pre >= 0.0, 1.0 - tail, tail)
    return pre * cdf, cdf + pre * (e * INV_SQRT_2PI)


def ffn_forward(orders, parts, table, z1_in, gain1, bias1, own_up, own_down_in, bias, gain2, bias2, *refs):
    pieces, refs = refs[:-16], refs[-16:]
    active, slope, z2_out, root2, pooled = refs[:5]
    weight, first, total, z1, z2, own_down, slabs, sems, own_sems, z1_sems, z2_sems = refs[5:]
    k = pl.program_id(0)
    steps = pl.num_programs(0)
    tiles = table[TILES]
    units = active.shape[2]
    arrivals = place_halves(table, orders, pieces, slabs, sems)
    own = [
        pltpu.make_async_copy(own_up, weight.at[:, :units], own_sems.at[0]),
        pltpu.make_async_copy(own_down_in, own_down, own_sems.at[1]),
    ]
    z1_copies = tile_copies(table, z1_in, z1, z1_sems)

    @pl.when(k == 0)
    def _():
        z1_copies(lambda copy: copy.start())
        start_all(own)
        z1_copies(lambda copy: copy.wait())

        def start(i, _):
            rows = tile_at(i)
            value = z1[rows, :] * gain1[...] + bias1[...]
            first[rows, :] = value.astype(LOW)
            total[rows, :] = value
            return 0

        lax.fori_loop(0, tiles, start, 0)
        wait_all(own)
        start_all(arrivals)

    @pl.when(k == 1)
    def _():
        wait_all(arrivals)

    place_weight(k, parts, weight, own_down, slabs)

    def work(n):
        for r in range(0, n, TILE):
            rows = slice(r, r + TILE)
            source = first[rows, :]
            for c in range(0, units, CHUNK):
                cols = slice(c, c + CHUNK)
                act, slp = gelu_parts(mm(source, weight[:, cols]) + bias[0, :, cols])
                active[0, rows, cols] = act.astype(LOW)
                slope[0, rows, cols] = slp.astype(LOW)
            total[rows, :] += mm(active[0, rows, :], weight[:, units:], NT)

    by_tiles(table, first.shape[0], work)

    @pl.when(k == steps - 1)
    def _():
        z2[pl.ds(pl.multiple_of(tiles * TILE, TILE), 128), :] = jnp.zeros((128, z2.shape[1]), F32)

        def finish(i, _):
            rows = tile_at(i)
            z, root = normalize(total[rows, :])
            z2[rows, :] = z
            root2[rows, :] = jnp.broadcast_to(root, (TILE, 128))
            return 0

        lax.fori_loop(0, tiles, finish, 0)
        z2_copies = tile_copies(table, z2, z2_out, z2_sems)
        z2_copies(lambda copy: copy.start())
        means = []
        for s in range(pooled.shape[0]):
            n = table[LENS + s]
            valid = lax.broadcasted_iota(jnp.int32, (128, z2.shape[1]), 0) < n
            rows = jnp.where(valid, z2[rows_of(table, s), :], 0.0)
            means.append(jnp.sum(rows, axis=0, keepdims=True) / n.astype(F32))
        pooled[...] = (jnp.concatenate(means, axis=0) * gain2[...] + bias2[...]).astype(LOW)
        z2_copies(lambda copy: copy.wait())


def weight_grad(table, turned, right, store):
    count, slab, rows = turned.shape

    def body(n):
        if slab % 16 == 0:
            left = turned[:, :, :n].reshape(count * slab, n)
        else:
            left = jnp.concatenate([turned[j, :, :n] for j in range(count)], axis=0)
        store(lambda columns: mm(left, right(n, columns)))

    by_tiles(table, rows, body)


def half_order(chips, bit):
    order = {}
    for m in range(chips):
        order[m] = sum(1 for other in range(m) if (other & bit) == (m & bit))
    return order


def split_send(mine, other, value, k, columns):
    chips, slab = mine.shape[0], mine.shape[2]
    for m in range(chips):
        mine[m, k, :, columns] = value[m * slab : (m + 1) * slab].astype(LOW)
        target, at = other(m)
        target[at, k, :, columns] = value[(chips + m) * slab : (chips + m + 1) * slab].astype(LOW)


def send_chunks(mine, early, late, bit, product):
    order = half_order(mine.shape[0], bit)

    def other(m):
        return (early if m & bit else late), order[m]

    for c in range(0, mine.shape[3], CHUNK):
        cols = slice(c, c + CHUNK)
        split_send(mine, other, product(cols), 0, cols)


def ffn_backward(
    orders, parts, table, pool, z2_in, root2, gain2, z1_in, root1, gain1, bias1, own_up, own_down_in,
    active, slope, *refs
):
    pieces, refs = refs[:-24], refs[-24:]
    down_mine, down_early, down_late, up_mine, up_early, up_late = refs[:6]
    attn_low, attn_t, sums, bias_sum = refs[6:10]
    weight, z1, z2, total, branch, branch_t, first_t, hidden, own_down, slabs = refs[10:20]
    sems, own_sems, z1_sems, z2_sems = refs[20:]
    k = pl.program_id(0)
    tiles = table[TILES]
    width, units = own_up.shape
    arrivals = place_halves(table, orders, pieces, slabs, sems)
    own = [
        pltpu.make_async_copy(own_up, weight.at[:, :units], own_sems.at[0]),
        pltpu.make_async_copy(own_down_in, own_down, own_sems.at[1]),
    ]
    z1_copies = tile_copies(table, z1_in, z1, z1_sems)
    z2_copies = tile_copies(table, z2_in, z2, z2_sems)

    @pl.when(k == 0)
    def _():
        z2_copies(lambda copy: copy.start())
        z1_copies(lambda copy: copy.start())
        start_all(own)
        total[...] = jnp.zeros_like(total)
        for s in range(attn_low.shape[0] // 128):
            n = table[LENS + s]
            valid = lax.broadcasted_iota(jnp.int32, (128, width), 0) < n
            row = pool[pl.ds(table[CHOSEN + s], 1), :] / n.astype(F32)
            total[rows_of(table, s), :] = jnp.where(valid, row, 0.0)
        sums[...] = jnp.zeros_like(sums)
        z2_copies(lambda copy: copy.wait())

        def start(i, _):
            rows = tile_at(i)
            grad = total[rows, :]
            z = z2[rows, :]
            sums[0:1, :] += jnp.sum(grad * z, axis=0, keepdims=True)
            sums[1:2, :] += jnp.sum(grad, axis=0, keepdims=True)
            value = normalize_back(z, root2[rows, 0:1], grad * gain2[...])
            low = value.astype(LOW)
            total[rows, :] = value
            branch[rows, :] = low
            turn(table, branch_t, rows, low)
            return 0

        lax.fori_loop(0, tiles, start, 0)
        z1_copies(lambda copy: copy.wait())

        def flip(i, _):
            rows = tile_at(i)
            turn(table, first_t, rows, (z1[rows, :] * gain1[...] + bias1[...]).astype(LOW))
            return 0

        lax.fori_loop(0, tiles, flip, 0)
        wait_all(own)
        start_all(arrivals)

    @pl.when(k == 1)
    def _():
        wait_all(arrivals)

    place_weight(k, parts, weight, own_down, slabs)
    weight_grad(
        table,
        branch_t,
        lambda n, cols: active[0, :n, cols],
        lambda product: send_chunks(down_mine, down_early, down_late, 1, product),
    )
    bias_sum[...] = jnp.zeros_like(bias_sum)

    def work(n):
        source = branch[:n, :]
        for c in range(0, units, CHUNK):
            cols = slice(c, c + CHUNK)
            grad = mm(source, weight[:, units + c : units + c + CHUNK])
            hid = (slope[0, :n, cols].astype(F32) * grad).astype(LOW)
            hidden[:n, cols] = hid
            bias_sum[0, :, cols] += jnp.sum(hid.astype(F32), axis=0, keepdims=True)
        total[:n, :] += mm(hidden[:n, :], weight[:, :units], NT)

    by_tiles(table, hidden.shape[0], work)
    weight_grad(
        table,
        first_t,
        lambda n, cols: hidden[:n, cols],
        lambda product: send_chunks(
            up_mine, up_early, up_late, up_mine.shape[0] // 2, product
        ),
    )

    @pl.when(k == pl.num_programs(0) - 1)
    def _():
        def finish(i, _):
            rows = tile_at(i)
            grad = total[rows, :]
            z = z1[rows, :]
            sums[2:3, :] += jnp.sum(grad * z, axis=0, keepdims=True)
            sums[3:4, :] += jnp.sum(grad, axis=0, keepdims=True)
            value = normalize_back(z, root1[rows, 0:1], grad * gain1[...])
            low = value.astype(LOW)
            attn_low[rows, :] = low
            turn(table, attn_t, rows, low)
            return 0

        lax.fori_loop(0, tiles, finish, 0)


def attention_backward(table, attn_low, wo, proj_in, probs_in, qkv_in, proj_grad_out, *refs):
    outs, refs = refs[:-7], refs[-7:]
    ctx_grad, proj, probs, qkv, proj_grad, sems, out_sem = refs
    sents, pairs = probs.shape[0], probs.shape[1]
    length = probs.shape[3]
    width = attn_low.shape[1]
    tiles = table[TILES]
    arrivals = [
        pltpu.make_async_copy(proj_in, proj, sems.at[0]),
        pltpu.make_async_copy(probs_in, probs, sems.at[1]),
        pltpu.make_async_copy(qkv_in, qkv, sems.at[2]),
    ]
    start_all(arrivals)
    ctx_grad[...] = jnp.zeros_like(ctx_grad)
    proj_grad[...] = jnp.zeros_like(proj_grad)

    def start(n):
        ctx_grad[:n, :] = mm(attn_low[:n, :], wo[...]).astype(LOW)

    by_tiles(table, attn_low.shape[0], start)
    wait_all(arrivals[:2])
    scale = HD**-0.5

    def attend(s, _):
        rows = rows_of(table, s)
        live = lax.broadcasted_iota(jnp.int32, (length, PAIR), 0) < table[LENS + s]
        for p in range(pairs):
            at = p * PAIR
            queries = proj[rows, at : at + PAIR]
            keys = split_heads(proj[rows, width + at : width + at + PAIR])
            values = split_heads(proj[rows, 2 * width + at : 2 * width + at + PAIR])
            grad = ctx_grad[rows, at : at + PAIR]
            grad = jnp.where(live, grad, jnp.zeros_like(grad))
            prob_grad = mm(values, grad, NT)
            score_grad = []
            for h in range(2):
                half = slice(h * length, (h + 1) * length)
                prob = probs[s, p, half, :].astype(F32)
                part = prob_grad[half]
                inner = jnp.sum(prob * part, axis=0, keepdims=True)
                score_grad.append((prob * (part - inner)).astype(LOW))
            score_grad = jnp.concatenate(score_grad, axis=0)
            proj_grad[rows, at : at + PAIR] = (mm(score_grad.T, keys) * scale).astype(LOW)
            proj_grad[rows, width + at : width + at + PAIR] = (
                join_heads(mm(score_grad, queries)) * scale
            ).astype(LOW)
            proj_grad[rows, 2 * width + at : 2 * width + at + PAIR] = join_heads(
                mm(probs[s, p], grad)
            ).astype(LOW)
        return 0

    lax.fori_loop(0, sents, attend, 0)
    proj_copy = pltpu.make_async_copy(proj_grad, proj_grad_out, out_sem.at[0])
    proj_copy.start()
    arrivals[2].wait()

    def finish(n):
        total = mm(proj_grad[:n, :], qkv[...], NT)
        ctx_grad[:n, :] = (attn_low[:n, :].astype(F32) + total).astype(LOW)

    by_tiles(table, attn_low.shape[0], finish)
    ctx_grad[pl.ds(pl.multiple_of(tiles * TILE, TILE), length), :] = jnp.zeros(
        (length, width), LOW
    )
    share = outs[0].shape[1]
    for k, out in enumerate(outs):
        first = table[LINE + k] * share
        position = lax.broadcasted_iota(jnp.int32, (share, width), 0) + first
        for s in range(sents):
            value = ctx_grad[pl.ds(pl.multiple_of(table[s] + first, 16), share), :]
            out[s] = jnp.where(position < table[LENS + s], value, jnp.zeros_like(value))
    proj_copy.wait()


def attention_weights(table, *refs):
    sources, (mine, other), (packed_t, attn_t, ctx, proj_grad, sems) = refs[:4], refs[4:6], refs[6:]
    width = ctx.shape[1]
    count = mine.shape[1]
    part = width // count
    copies = [
        pltpu.make_async_copy(source, target, sems.at[i])
        for i, (source, target) in enumerate(zip(sources[:3], (packed_t, attn_t, ctx)))
    ]
    for p in range(3):
        cols = slice(p * width, (p + 1) * width)
        copies.append(
            pltpu.make_async_copy(sources[3].at[:, cols], proj_grad.at[:, cols], sems.at[3 + p])
        )
    order = [copies[1], copies[2], copies[0]] + copies[3:]
    start_all(order)

    def store(p, product):
        value = product(slice(p * width, (p + 1) * width) if p < 3 else slice(None))
        for k in range(count):
            split_send(
                mine,
                lambda m: (other, m),
                value[:, k * part : (k + 1) * part],
                k,
                slice(p * part, (p + 1) * part),
            )

    wait_all(order[:2])
    weight_grad(
        table, attn_t, lambda n, cols: ctx[:n, cols], lambda product: store(3, product)
    )
    order[2].wait()
    for p in range(3):
        order[3 + p].wait()
        weight_grad(
            table,
            packed_t,
            lambda n, cols: proj_grad[:n, cols],
            lambda product: store(p, product),
        )


def stacked_pieces(stacks):
    return [stack.at[i] for stack in stacks for i in range(stack.shape[0])]


def place_grads(table, near, far, straight, turned, slabs, flat, sems):
    count, slab = slabs.shape[0], slabs.shape[1]
    arrivals = place_pieces(table, stacked_pieces((near, far)), slabs, sems)
    start_all(arrivals)
    wait_all(arrivals)
    width = straight.shape[1]
    for j in range(count):
        rows = slice(j * slab, (j + 1) * slab)
        straight[rows, :] = slabs[j, :, :width].astype(F32)
        flat[rows, :] = slabs[j, :, width:].astype(F32)
    turned[...] = flat[...].T


def place_attention_grads(table, near, far, qkv, wo, slabs, flat, sems):
    count, slab = slabs.shape[0], slabs.shape[1]
    arrivals = place_pieces(table, stacked_pieces((near, far)), slabs, sems)
    start_all(arrivals)
    wait_all(arrivals)
    for j in range(count):
        flat[j * slab : (j + 1) * slab, :] = slabs[j].astype(F32)
    part = wo.shape[0]
    heads = part // HD
    for p in range(3):
        piece = flat[:, p * part : (p + 1) * part].T
        for h in range(heads):
            target = (h * 3 + p) * HD
            qkv[target : target + HD, :] = piece[h * HD : (h + 1) * HD, :]
    wo[...] = flat[:, 3 * part :].T


COST = 1000000
SMEM = pl.BlockSpec(memory_space=pltpu.SMEM)
VMEM = pl.BlockSpec(memory_space=pltpu.VMEM)
ANY = pl.BlockSpec(memory_space=pl.ANY)


def shape(dims, dtype):
    return jax.ShapeDtypeStruct(dims, dtype)


def params():
    return pltpu.CompilerParams(vmem_limit_bytes=VMEM_BYTES)


def cost(flops, nbytes):
    return pl.CostEstimate(flops=flops // COST, bytes_accessed=nbytes // COST, transcendentals=0)


def add(*terms):
    return sum(term.astype(F32) for term in terms)


def swap(value, mask, axis="dp"):
    return lax.ppermute(value, axis, [(i, i ^ mask) for i in range(lax.axis_size(axis))])


def bits_of(count):
    return [1 << i for i in range(count.bit_length() - 1)]


def take(values, index, axis=0):
    return lax.dynamic_index_in_dim(values, index, axis, False, allow_negative_indices=False)


def cut(values, start, size, axis):
    return lax.dynamic_slice_in_dim(values, start, size, axis, allow_negative_indices=False)


def tie(*values):
    return lax.optimization_barrier(values)


def gather_line(piece):
    n = lax.axis_size("tensor")
    return jnp.concatenate([swap(piece, k, "tensor") for k in range(1, n)], axis=1)


def gather_chips(value):
    return [value] + [swap(value, 2 * m) for m in range(1, lax.axis_size("dp") // 2)]


def gather_cores(near):
    return near + [swap(item, 1) for item in near]


def gather_plane(value):
    return gather_cores(gather_chips(value))


def pick(term, side, bit):
    dims = term.shape
    view = term.reshape((dims[0] // (2 * bit), 2, bit) + dims[1:])[:, side]
    return view.reshape((dims[0] // 2,) + dims[1:])


def sent(terms, bit):
    return add(*[pick(term, 1, bit) for term in terms]).astype(LOW)


def kept(terms, bit, landed):
    return [pick(term, 0, bit) for term in terms] + [landed]


def reduce_line(terms):
    for bit in bits_of(lax.axis_size("tensor")):
        terms = kept(terms, 1, swap(sent(terms, 1), bit, "tensor"))
    return add(*terms)[0].astype(LOW)


def reduce_chips(terms, bits):
    for bit in bits:
        terms = kept(terms, 1, swap(sent(terms, 1), 2 * bit))
    return terms


def shards(
    tokens,
    lengths,
    partner,
    w_qkv,
    w_out,
    ln1_gain,
    ln1_bias,
    up_weight,
    up_projection_bias,
    down_weight,
    ln2_gain,
    ln2_bias,
    cot_pooled,
    cot_paired,
):
    dp_count = lax.axis_size("dp")
    t_count = lax.axis_size("tensor")
    dp_me = lax.axis_index("dp")
    t_me = lax.axis_index("tensor")
    length, sentences, width = tokens.shape
    mine = sentences // t_count
    rows = mine * length
    pad = rows + length
    slab = width // dp_count
    chips = dp_count // 2
    heads = w_qkv.shape[1] // (3 * HD)
    units = up_weight.shape[1]
    ctx_cols = w_out.shape[0]
    block = 4 * ctx_cols

    def by_part(weight):
        return weight.reshape(-1, heads, 3, HD).transpose(0, 2, 1, 3).reshape(weight.shape)

    def rows_piece(weight):
        return cut(weight, dp_me * slab, slab, 0)

    def columns_piece(weight):
        return cut(weight, dp_me * slab, slab, 1).T

    attn_piece = jnp.concatenate([by_part(rows_piece(w_qkv)), columns_piece(w_out)], axis=1)
    attn_piece, up_early, down_early = tie(attn_piece, up_weight, down_weight)
    line_bits = bits_of(t_count)[::-1]

    def widen_line(parts, bit):
        return parts + [swap(jnp.concatenate(parts, axis=1), bit, "tensor")]

    def line_order():
        order = [0]
        for bit in line_bits:
            order += [item ^ bit for item in order]
        return order

    def by_distance(parts, columns):
        wide = jnp.concatenate(parts, axis=1)
        order = line_order()
        return [wide[:, order.index(d) * columns : (order.index(d) + 1) * columns] for d in range(t_count)]

    attn_parts = widen_line([attn_piece], line_bits[0])
    ffn_piece = jnp.concatenate([rows_piece(up_early), columns_piece(down_early)], axis=1)
    attn_parts[1], ffn_piece, up_projection_bias = tie(attn_parts[1], ffn_piece, up_projection_bias)
    for bit in line_bits[1:]:
        attn_parts = widen_line(attn_parts, bit)
    ffn_parts = widen_line([ffn_piece], line_bits[0])
    bias_parts = widen_line([up_projection_bias.reshape(1, units)], line_bits[0])
    attn_line = jnp.concatenate(by_distance(attn_parts, block)[1:], axis=1)

    order = np.arange(sentences)
    ahead = (lengths[None, :] > lengths[:, None]) | (
        (lengths[None, :] == lengths[:, None]) & (order[None, :] < order[:, None])
    )
    rank = jnp.sum(ahead.astype(jnp.int32), axis=1)
    row = rank // t_count
    column = rank % t_count
    column = jnp.where(row % 2 == 0, column, t_count - 1 - column)
    mine_here = (column == t_me)[None, :] & (row[None, :] == order[:mine, None])
    chosen = jnp.sum(jnp.where(mine_here, order[None, :], 0), axis=1)
    counts = jnp.sum(jnp.where(mine_here, lengths[None, :], 0), axis=1)
    source = (column ^ t_me) * mine + row
    taken = (counts + 15) & ~15
    ends = jnp.sum(jnp.where(np.tri(mine, dtype=bool), taken[None, :], 0), axis=1)
    devices = np.arange(dp_count)
    distance = 2 * np.arange(chips)
    near = devices[:, None] ^ distance[None, :]
    spots = np.concatenate([near, near ^ 1], axis=1)
    lines = np.arange(t_count)[:, None] ^ np.arange(t_count)[None, :]
    apart = devices[:, None] ^ devices[None, :]
    fixed = np.zeros((dp_count, DEST - PLACE + dp_count), np.int32)
    fixed[:, :dp_count] = spots
    fixed[:, DEST - PLACE :] = apart % 2 * chips + apart // 2
    line_fixed = np.zeros((t_count, CHOSEN - LINE), np.int32)
    line_fixed[:, :t_count] = lines
    table = jnp.concatenate(
        [
            ends - taken,
            np.zeros(LENS - mine, np.int32),
            counts,
            np.zeros(TILES - LENS - mine, np.int32),
            (ends[-1:] + (TILE - 1)) >> (TILE.bit_length() - 1),
            take(jnp.asarray(line_fixed), t_me),
            chosen,
            np.zeros(PLACE - CHOSEN - mine, np.int32),
            take(jnp.asarray(fixed), dp_me),
        ]
    ).astype(jnp.int32)
    attn_line, chosen = tie(attn_line, chosen)
    turn_shape = shape((dp_count, slab, rows), LOW)
    packed, packed_t = pl.pallas_call(
        pack,
        out_shape=(shape((pad, width), LOW), turn_shape),
        in_specs=[SMEM, SMEM, VMEM],
        out_specs=(VMEM,) * 2,
        scratch_shapes=[pltpu.VMEM((mine, length, width), LOW)],
        compiler_params=params(),
        cost_estimate=cost(0, 8 * rows * width),
        name="pack",
    )(table, chosen, tokens)

    attn_chips = gather_chips(attn_line)
    for bit in line_bits[1:]:
        ffn_parts = widen_line(ffn_parts, bit)
        bias_parts = widen_line(bias_parts, bit)
    bias_all = jnp.stack(by_distance(bias_parts, units))
    *attn_chips, packed = tie(*attn_chips, packed)
    attn_pieces = gather_cores(attn_chips)
    ffn_line = jnp.concatenate(by_distance(ffn_parts, 2 * units)[1:], axis=1)
    middle = ffn_line.shape[1] // 2
    plane_bits = bits_of(chips)
    spread, orders = [], []
    for half, path in ((ffn_line[:, :middle], plane_bits), (ffn_line[:, middle:], plane_bits[::-1])):
        group, order = half[None], [0]
        for bit in path[:-1]:
            group = jnp.concatenate([group, swap(group, 2 * bit)])
            order = order + [item ^ bit for item in order]
        spread.append(group)
        orders += [order, [item ^ path[-1] for item in order]]
    attn_pieces[0], bias_all, *spread = tie(attn_pieces[0], bias_all, *spread)
    later = [swap(spread[0], 2 * plane_bits[-1]), swap(spread[1], 2 * plane_bits[0])]
    pairs = width // PAIR
    probs_shape = (mine, pairs, 2 * length, length)
    proj, ctx, probs, qkv, wo, z1, root1 = pl.pallas_call(
        attention_forward,
        out_shape=(
            shape((pad, 3 * width), LOW),
            shape((pad, width), LOW),
            shape(probs_shape, LOW),
            shape((width, 3 * width), LOW),
            shape((width, width), LOW),
            shape((rows, width), F32),
            shape((rows, 128), F32),
        ),
        in_specs=[SMEM, VMEM, VMEM, VMEM] + [ANY] * dp_count,
        out_specs=(ANY,) * 6 + (VMEM,),
        scratch_shapes=[
            pltpu.VMEM((pad, 3 * width), LOW),
            pltpu.VMEM((pad, width), LOW),
            pltpu.VMEM(probs_shape, LOW),
            pltpu.VMEM((width, 3 * width), LOW),
            pltpu.VMEM((width, width), LOW),
            pltpu.VMEM((rows, width), F32),
            pltpu.VMEM((dp_count, slab, (t_count - 1) * block), LOW),
            pltpu.SemaphoreType.DMA((dp_count,)),
            pltpu.SemaphoreType.DMA((3,)),
            pltpu.SemaphoreType.DMA((2,)),
            pltpu.SemaphoreType.DMA((rows // TILE,)),
        ],
        compiler_params=params(),
        cost_estimate=cost(8 * rows * width * width, 30 * rows * width),
        name="attention_forward",
    )(table, packed, w_qkv.T, w_out, *attn_pieces)
    *later, z1 = tie(*later, z1)
    ffn_pieces = [spread[0], later[0], spread[1], later[1]]
    ffn_pieces += [swap(item, 1) for item in ffn_pieces]

    gain1, bias1 = ln1_gain.reshape(1, width), ln1_bias.reshape(1, width)
    gain2, bias2 = ln2_gain.reshape(1, width), ln2_bias.reshape(1, width)

    def whole(*dims):
        return pl.BlockSpec(dims, lambda k, table: (0,) * len(dims))

    def call(kernel, outs, ins, out_specs, scratch, flops, nbytes):
        return pl.pallas_call(
            functools.partial(kernel, orders, t_count),
            out_shape=outs,
            grid_spec=pltpu.PrefetchScalarGridSpec(
                num_scalar_prefetch=1,
                grid=(t_count,),
                in_specs=ins,
                out_specs=out_specs,
                scratch_shapes=scratch,
            ),
            compiler_params=params(),
            cost_estimate=cost(flops, nbytes),
            name=kernel.__name__,
        )

    act_spec = pl.BlockSpec((1, rows, units), lambda k, table: (k, 0, 0))
    bias_spec = pl.BlockSpec((1, 1, units), lambda k, table: (k, 0, 0))
    line = whole(1, width)
    full = whole(rows, width)
    root_spec = whole(rows, 128)
    act_shape = shape((t_count, rows, units), LOW)
    weight_scratch = [
        pltpu.VMEM((units, width), LOW),
        pltpu.VMEM((dp_count, slab, (t_count - 1) * 2 * units), LOW),
        pltpu.SemaphoreType.DMA((2 * dp_count,)),
        pltpu.SemaphoreType.DMA((2,)),
        pltpu.SemaphoreType.DMA((rows // TILE,)),
        pltpu.SemaphoreType.DMA((rows // TILE,)),
    ]
    active, slope, z2, root2, pooled = call(
        ffn_forward,
        (
            act_shape,
            act_shape,
            shape((rows, width), F32),
            shape((rows, 128), F32),
            shape((mine, width), LOW),
        ),
        [ANY, line, line, ANY, ANY, bias_spec, line, line] + [ANY] * len(ffn_pieces),
        (act_spec, act_spec, ANY, root_spec, whole(mine, width)),
        [
            pltpu.VMEM((width, 2 * units), LOW),
            pltpu.VMEM((rows, width), LOW),
            pltpu.VMEM((rows, width), F32),
            pltpu.VMEM((rows, width), F32),
            pltpu.VMEM((pad, width), F32),
        ]
        + weight_scratch,
        4 * rows * width * units * t_count,
        40 * rows * width,
    )(table, z1, gain1, bias1, up_weight, down_weight, bias_all, gain2, bias2, *ffn_pieces)

    line_pooled = jnp.stack([pooled] + [swap(pooled, k, "tensor") for k in range(1, t_count)])
    returned = line_pooled.reshape(sentences, width)[source]
    both = jnp.concatenate([returned, cot_paired])
    everyone = jnp.stack(gather_plane(both)).reshape(-1, width)
    apart = (partner // sentences) ^ dp_me
    base = ((apart & 1) * chips + (apart >> 1)) * (2 * sentences) + partner % sentences
    partner_pooled = everyone[base].astype(F32)
    partner_cot = everyone[base + sentences].astype(F32)
    paired = (returned.astype(F32) * partner_pooled).astype(LOW)
    pool_grad = cot_pooled.astype(F32) + partner_pooled * (cot_paired.astype(F32) + partner_cot)
    pool_grad = pool_grad.astype(LOW).astype(F32)

    send_spec = pl.BlockSpec((chips, 1, slab, units), lambda k, table: (0, k, 0, 0))
    send_shape = shape((chips, t_count, slab, units), LOW)
    half_spec = pl.BlockSpec((chips // 2, 1, slab, units), lambda k, table: (0, k, 0, 0))
    half_shape = shape((chips // 2, t_count, slab, units), LOW)
    down_mine, down_early, down_late, up_mine, up_early, up_late, *small_parts = call(
        ffn_backward,
        (send_shape, half_shape, half_shape) * 2
        + (
            shape((rows, width), LOW),
            turn_shape,
            shape((4, width), F32),
            shape((t_count, 1, units), F32),
        ),
        [whole(sentences, width), ANY, root_spec, line, ANY, root_spec, line, line, ANY, ANY]
        + [act_spec, act_spec]
        + [ANY] * len(ffn_pieces),
        (send_spec, half_spec, half_spec) * 2
        + (full, whole(dp_count, slab, rows), whole(4, width), bias_spec),
        [
            pltpu.VMEM((width, 2 * units), LOW),
            pltpu.VMEM((rows, width), F32),
            pltpu.VMEM((rows, width), F32),
            pltpu.VMEM((pad, width), F32),
            pltpu.VMEM((rows, width), LOW),
            pltpu.VMEM((dp_count, slab, rows), LOW),
            pltpu.VMEM((dp_count, slab, rows), LOW),
            pltpu.VMEM((rows, units), LOW),
        ]
        + weight_scratch,
        8 * rows * width * units * t_count,
        60 * rows * width,
    )(
        table, pool_grad, z2, root2, gain2, z1, root1, gain1, bias1, up_weight, down_weight,
        active, slope, *ffn_pieces
    )

    attn_low, attn_t, sums, bias_sum = small_parts

    def small_step(norms, bias_part, mask):
        half = bias_part.shape[0] // 2
        split = bias_part.reshape(half, 2, units)
        got = swap(jnp.concatenate([split[:, 1], norms]), mask, "tensor")
        return norms, got, split[:, 0]

    def small_sum(norms, got, bias_part):
        half = bias_part.shape[0]
        return norms + got[half:], bias_part + got[:half]

    chip_bits = bits_of(chips)
    high = chip_bits[-1]
    down_early, up_early = swap(down_early, 1), swap(up_early, 1)
    small = jnp.concatenate([bias_sum.reshape(t_count, units), sums])
    small = small + swap(small, 1)
    down_sent, up_sent, small, attn_low = tie(
        add(pick(down_mine, 1, 1), down_early).astype(LOW),
        add(pick(up_mine, 1, high), up_early).astype(LOW),
        small,
        attn_low,
    )
    down_got, up_got = swap(down_sent, 2), swap(up_sent, 2 * high)
    down_late, up_late, small, attn_t = tie(down_late, up_late, small, attn_t)
    norms, small_got, bias_part = small_step(small[t_count:], small[:t_count], 1)
    down_late, up_late = swap(down_late, 1), swap(up_late, 1)

    share = length // t_count
    proj_grad, *input_blocks = pl.pallas_call(
        attention_backward,
        out_shape=(shape((pad, 3 * width), LOW),)
        + (shape((mine, share, width), LOW),) * t_count,
        in_specs=[SMEM, VMEM, VMEM, ANY, ANY, ANY],
        out_specs=(ANY,) + (VMEM,) * t_count,
        scratch_shapes=[
            pltpu.VMEM((pad, width), LOW),
            pltpu.VMEM((pad, 3 * width), LOW),
            pltpu.VMEM(probs_shape, LOW),
            pltpu.VMEM((width, 3 * width), LOW),
            pltpu.VMEM((pad, 3 * width), LOW),
            pltpu.SemaphoreType.DMA((3,)),
            pltpu.SemaphoreType.DMA((1,)),
        ],
        compiler_params=params(),
        cost_estimate=cost(12 * rows * width * width, 30 * rows * width),
        name="attention_backward",
    )(table, attn_low, wo, proj, probs, qkv)

    down_got, up_got, down_late, up_late, small_got, proj_grad, *input_blocks = tie(
        down_got, up_got, down_late, up_late, small_got, proj_grad, *input_blocks
    )
    norms, bias_part = small_sum(norms, small_got, bias_part)
    down_terms = [pick(down_mine, 0, 1), down_late, down_got]
    up_terms = [pick(up_mine, 0, high), up_late, up_got]
    for low, top in zip(chip_bits[1:-1], chip_bits[1:-1][::-1]):
        down_terms = kept(down_terms, 1, swap(sent(down_terms, 1), 2 * low))
        up_terms = kept(up_terms, top, swap(sent(up_terms, top), 2 * top))
    down_sent, up_sent, norms, proj_grad, *input_blocks = tie(
        sent(down_terms, 1), sent(up_terms, 1), norms, proj_grad, *input_blocks
    )
    norms, small_got, bias_part = small_step(norms, bias_part, 2)
    down_got, up_got = swap(down_sent, 2 * high), swap(up_sent, 2)
    input_landed = [input_blocks[0]] + [None] * (t_count - 1)
    input_landed[2] = swap(input_blocks[2], 2, "tensor")
    input_landed[1] = swap(input_blocks[1], 1, "tensor")

    attn_mine, attn_other = pl.pallas_call(
        attention_weights,
        out_shape=(shape((chips, t_count, slab, block), LOW),) * 2,
        in_specs=[SMEM] + [ANY] * 4,
        out_specs=(VMEM,) * 2,
        scratch_shapes=[
            pltpu.VMEM((dp_count, slab, rows), LOW),
            pltpu.VMEM((dp_count, slab, rows), LOW),
            pltpu.VMEM((pad, width), LOW),
            pltpu.VMEM((pad, 3 * width), LOW),
            pltpu.SemaphoreType.DMA((6,)),
        ],
        compiler_params=params(),
        cost_estimate=cost(8 * rows * width * width, 30 * rows * width),
        name="attention_weights",
    )(table, packed_t, attn_t, ctx, proj_grad)

    def finish(kernel, near, outs, flat):
        near = jnp.stack(near)
        far = swap(near, 1)
        return pl.pallas_call(
            kernel,
            out_shape=tuple(shape(dims, F32) for dims in outs),
            in_specs=[SMEM, ANY, ANY],
            out_specs=(VMEM,) * 2,
            scratch_shapes=[
                pltpu.VMEM((dp_count,) + near.shape[1:], LOW),
                pltpu.VMEM((width, flat), F32),
                pltpu.SemaphoreType.DMA((dp_count,)),
            ],
            compiler_params=params(),
            cost_estimate=cost(0, 8 * width * near.shape[2]),
            name=kernel.__name__,
        )(table, near, far)

    attn_other, small_got, down_got, up_got, input_landed[1], input_landed[2] = tie(
        attn_other, small_got, down_got, up_got, input_landed[1], input_landed[2]
    )
    norms, bias_part = small_sum(norms, small_got, bias_part)
    small = jnp.concatenate([bias_part, norms])
    attn_got = swap(attn_other, 1)
    attn_sent = [add(attn_mine[m], attn_got[m]).astype(LOW) for m in range(1, chips)]
    ffn_line = jnp.concatenate(
        [add(*kept(up_terms, 1, up_got))[0], add(*kept(down_terms, 1, down_got))[0]], axis=2
    )
    ffn_line = [ffn_line.astype(LOW)]
    ffn_sent, small, *attn_sent = tie(sent(ffn_line, 1), small, *attn_sent)
    attn_got = [attn_got[0]] + [swap(item, 2 * m) for m, item in zip(range(1, chips), attn_sent)]
    ffn_got = swap(ffn_sent, 1, "tensor")
    small_got = swap(small, 2)

    ffn_line = kept(ffn_line, 1, ffn_got)
    ffn_got = swap(sent(ffn_line, 1), 2, "tensor")
    *attn_got, ffn_got, small_got = tie(*attn_got, ffn_got, small_got)
    small = small + small_got
    attn_line = [add(attn_mine[0], *attn_got).astype(LOW)]
    ffn_sum = add(*kept(ffn_line, 1, ffn_got))[0].astype(LOW)
    attn_sent, ffn_sum, small = tie(sent(attn_line, 1), ffn_sum, small)
    small_got = swap(small, 4)
    attn_got = swap(attn_sent, 1, "tensor")
    ffn_chips = gather_chips(ffn_sum)
    attn_line = kept(attn_line, 1, attn_got)
    attn_got = swap(sent(attn_line, 1), 2, "tensor")
    attn_got, small_got, input_blocks[3], *ffn_chips = tie(
        attn_got, small_got, input_blocks[3], *ffn_chips
    )
    small = small + small_got
    for mask in bits_of(dp_count)[3:]:
        small = small + swap(small, mask)
    attn_sum = add(*kept(attn_line, 1, attn_got))[0].astype(LOW)
    attn_sum, input_blocks[3], ffn_chips[0] = tie(attn_sum, input_blocks[3], ffn_chips[0])
    attn_chips = gather_chips(attn_sum)
    input_landed[3] = swap(input_blocks[3], 3, "tensor")
    up_grad, down_grad = finish(place_grads, ffn_chips, ((width, units), (units, width)), units)
    attn_chips[0], up_grad, input_landed[3] = tie(attn_chips[0], up_grad, input_landed[3])
    qkv_grad, out_grad = finish(
        place_attention_grads, attn_chips, ((3 * ctx_cols, width), (ctx_cols, width)), block
    )
    home = pl.pallas_call(
        send_home,
        out_shape=shape((share, sentences, width), LOW),
        in_specs=[VMEM] * (1 + t_count),
        out_specs=VMEM,
        compiler_params=params(),
        cost_estimate=cost(0, 4 * share * sentences * width),
        name="send_home",
    )(jnp.tile(source, STEP).reshape(-1, 1), *input_landed)
    bias_sum, norms = small[0], small[1:]
    return (
        returned,
        paired,
        home,
        qkv_grad.T,
        out_grad,
        norms[2],
        norms[3],
        up_grad,
        bias_sum,
        down_grad,
        norms[0],
        norms[1],
    )


def solution(mesh):
    placed = (
        P(None, "dp", None),
        P("dp"),
        P("dp"),
        P(None, "tensor"),
        P("tensor", None),
        P(),
        P(),
        P(None, "tensor"),
        P("tensor"),
        P("tensor", None),
        P(),
        P(),
        P("dp", None),
        P("dp", None),
    )
    return jax.shard_map(
        shards,
        mesh=mesh,
        in_specs=placed,
        out_specs=(
            P("dp", None),
            P("dp", None),
            P("tensor", "dp", None),
            P(None, "tensor"),
            P("tensor", None),
            P(),
            P(),
            P(None, "tensor"),
            P("tensor"),
            P("tensor", None),
            P(),
            P(),
        ),
        check_vma=False,
    )
```

```python
import functools

import jax
import jax.numpy as jnp
import numpy as np
from jax import lax
from jax.experimental import pallas as pl
from jax.experimental.pallas import tpu as pltpu
from jax.sharding import PartitionSpec as P

HD = 64
EPSILON = 1e-06
LOW = jnp.bfloat16
F32 = jnp.float32
INV_SQRT_2PI = 0.3989422804014327
SQRT_HALF = 0.7071067811865476
TILE = 256
CHUNK = 256
STEP = 16
MASKED = -1000000000.0
LOG2_E = 1.4426950408889634
VMEM_BYTES = 60 * 2**20
NN = (((1,), (0,)), ((), ()))
NT = (((1,), (1,)), ((), ()))
PAIR = 2 * HD
LENS, TILES, LINE, CHOSEN, PLACE, DEST = 16, 32, 33, 40, 48, 80


def mm(a, b, dims=NN):
    return lax.dot_general(a, b, dims, preferred_element_type=F32)


def rows_of(table, s):
    return pl.ds(pl.multiple_of(table[s], 16), 128)


def tile_at(i):
    return pl.ds(pl.multiple_of(i * TILE, TILE), TILE)


def normalize(values):
    center = values - jnp.mean(values, axis=-1, keepdims=True)
    spread = jnp.mean(center * center, axis=-1, keepdims=True)
    root = lax.rsqrt(spread + EPSILON)
    return center * root, root


def normalize_back(z, root, dz):
    return root * (
        dz - jnp.mean(dz, -1, keepdims=True) - z * jnp.mean(dz * z, -1, keepdims=True)
    )


def split_heads(pair):
    first = lax.broadcasted_iota(jnp.int32, pair.shape, 1) < HD
    zero = jnp.zeros_like(pair)
    return jnp.concatenate([jnp.where(first, pair, zero), jnp.where(first, zero, pair)], axis=0)


def join_heads(split):
    n = split.shape[0] // 2
    first = lax.broadcasted_iota(jnp.int32, (n, PAIR), 1) < HD
    return jnp.where(first, split[:n], split[n:])


def place_pieces(table, pieces, slabs, sems):
    copies = []
    for i, piece in enumerate(pieces):
        copies.append(pltpu.make_async_copy(piece, slabs.at[table[PLACE + i]], sems.at[i]))
    return copies


def turn(table, turned, rows, value):
    flat = value.T
    count, slab = turned.shape[0], turned.shape[1]
    for j in range(count):
        turned[table[DEST + j], :, rows] = flat[j * slab : (j + 1) * slab, :]


def pack(table, chosen, tokens, packed, packed_t, x):
    sents, length, width = x.shape
    total = tokens.shape[1]
    depth = total * STEP
    column = lax.broadcasted_iota(jnp.int32, (STEP, depth), 1)
    position = lax.broadcasted_iota(jnp.int32, (STEP, depth), 0)
    here = (column // total) == position
    pick = [here & ((column % total) == chosen[s]) for s in range(sents)]
    pick = jnp.concatenate([jnp.where(item, 1.0, 0.0).astype(LOW) for item in pick], axis=0)
    for block in range(length // STEP):
        rows = slice(block * STEP, (block + 1) * STEP)
        found = mm(pick, tokens[rows].reshape(depth, width)).astype(LOW)
        for s in range(sents):
            x[s, rows, :] = found[s * STEP : (s + 1) * STEP]
    packed[...] = jnp.zeros_like(packed)

    def place(s, _):
        packed[rows_of(table, s), :] = x[s]
        return 0

    lax.fori_loop(0, sents, place, 0)

    def flip(i, _):
        rows = tile_at(i)
        turn(table, packed_t, rows, packed[rows, :])
        return 0

    lax.fori_loop(0, table[TILES], flip, 0)


def send_home(source, *refs):
    blocks, home = refs[:-1], refs[-1]
    share, total, width = home.shape
    depth = total * STEP
    column = lax.broadcasted_iota(jnp.int32, (depth, depth), 1)
    row = lax.broadcasted_iota(jnp.int32, (depth, depth), 0)
    pick = ((column % STEP) == (row // total)) & ((column // STEP) == source[...])
    pick = jnp.where(pick, 1.0, 0.0).astype(LOW)
    for block in range(share // STEP):
        rows = slice(block * STEP, (block + 1) * STEP)
        values = [item[:, rows, :].reshape(-1, width) for item in blocks]
        found = mm(pick, jnp.concatenate(values, axis=0)).astype(LOW)
        home[rows] = found.reshape(STEP, total, width)


def start_all(copies):
    for copy in copies:
        copy.start()


def wait_all(copies):
    for copy in copies:
        copy.wait()


def place_halves(table, orders, arrays, slabs, sems):
    chips, half = slabs.shape[0] // 2, slabs.shape[2] // 2
    copies = []
    for side in range(2):
        for group, order in enumerate(orders):
            columns = slice(0, half) if group < len(orders) // 2 else slice(half, 2 * half)
            source = arrays[side * len(orders) + group]
            for i, m in enumerate(order):
                target = slabs.at[table[PLACE + side * chips + m], :, columns]
                copies.append(
                    pltpu.make_async_copy(source.at[i], target, sems.at[len(copies)])
                )
    return copies


def by_tiles(table, rows, body):
    for n in range(1, rows // TILE + 1):

        @pl.when(table[TILES] == n)
        def _():
            body(n * TILE)


def tile_copies(table, source, target, sems):
    def at(i):
        rows = slice(i * TILE, (i + 1) * TILE)
        return pltpu.make_async_copy(source.at[rows], target.at[rows], sems.at[i])

    def each(act):
        for i in range(sems.shape[0]):

            @pl.when(i < table[TILES])
            def _():
                act(at(i))

    return each


def place_weight(k, steps, weight, own_down, slabs):
    count, slab = slabs.shape[0], slabs.shape[1]
    columns = weight.shape[1]

    @pl.when(k == 0)
    def _():
        weight[:, columns // 2 :] = own_down[...].T

    for t in range(1, steps):

        @pl.when(k == t)
        def _():
            for j in range(count):
                weight[j * slab : (j + 1) * slab, :] = slabs[
                    j, :, (t - 1) * columns : t * columns
                ]


def attention_forward(table, packed, own_qkv, own_out, *refs):
    pieces, refs = refs[:-18], refs[-18:]
    proj_out, ctx_out, probs_out, qkv_out, wo_out, z1_out, root1 = refs[:7]
    proj, ctx, probs, qkv, wo, z1, slabs, sems, out_sems, wide_sems, z1_sems = refs[7:]
    sents, pairs = probs.shape[0], probs.shape[1]
    width = packed.shape[1]
    length = probs.shape[3]
    part = own_out.shape[0]
    block = 4 * part
    heads = part // HD
    arrivals = place_pieces(table, pieces, slabs, sems)
    start_all(arrivals)
    count, slab = slabs.shape[0], slabs.shape[1]
    for h in range(heads):
        for p in range(3):
            source = (h * 3 + p) * HD
            qkv[:, p * width + h * HD : p * width + (h + 1) * HD] = own_qkv[
                source : source + HD, :
            ].T
    wo[:, :part] = own_out[...].T
    ctx[...] = jnp.zeros_like(ctx)
    tiles = table[TILES]
    end = pl.ds(pl.multiple_of(tiles * TILE, TILE), length)
    proj[end, :] = jnp.zeros((length, 3 * width), LOW)
    wait_all(arrivals)
    for j in range(count):
        rows = slice(j * slab, (j + 1) * slab)
        for k in range(1, width // part):
            base = (k - 1) * block
            for p in range(3):
                qkv[rows, p * width + k * part : p * width + (k + 1) * part] = slabs[
                    j, :, base + p * part : base + (p + 1) * part
                ]
            wo[rows, k * part : (k + 1) * part] = slabs[j, :, base + 3 * part : base + block]
    wide_copies = [
        pltpu.make_async_copy(qkv, qkv_out, wide_sems.at[0]),
        pltpu.make_async_copy(wo, wo_out, wide_sems.at[1]),
    ]
    start_all(wide_copies)

    def project(n):
        source = packed[:n, :]
        for c in range(0, 3 * width, CHUNK):
            cols = slice(c, c + CHUNK)
            proj[:n, cols] = mm(source, qkv[:, cols]).astype(LOW)

    by_tiles(table, z1.shape[0], project)
    proj_copy = pltpu.make_async_copy(proj, proj_out, out_sems.at[0])
    proj_copy.start()

    def attend(s, _):
        rows = rows_of(table, s)
        valid = lax.broadcasted_iota(jnp.int32, (length, length), 0) < table[LENS + s]
        for p in range(pairs):
            at = p * PAIR
            queries = proj[rows, at : at + PAIR]
            keys = split_heads(proj[rows, width + at : width + at + PAIR])
            values = split_heads(proj[rows, 2 * width + at : 2 * width + at + PAIR])
            scores = mm(keys, queries, NT)
            for h in range(2):
                half = slice(h * length, (h + 1) * length)
                score = jnp.where(valid, scores[half], MASKED)
                top = jnp.max(score, axis=0, keepdims=True)
                score = jnp.exp2((score - top) * (HD**-0.5 * LOG2_E))
                total = jnp.sum(score, axis=0, keepdims=True)
                probs[s, p, half, :] = (score * (1.0 / total)).astype(LOW)
            ctx[rows, at : at + PAIR] = mm(probs[s, p].T, values).astype(LOW)
        return 0

    lax.fori_loop(0, sents, attend, 0)
    ctx_copies = [
        pltpu.make_async_copy(ctx, ctx_out, out_sems.at[1]),
        pltpu.make_async_copy(probs, probs_out, out_sems.at[2]),
    ]
    start_all(ctx_copies)

    for i in range(z1_sems.shape[0]):
        rows = slice(i * TILE, (i + 1) * TILE)

        @pl.when(i < tiles)
        def _():
            attended = mm(ctx[rows, :], wo[...], NT)
            z, root = normalize(packed[rows, :].astype(F32) + attended)
            z1[rows, :] = z
            root1[rows, :] = jnp.broadcast_to(root, (TILE, 128))
            pltpu.make_async_copy(z1.at[rows], z1_out.at[rows], z1_sems.at[i]).start()

    tile_copies(table, z1, z1_out, z1_sems)(lambda copy: copy.wait())
    wait_all(wide_copies + [proj_copy] + ctx_copies)


def gelu_parts(pre):
    t = pl.reciprocal(1.0 + jnp.abs(pre) * (0.3275911 * SQRT_HALF))
    poly = 0.5 * 1.061405429
    for c in (-1.453152027, 1.421413741, -0.284496736, 0.254829592):
        poly = poly * t + 0.5 * c
    e = jnp.exp2(pre * pre * (-0.5 * LOG2_E))
    tail = poly * t * e
    cdf = jnp.where(pre >= 0.0, 1.0 - tail, tail)
    return pre * cdf, cdf + pre * (e * INV_SQRT_2PI)


def ffn_forward(orders, parts, table, z1_in, gain1, bias1, own_up, own_down_in, bias, gain2, bias2, *refs):
    pieces, refs = refs[:-16], refs[-16:]
    active, slope, z2_out, root2, pooled = refs[:5]
    weight, first, total, z1, z2, own_down, slabs, sems, own_sems, z1_sems, z2_sems = refs[5:]
    k = pl.program_id(0)
    steps = pl.num_programs(0)
    tiles = table[TILES]
    units = active.shape[2]
    arrivals = place_halves(table, orders, pieces, slabs, sems)
    own = [
        pltpu.make_async_copy(own_up, weight.at[:, :units], own_sems.at[0]),
        pltpu.make_async_copy(own_down_in, own_down, own_sems.at[1]),
    ]
    z1_copies = tile_copies(table, z1_in, z1, z1_sems)

    @pl.when(k == 0)
    def _():
        z1_copies(lambda copy: copy.start())
        start_all(own)
        z1_copies(lambda copy: copy.wait())

        def start(i, _):
            rows = tile_at(i)
            value = z1[rows, :] * gain1[...] + bias1[...]
            first[rows, :] = value.astype(LOW)
            total[rows, :] = value
            return 0

        lax.fori_loop(0, tiles, start, 0)
        wait_all(own)
        start_all(arrivals)

    @pl.when(k == 1)
    def _():
        wait_all(arrivals)

    place_weight(k, parts, weight, own_down, slabs)

    def work(n):
        for r in range(0, n, TILE):
            rows = slice(r, r + TILE)
            source = first[rows, :]
            for c in range(0, units, CHUNK):
                cols = slice(c, c + CHUNK)
                act, slp = gelu_parts(mm(source, weight[:, cols]) + bias[0, :, cols])
                active[0, rows, cols] = act.astype(LOW)
                slope[0, rows, cols] = slp.astype(LOW)
            total[rows, :] += mm(active[0, rows, :], weight[:, units:], NT)

    by_tiles(table, first.shape[0], work)

    @pl.when(k == steps - 1)
    def _():
        z2[pl.ds(pl.multiple_of(tiles * TILE, TILE), 128), :] = jnp.zeros((128, z2.shape[1]), F32)

        def finish(i, _):
            rows = tile_at(i)
            z, root = normalize(total[rows, :])
            z2[rows, :] = z
            root2[rows, :] = jnp.broadcast_to(root, (TILE, 128))
            return 0

        lax.fori_loop(0, tiles, finish, 0)
        z2_copies = tile_copies(table, z2, z2_out, z2_sems)
        z2_copies(lambda copy: copy.start())
        means = []
        for s in range(pooled.shape[0]):
            n = table[LENS + s]
            valid = lax.broadcasted_iota(jnp.int32, (128, z2.shape[1]), 0) < n
            rows = jnp.where(valid, z2[rows_of(table, s), :], 0.0)
            means.append(jnp.sum(rows, axis=0, keepdims=True) / n.astype(F32))
        pooled[...] = (jnp.concatenate(means, axis=0) * gain2[...] + bias2[...]).astype(LOW)
        z2_copies(lambda copy: copy.wait())


def weight_grad(table, turned, right, store):
    count, slab, rows = turned.shape

    def body(n):
        if slab % 16 == 0:
            left = turned[:, :, :n].reshape(count * slab, n)
        else:
            left = jnp.concatenate([turned[j, :, :n] for j in range(count)], axis=0)
        store(lambda columns: mm(left, right(n, columns)))

    by_tiles(table, rows, body)


def half_order(chips, bit):
    order = {}
    for m in range(chips):
        order[m] = sum(1 for other in range(m) if (other & bit) == (m & bit))
    return order


def split_send(mine, other, value, k, columns):
    chips, slab = mine.shape[0], mine.shape[2]
    for m in range(chips):
        mine[m, k, :, columns] = value[m * slab : (m + 1) * slab].astype(LOW)
        target, at = other(m)
        target[at, k, :, columns] = value[(chips + m) * slab : (chips + m + 1) * slab].astype(LOW)


def send_chunks(mine, early, late, bit, product):
    order = half_order(mine.shape[0], bit)

    def other(m):
        return (early if m & bit else late), order[m]

    for c in range(0, mine.shape[3], CHUNK):
        cols = slice(c, c + CHUNK)
        split_send(mine, other, product(cols), 0, cols)


def ffn_backward(
    orders, parts, table, pool, z2_in, root2, gain2, z1_in, root1, gain1, bias1, own_up, own_down_in,
    active, slope, *refs
):
    pieces, refs = refs[:-24], refs[-24:]
    down_mine, down_early, down_late, up_mine, up_early, up_late = refs[:6]
    attn_low, attn_t, sums, bias_sum = refs[6:10]
    weight, z1, z2, total, branch, branch_t, first_t, hidden, own_down, slabs = refs[10:20]
    sems, own_sems, z1_sems, z2_sems = refs[20:]
    k = pl.program_id(0)
    tiles = table[TILES]
    width, units = own_up.shape
    arrivals = place_halves(table, orders, pieces, slabs, sems)
    own = [
        pltpu.make_async_copy(own_up, weight.at[:, :units], own_sems.at[0]),
        pltpu.make_async_copy(own_down_in, own_down, own_sems.at[1]),
    ]
    z1_copies = tile_copies(table, z1_in, z1, z1_sems)
    z2_copies = tile_copies(table, z2_in, z2, z2_sems)

    @pl.when(k == 0)
    def _():
        z2_copies(lambda copy: copy.start())
        z1_copies(lambda copy: copy.start())
        start_all(own)
        total[...] = jnp.zeros_like(total)
        for s in range(attn_low.shape[0] // 128):
            n = table[LENS + s]
            valid = lax.broadcasted_iota(jnp.int32, (128, width), 0) < n
            row = pool[pl.ds(table[CHOSEN + s], 1), :] / n.astype(F32)
            total[rows_of(table, s), :] = jnp.where(valid, row, 0.0)
        sums[...] = jnp.zeros_like(sums)
        z2_copies(lambda copy: copy.wait())

        def start(i, _):
            rows = tile_at(i)
            grad = total[rows, :]
            z = z2[rows, :]
            sums[0:1, :] += jnp.sum(grad * z, axis=0, keepdims=True)
            sums[1:2, :] += jnp.sum(grad, axis=0, keepdims=True)
            value = normalize_back(z, root2[rows, 0:1], grad * gain2[...])
            low = value.astype(LOW)
            total[rows, :] = value
            branch[rows, :] = low
            turn(table, branch_t, rows, low)
            return 0

        lax.fori_loop(0, tiles, start, 0)
        z1_copies(lambda copy: copy.wait())

        def flip(i, _):
            rows = tile_at(i)
            turn(table, first_t, rows, (z1[rows, :] * gain1[...] + bias1[...]).astype(LOW))
            return 0

        lax.fori_loop(0, tiles, flip, 0)
        wait_all(own)
        start_all(arrivals)

    @pl.when(k == 1)
    def _():
        wait_all(arrivals)

    place_weight(k, parts, weight, own_down, slabs)
    weight_grad(
        table,
        branch_t,
        lambda n, cols: active[0, :n, cols],
        lambda product: send_chunks(down_mine, down_early, down_late, 1, product),
    )
    bias_sum[...] = jnp.zeros_like(bias_sum)

    def work(n):
        source = branch[:n, :]
        for c in range(0, units, CHUNK):
            cols = slice(c, c + CHUNK)
            grad = mm(source, weight[:, units + c : units + c + CHUNK])
            hid = (slope[0, :n, cols].astype(F32) * grad).astype(LOW)
            hidden[:n, cols] = hid
            bias_sum[0, :, cols] += jnp.sum(hid.astype(F32), axis=0, keepdims=True)
        total[:n, :] += mm(hidden[:n, :], weight[:, :units], NT)

    by_tiles(table, hidden.shape[0], work)
    weight_grad(
        table,
        first_t,
        lambda n, cols: hidden[:n, cols],
        lambda product: send_chunks(
            up_mine, up_early, up_late, up_mine.shape[0] // 2, product
        ),
    )

    @pl.when(k == pl.num_programs(0) - 1)
    def _():
        def finish(i, _):
            rows = tile_at(i)
            grad = total[rows, :]
            z = z1[rows, :]
            sums[2:3, :] += jnp.sum(grad * z, axis=0, keepdims=True)
            sums[3:4, :] += jnp.sum(grad, axis=0, keepdims=True)
            value = normalize_back(z, root1[rows, 0:1], grad * gain1[...])
            low = value.astype(LOW)
            attn_low[rows, :] = low
            turn(table, attn_t, rows, low)
            return 0

        lax.fori_loop(0, tiles, finish, 0)


def attention_backward(table, attn_low, wo, proj_in, probs_in, qkv_in, proj_grad_out, *refs):
    outs, refs = refs[:-7], refs[-7:]
    ctx_grad, proj, probs, qkv, proj_grad, sems, out_sem = refs
    sents, pairs = probs.shape[0], probs.shape[1]
    length = probs.shape[3]
    width = attn_low.shape[1]
    tiles = table[TILES]
    arrivals = [
        pltpu.make_async_copy(proj_in, proj, sems.at[0]),
        pltpu.make_async_copy(probs_in, probs, sems.at[1]),
        pltpu.make_async_copy(qkv_in, qkv, sems.at[2]),
    ]
    start_all(arrivals)
    ctx_grad[...] = jnp.zeros_like(ctx_grad)
    proj_grad[...] = jnp.zeros_like(proj_grad)

    def start(n):
        ctx_grad[:n, :] = mm(attn_low[:n, :], wo[...]).astype(LOW)

    by_tiles(table, attn_low.shape[0], start)
    wait_all(arrivals[:2])
    scale = HD**-0.5

    def attend(s, _):
        rows = rows_of(table, s)
        live = lax.broadcasted_iota(jnp.int32, (length, PAIR), 0) < table[LENS + s]
        for p in range(pairs):
            at = p * PAIR
            queries = proj[rows, at : at + PAIR]
            keys = split_heads(proj[rows, width + at : width + at + PAIR])
            values = split_heads(proj[rows, 2 * width + at : 2 * width + at + PAIR])
            grad = ctx_grad[rows, at : at + PAIR]
            grad = jnp.where(live, grad, jnp.zeros_like(grad))
            prob_grad = mm(values, grad, NT)
            score_grad = []
            for h in range(2):
                half = slice(h * length, (h + 1) * length)
                prob = probs[s, p, half, :].astype(F32)
                part = prob_grad[half]
                inner = jnp.sum(prob * part, axis=0, keepdims=True)
                score_grad.append((prob * (part - inner)).astype(LOW))
            score_grad = jnp.concatenate(score_grad, axis=0)
            proj_grad[rows, at : at + PAIR] = (mm(score_grad.T, keys) * scale).astype(LOW)
            proj_grad[rows, width + at : width + at + PAIR] = (
                join_heads(mm(score_grad, queries)) * scale
            ).astype(LOW)
            proj_grad[rows, 2 * width + at : 2 * width + at + PAIR] = join_heads(
                mm(probs[s, p], grad)
            ).astype(LOW)
        return 0

    lax.fori_loop(0, sents, attend, 0)
    proj_copy = pltpu.make_async_copy(proj_grad, proj_grad_out, out_sem.at[0])
    proj_copy.start()
    arrivals[2].wait()

    def finish(n):
        total = mm(proj_grad[:n, :], qkv[...], NT)
        ctx_grad[:n, :] = (attn_low[:n, :].astype(F32) + total).astype(LOW)

    by_tiles(table, attn_low.shape[0], finish)
    ctx_grad[pl.ds(pl.multiple_of(tiles * TILE, TILE), length), :] = jnp.zeros(
        (length, width), LOW
    )
    share = outs[0].shape[1]
    for k, out in enumerate(outs):
        first = table[LINE + k] * share
        position = lax.broadcasted_iota(jnp.int32, (share, width), 0) + first
        for s in range(sents):
            value = ctx_grad[pl.ds(pl.multiple_of(table[s] + first, 16), share), :]
            out[s] = jnp.where(position < table[LENS + s], value, jnp.zeros_like(value))
    proj_copy.wait()


def attention_weights(table, *refs):
    sources, (mine, other), (packed_t, attn_t, ctx, proj_grad, sems) = refs[:4], refs[4:6], refs[6:]
    width = ctx.shape[1]
    count = mine.shape[1]
    part = width // count
    copies = [
        pltpu.make_async_copy(source, target, sems.at[i])
        for i, (source, target) in enumerate(zip(sources[:3], (packed_t, attn_t, ctx)))
    ]
    for p in range(3):
        cols = slice(p * width, (p + 1) * width)
        copies.append(
            pltpu.make_async_copy(sources[3].at[:, cols], proj_grad.at[:, cols], sems.at[3 + p])
        )
    order = [copies[1], copies[2], copies[0]] + copies[3:]
    start_all(order)

    def store(p, product):
        value = product(slice(p * width, (p + 1) * width) if p < 3 else slice(None))
        for k in range(count):
            split_send(
                mine,
                lambda m: (other, m),
                value[:, k * part : (k + 1) * part],
                k,
                slice(p * part, (p + 1) * part),
            )

    wait_all(order[:2])
    weight_grad(
        table, attn_t, lambda n, cols: ctx[:n, cols], lambda product: store(3, product)
    )
    order[2].wait()
    for p in range(3):
        order[3 + p].wait()
        weight_grad(
            table,
            packed_t,
            lambda n, cols: proj_grad[:n, cols],
            lambda product: store(p, product),
        )


def stacked_pieces(stacks):
    return [stack.at[i] for stack in stacks for i in range(stack.shape[0])]


def place_grads(table, near, far, straight, turned, slabs, flat, sems):
    count, slab = slabs.shape[0], slabs.shape[1]
    arrivals = place_pieces(table, stacked_pieces((near, far)), slabs, sems)
    start_all(arrivals)
    wait_all(arrivals)
    width = straight.shape[1]
    for j in range(count):
        rows = slice(j * slab, (j + 1) * slab)
        straight[rows, :] = slabs[j, :, :width].astype(F32)
        flat[rows, :] = slabs[j, :, width:].astype(F32)
    turned[...] = flat[...].T


def place_attention_grads(table, near, far, qkv, wo, slabs, flat, sems):
    count, slab = slabs.shape[0], slabs.shape[1]
    arrivals = place_pieces(table, stacked_pieces((near, far)), slabs, sems)
    start_all(arrivals)
    wait_all(arrivals)
    for j in range(count):
        flat[j * slab : (j + 1) * slab, :] = slabs[j].astype(F32)
    part = wo.shape[0]
    heads = part // HD
    for p in range(3):
        piece = flat[:, p * part : (p + 1) * part].T
        for h in range(heads):
            target = (h * 3 + p) * HD
            qkv[target : target + HD, :] = piece[h * HD : (h + 1) * HD, :]
    wo[...] = flat[:, 3 * part :].T


COST = 1000000
SMEM = pl.BlockSpec(memory_space=pltpu.SMEM)
VMEM = pl.BlockSpec(memory_space=pltpu.VMEM)
ANY = pl.BlockSpec(memory_space=pl.ANY)


def shape(dims, dtype):
    return jax.ShapeDtypeStruct(dims, dtype)


def params():
    return pltpu.CompilerParams(vmem_limit_bytes=VMEM_BYTES)


def cost(flops, nbytes):
    return pl.CostEstimate(flops=flops // COST, bytes_accessed=nbytes // COST, transcendentals=0)


def add(*terms):
    return sum(term.astype(F32) for term in terms)


def swap(value, mask, axis="dp"):
    return lax.ppermute(value, axis, [(i, i ^ mask) for i in range(lax.axis_size(axis))])


def bits_of(count):
    return [1 << i for i in range(count.bit_length() - 1)]


def take(values, index, axis=0):
    return lax.dynamic_index_in_dim(values, index, axis, False, allow_negative_indices=False)


def cut(values, start, size, axis):
    return lax.dynamic_slice_in_dim(values, start, size, axis, allow_negative_indices=False)


def tie(*values):
    return lax.optimization_barrier(values)


def gather_line(piece):
    n = lax.axis_size("tensor")
    return jnp.concatenate([swap(piece, k, "tensor") for k in range(1, n)], axis=1)


def gather_chips(value):
    return [value] + [swap(value, 2 * m) for m in range(1, lax.axis_size("dp") // 2)]


def gather_cores(near):
    return near + [swap(item, 1) for item in near]


def gather_plane(value):
    return gather_cores(gather_chips(value))


def pick(term, side, bit):
    dims = term.shape
    view = term.reshape((dims[0] // (2 * bit), 2, bit) + dims[1:])[:, side]
    return view.reshape((dims[0] // 2,) + dims[1:])


def sent(terms, bit):
    return add(*[pick(term, 1, bit) for term in terms]).astype(LOW)


def kept(terms, bit, landed):
    return [pick(term, 0, bit) for term in terms] + [landed]


def reduce_line(terms):
    for bit in bits_of(lax.axis_size("tensor")):
        terms = kept(terms, 1, swap(sent(terms, 1), bit, "tensor"))
    return add(*terms)[0].astype(LOW)


def reduce_chips(terms, bits):
    for bit in bits:
        terms = kept(terms, 1, swap(sent(terms, 1), 2 * bit))
    return terms


def shards(
    tokens,
    lengths,
    partner,
    w_qkv,
    w_out,
    ln1_gain,
    ln1_bias,
    up_weight,
    up_projection_bias,
    down_weight,
    ln2_gain,
    ln2_bias,
    cot_pooled,
    cot_paired,
):
    dp_count = lax.axis_size("dp")
    t_count = lax.axis_size("tensor")
    dp_me = lax.axis_index("dp")
    t_me = lax.axis_index("tensor")
    length, sentences, width = tokens.shape
    mine = sentences // t_count
    rows = mine * length
    pad = rows + length
    slab = width // dp_count
    chips = dp_count // 2
    heads = w_qkv.shape[1] // (3 * HD)
    units = up_weight.shape[1]
    ctx_cols = w_out.shape[0]
    block = 4 * ctx_cols

    def by_part(weight):
        return weight.reshape(-1, heads, 3, HD).transpose(0, 2, 1, 3).reshape(weight.shape)

    def rows_piece(weight):
        return cut(weight, dp_me * slab, slab, 0)

    def columns_piece(weight):
        return cut(weight, dp_me * slab, slab, 1).T

    attn_piece = jnp.concatenate([by_part(rows_piece(w_qkv)), columns_piece(w_out)], axis=1)
    attn_piece, up_early, down_early = tie(attn_piece, up_weight, down_weight)
    near_bits = bits_of(t_count)
    line_bits = near_bits[::-1]

    def widen_line(parts, bit):
        return parts + [swap(jnp.concatenate(parts, axis=1), bit, "tensor")]

    def line_order(bits):
        order = [0]
        for bit in bits:
            order += [item ^ bit for item in order]
        return order

    def by_distance(parts, columns, bits):
        wide = jnp.concatenate(parts, axis=1)
        order = line_order(bits)
        return [wide[:, order.index(d) * columns : (order.index(d) + 1) * columns] for d in range(t_count)]

    attn_parts = widen_line([attn_piece], line_bits[0])
    ffn_piece = jnp.concatenate([rows_piece(up_early), columns_piece(down_early)], axis=1)
    for bit in line_bits[1:]:
        attn_parts = widen_line(attn_parts, bit)
    ffn_parts = widen_line([ffn_piece], near_bits[0])
    bias_parts = widen_line([up_projection_bias.reshape(1, units)], near_bits[0])
    attn_line = jnp.concatenate(by_distance(attn_parts, block, line_bits)[1:], axis=1)

    order = np.arange(sentences)
    ahead = (lengths[None, :] > lengths[:, None]) | (
        (lengths[None, :] == lengths[:, None]) & (order[None, :] < order[:, None])
    )
    rank = jnp.sum(ahead.astype(jnp.int32), axis=1)
    row = rank // t_count
    column = rank % t_count
    column = jnp.where(row % 2 == 0, column, t_count - 1 - column)
    mine_here = (column == t_me)[None, :] & (row[None, :] == order[:mine, None])
    chosen = jnp.sum(jnp.where(mine_here, order[None, :], 0), axis=1)
    counts = jnp.sum(jnp.where(mine_here, lengths[None, :], 0), axis=1)
    source = (column ^ t_me) * mine + row
    taken = (counts + 15) & ~15
    ends = jnp.sum(jnp.where(np.tri(mine, dtype=bool), taken[None, :], 0), axis=1)
    devices = np.arange(dp_count)
    distance = 2 * np.arange(chips)
    near = devices[:, None] ^ distance[None, :]
    spots = np.concatenate([near, near ^ 1], axis=1)
    lines = np.arange(t_count)[:, None] ^ np.arange(t_count)[None, :]
    apart = devices[:, None] ^ devices[None, :]
    fixed = np.zeros((dp_count, DEST - PLACE + dp_count), np.int32)
    fixed[:, :dp_count] = spots
    fixed[:, DEST - PLACE :] = apart % 2 * chips + apart // 2
    line_fixed = np.zeros((t_count, CHOSEN - LINE), np.int32)
    line_fixed[:, :t_count] = lines
    table = jnp.concatenate(
        [
            ends - taken,
            np.zeros(LENS - mine, np.int32),
            counts,
            np.zeros(TILES - LENS - mine, np.int32),
            (ends[-1:] + (TILE - 1)) >> (TILE.bit_length() - 1),
            take(jnp.asarray(line_fixed), t_me),
            chosen,
            np.zeros(PLACE - CHOSEN - mine, np.int32),
            take(jnp.asarray(fixed), dp_me),
        ]
    ).astype(jnp.int32)
    attn_line, chosen = tie(attn_line, chosen)
    turn_shape = shape((dp_count, slab, rows), LOW)
    packed, packed_t = pl.pallas_call(
        pack,
        out_shape=(shape((pad, width), LOW), turn_shape),
        in_specs=[SMEM, SMEM, VMEM],
        out_specs=(VMEM,) * 2,
        scratch_shapes=[pltpu.VMEM((mine, length, width), LOW)],
        compiler_params=params(),
        cost_estimate=cost(0, 8 * rows * width),
        name="pack",
    )(table, chosen, tokens)

    attn_chips = gather_chips(attn_line)
    for bit in near_bits[1:]:
        ffn_parts = widen_line(ffn_parts, bit)
        bias_parts = widen_line(bias_parts, bit)
    ffn_parts[-1], bias_parts[-1], packed = tie(ffn_parts[-1], bias_parts[-1], packed)
    bias_all = jnp.stack(by_distance(bias_parts, units, near_bits))
    *attn_chips, packed = tie(*attn_chips, packed)
    attn_pieces = gather_cores(attn_chips)
    ffn_line = jnp.concatenate(by_distance(ffn_parts, 2 * units, near_bits)[1:], axis=1)
    middle = ffn_line.shape[1] // 2
    plane_bits = bits_of(chips)
    spread, orders = [], []
    for half, path in ((ffn_line[:, :middle], plane_bits), (ffn_line[:, middle:], plane_bits[::-1])):
        group, order = half[None], [0]
        for bit in path[:-1]:
            group = jnp.concatenate([group, swap(group, 2 * bit)])
            order = order + [item ^ bit for item in order]
        spread.append(group)
        orders += [order, [item ^ path[-1] for item in order]]
    attn_pieces[0], bias_all, *spread = tie(attn_pieces[0], bias_all, *spread)
    later = [swap(spread[0], 2 * plane_bits[-1]), swap(spread[1], 2 * plane_bits[0])]
    pairs = width // PAIR
    probs_shape = (mine, pairs, 2 * length, length)
    proj, ctx, probs, qkv, wo, z1, root1 = pl.pallas_call(
        attention_forward,
        out_shape=(
            shape((pad, 3 * width), LOW),
            shape((pad, width), LOW),
            shape(probs_shape, LOW),
            shape((width, 3 * width), LOW),
            shape((width, width), LOW),
            shape((rows, width), F32),
            shape((rows, 128), F32),
        ),
        in_specs=[SMEM, VMEM, VMEM, VMEM] + [ANY] * dp_count,
        out_specs=(ANY,) * 6 + (VMEM,),
        scratch_shapes=[
            pltpu.VMEM((pad, 3 * width), LOW),
            pltpu.VMEM((pad, width), LOW),
            pltpu.VMEM(probs_shape, LOW),
            pltpu.VMEM((width, 3 * width), LOW),
            pltpu.VMEM((width, width), LOW),
            pltpu.VMEM((rows, width), F32),
            pltpu.VMEM((dp_count, slab, (t_count - 1) * block), LOW),
            pltpu.SemaphoreType.DMA((dp_count,)),
            pltpu.SemaphoreType.DMA((3,)),
            pltpu.SemaphoreType.DMA((2,)),
            pltpu.SemaphoreType.DMA((rows // TILE,)),
        ],
        compiler_params=params(),
        cost_estimate=cost(8 * rows * width * width, 30 * rows * width),
        name="attention_forward",
    )(table, packed, w_qkv.T, w_out, *attn_pieces)
    *later, z1 = tie(*later, z1)
    ffn_pieces = [spread[0], later[0], spread[1], later[1]]
    ffn_pieces += [swap(item, 1) for item in ffn_pieces]

    gain1, bias1 = ln1_gain.reshape(1, width), ln1_bias.reshape(1, width)
    gain2, bias2 = ln2_gain.reshape(1, width), ln2_bias.reshape(1, width)

    def whole(*dims):
        return pl.BlockSpec(dims, lambda k, table: (0,) * len(dims))

    def call(kernel, outs, ins, out_specs, scratch, flops, nbytes):
        return pl.pallas_call(
            functools.partial(kernel, orders, t_count),
            out_shape=outs,
            grid_spec=pltpu.PrefetchScalarGridSpec(
                num_scalar_prefetch=1,
                grid=(t_count,),
                in_specs=ins,
                out_specs=out_specs,
                scratch_shapes=scratch,
            ),
            compiler_params=params(),
            cost_estimate=cost(flops, nbytes),
            name=kernel.__name__,
        )

    act_spec = pl.BlockSpec((1, rows, units), lambda k, table: (k, 0, 0))
    bias_spec = pl.BlockSpec((1, 1, units), lambda k, table: (k, 0, 0))
    line = whole(1, width)
    full = whole(rows, width)
    root_spec = whole(rows, 128)
    act_shape = shape((t_count, rows, units), LOW)
    weight_scratch = [
        pltpu.VMEM((units, width), LOW),
        pltpu.VMEM((dp_count, slab, (t_count - 1) * 2 * units), LOW),
        pltpu.SemaphoreType.DMA((2 * dp_count,)),
        pltpu.SemaphoreType.DMA((2,)),
        pltpu.SemaphoreType.DMA((rows // TILE,)),
        pltpu.SemaphoreType.DMA((rows // TILE,)),
    ]
    active, slope, z2, root2, pooled = call(
        ffn_forward,
        (
            act_shape,
            act_shape,
            shape((rows, width), F32),
            shape((rows, 128), F32),
            shape((mine, width), LOW),
        ),
        [ANY, line, line, ANY, ANY, bias_spec, line, line] + [ANY] * len(ffn_pieces),
        (act_spec, act_spec, ANY, root_spec, whole(mine, width)),
        [
            pltpu.VMEM((width, 2 * units), LOW),
            pltpu.VMEM((rows, width), LOW),
            pltpu.VMEM((rows, width), F32),
            pltpu.VMEM((rows, width), F32),
            pltpu.VMEM((pad, width), F32),
        ]
        + weight_scratch,
        4 * rows * width * units * t_count,
        40 * rows * width,
    )(table, z1, gain1, bias1, up_weight, down_weight, bias_all, gain2, bias2, *ffn_pieces)

    line_pooled = jnp.stack([pooled] + [swap(pooled, k, "tensor") for k in range(1, t_count)])
    returned = line_pooled.reshape(sentences, width)[source]
    both = jnp.concatenate([returned, cot_paired])
    everyone = jnp.stack(gather_plane(both)).reshape(-1, width)
    apart = (partner // sentences) ^ dp_me
    base = ((apart & 1) * chips + (apart >> 1)) * (2 * sentences) + partner % sentences
    partner_pooled = everyone[base].astype(F32)
    partner_cot = everyone[base + sentences].astype(F32)
    paired = (returned.astype(F32) * partner_pooled).astype(LOW)
    pool_grad = cot_pooled.astype(F32) + partner_pooled * (cot_paired.astype(F32) + partner_cot)
    pool_grad = pool_grad.astype(LOW).astype(F32)

    send_spec = pl.BlockSpec((chips, 1, slab, units), lambda k, table: (0, k, 0, 0))
    send_shape = shape((chips, t_count, slab, units), LOW)
    half_spec = pl.BlockSpec((chips // 2, 1, slab, units), lambda k, table: (0, k, 0, 0))
    half_shape = shape((chips // 2, t_count, slab, units), LOW)
    down_mine, down_early, down_late, up_mine, up_early, up_late, *small_parts = call(
        ffn_backward,
        (send_shape, half_shape, half_shape) * 2
        + (
            shape((rows, width), LOW),
            turn_shape,
            shape((4, width), F32),
            shape((t_count, 1, units), F32),
        ),
        [whole(sentences, width), ANY, root_spec, line, ANY, root_spec, line, line, ANY, ANY]
        + [act_spec, act_spec]
        + [ANY] * len(ffn_pieces),
        (send_spec, half_spec, half_spec) * 2
        + (full, whole(dp_count, slab, rows), whole(4, width), bias_spec),
        [
            pltpu.VMEM((width, 2 * units), LOW),
            pltpu.VMEM((rows, width), F32),
            pltpu.VMEM((rows, width), F32),
            pltpu.VMEM((pad, width), F32),
            pltpu.VMEM((rows, width), LOW),
            pltpu.VMEM((dp_count, slab, rows), LOW),
            pltpu.VMEM((dp_count, slab, rows), LOW),
            pltpu.VMEM((rows, units), LOW),
        ]
        + weight_scratch,
        8 * rows * width * units * t_count,
        60 * rows * width,
    )(
        table, pool_grad, z2, root2, gain2, z1, root1, gain1, bias1, up_weight, down_weight,
        active, slope, *ffn_pieces
    )

    attn_low, attn_t, sums, bias_sum = small_parts

    def small_step(norms, bias_part, mask):
        half = bias_part.shape[0] // 2
        split = bias_part.reshape(half, 2, units)
        got = swap(jnp.concatenate([split[:, 1], norms]), mask, "tensor")
        return norms, got, split[:, 0]

    def small_sum(norms, got, bias_part):
        half = bias_part.shape[0]
        return norms + got[half:], bias_part + got[:half]

    chip_bits = bits_of(chips)
    high = chip_bits[-1]
    down_early, up_early = swap(down_early, 1), swap(up_early, 1)
    small = jnp.concatenate([bias_sum.reshape(t_count, units), sums])
    down_sent, up_sent, small, attn_low = tie(
        add(pick(down_mine, 1, 1), down_early).astype(LOW),
        add(pick(up_mine, 1, high), up_early).astype(LOW),
        small,
        attn_low,
    )
    down_got, up_got = swap(down_sent, 2), swap(up_sent, 2 * high)
    down_late, up_late, small, attn_t = tie(down_late, up_late, small, attn_t)
    norms, small_got, bias_part = small_step(small[t_count:], small[:t_count], 1)
    down_late, up_late = swap(down_late, 1), swap(up_late, 1)

    share = length // t_count
    proj_grad, *input_blocks = pl.pallas_call(
        attention_backward,
        out_shape=(shape((pad, 3 * width), LOW),)
        + (shape((mine, share, width), LOW),) * t_count,
        in_specs=[SMEM, VMEM, VMEM, ANY, ANY, ANY],
        out_specs=(ANY,) + (VMEM,) * t_count,
        scratch_shapes=[
            pltpu.VMEM((pad, width), LOW),
            pltpu.VMEM((pad, 3 * width), LOW),
            pltpu.VMEM(probs_shape, LOW),
            pltpu.VMEM((width, 3 * width), LOW),
            pltpu.VMEM((pad, 3 * width), LOW),
            pltpu.SemaphoreType.DMA((3,)),
            pltpu.SemaphoreType.DMA((1,)),
        ],
        compiler_params=params(),
        cost_estimate=cost(12 * rows * width * width, 30 * rows * width),
        name="attention_backward",
    )(table, attn_low, wo, proj, probs, qkv)

    down_got, up_got, down_late, up_late, small_got, proj_grad, *input_blocks = tie(
        down_got, up_got, down_late, up_late, small_got, proj_grad, *input_blocks
    )
    norms, bias_part = small_sum(norms, small_got, bias_part)
    down_terms = [pick(down_mine, 0, 1), down_late, down_got]
    up_terms = [pick(up_mine, 0, high), up_late, up_got]
    for low, top in zip(chip_bits[1:-1], chip_bits[1:-1][::-1]):
        down_terms = kept(down_terms, 1, swap(sent(down_terms, 1), 2 * low))
        up_terms = kept(up_terms, top, swap(sent(up_terms, top), 2 * top))
    down_sent, up_sent, norms, proj_grad, *input_blocks = tie(
        sent(down_terms, 1), sent(up_terms, 1), norms, proj_grad, *input_blocks
    )
    norms, small_got, bias_part = small_step(norms, bias_part, 2)
    down_got, up_got = swap(down_sent, 2 * high), swap(up_sent, 2)
    input_landed = [input_blocks[0]] + [None] * (t_count - 1)
    input_landed[1] = swap(input_blocks[1], 1, "tensor")

    attn_mine, attn_other = pl.pallas_call(
        attention_weights,
        out_shape=(shape((chips, t_count, slab, block), LOW),) * 2,
        in_specs=[SMEM] + [ANY] * 4,
        out_specs=(VMEM,) * 2,
        scratch_shapes=[
            pltpu.VMEM((dp_count, slab, rows), LOW),
            pltpu.VMEM((dp_count, slab, rows), LOW),
            pltpu.VMEM((pad, width), LOW),
            pltpu.VMEM((pad, 3 * width), LOW),
            pltpu.SemaphoreType.DMA((6,)),
        ],
        compiler_params=params(),
        cost_estimate=cost(8 * rows * width * width, 30 * rows * width),
        name="attention_weights",
    )(table, packed_t, attn_t, ctx, proj_grad)

    def finish(kernel, near, outs, flat):
        near = jnp.stack(near)
        far = swap(near, 1)
        return pl.pallas_call(
            kernel,
            out_shape=tuple(shape(dims, F32) for dims in outs),
            in_specs=[SMEM, ANY, ANY],
            out_specs=(VMEM,) * 2,
            scratch_shapes=[
                pltpu.VMEM((dp_count,) + near.shape[1:], LOW),
                pltpu.VMEM((width, flat), F32),
                pltpu.SemaphoreType.DMA((dp_count,)),
            ],
            compiler_params=params(),
            cost_estimate=cost(0, 8 * width * near.shape[2]),
            name=kernel.__name__,
        )(table, near, far)

    attn_other, small_got, down_got, up_got, input_landed[1] = tie(
        attn_other, small_got, down_got, up_got, input_landed[1]
    )
    norms, bias_part = small_sum(norms, small_got, bias_part)
    small = jnp.concatenate([bias_part, norms])
    attn_got = swap(attn_other, 1)
    attn_sent = [add(attn_mine[m], attn_got[m]).astype(LOW) for m in range(1, chips)]
    ffn_line = jnp.concatenate(
        [add(*kept(up_terms, 1, up_got))[0], add(*kept(down_terms, 1, down_got))[0]], axis=2
    )
    ffn_line = [ffn_line.astype(LOW)]
    ffn_sent, input_blocks[2], *attn_sent = tie(
        sent(ffn_line, 1), input_blocks[2], *attn_sent
    )
    attn_got = [attn_got[0]] + [swap(item, 2 * m) for m, item in zip(range(1, chips), attn_sent)]
    ffn_got = swap(ffn_sent, 1, "tensor")
    input_landed[2] = swap(input_blocks[2], 2, "tensor")

    ffn_line = kept(ffn_line, 1, ffn_got)
    ffn_got = swap(sent(ffn_line, 1), 2, "tensor")
    *attn_got, ffn_got, small, input_landed[2] = tie(*attn_got, ffn_got, small, input_landed[2])
    attn_line = [add(attn_mine[0], *attn_got).astype(LOW)]
    ffn_sum = add(*kept(ffn_line, 1, ffn_got))[0].astype(LOW)
    attn_sent, ffn_sum, small = tie(sent(attn_line, 1), ffn_sum, small)
    small_got = swap(small, 2)
    attn_got = swap(attn_sent, 1, "tensor")
    ffn_chips = gather_chips(ffn_sum)
    attn_line = kept(attn_line, 1, attn_got)
    attn_got = swap(sent(attn_line, 1), 2, "tensor")
    attn_got, small_got, input_blocks[3], *ffn_chips = tie(
        attn_got, small_got, input_blocks[3], *ffn_chips
    )
    small = small + small_got
    for mask in bits_of(dp_count)[3:]:
        small = small + swap(small, mask)
    attn_sum = add(*kept(attn_line, 1, attn_got))[0].astype(LOW)
    attn_sum, input_blocks[3], ffn_chips[0] = tie(attn_sum, input_blocks[3], ffn_chips[0])
    attn_chips = gather_chips(attn_sum)
    input_landed[3] = swap(input_blocks[3], 3, "tensor")
    up_grad, down_grad = finish(place_grads, ffn_chips, ((width, units), (units, width)), units)
    small_got = swap(small, 4)
    attn_chips[0], up_grad, input_landed[3], small_got = tie(
        attn_chips[0], up_grad, input_landed[3], small_got
    )
    small = small + small_got
    small_got = swap(small, 1)
    qkv_grad, out_grad = finish(
        place_attention_grads, attn_chips, ((3 * ctx_cols, width), (ctx_cols, width)), block
    )
    home = pl.pallas_call(
        send_home,
        out_shape=shape((share, sentences, width), LOW),
        in_specs=[VMEM] * (1 + t_count),
        out_specs=VMEM,
        compiler_params=params(),
        cost_estimate=cost(0, 4 * share * sentences * width),
        name="send_home",
    )(jnp.tile(source, STEP).reshape(-1, 1), *input_landed)
    small = small + small_got
    bias_sum, norms = small[0], small[1:]
    return (
        returned,
        paired,
        home,
        qkv_grad.T,
        out_grad,
        norms[2],
        norms[3],
        up_grad,
        bias_sum,
        down_grad,
        norms[0],
        norms[1],
    )


def solution(mesh):
    placed = (
        P(None, "dp", None),
        P("dp"),
        P("dp"),
        P(None, "tensor"),
        P("tensor", None),
        P(),
        P(),
        P(None, "tensor"),
        P("tensor"),
        P("tensor", None),
        P(),
        P(),
        P("dp", None),
        P("dp", None),
    )
    return jax.shard_map(
        shards,
        mesh=mesh,
        in_specs=placed,
        out_specs=(
            P("dp", None),
            P("dp", None),
            P("tensor", "dp", None),
            P(None, "tensor"),
            P("tensor", None),
            P(),
            P(),
            P(None, "tensor"),
            P("tensor"),
            P("tensor", None),
            P(),
            P(),
        ),
        check_vma=False,
    )
```

```python
import functools

import jax
import jax.numpy as jnp
import numpy as np
from jax import lax
from jax.experimental import pallas as pl
from jax.experimental.pallas import tpu as pltpu
from jax.sharding import PartitionSpec as P

HD = 64
EPSILON = 1e-06
LOW = jnp.bfloat16
F32 = jnp.float32
INV_SQRT_2PI = 0.3989422804014327
SQRT_HALF = 0.7071067811865476
TILE = 256
CHUNK = 256
STEP = 16
MASKED = -1000000000.0
LOG2_E = 1.4426950408889634
VMEM_BYTES = 60 * 2**20
NN = (((1,), (0,)), ((), ()))
NT = (((1,), (1,)), ((), ()))
PAIR = 2 * HD
LENS, TILES, LINE, CHOSEN, PLACE, DEST = 16, 32, 33, 40, 48, 80


def mm(a, b, dims=NN):
    return lax.dot_general(a, b, dims, preferred_element_type=F32)


def rows_of(table, s):
    return pl.ds(pl.multiple_of(table[s], 16), 128)


def tile_at(i):
    return pl.ds(pl.multiple_of(i * TILE, TILE), TILE)


def normalize(values):
    center = values - jnp.mean(values, axis=-1, keepdims=True)
    spread = jnp.mean(center * center, axis=-1, keepdims=True)
    root = lax.rsqrt(spread + EPSILON)
    return center * root, root


def normalize_back(z, root, dz):
    return root * (
        dz - jnp.mean(dz, -1, keepdims=True) - z * jnp.mean(dz * z, -1, keepdims=True)
    )


def split_heads(pair):
    first = lax.broadcasted_iota(jnp.int32, pair.shape, 1) < HD
    zero = jnp.zeros_like(pair)
    return jnp.concatenate([jnp.where(first, pair, zero), jnp.where(first, zero, pair)], axis=0)


def join_heads(split):
    n = split.shape[0] // 2
    first = lax.broadcasted_iota(jnp.int32, (n, PAIR), 1) < HD
    return jnp.where(first, split[:n], split[n:])


def place_pieces(table, pieces, slabs, sems):
    copies = []
    for i, piece in enumerate(pieces):
        copies.append(pltpu.make_async_copy(piece, slabs.at[table[PLACE + i]], sems.at[i]))
    return copies


def turn(table, turned, rows, value):
    flat = value.T
    count, slab = turned.shape[0], turned.shape[1]
    for j in range(count):
        turned[table[DEST + j], :, rows] = flat[j * slab : (j + 1) * slab, :]


def pack(table, chosen, tokens, packed, packed_t, x):
    sents, length, width = x.shape
    total = tokens.shape[1]
    depth = total * STEP
    column = lax.broadcasted_iota(jnp.int32, (STEP, depth), 1)
    position = lax.broadcasted_iota(jnp.int32, (STEP, depth), 0)
    here = (column // total) == position
    pick = [here & ((column % total) == chosen[s]) for s in range(sents)]
    pick = jnp.concatenate([jnp.where(item, 1.0, 0.0).astype(LOW) for item in pick], axis=0)
    for block in range(length // STEP):
        rows = slice(block * STEP, (block + 1) * STEP)
        found = mm(pick, tokens[rows].reshape(depth, width)).astype(LOW)
        for s in range(sents):
            x[s, rows, :] = found[s * STEP : (s + 1) * STEP]
    packed[...] = jnp.zeros_like(packed)

    def place(s, _):
        packed[rows_of(table, s), :] = x[s]
        return 0

    lax.fori_loop(0, sents, place, 0)

    def flip(i, _):
        rows = tile_at(i)
        turn(table, packed_t, rows, packed[rows, :])
        return 0

    lax.fori_loop(0, table[TILES], flip, 0)


def send_home(source, *refs):
    blocks, home = refs[:-1], refs[-1]
    share, total, width = home.shape
    depth = total * STEP
    column = lax.broadcasted_iota(jnp.int32, (depth, depth), 1)
    row = lax.broadcasted_iota(jnp.int32, (depth, depth), 0)
    pick = ((column % STEP) == (row // total)) & ((column // STEP) == source[...])
    pick = jnp.where(pick, 1.0, 0.0).astype(LOW)
    for block in range(share // STEP):
        rows = slice(block * STEP, (block + 1) * STEP)
        values = [item[:, rows, :].reshape(-1, width) for item in blocks]
        found = mm(pick, jnp.concatenate(values, axis=0)).astype(LOW)
        home[rows] = found.reshape(STEP, total, width)


def start_all(copies):
    for copy in copies:
        copy.start()


def wait_all(copies):
    for copy in copies:
        copy.wait()


def place_halves(table, orders, arrays, slabs, sems):
    chips, half = slabs.shape[0] // 2, slabs.shape[2] // 2
    copies = []
    for side in range(2):
        for group, order in enumerate(orders):
            columns = slice(0, half) if group < len(orders) // 2 else slice(half, 2 * half)
            source = arrays[side * len(orders) + group]
            for i, m in enumerate(order):
                target = slabs.at[table[PLACE + side * chips + m], :, columns]
                copies.append(
                    pltpu.make_async_copy(source.at[i], target, sems.at[len(copies)])
                )
    return copies


def by_tiles(table, rows, body):
    for n in range(1, rows // TILE + 1):

        @pl.when(table[TILES] == n)
        def _():
            body(n * TILE)


def tile_copies(table, source, target, sems):
    def at(i):
        rows = slice(i * TILE, (i + 1) * TILE)
        return pltpu.make_async_copy(source.at[rows], target.at[rows], sems.at[i])

    def each(act):
        for i in range(sems.shape[0]):

            @pl.when(i < table[TILES])
            def _():
                act(at(i))

    return each


def place_weight(k, steps, weight, own_down, slabs):
    count, slab = slabs.shape[0], slabs.shape[1]
    columns = weight.shape[1]

    @pl.when(k == 0)
    def _():
        weight[:, columns // 2 :] = own_down[...].T

    for t in range(1, steps):

        @pl.when(k == t)
        def _():
            for j in range(count):
                weight[j * slab : (j + 1) * slab, :] = slabs[
                    j, :, (t - 1) * columns : t * columns
                ]


def attention_forward(table, packed, own_qkv, own_out, *refs):
    pieces, refs = refs[:-18], refs[-18:]
    proj_out, ctx_out, probs_out, qkv_out, wo_out, z1_out, root1 = refs[:7]
    proj, ctx, probs, qkv, wo, z1, slabs, sems, out_sems, wide_sems, z1_sems = refs[7:]
    sents, pairs = probs.shape[0], probs.shape[1]
    width = packed.shape[1]
    length = probs.shape[3]
    part = own_out.shape[0]
    block = 4 * part
    heads = part // HD
    arrivals = place_pieces(table, pieces, slabs, sems)
    start_all(arrivals)
    count, slab = slabs.shape[0], slabs.shape[1]
    for h in range(heads):
        for p in range(3):
            source = (h * 3 + p) * HD
            qkv[:, p * width + h * HD : p * width + (h + 1) * HD] = own_qkv[
                source : source + HD, :
            ].T
    wo[:, :part] = own_out[...].T
    ctx[...] = jnp.zeros_like(ctx)
    tiles = table[TILES]
    end = pl.ds(pl.multiple_of(tiles * TILE, TILE), length)
    proj[end, :] = jnp.zeros((length, 3 * width), LOW)
    wait_all(arrivals)
    for j in range(count):
        rows = slice(j * slab, (j + 1) * slab)
        for k in range(1, width // part):
            base = (k - 1) * block
            for p in range(3):
                qkv[rows, p * width + k * part : p * width + (k + 1) * part] = slabs[
                    j, :, base + p * part : base + (p + 1) * part
                ]
            wo[rows, k * part : (k + 1) * part] = slabs[j, :, base + 3 * part : base + block]
    wide_copies = [
        pltpu.make_async_copy(qkv, qkv_out, wide_sems.at[0]),
        pltpu.make_async_copy(wo, wo_out, wide_sems.at[1]),
    ]
    start_all(wide_copies)

    def project(n):
        source = packed[:n, :]
        for c in range(0, 3 * width, CHUNK):
            cols = slice(c, c + CHUNK)
            proj[:n, cols] = mm(source, qkv[:, cols]).astype(LOW)

    by_tiles(table, z1.shape[0], project)
    proj_copy = pltpu.make_async_copy(proj, proj_out, out_sems.at[0])
    proj_copy.start()

    def attend(s, _):
        rows = rows_of(table, s)
        valid = lax.broadcasted_iota(jnp.int32, (length, length), 0) < table[LENS + s]
        for p in range(pairs):
            at = p * PAIR
            queries = proj[rows, at : at + PAIR]
            keys = split_heads(proj[rows, width + at : width + at + PAIR])
            values = split_heads(proj[rows, 2 * width + at : 2 * width + at + PAIR])
            scores = mm(keys, queries, NT)
            prob = []
            for h in range(2):
                score = jnp.where(valid, scores[h * length : (h + 1) * length], MASKED)
                top = jnp.max(score, axis=0, keepdims=True)
                score = jnp.exp2((score - top) * (HD**-0.5 * LOG2_E))
                total = jnp.sum(score, axis=0, keepdims=True)
                prob.append((score * (1.0 / total)).astype(LOW))
            prob = jnp.concatenate(prob, axis=0)
            probs[s, p] = prob
            ctx[rows, at : at + PAIR] = mm(prob.T, values).astype(LOW)
        return 0

    lax.fori_loop(0, sents, attend, 0, unroll=4)
    ctx_copies = [
        pltpu.make_async_copy(ctx, ctx_out, out_sems.at[1]),
        pltpu.make_async_copy(probs, probs_out, out_sems.at[2]),
    ]
    start_all(ctx_copies)

    for i in range(z1_sems.shape[0]):
        rows = slice(i * TILE, (i + 1) * TILE)

        @pl.when(i < tiles)
        def _():
            attended = mm(ctx[rows, :], wo[...], NT)
            z, root = normalize(packed[rows, :].astype(F32) + attended)
            z1[rows, :] = z
            root1[rows, :] = jnp.broadcast_to(root, (TILE, 128))
            pltpu.make_async_copy(z1.at[rows], z1_out.at[rows], z1_sems.at[i]).start()

    tile_copies(table, z1, z1_out, z1_sems)(lambda copy: copy.wait())
    wait_all(wide_copies + [proj_copy] + ctx_copies)


def gelu_parts(pre):
    t = pl.reciprocal(1.0 + jnp.abs(pre) * (0.3275911 * SQRT_HALF))
    poly = 0.5 * 1.061405429
    for c in (-1.453152027, 1.421413741, -0.284496736, 0.254829592):
        poly = poly * t + 0.5 * c
    e = jnp.exp2(pre * pre * (-0.5 * LOG2_E))
    tail = poly * t * e
    cdf = jnp.where(pre >= 0.0, 1.0 - tail, tail)
    return pre * cdf, cdf + pre * (e * INV_SQRT_2PI)


def ffn_forward(orders, parts, table, z1_in, gain1, bias1, own_up, own_down_in, bias, gain2, bias2, *refs):
    pieces, refs = refs[:-16], refs[-16:]
    active, slope, z2_out, root2, pooled = refs[:5]
    weight, first, total, z1, z2, own_down, slabs, sems, own_sems, z1_sems, z2_sems = refs[5:]
    k = pl.program_id(0)
    steps = pl.num_programs(0)
    tiles = table[TILES]
    units = active.shape[2]
    arrivals = place_halves(table, orders, pieces, slabs, sems)
    own = [
        pltpu.make_async_copy(own_up, weight.at[:, :units], own_sems.at[0]),
        pltpu.make_async_copy(own_down_in, own_down, own_sems.at[1]),
    ]
    z1_copies = tile_copies(table, z1_in, z1, z1_sems)

    @pl.when(k == 0)
    def _():
        z1_copies(lambda copy: copy.start())
        start_all(own)
        z1_copies(lambda copy: copy.wait())

        def start(i, _):
            rows = tile_at(i)
            value = z1[rows, :] * gain1[...] + bias1[...]
            first[rows, :] = value.astype(LOW)
            total[rows, :] = value
            return 0

        lax.fori_loop(0, tiles, start, 0)
        wait_all(own)
        start_all(arrivals)

    @pl.when(k == 1)
    def _():
        wait_all(arrivals)

    place_weight(k, parts, weight, own_down, slabs)

    def work(n):
        for r in range(0, n, TILE):
            rows = slice(r, r + TILE)
            source = first[rows, :]
            for c in range(0, units, CHUNK):
                cols = slice(c, c + CHUNK)
                act, slp = gelu_parts(mm(source, weight[:, cols]) + bias[0, :, cols])
                active[0, rows, cols] = act.astype(LOW)
                slope[0, rows, cols] = slp.astype(LOW)
            total[rows, :] += mm(active[0, rows, :], weight[:, units:], NT)

    by_tiles(table, first.shape[0], work)

    @pl.when(k == steps - 1)
    def _():
        z2[pl.ds(pl.multiple_of(tiles * TILE, TILE), 128), :] = jnp.zeros((128, z2.shape[1]), F32)

        def finish(i, _):
            rows = tile_at(i)
            z, root = normalize(total[rows, :])
            z2[rows, :] = z
            root2[rows, :] = jnp.broadcast_to(root, (TILE, 128))
            return 0

        lax.fori_loop(0, tiles, finish, 0)
        z2_copies = tile_copies(table, z2, z2_out, z2_sems)
        z2_copies(lambda copy: copy.start())
        means = []
        for s in range(pooled.shape[0]):
            n = table[LENS + s]
            valid = lax.broadcasted_iota(jnp.int32, (128, z2.shape[1]), 0) < n
            rows = jnp.where(valid, z2[rows_of(table, s), :], 0.0)
            means.append(jnp.sum(rows, axis=0, keepdims=True) / n.astype(F32))
        pooled[...] = (jnp.concatenate(means, axis=0) * gain2[...] + bias2[...]).astype(LOW)
        z2_copies(lambda copy: copy.wait())


def weight_grad(table, turned, right, store):
    count, slab, rows = turned.shape

    def body(n):
        if slab % 16 == 0:
            left = turned[:, :, :n].reshape(count * slab, n)
        else:
            left = jnp.concatenate([turned[j, :, :n] for j in range(count)], axis=0)
        store(lambda columns: mm(left, right(n, columns)))

    by_tiles(table, rows, body)


def half_order(chips, bit):
    order = {}
    for m in range(chips):
        order[m] = sum(1 for other in range(m) if (other & bit) == (m & bit))
    return order


def split_send(mine, other, value, k, columns):
    chips, slab = mine.shape[0], mine.shape[2]
    for m in range(chips):
        mine[m, k, :, columns] = value[m * slab : (m + 1) * slab].astype(LOW)
        target, at = other(m)
        target[at, k, :, columns] = value[(chips + m) * slab : (chips + m + 1) * slab].astype(LOW)


def send_chunks(mine, early, late, bit, product):
    order = half_order(mine.shape[0], bit)

    def other(m):
        return (early if m & bit else late), order[m]

    for c in range(0, mine.shape[3], CHUNK):
        cols = slice(c, c + CHUNK)
        split_send(mine, other, product(cols), 0, cols)


def ffn_backward(
    orders, parts, table, pool, z2_in, root2, gain2, z1_in, root1, gain1, bias1, own_up, own_down_in,
    active, slope, *refs
):
    pieces, refs = refs[:-24], refs[-24:]
    down_mine, down_early, down_late, up_mine, up_early, up_late = refs[:6]
    attn_low, attn_t, sums, bias_sum = refs[6:10]
    weight, z1, z2, total, branch, branch_t, first_t, hidden, own_down, slabs = refs[10:20]
    sems, own_sems, z1_sems, z2_sems = refs[20:]
    k = pl.program_id(0)
    tiles = table[TILES]
    width, units = own_up.shape
    arrivals = place_halves(table, orders, pieces, slabs, sems)
    own = [
        pltpu.make_async_copy(own_up, weight.at[:, :units], own_sems.at[0]),
        pltpu.make_async_copy(own_down_in, own_down, own_sems.at[1]),
    ]
    z1_copies = tile_copies(table, z1_in, z1, z1_sems)
    z2_copies = tile_copies(table, z2_in, z2, z2_sems)

    @pl.when(k == 0)
    def _():
        z2_copies(lambda copy: copy.start())
        z1_copies(lambda copy: copy.start())
        start_all(own)
        total[...] = jnp.zeros_like(total)
        for s in range(attn_low.shape[0] // 128):
            n = table[LENS + s]
            valid = lax.broadcasted_iota(jnp.int32, (128, width), 0) < n
            row = pool[pl.ds(table[CHOSEN + s], 1), :] / n.astype(F32)
            total[rows_of(table, s), :] = jnp.where(valid, row, 0.0)
        sums[...] = jnp.zeros_like(sums)
        z2_copies(lambda copy: copy.wait())

        def start(i, _):
            rows = tile_at(i)
            grad = total[rows, :]
            z = z2[rows, :]
            sums[0:1, :] += jnp.sum(grad * z, axis=0, keepdims=True)
            sums[1:2, :] += jnp.sum(grad, axis=0, keepdims=True)
            value = normalize_back(z, root2[rows, 0:1], grad * gain2[...])
            low = value.astype(LOW)
            total[rows, :] = value
            branch[rows, :] = low
            turn(table, branch_t, rows, low)
            return 0

        lax.fori_loop(0, tiles, start, 0)
        z1_copies(lambda copy: copy.wait())

        def flip(i, _):
            rows = tile_at(i)
            turn(table, first_t, rows, (z1[rows, :] * gain1[...] + bias1[...]).astype(LOW))
            return 0

        lax.fori_loop(0, tiles, flip, 0)
        wait_all(own)
        start_all(arrivals)

    @pl.when(k == 1)
    def _():
        wait_all(arrivals)

    place_weight(k, parts, weight, own_down, slabs)
    weight_grad(
        table,
        branch_t,
        lambda n, cols: active[0, :n, cols],
        lambda product: send_chunks(down_mine, down_early, down_late, 1, product),
    )
    bias_sum[...] = jnp.zeros_like(bias_sum)

    def work(n):
        source = branch[:n, :]
        for c in range(0, units, CHUNK):
            cols = slice(c, c + CHUNK)
            grad = mm(source, weight[:, units + c : units + c + CHUNK])
            hid = (slope[0, :n, cols].astype(F32) * grad).astype(LOW)
            hidden[:n, cols] = hid
            bias_sum[0, :, cols] += jnp.sum(hid.astype(F32), axis=0, keepdims=True)
        total[:n, :] += mm(hidden[:n, :], weight[:, :units], NT)

    by_tiles(table, hidden.shape[0], work)
    weight_grad(
        table,
        first_t,
        lambda n, cols: hidden[:n, cols],
        lambda product: send_chunks(
            up_mine, up_early, up_late, up_mine.shape[0] // 2, product
        ),
    )

    @pl.when(k == pl.num_programs(0) - 1)
    def _():
        def finish(i, _):
            rows = tile_at(i)
            grad = total[rows, :]
            z = z1[rows, :]
            sums[2:3, :] += jnp.sum(grad * z, axis=0, keepdims=True)
            sums[3:4, :] += jnp.sum(grad, axis=0, keepdims=True)
            value = normalize_back(z, root1[rows, 0:1], grad * gain1[...])
            low = value.astype(LOW)
            attn_low[rows, :] = low
            turn(table, attn_t, rows, low)
            return 0

        lax.fori_loop(0, tiles, finish, 0)


def attention_backward(table, attn_low, wo, proj_in, probs_in, qkv_in, proj_grad_out, *refs):
    outs, refs = refs[:-7], refs[-7:]
    ctx_grad, proj, probs, qkv, proj_grad, sems, out_sem = refs
    sents, pairs = probs.shape[0], probs.shape[1]
    length = probs.shape[3]
    width = attn_low.shape[1]
    tiles = table[TILES]
    arrivals = [
        pltpu.make_async_copy(proj_in, proj, sems.at[0]),
        pltpu.make_async_copy(probs_in, probs, sems.at[1]),
        pltpu.make_async_copy(qkv_in, qkv, sems.at[2]),
    ]
    start_all(arrivals)
    ctx_grad[...] = jnp.zeros_like(ctx_grad)
    proj_grad[...] = jnp.zeros_like(proj_grad)

    def start(n):
        ctx_grad[:n, :] = mm(attn_low[:n, :], wo[...]).astype(LOW)

    by_tiles(table, attn_low.shape[0], start)
    wait_all(arrivals[:2])
    scale = HD**-0.5

    def attend(s, _):
        rows = rows_of(table, s)
        live = lax.broadcasted_iota(jnp.int32, (length, PAIR), 0) < table[LENS + s]
        for p in range(pairs):
            at = p * PAIR
            queries = proj[rows, at : at + PAIR]
            keys = split_heads(proj[rows, width + at : width + at + PAIR])
            values = split_heads(proj[rows, 2 * width + at : 2 * width + at + PAIR])
            grad = ctx_grad[rows, at : at + PAIR]
            grad = jnp.where(live, grad, jnp.zeros_like(grad))
            prob_grad = mm(values, grad, NT)
            score_grad = []
            for h in range(2):
                half = slice(h * length, (h + 1) * length)
                prob = probs[s, p, half, :].astype(F32)
                part = prob_grad[half]
                inner = jnp.sum(prob * part, axis=0, keepdims=True)
                score_grad.append((prob * (part - inner)).astype(LOW))
            score_grad = jnp.concatenate(score_grad, axis=0)
            proj_grad[rows, at : at + PAIR] = (mm(score_grad.T, keys) * scale).astype(LOW)
            proj_grad[rows, width + at : width + at + PAIR] = (
                join_heads(mm(score_grad, queries)) * scale
            ).astype(LOW)
            proj_grad[rows, 2 * width + at : 2 * width + at + PAIR] = join_heads(
                mm(probs[s, p], grad)
            ).astype(LOW)
        return 0

    lax.fori_loop(0, sents, attend, 0, unroll=4)
    proj_copy = pltpu.make_async_copy(proj_grad, proj_grad_out, out_sem.at[0])
    proj_copy.start()
    arrivals[2].wait()

    def finish(n):
        total = mm(proj_grad[:n, :], qkv[...], NT)
        ctx_grad[:n, :] = (attn_low[:n, :].astype(F32) + total).astype(LOW)

    by_tiles(table, attn_low.shape[0], finish)
    ctx_grad[pl.ds(pl.multiple_of(tiles * TILE, TILE), length), :] = jnp.zeros(
        (length, width), LOW
    )
    share = outs[0].shape[1]
    for k, out in enumerate(outs):
        first = table[LINE + k] * share
        position = lax.broadcasted_iota(jnp.int32, (share, width), 0) + first
        for s in range(sents):
            value = ctx_grad[pl.ds(pl.multiple_of(table[s] + first, 16), share), :]
            out[s] = jnp.where(position < table[LENS + s], value, jnp.zeros_like(value))
    proj_copy.wait()


def attention_weights(table, *refs):
    sources, (mine, other), (packed_t, attn_t, ctx, proj_grad, sems) = refs[:4], refs[4:6], refs[6:]
    width = ctx.shape[1]
    count = mine.shape[1]
    part = width // count
    copies = [
        pltpu.make_async_copy(source, target, sems.at[i])
        for i, (source, target) in enumerate(zip(sources[:3], (packed_t, attn_t, ctx)))
    ]
    for p in range(3):
        cols = slice(p * width, (p + 1) * width)
        copies.append(
            pltpu.make_async_copy(sources[3].at[:, cols], proj_grad.at[:, cols], sems.at[3 + p])
        )
    order = [copies[1], copies[2], copies[0]] + copies[3:]
    start_all(order)

    def store(p, product):
        value = product(slice(p * width, (p + 1) * width) if p < 3 else slice(None))
        for k in range(count):
            split_send(
                mine,
                lambda m: (other, m),
                value[:, k * part : (k + 1) * part],
                k,
                slice(p * part, (p + 1) * part),
            )

    wait_all(order[:2])
    weight_grad(
        table, attn_t, lambda n, cols: ctx[:n, cols], lambda product: store(3, product)
    )
    order[2].wait()
    for p in range(3):
        order[3 + p].wait()
        weight_grad(
            table,
            packed_t,
            lambda n, cols: proj_grad[:n, cols],
            lambda product: store(p, product),
        )


def stacked_pieces(stacks):
    return [stack.at[i] for stack in stacks for i in range(stack.shape[0])]


def place_grads(table, near, far, straight, turned, slabs, flat, sems):
    count, slab = slabs.shape[0], slabs.shape[1]
    arrivals = place_pieces(table, stacked_pieces((near, far)), slabs, sems)
    start_all(arrivals)
    wait_all(arrivals)
    width = straight.shape[1]
    for j in range(count):
        rows = slice(j * slab, (j + 1) * slab)
        straight[rows, :] = slabs[j, :, :width].astype(F32)
        flat[rows, :] = slabs[j, :, width:].astype(F32)
    turned[...] = flat[...].T


def place_attention_grads(table, near, far, qkv, wo, slabs, flat, sems):
    count, slab = slabs.shape[0], slabs.shape[1]
    arrivals = place_pieces(table, stacked_pieces((near, far)), slabs, sems)
    start_all(arrivals)
    wait_all(arrivals)
    for j in range(count):
        flat[j * slab : (j + 1) * slab, :] = slabs[j].astype(F32)
    part = wo.shape[0]
    heads = part // HD
    for p in range(3):
        piece = flat[:, p * part : (p + 1) * part].T
        for h in range(heads):
            target = (h * 3 + p) * HD
            qkv[target : target + HD, :] = piece[h * HD : (h + 1) * HD, :]
    wo[...] = flat[:, 3 * part :].T


COST = 1000000
SMEM = pl.BlockSpec(memory_space=pltpu.SMEM)
VMEM = pl.BlockSpec(memory_space=pltpu.VMEM)
ANY = pl.BlockSpec(memory_space=pl.ANY)


def shape(dims, dtype):
    return jax.ShapeDtypeStruct(dims, dtype)


def params():
    return pltpu.CompilerParams(vmem_limit_bytes=VMEM_BYTES)


def cost(flops, nbytes):
    return pl.CostEstimate(flops=flops // COST, bytes_accessed=nbytes // COST, transcendentals=0)


def add(*terms):
    return sum(term.astype(F32) for term in terms)


def swap(value, mask, axis="dp"):
    return lax.ppermute(value, axis, [(i, i ^ mask) for i in range(lax.axis_size(axis))])


def bits_of(count):
    return [1 << i for i in range(count.bit_length() - 1)]


def take(values, index, axis=0):
    return lax.dynamic_index_in_dim(values, index, axis, False, allow_negative_indices=False)


def cut(values, start, size, axis):
    return lax.dynamic_slice_in_dim(values, start, size, axis, allow_negative_indices=False)


def tie(*values):
    return lax.optimization_barrier(values)


def gather_line(piece):
    n = lax.axis_size("tensor")
    return jnp.concatenate([swap(piece, k, "tensor") for k in range(1, n)], axis=1)


def gather_chips(value):
    return [value] + [swap(value, 2 * m) for m in range(1, lax.axis_size("dp") // 2)]


def gather_cores(near):
    return near + [swap(item, 1) for item in near]


def gather_plane(value):
    return gather_cores(gather_chips(value))


def pick(term, side, bit):
    dims = term.shape
    view = term.reshape((dims[0] // (2 * bit), 2, bit) + dims[1:])[:, side]
    return view.reshape((dims[0] // 2,) + dims[1:])


def sent(terms, bit):
    return add(*[pick(term, 1, bit) for term in terms]).astype(LOW)


def kept(terms, bit, landed):
    return [pick(term, 0, bit) for term in terms] + [landed]


def reduce_line(terms):
    for bit in bits_of(lax.axis_size("tensor")):
        terms = kept(terms, 1, swap(sent(terms, 1), bit, "tensor"))
    return add(*terms)[0].astype(LOW)


def reduce_chips(terms, bits):
    for bit in bits:
        terms = kept(terms, 1, swap(sent(terms, 1), 2 * bit))
    return terms


def shards(
    tokens,
    lengths,
    partner,
    w_qkv,
    w_out,
    ln1_gain,
    ln1_bias,
    up_weight,
    up_projection_bias,
    down_weight,
    ln2_gain,
    ln2_bias,
    cot_pooled,
    cot_paired,
):
    dp_count = lax.axis_size("dp")
    t_count = lax.axis_size("tensor")
    dp_me = lax.axis_index("dp")
    t_me = lax.axis_index("tensor")
    length, sentences, width = tokens.shape
    mine = sentences // t_count
    rows = mine * length
    pad = rows + length
    slab = width // dp_count
    chips = dp_count // 2
    heads = w_qkv.shape[1] // (3 * HD)
    units = up_weight.shape[1]
    ctx_cols = w_out.shape[0]
    block = 4 * ctx_cols

    def by_part(weight):
        return weight.reshape(-1, heads, 3, HD).transpose(0, 2, 1, 3).reshape(weight.shape)

    def rows_piece(weight):
        return cut(weight, dp_me * slab, slab, 0)

    def columns_piece(weight):
        return cut(weight, dp_me * slab, slab, 1).T

    attn_piece = jnp.concatenate([by_part(rows_piece(w_qkv)), columns_piece(w_out)], axis=1)
    attn_piece, up_early, down_early = tie(attn_piece, up_weight, down_weight)
    near_bits = bits_of(t_count)
    line_bits = near_bits[::-1]

    def widen_line(parts, bit):
        return parts + [swap(jnp.concatenate(parts, axis=1), bit, "tensor")]

    def line_order(bits):
        order = [0]
        for bit in bits:
            order += [item ^ bit for item in order]
        return order

    def by_distance(parts, columns, bits):
        wide = jnp.concatenate(parts, axis=1)
        order = line_order(bits)
        return [wide[:, order.index(d) * columns : (order.index(d) + 1) * columns] for d in range(t_count)]

    attn_parts = widen_line([attn_piece], line_bits[0])
    ffn_piece = jnp.concatenate([rows_piece(up_early), columns_piece(down_early)], axis=1)
    for bit in line_bits[1:]:
        attn_parts = widen_line(attn_parts, bit)
    ffn_parts = widen_line([ffn_piece], near_bits[0])
    bias_parts = widen_line([up_projection_bias.reshape(1, units)], near_bits[0])
    attn_line = jnp.concatenate(by_distance(attn_parts, block, line_bits)[1:], axis=1)

    order = np.arange(sentences)
    ahead = (lengths[None, :] > lengths[:, None]) | (
        (lengths[None, :] == lengths[:, None]) & (order[None, :] < order[:, None])
    )
    rank = jnp.sum(ahead.astype(jnp.int32), axis=1)
    row = rank // t_count
    column = rank % t_count
    column = jnp.where(row % 2 == 0, column, t_count - 1 - column)
    mine_here = (column == t_me)[None, :] & (row[None, :] == order[:mine, None])
    chosen = jnp.sum(jnp.where(mine_here, order[None, :], 0), axis=1)
    counts = jnp.sum(jnp.where(mine_here, lengths[None, :], 0), axis=1)
    source = (column ^ t_me) * mine + row
    taken = (counts + 15) & ~15
    ends = jnp.sum(jnp.where(np.tri(mine, dtype=bool), taken[None, :], 0), axis=1)
    devices = np.arange(dp_count)
    distance = 2 * np.arange(chips)
    near = devices[:, None] ^ distance[None, :]
    spots = np.concatenate([near, near ^ 1], axis=1)
    lines = np.arange(t_count)[:, None] ^ np.arange(t_count)[None, :]
    apart = devices[:, None] ^ devices[None, :]
    fixed = np.zeros((dp_count, DEST - PLACE + dp_count), np.int32)
    fixed[:, :dp_count] = spots
    fixed[:, DEST - PLACE :] = apart % 2 * chips + apart // 2
    line_fixed = np.zeros((t_count, CHOSEN - LINE), np.int32)
    line_fixed[:, :t_count] = lines
    table = jnp.concatenate(
        [
            ends - taken,
            np.zeros(LENS - mine, np.int32),
            counts,
            np.zeros(TILES - LENS - mine, np.int32),
            (ends[-1:] + (TILE - 1)) >> (TILE.bit_length() - 1),
            take(jnp.asarray(line_fixed), t_me),
            chosen,
            np.zeros(PLACE - CHOSEN - mine, np.int32),
            take(jnp.asarray(fixed), dp_me),
        ]
    ).astype(jnp.int32)
    attn_line, chosen = tie(attn_line, chosen)
    turn_shape = shape((dp_count, slab, rows), LOW)
    packed, packed_t = pl.pallas_call(
        pack,
        out_shape=(shape((pad, width), LOW), turn_shape),
        in_specs=[SMEM, SMEM, VMEM],
        out_specs=(VMEM,) * 2,
        scratch_shapes=[pltpu.VMEM((mine, length, width), LOW)],
        compiler_params=params(),
        cost_estimate=cost(0, 8 * rows * width),
        name="pack",
    )(table, chosen, tokens)

    attn_chips = gather_chips(attn_line)
    for bit in near_bits[1:]:
        ffn_parts = widen_line(ffn_parts, bit)
        bias_parts = widen_line(bias_parts, bit)
    ffn_parts[-1], bias_parts[-1], packed = tie(ffn_parts[-1], bias_parts[-1], packed)
    bias_all = jnp.stack(by_distance(bias_parts, units, near_bits))
    *attn_chips, packed = tie(*attn_chips, packed)
    attn_pieces = gather_cores(attn_chips)
    ffn_line = jnp.concatenate(by_distance(ffn_parts, 2 * units, near_bits)[1:], axis=1)
    middle = ffn_line.shape[1] // 2
    plane_bits = bits_of(chips)
    spread, orders = [], []
    for half, path in ((ffn_line[:, :middle], plane_bits), (ffn_line[:, middle:], plane_bits[::-1])):
        group, order = half[None], [0]
        for bit in path[:-1]:
            group = jnp.concatenate([group, swap(group, 2 * bit)])
            order = order + [item ^ bit for item in order]
        spread.append(group)
        orders += [order, [item ^ path[-1] for item in order]]
    attn_pieces[0], bias_all, *spread = tie(attn_pieces[0], bias_all, *spread)
    later = [swap(spread[0], 2 * plane_bits[-1]), swap(spread[1], 2 * plane_bits[0])]
    pairs = width // PAIR
    probs_shape = (mine, pairs, 2 * length, length)
    proj, ctx, probs, qkv, wo, z1, root1 = pl.pallas_call(
        attention_forward,
        out_shape=(
            shape((pad, 3 * width), LOW),
            shape((pad, width), LOW),
            shape(probs_shape, LOW),
            shape((width, 3 * width), LOW),
            shape((width, width), LOW),
            shape((rows, width), F32),
            shape((rows, 128), F32),
        ),
        in_specs=[SMEM, VMEM, VMEM, VMEM] + [ANY] * dp_count,
        out_specs=(ANY,) * 6 + (VMEM,),
        scratch_shapes=[
            pltpu.VMEM((pad, 3 * width), LOW),
            pltpu.VMEM((pad, width), LOW),
            pltpu.VMEM(probs_shape, LOW),
            pltpu.VMEM((width, 3 * width), LOW),
            pltpu.VMEM((width, width), LOW),
            pltpu.VMEM((rows, width), F32),
            pltpu.VMEM((dp_count, slab, (t_count - 1) * block), LOW),
            pltpu.SemaphoreType.DMA((dp_count,)),
            pltpu.SemaphoreType.DMA((3,)),
            pltpu.SemaphoreType.DMA((2,)),
            pltpu.SemaphoreType.DMA((rows // TILE,)),
        ],
        compiler_params=params(),
        cost_estimate=cost(8 * rows * width * width, 30 * rows * width),
        name="attention_forward",
    )(table, packed, w_qkv.T, w_out, *attn_pieces)
    *later, z1 = tie(*later, z1)
    ffn_pieces = [spread[0], later[0], spread[1], later[1]]
    ffn_pieces += [swap(item, 1) for item in ffn_pieces]

    gain1, bias1 = ln1_gain.reshape(1, width), ln1_bias.reshape(1, width)
    gain2, bias2 = ln2_gain.reshape(1, width), ln2_bias.reshape(1, width)

    def whole(*dims):
        return pl.BlockSpec(dims, lambda k, table: (0,) * len(dims))

    def call(kernel, outs, ins, out_specs, scratch, flops, nbytes):
        return pl.pallas_call(
            functools.partial(kernel, orders, t_count),
            out_shape=outs,
            grid_spec=pltpu.PrefetchScalarGridSpec(
                num_scalar_prefetch=1,
                grid=(t_count,),
                in_specs=ins,
                out_specs=out_specs,
                scratch_shapes=scratch,
            ),
            compiler_params=params(),
            cost_estimate=cost(flops, nbytes),
            name=kernel.__name__,
        )

    act_spec = pl.BlockSpec((1, rows, units), lambda k, table: (k, 0, 0))
    bias_spec = pl.BlockSpec((1, 1, units), lambda k, table: (k, 0, 0))
    line = whole(1, width)
    full = whole(rows, width)
    root_spec = whole(rows, 128)
    act_shape = shape((t_count, rows, units), LOW)
    weight_scratch = [
        pltpu.VMEM((units, width), LOW),
        pltpu.VMEM((dp_count, slab, (t_count - 1) * 2 * units), LOW),
        pltpu.SemaphoreType.DMA((2 * dp_count,)),
        pltpu.SemaphoreType.DMA((2,)),
        pltpu.SemaphoreType.DMA((rows // TILE,)),
        pltpu.SemaphoreType.DMA((rows // TILE,)),
    ]
    active, slope, z2, root2, pooled = call(
        ffn_forward,
        (
            act_shape,
            act_shape,
            shape((rows, width), F32),
            shape((rows, 128), F32),
            shape((mine, width), LOW),
        ),
        [ANY, line, line, ANY, ANY, bias_spec, line, line] + [ANY] * len(ffn_pieces),
        (act_spec, act_spec, ANY, root_spec, whole(mine, width)),
        [
            pltpu.VMEM((width, 2 * units), LOW),
            pltpu.VMEM((rows, width), LOW),
            pltpu.VMEM((rows, width), F32),
            pltpu.VMEM((rows, width), F32),
            pltpu.VMEM((pad, width), F32),
        ]
        + weight_scratch,
        4 * rows * width * units * t_count,
        40 * rows * width,
    )(table, z1, gain1, bias1, up_weight, down_weight, bias_all, gain2, bias2, *ffn_pieces)

    line_pooled = jnp.stack([pooled] + [swap(pooled, k, "tensor") for k in range(1, t_count)])
    returned = line_pooled.reshape(sentences, width)[source]
    both = jnp.concatenate([returned, cot_paired])
    everyone = jnp.stack(gather_plane(both)).reshape(-1, width)
    apart = (partner // sentences) ^ dp_me
    base = ((apart & 1) * chips + (apart >> 1)) * (2 * sentences) + partner % sentences
    partner_pooled = everyone[base].astype(F32)
    partner_cot = everyone[base + sentences].astype(F32)
    paired = (returned.astype(F32) * partner_pooled).astype(LOW)
    pool_grad = cot_pooled.astype(F32) + partner_pooled * (cot_paired.astype(F32) + partner_cot)
    pool_grad = pool_grad.astype(LOW).astype(F32)

    send_spec = pl.BlockSpec((chips, 1, slab, units), lambda k, table: (0, k, 0, 0))
    send_shape = shape((chips, t_count, slab, units), LOW)
    half_spec = pl.BlockSpec((chips // 2, 1, slab, units), lambda k, table: (0, k, 0, 0))
    half_shape = shape((chips // 2, t_count, slab, units), LOW)
    down_mine, down_early, down_late, up_mine, up_early, up_late, *small_parts = call(
        ffn_backward,
        (send_shape, half_shape, half_shape) * 2
        + (
            shape((rows, width), LOW),
            turn_shape,
            shape((4, width), F32),
            shape((t_count, 1, units), F32),
        ),
        [whole(sentences, width), ANY, root_spec, line, ANY, root_spec, line, line, ANY, ANY]
        + [act_spec, act_spec]
        + [ANY] * len(ffn_pieces),
        (send_spec, half_spec, half_spec) * 2
        + (full, whole(dp_count, slab, rows), whole(4, width), bias_spec),
        [
            pltpu.VMEM((width, 2 * units), LOW),
            pltpu.VMEM((rows, width), F32),
            pltpu.VMEM((rows, width), F32),
            pltpu.VMEM((pad, width), F32),
            pltpu.VMEM((rows, width), LOW),
            pltpu.VMEM((dp_count, slab, rows), LOW),
            pltpu.VMEM((dp_count, slab, rows), LOW),
            pltpu.VMEM((rows, units), LOW),
        ]
        + weight_scratch,
        8 * rows * width * units * t_count,
        60 * rows * width,
    )(
        table, pool_grad, z2, root2, gain2, z1, root1, gain1, bias1, up_weight, down_weight,
        active, slope, *ffn_pieces
    )

    attn_low, attn_t, sums, bias_sum = small_parts

    def small_step(norms, bias_part, mask):
        half = bias_part.shape[0] // 2
        split = bias_part.reshape(half, 2, units)
        got = swap(jnp.concatenate([split[:, 1], norms]), mask, "tensor")
        return norms, got, split[:, 0]

    def small_sum(norms, got, bias_part):
        half = bias_part.shape[0]
        return norms + got[half:], bias_part + got[:half]

    chip_bits = bits_of(chips)
    high = chip_bits[-1]
    down_early, up_early = swap(down_early, 1), swap(up_early, 1)
    small = jnp.concatenate([bias_sum.reshape(t_count, units), sums])
    down_sent, up_sent, small, attn_low = tie(
        add(pick(down_mine, 1, 1), down_early).astype(LOW),
        add(pick(up_mine, 1, high), up_early).astype(LOW),
        small,
        attn_low,
    )
    down_got, up_got = swap(down_sent, 2), swap(up_sent, 2 * high)
    down_late, up_late, small, attn_t = tie(down_late, up_late, small, attn_t)
    norms, small_got, bias_part = small_step(small[t_count:], small[:t_count], 1)
    down_late, up_late = swap(down_late, 1), swap(up_late, 1)

    share = length // t_count
    proj_grad, *input_blocks = pl.pallas_call(
        attention_backward,
        out_shape=(shape((pad, 3 * width), LOW),)
        + (shape((mine, share, width), LOW),) * t_count,
        in_specs=[SMEM, VMEM, VMEM, ANY, ANY, ANY],
        out_specs=(ANY,) + (VMEM,) * t_count,
        scratch_shapes=[
            pltpu.VMEM((pad, width), LOW),
            pltpu.VMEM((pad, 3 * width), LOW),
            pltpu.VMEM(probs_shape, LOW),
            pltpu.VMEM((width, 3 * width), LOW),
            pltpu.VMEM((pad, 3 * width), LOW),
            pltpu.SemaphoreType.DMA((3,)),
            pltpu.SemaphoreType.DMA((1,)),
        ],
        compiler_params=params(),
        cost_estimate=cost(12 * rows * width * width, 30 * rows * width),
        name="attention_backward",
    )(table, attn_low, wo, proj, probs, qkv)

    down_got, up_got, down_late, up_late, small_got, proj_grad, *input_blocks = tie(
        down_got, up_got, down_late, up_late, small_got, proj_grad, *input_blocks
    )
    norms, bias_part = small_sum(norms, small_got, bias_part)
    down_terms = [pick(down_mine, 0, 1), down_late, down_got]
    up_terms = [pick(up_mine, 0, high), up_late, up_got]
    for low, top in zip(chip_bits[1:-1], chip_bits[1:-1][::-1]):
        down_terms = kept(down_terms, 1, swap(sent(down_terms, 1), 2 * low))
        up_terms = kept(up_terms, top, swap(sent(up_terms, top), 2 * top))
    down_sent, up_sent, norms, proj_grad, *input_blocks = tie(
        sent(down_terms, 1), sent(up_terms, 1), norms, proj_grad, *input_blocks
    )
    norms, small_got, bias_part = small_step(norms, bias_part, 2)
    down_got, up_got = swap(down_sent, 2 * high), swap(up_sent, 2)
    input_landed = [input_blocks[0]] + [None] * (t_count - 1)
    input_landed[1] = swap(input_blocks[1], 1, "tensor")

    attn_mine, attn_other = pl.pallas_call(
        attention_weights,
        out_shape=(shape((chips, t_count, slab, block), LOW),) * 2,
        in_specs=[SMEM] + [ANY] * 4,
        out_specs=(VMEM,) * 2,
        scratch_shapes=[
            pltpu.VMEM((dp_count, slab, rows), LOW),
            pltpu.VMEM((dp_count, slab, rows), LOW),
            pltpu.VMEM((pad, width), LOW),
            pltpu.VMEM((pad, 3 * width), LOW),
            pltpu.SemaphoreType.DMA((6,)),
        ],
        compiler_params=params(),
        cost_estimate=cost(8 * rows * width * width, 30 * rows * width),
        name="attention_weights",
    )(table, packed_t, attn_t, ctx, proj_grad)

    def finish(kernel, near, outs, flat):
        near = jnp.stack(near)
        far = swap(near, 1)
        return pl.pallas_call(
            kernel,
            out_shape=tuple(shape(dims, F32) for dims in outs),
            in_specs=[SMEM, ANY, ANY],
            out_specs=(VMEM,) * 2,
            scratch_shapes=[
                pltpu.VMEM((dp_count,) + near.shape[1:], LOW),
                pltpu.VMEM((width, flat), F32),
                pltpu.SemaphoreType.DMA((dp_count,)),
            ],
            compiler_params=params(),
            cost_estimate=cost(0, 8 * width * near.shape[2]),
            name=kernel.__name__,
        )(table, near, far)

    attn_other, small_got, down_got, up_got, input_landed[1] = tie(
        attn_other, small_got, down_got, up_got, input_landed[1]
    )
    norms, bias_part = small_sum(norms, small_got, bias_part)
    small = jnp.concatenate([bias_part, norms])
    attn_got = swap(attn_other, 1)
    attn_sent = [add(attn_mine[m], attn_got[m]).astype(LOW) for m in range(1, chips)]
    ffn_line = jnp.concatenate(
        [add(*kept(up_terms, 1, up_got))[0], add(*kept(down_terms, 1, down_got))[0]], axis=2
    )
    ffn_line = [ffn_line.astype(LOW)]
    ffn_sent, input_blocks[2], *attn_sent = tie(
        sent(ffn_line, 1), input_blocks[2], *attn_sent
    )
    attn_got = [attn_got[0]] + [swap(item, 2 * m) for m, item in zip(range(1, chips), attn_sent)]
    ffn_got = swap(ffn_sent, 1, "tensor")
    input_landed[2] = swap(input_blocks[2], 2, "tensor")

    ffn_line = kept(ffn_line, 1, ffn_got)
    ffn_got = swap(sent(ffn_line, 1), 2, "tensor")
    *attn_got, ffn_got, small, input_landed[2] = tie(*attn_got, ffn_got, small, input_landed[2])
    attn_line = [add(attn_mine[0], *attn_got).astype(LOW)]
    ffn_sum = add(*kept(ffn_line, 1, ffn_got))[0].astype(LOW)
    attn_sent, ffn_sum, small = tie(sent(attn_line, 1), ffn_sum, small)
    small_got = swap(small, 2)
    attn_got = swap(attn_sent, 1, "tensor")
    ffn_chips = gather_chips(ffn_sum)
    attn_line = kept(attn_line, 1, attn_got)
    attn_got = swap(sent(attn_line, 1), 2, "tensor")
    attn_got, small_got, input_blocks[3], *ffn_chips = tie(
        attn_got, small_got, input_blocks[3], *ffn_chips
    )
    small = small + small_got
    for mask in bits_of(dp_count)[3:]:
        small = small + swap(small, mask)
    attn_sum = add(*kept(attn_line, 1, attn_got))[0].astype(LOW)
    attn_sum, input_blocks[3], ffn_chips[0] = tie(attn_sum, input_blocks[3], ffn_chips[0])
    attn_chips = gather_chips(attn_sum)
    input_landed[3] = swap(input_blocks[3], 3, "tensor")
    up_grad, down_grad = finish(place_grads, ffn_chips, ((width, units), (units, width)), units)
    small_got = swap(small, 4)
    attn_chips[0], up_grad, input_landed[3], small_got = tie(
        attn_chips[0], up_grad, input_landed[3], small_got
    )
    small = small + small_got
    small_got = swap(small, 1)
    qkv_grad, out_grad = finish(
        place_attention_grads, attn_chips, ((3 * ctx_cols, width), (ctx_cols, width)), block
    )
    home = pl.pallas_call(
        send_home,
        out_shape=shape((share, sentences, width), LOW),
        in_specs=[VMEM] * (1 + t_count),
        out_specs=VMEM,
        compiler_params=params(),
        cost_estimate=cost(0, 4 * share * sentences * width),
        name="send_home",
    )(jnp.tile(source, STEP).reshape(-1, 1), *input_landed)
    small = small + small_got
    bias_sum, norms = small[0], small[1:]
    return (
        returned,
        paired,
        home,
        qkv_grad.T,
        out_grad,
        norms[2],
        norms[3],
        up_grad,
        bias_sum,
        down_grad,
        norms[0],
        norms[1],
    )


def solution(mesh):
    placed = (
        P(None, "dp", None),
        P("dp"),
        P("dp"),
        P(None, "tensor"),
        P("tensor", None),
        P(),
        P(),
        P(None, "tensor"),
        P("tensor"),
        P("tensor", None),
        P(),
        P(),
        P("dp", None),
        P("dp", None),
    )
    return jax.shard_map(
        shards,
        mesh=mesh,
        in_specs=placed,
        out_specs=(
            P("dp", None),
            P("dp", None),
            P("tensor", "dp", None),
            P(None, "tensor"),
            P("tensor", None),
            P(),
            P(),
            P(None, "tensor"),
            P("tensor"),
            P("tensor", None),
            P(),
            P(),
        ),
        check_vma=False,
    )
```

```python
import functools

import jax
import jax.numpy as jnp
import numpy as np
from jax import lax
from jax.experimental import pallas as pl
from jax.experimental.pallas import tpu as pltpu
from jax.sharding import PartitionSpec as P

HD = 64
EPSILON = 1e-06
LOW = jnp.bfloat16
F32 = jnp.float32
INV_SQRT_2PI = 0.3989422804014327
SQRT_HALF = 0.7071067811865476
TILE = 256
CHUNK = 256
STEP = 16
MASKED = -1000000000.0
LOG2_E = 1.4426950408889634
VMEM_BYTES = 60 * 2**20
NN = (((1,), (0,)), ((), ()))
NT = (((1,), (1,)), ((), ()))
PAIR = 2 * HD
LENS, TILES, LINE, CHOSEN, PLACE, DEST = 16, 32, 33, 40, 48, 80


def mm(a, b, dims=NN):
    return lax.dot_general(a, b, dims, preferred_element_type=F32)


def rows_of(table, s):
    return pl.ds(pl.multiple_of(table[s], 16), 128)


def tile_at(i):
    return pl.ds(pl.multiple_of(i * TILE, TILE), TILE)


def normalize(values):
    center = values - jnp.mean(values, axis=-1, keepdims=True)
    spread = jnp.mean(center * center, axis=-1, keepdims=True)
    root = lax.rsqrt(spread + EPSILON)
    return center * root, root


def normalize_back(z, root, dz):
    return root * (
        dz - jnp.mean(dz, -1, keepdims=True) - z * jnp.mean(dz * z, -1, keepdims=True)
    )


def split_heads(pair):
    first = lax.broadcasted_iota(jnp.int32, pair.shape, 1) < HD
    zero = jnp.zeros_like(pair)
    return jnp.concatenate([jnp.where(first, pair, zero), jnp.where(first, zero, pair)], axis=0)


def join_heads(split):
    n = split.shape[0] // 2
    first = lax.broadcasted_iota(jnp.int32, (n, PAIR), 1) < HD
    return jnp.where(first, split[:n], split[n:])


def place_pieces(table, pieces, slabs, sems):
    copies = []
    for i, piece in enumerate(pieces):
        copies.append(pltpu.make_async_copy(piece, slabs.at[table[PLACE + i]], sems.at[i]))
    return copies


def turn(table, turned, rows, value):
    flat = value.T
    count, slab = turned.shape[0], turned.shape[1]
    for j in range(count):
        turned[table[DEST + j], :, rows] = flat[j * slab : (j + 1) * slab, :]


def pack(table, chosen, tokens, packed, packed_t, x):
    sents, length, width = x.shape
    total = tokens.shape[1]
    depth = total * STEP
    column = lax.broadcasted_iota(jnp.int32, (STEP, depth), 1)
    position = lax.broadcasted_iota(jnp.int32, (STEP, depth), 0)
    here = (column // total) == position
    pick = [here & ((column % total) == chosen[s]) for s in range(sents)]
    pick = jnp.concatenate([jnp.where(item, 1.0, 0.0).astype(LOW) for item in pick], axis=0)
    for block in range(length // STEP):
        rows = slice(block * STEP, (block + 1) * STEP)
        found = mm(pick, tokens[rows].reshape(depth, width)).astype(LOW)
        for s in range(sents):
            x[s, rows, :] = found[s * STEP : (s + 1) * STEP]
    packed[...] = jnp.zeros_like(packed)

    def place(s, _):
        packed[rows_of(table, s), :] = x[s]
        return 0

    lax.fori_loop(0, sents, place, 0)

    def flip(i, _):
        rows = tile_at(i)
        turn(table, packed_t, rows, packed[rows, :])
        return 0

    lax.fori_loop(0, table[TILES], flip, 0)


def send_home(source, *refs):
    blocks, home = refs[:-1], refs[-1]
    share, total, width = home.shape
    depth = total * STEP
    column = lax.broadcasted_iota(jnp.int32, (depth, depth), 1)
    row = lax.broadcasted_iota(jnp.int32, (depth, depth), 0)
    pick = ((column % STEP) == (row // total)) & ((column // STEP) == source[...])
    pick = jnp.where(pick, 1.0, 0.0).astype(LOW)
    for block in range(share // STEP):
        rows = slice(block * STEP, (block + 1) * STEP)
        values = [item[:, rows, :].reshape(-1, width) for item in blocks]
        found = mm(pick, jnp.concatenate(values, axis=0)).astype(LOW)
        home[rows] = found.reshape(STEP, total, width)


def start_all(copies):
    for copy in copies:
        copy.start()


def wait_all(copies):
    for copy in copies:
        copy.wait()


def place_halves(table, orders, arrays, slabs, sems):
    chips, half = slabs.shape[0] // 2, slabs.shape[2] // 2
    copies = []
    for side in range(2):
        for group, order in enumerate(orders):
            columns = slice(0, half) if group < len(orders) // 2 else slice(half, 2 * half)
            source = arrays[side * len(orders) + group]
            for i, m in enumerate(order):
                target = slabs.at[table[PLACE + side * chips + m], :, columns]
                copies.append(
                    pltpu.make_async_copy(source.at[i], target, sems.at[len(copies)])
                )
    return copies


def by_tiles(table, rows, body):
    for n in range(1, rows // TILE + 1):

        @pl.when(table[TILES] == n)
        def _():
            body(n * TILE)


def tile_copies(table, source, target, sems):
    def at(i):
        rows = slice(i * TILE, (i + 1) * TILE)
        return pltpu.make_async_copy(source.at[rows], target.at[rows], sems.at[i])

    def each(act):
        for i in range(sems.shape[0]):

            @pl.when(i < table[TILES])
            def _():
                act(at(i))

    return each


def place_weight(k, steps, weight, own_down, slabs):
    count, slab = slabs.shape[0], slabs.shape[1]
    columns = weight.shape[1]

    @pl.when(k == 0)
    def _():
        weight[:, columns // 2 :] = own_down[...].T

    for t in range(1, steps):

        @pl.when(k == t)
        def _():
            for j in range(count):
                weight[j * slab : (j + 1) * slab, :] = slabs[
                    j, :, (t - 1) * columns : t * columns
                ]


def attention_forward(table, packed, own_qkv, own_out, *refs):
    pieces, refs = refs[:-18], refs[-18:]
    proj_out, ctx_out, probs_out, qkv_out, wo_out, z1_out, root1 = refs[:7]
    proj, ctx, probs, qkv, wo, z1, slabs, sems, out_sems, wide_sems, z1_sems = refs[7:]
    sents, pairs = probs.shape[0], probs.shape[1]
    width = packed.shape[1]
    length = probs.shape[3]
    part = own_out.shape[0]
    block = 4 * part
    heads = part // HD
    arrivals = place_pieces(table, pieces, slabs, sems)
    start_all(arrivals)
    count, slab = slabs.shape[0], slabs.shape[1]
    for h in range(heads):
        for p in range(3):
            source = (h * 3 + p) * HD
            qkv[:, p * width + h * HD : p * width + (h + 1) * HD] = own_qkv[
                source : source + HD, :
            ].T
    wo[:, :part] = own_out[...].T
    ctx[...] = jnp.zeros_like(ctx)
    tiles = table[TILES]
    end = pl.ds(pl.multiple_of(tiles * TILE, TILE), length)
    proj[end, :] = jnp.zeros((length, 3 * width), LOW)
    wait_all(arrivals)
    for j in range(count):
        rows = slice(j * slab, (j + 1) * slab)
        for k in range(1, width // part):
            base = (k - 1) * block
            for p in range(3):
                qkv[rows, p * width + k * part : p * width + (k + 1) * part] = slabs[
                    j, :, base + p * part : base + (p + 1) * part
                ]
            wo[rows, k * part : (k + 1) * part] = slabs[j, :, base + 3 * part : base + block]
    wide_copies = [
        pltpu.make_async_copy(qkv, qkv_out, wide_sems.at[0]),
        pltpu.make_async_copy(wo, wo_out, wide_sems.at[1]),
    ]
    start_all(wide_copies)

    def project(n):
        source = packed[:n, :]
        for c in range(0, 3 * width, CHUNK):
            cols = slice(c, c + CHUNK)
            proj[:n, cols] = mm(source, qkv[:, cols]).astype(LOW)

    by_tiles(table, z1.shape[0], project)
    proj_copy = pltpu.make_async_copy(proj, proj_out, out_sems.at[0])
    proj_copy.start()

    def attend(s, _):
        rows = rows_of(table, s)
        valid = lax.broadcasted_iota(jnp.int32, (length, length), 0) < table[LENS + s]
        for p in range(pairs):
            at = p * PAIR
            queries = proj[rows, at : at + PAIR]
            keys = split_heads(proj[rows, width + at : width + at + PAIR])
            values = split_heads(proj[rows, 2 * width + at : 2 * width + at + PAIR])
            scores = mm(keys, queries, NT)
            prob = []
            for h in range(2):
                score = jnp.where(valid, scores[h * length : (h + 1) * length], MASKED)
                top = jnp.max(score, axis=0, keepdims=True)
                score = jnp.exp2((score - top) * (HD**-0.5 * LOG2_E))
                total = jnp.sum(score, axis=0, keepdims=True)
                prob.append((score * (1.0 / total)).astype(LOW))
            prob = jnp.concatenate(prob, axis=0)
            probs[s, p] = prob
            ctx[rows, at : at + PAIR] = mm(prob.T, values).astype(LOW)
        return 0

    lax.fori_loop(0, sents, attend, 0, unroll=4)
    ctx_copies = [
        pltpu.make_async_copy(ctx, ctx_out, out_sems.at[1]),
        pltpu.make_async_copy(probs, probs_out, out_sems.at[2]),
    ]
    start_all(ctx_copies)

    for i in range(z1_sems.shape[0]):
        rows = slice(i * TILE, (i + 1) * TILE)

        @pl.when(i < tiles)
        def _():
            attended = mm(ctx[rows, :], wo[...], NT)
            z, root = normalize(packed[rows, :].astype(F32) + attended)
            z1[rows, :] = z
            root1[rows, :] = jnp.broadcast_to(root, (TILE, 128))
            pltpu.make_async_copy(z1.at[rows], z1_out.at[rows], z1_sems.at[i]).start()

    tile_copies(table, z1, z1_out, z1_sems)(lambda copy: copy.wait())
    wait_all(wide_copies + [proj_copy] + ctx_copies)


def gelu_parts(pre):
    t = pl.reciprocal(1.0 + jnp.abs(pre) * (0.3275911 * SQRT_HALF))
    poly = 0.5 * 1.061405429
    for c in (-1.453152027, 1.421413741, -0.284496736, 0.254829592):
        poly = poly * t + 0.5 * c
    e = jnp.exp2(pre * pre * (-0.5 * LOG2_E))
    tail = poly * t * e
    cdf = jnp.where(pre >= 0.0, 1.0 - tail, tail)
    return pre * cdf, cdf + pre * (e * INV_SQRT_2PI)


def ffn_forward(orders, parts, table, z1_in, gain1, bias1, own_up, own_down_in, bias, gain2, bias2, *refs):
    pieces, refs = refs[:-16], refs[-16:]
    active, slope, z2_out, root2, pooled = refs[:5]
    weight, first, total, z1, z2, own_down, slabs, sems, own_sems, z1_sems, z2_sems = refs[5:]
    k = pl.program_id(0)
    steps = pl.num_programs(0)
    tiles = table[TILES]
    units = active.shape[2]
    arrivals = place_halves(table, orders, pieces, slabs, sems)
    own = [
        pltpu.make_async_copy(own_up, weight.at[:, :units], own_sems.at[0]),
        pltpu.make_async_copy(own_down_in, own_down, own_sems.at[1]),
    ]
    z1_copies = tile_copies(table, z1_in, z1, z1_sems)

    @pl.when(k == 0)
    def _():
        z1_copies(lambda copy: copy.start())
        start_all(own)
        z1_copies(lambda copy: copy.wait())

        def start(i, _):
            rows = tile_at(i)
            value = z1[rows, :] * gain1[...] + bias1[...]
            first[rows, :] = value.astype(LOW)
            total[rows, :] = value
            return 0

        lax.fori_loop(0, tiles, start, 0)
        wait_all(own)
        start_all(arrivals)

    @pl.when(k == 1)
    def _():
        wait_all(arrivals)

    place_weight(k, parts, weight, own_down, slabs)

    def work(n):
        for r in range(0, n, TILE):
            rows = slice(r, r + TILE)
            source = first[rows, :]
            for c in range(0, units, CHUNK):
                cols = slice(c, c + CHUNK)
                act, slp = gelu_parts(mm(source, weight[:, cols]) + bias[0, :, cols])
                active[0, rows, cols] = act.astype(LOW)
                slope[0, rows, cols] = slp.astype(LOW)
            total[rows, :] += mm(active[0, rows, :], weight[:, units:], NT)

    by_tiles(table, first.shape[0], work)

    @pl.when(k == steps - 1)
    def _():
        z2[pl.ds(pl.multiple_of(tiles * TILE, TILE), 128), :] = jnp.zeros((128, z2.shape[1]), F32)

        def finish(i, _):
            rows = tile_at(i)
            z, root = normalize(total[rows, :])
            z2[rows, :] = z
            root2[rows, :] = jnp.broadcast_to(root, (TILE, 128))
            return 0

        lax.fori_loop(0, tiles, finish, 0)
        z2_copies = tile_copies(table, z2, z2_out, z2_sems)
        z2_copies(lambda copy: copy.start())
        means = []
        for s in range(pooled.shape[0]):
            n = table[LENS + s]
            valid = lax.broadcasted_iota(jnp.int32, (128, z2.shape[1]), 0) < n
            rows = jnp.where(valid, z2[rows_of(table, s), :], 0.0)
            means.append(jnp.sum(rows, axis=0, keepdims=True) / n.astype(F32))
        pooled[...] = (jnp.concatenate(means, axis=0) * gain2[...] + bias2[...]).astype(LOW)
        z2_copies(lambda copy: copy.wait())


def weight_grad(table, turned, right, store):
    count, slab, rows = turned.shape

    def body(n):
        if slab % 16 == 0:
            left = turned[:, :, :n].reshape(count * slab, n)
        else:
            left = jnp.concatenate([turned[j, :, :n] for j in range(count)], axis=0)
        store(lambda columns: mm(left, right(n, columns)))

    by_tiles(table, rows, body)


def half_order(chips, bit):
    order = {}
    for m in range(chips):
        order[m] = sum(1 for other in range(m) if (other & bit) == (m & bit))
    return order


def split_send(mine, other, value, k, columns):
    chips, slab = mine.shape[0], mine.shape[2]
    for m in range(chips):
        mine[m, k, :, columns] = value[m * slab : (m + 1) * slab].astype(LOW)
        target, at = other(m)
        target[at, k, :, columns] = value[(chips + m) * slab : (chips + m + 1) * slab].astype(LOW)


def send_chunks(mine, early, late, bit, product):
    order = half_order(mine.shape[0], bit)

    def other(m):
        return (early if m & bit else late), order[m]

    for c in range(0, mine.shape[3], CHUNK):
        cols = slice(c, c + CHUNK)
        split_send(mine, other, product(cols), 0, cols)


def ffn_backward(
    orders, parts, table, pool, z2_in, root2, gain2, z1_in, root1, gain1, bias1, own_up, own_down_in,
    active, slope, *refs
):
    pieces, refs = refs[:-24], refs[-24:]
    down_mine, down_early, down_late, up_mine, up_early, up_late = refs[:6]
    attn_low, attn_t, sums, bias_sum = refs[6:10]
    weight, z1, z2, total, branch, branch_t, first_t, hidden, own_down, slabs = refs[10:20]
    sems, own_sems, z1_sems, z2_sems = refs[20:]
    k = pl.program_id(0)
    tiles = table[TILES]
    width, units = own_up.shape
    arrivals = place_halves(table, orders, pieces, slabs, sems)
    own = [
        pltpu.make_async_copy(own_up, weight.at[:, :units], own_sems.at[0]),
        pltpu.make_async_copy(own_down_in, own_down, own_sems.at[1]),
    ]
    z1_copies = tile_copies(table, z1_in, z1, z1_sems)
    z2_copies = tile_copies(table, z2_in, z2, z2_sems)

    @pl.when(k == 0)
    def _():
        z2_copies(lambda copy: copy.start())
        z1_copies(lambda copy: copy.start())
        start_all(own)
        total[...] = jnp.zeros_like(total)
        for s in range(attn_low.shape[0] // 128):
            n = table[LENS + s]
            valid = lax.broadcasted_iota(jnp.int32, (128, width), 0) < n
            row = pool[pl.ds(table[CHOSEN + s], 1), :] / n.astype(F32)
            total[rows_of(table, s), :] = jnp.where(valid, row, 0.0)
        sums[...] = jnp.zeros_like(sums)
        z2_copies(lambda copy: copy.wait())

        def start(i, _):
            rows = tile_at(i)
            grad = total[rows, :]
            z = z2[rows, :]
            sums[0:1, :] += jnp.sum(grad * z, axis=0, keepdims=True)
            sums[1:2, :] += jnp.sum(grad, axis=0, keepdims=True)
            value = normalize_back(z, root2[rows, 0:1], grad * gain2[...])
            low = value.astype(LOW)
            total[rows, :] = value
            branch[rows, :] = low
            turn(table, branch_t, rows, low)
            return 0

        lax.fori_loop(0, tiles, start, 0)
        z1_copies(lambda copy: copy.wait())

        def flip(i, _):
            rows = tile_at(i)
            turn(table, first_t, rows, (z1[rows, :] * gain1[...] + bias1[...]).astype(LOW))
            return 0

        lax.fori_loop(0, tiles, flip, 0)
        wait_all(own)
        start_all(arrivals)

    @pl.when(k == 1)
    def _():
        wait_all(arrivals)

    place_weight(k, parts, weight, own_down, slabs)
    weight_grad(
        table,
        branch_t,
        lambda n, cols: active[0, :n, cols],
        lambda product: send_chunks(down_mine, down_early, down_late, 1, product),
    )
    bias_sum[...] = jnp.zeros_like(bias_sum)

    def work(n):
        source = branch[:n, :]
        for c in range(0, units, CHUNK):
            cols = slice(c, c + CHUNK)
            grad = mm(source, weight[:, units + c : units + c + CHUNK])
            hid = (slope[0, :n, cols].astype(F32) * grad).astype(LOW)
            hidden[:n, cols] = hid
            bias_sum[0, :, cols] += jnp.sum(hid.astype(F32), axis=0, keepdims=True)
        total[:n, :] += mm(hidden[:n, :], weight[:, :units], NT)

    by_tiles(table, hidden.shape[0], work)
    weight_grad(
        table,
        first_t,
        lambda n, cols: hidden[:n, cols],
        lambda product: send_chunks(
            up_mine, up_early, up_late, up_mine.shape[0] // 2, product
        ),
    )

    @pl.when(k == pl.num_programs(0) - 1)
    def _():
        def finish(i, _):
            rows = tile_at(i)
            grad = total[rows, :]
            z = z1[rows, :]
            sums[2:3, :] += jnp.sum(grad * z, axis=0, keepdims=True)
            sums[3:4, :] += jnp.sum(grad, axis=0, keepdims=True)
            value = normalize_back(z, root1[rows, 0:1], grad * gain1[...])
            low = value.astype(LOW)
            attn_low[rows, :] = low
            turn(table, attn_t, rows, low)
            return 0

        lax.fori_loop(0, tiles, finish, 0)


def attention_backward(table, attn_low, wo, proj_in, probs_in, qkv_in, proj_grad_out, *refs):
    outs, refs = refs[:-7], refs[-7:]
    ctx_grad, proj, probs, qkv, proj_grad, sems, out_sem = refs
    sents, pairs = probs.shape[0], probs.shape[1]
    length = probs.shape[3]
    width = attn_low.shape[1]
    tiles = table[TILES]
    arrivals = [
        pltpu.make_async_copy(proj_in, proj, sems.at[0]),
        pltpu.make_async_copy(probs_in, probs, sems.at[1]),
        pltpu.make_async_copy(qkv_in, qkv, sems.at[2]),
    ]
    start_all(arrivals)
    ctx_grad[...] = jnp.zeros_like(ctx_grad)
    proj_grad[...] = jnp.zeros_like(proj_grad)

    def start(n):
        ctx_grad[:n, :] = mm(attn_low[:n, :], wo[...]).astype(LOW)

    by_tiles(table, attn_low.shape[0], start)
    wait_all(arrivals[:2])
    scale = HD**-0.5

    def attend(s, _):
        rows = rows_of(table, s)
        live = lax.broadcasted_iota(jnp.int32, (length, PAIR), 0) < table[LENS + s]
        for p in range(pairs):
            at = p * PAIR
            queries = proj[rows, at : at + PAIR]
            keys = split_heads(proj[rows, width + at : width + at + PAIR])
            values = split_heads(proj[rows, 2 * width + at : 2 * width + at + PAIR])
            grad = ctx_grad[rows, at : at + PAIR]
            grad = jnp.where(live, grad, jnp.zeros_like(grad))
            prob_grad = mm(values, grad, NT)
            score_grad = []
            for h in range(2):
                half = slice(h * length, (h + 1) * length)
                prob = probs[s, p, half, :].astype(F32)
                part = prob_grad[half]
                inner = jnp.sum(prob * part, axis=0, keepdims=True)
                score_grad.append((prob * (part - inner)).astype(LOW))
            score_grad = jnp.concatenate(score_grad, axis=0)
            proj_grad[rows, at : at + PAIR] = (mm(score_grad.T, keys) * scale).astype(LOW)
            proj_grad[rows, width + at : width + at + PAIR] = (
                join_heads(mm(score_grad, queries)) * scale
            ).astype(LOW)
            proj_grad[rows, 2 * width + at : 2 * width + at + PAIR] = join_heads(
                mm(probs[s, p], grad)
            ).astype(LOW)
        return 0

    lax.fori_loop(0, sents, attend, 0, unroll=4)
    proj_copy = pltpu.make_async_copy(proj_grad, proj_grad_out, out_sem.at[0])
    proj_copy.start()
    arrivals[2].wait()

    def finish(n):
        total = mm(proj_grad[:n, :], qkv[...], NT)
        ctx_grad[:n, :] = (attn_low[:n, :].astype(F32) + total).astype(LOW)

    by_tiles(table, attn_low.shape[0], finish)
    ctx_grad[pl.ds(pl.multiple_of(tiles * TILE, TILE), length), :] = jnp.zeros(
        (length, width), LOW
    )
    share = outs[0].shape[1]
    for k, out in enumerate(outs):
        first = table[LINE + k] * share
        position = lax.broadcasted_iota(jnp.int32, (share, width), 0) + first
        for s in range(sents):
            value = ctx_grad[pl.ds(pl.multiple_of(table[s] + first, 16), share), :]
            out[s] = jnp.where(position < table[LENS + s], value, jnp.zeros_like(value))
    proj_copy.wait()


def attention_weights(table, *refs):
    sources, (mine, other), (packed_t, attn_t, ctx, proj_grad, sems) = refs[:4], refs[4:6], refs[6:]
    width = ctx.shape[1]
    count = mine.shape[1]
    part = width // count
    copies = [
        pltpu.make_async_copy(source, target, sems.at[i])
        for i, (source, target) in enumerate(zip(sources[:3], (packed_t, attn_t, ctx)))
    ]
    for p in range(3):
        cols = slice(p * width, (p + 1) * width)
        copies.append(
            pltpu.make_async_copy(sources[3].at[:, cols], proj_grad.at[:, cols], sems.at[3 + p])
        )
    order = [copies[1], copies[2], copies[0]] + copies[3:]
    start_all(order)

    def store(p, product):
        value = product(slice(p * width, (p + 1) * width) if p < 3 else slice(None))
        for k in range(count):
            split_send(
                mine,
                lambda m: (other, m),
                value[:, k * part : (k + 1) * part],
                k,
                slice(p * part, (p + 1) * part),
            )

    wait_all(order[:2])
    weight_grad(
        table, attn_t, lambda n, cols: ctx[:n, cols], lambda product: store(3, product)
    )
    order[2].wait()
    for p in range(3):
        order[3 + p].wait()
        weight_grad(
            table,
            packed_t,
            lambda n, cols: proj_grad[:n, cols],
            lambda product: store(p, product),
        )


def stacked_pieces(stacks):
    return [stack.at[i] for stack in stacks for i in range(stack.shape[0])]


def place_grads(table, near, far, straight, turned, slabs, flat, sems):
    count, slab = slabs.shape[0], slabs.shape[1]
    arrivals = place_pieces(table, stacked_pieces((near, far)), slabs, sems)
    start_all(arrivals)
    wait_all(arrivals)
    width = straight.shape[1]
    for j in range(count):
        rows = slice(j * slab, (j + 1) * slab)
        straight[rows, :] = slabs[j, :, :width].astype(F32)
        flat[rows, :] = slabs[j, :, width:].astype(F32)
    turned[...] = flat[...].T


def place_attention_grads(table, near, far, qkv, wo, slabs, flat, sems):
    count, slab = slabs.shape[0], slabs.shape[1]
    arrivals = place_pieces(table, stacked_pieces((near, far)), slabs, sems)
    start_all(arrivals)
    wait_all(arrivals)
    for j in range(count):
        flat[j * slab : (j + 1) * slab, :] = slabs[j].astype(F32)
    part = wo.shape[0]
    heads = part // HD
    for p in range(3):
        piece = flat[:, p * part : (p + 1) * part].T
        for h in range(heads):
            target = (h * 3 + p) * HD
            qkv[target : target + HD, :] = piece[h * HD : (h + 1) * HD, :]
    wo[...] = flat[:, 3 * part :].T


COST = 1000000
SMEM = pl.BlockSpec(memory_space=pltpu.SMEM)
VMEM = pl.BlockSpec(memory_space=pltpu.VMEM)
ANY = pl.BlockSpec(memory_space=pl.ANY)


def shape(dims, dtype):
    return jax.ShapeDtypeStruct(dims, dtype)


def params():
    return pltpu.CompilerParams(vmem_limit_bytes=VMEM_BYTES)


def cost(flops, nbytes):
    return pl.CostEstimate(flops=flops // COST, bytes_accessed=nbytes // COST, transcendentals=0)


def add(*terms):
    return sum(term.astype(F32) for term in terms)


def swap(value, mask, axis="dp"):
    return lax.ppermute(value, axis, [(i, i ^ mask) for i in range(lax.axis_size(axis))])


def bits_of(count):
    return [1 << i for i in range(count.bit_length() - 1)]


def take(values, index, axis=0):
    return lax.dynamic_index_in_dim(values, index, axis, False, allow_negative_indices=False)


def cut(values, start, size, axis):
    return lax.dynamic_slice_in_dim(values, start, size, axis, allow_negative_indices=False)


def tie(*values):
    return lax.optimization_barrier(values)


def gather_line(piece):
    n = lax.axis_size("tensor")
    return jnp.concatenate([swap(piece, k, "tensor") for k in range(1, n)], axis=1)


def gather_chips(value):
    return [value] + [swap(value, 2 * m) for m in range(1, lax.axis_size("dp") // 2)]


def gather_cores(near):
    return near + [swap(item, 1) for item in near]


def gather_plane(value):
    return gather_cores(gather_chips(value))


def pick(term, side, bit):
    dims = term.shape
    view = term.reshape((dims[0] // (2 * bit), 2, bit) + dims[1:])[:, side]
    return view.reshape((dims[0] // 2,) + dims[1:])


def sent(terms, bit):
    return add(*[pick(term, 1, bit) for term in terms]).astype(LOW)


def kept(terms, bit, landed):
    return [pick(term, 0, bit) for term in terms] + [landed]


def reduce_line(terms):
    for bit in bits_of(lax.axis_size("tensor")):
        terms = kept(terms, 1, swap(sent(terms, 1), bit, "tensor"))
    return add(*terms)[0].astype(LOW)


def reduce_chips(terms, bits):
    for bit in bits:
        terms = kept(terms, 1, swap(sent(terms, 1), 2 * bit))
    return terms


def shards(
    tokens,
    lengths,
    partner,
    w_qkv,
    w_out,
    ln1_gain,
    ln1_bias,
    up_weight,
    up_projection_bias,
    down_weight,
    ln2_gain,
    ln2_bias,
    cot_pooled,
    cot_paired,
):
    dp_count = lax.axis_size("dp")
    t_count = lax.axis_size("tensor")
    dp_me = lax.axis_index("dp")
    t_me = lax.axis_index("tensor")
    length, sentences, width = tokens.shape
    mine = sentences // t_count
    rows = mine * length
    pad = rows + length
    slab = width // dp_count
    chips = dp_count // 2
    heads = w_qkv.shape[1] // (3 * HD)
    units = up_weight.shape[1]
    ctx_cols = w_out.shape[0]
    block = 4 * ctx_cols

    def by_part(weight):
        return weight.reshape(-1, heads, 3, HD).transpose(0, 2, 1, 3).reshape(weight.shape)

    def rows_piece(weight):
        return cut(weight, dp_me * slab, slab, 0)

    def columns_piece(weight):
        return cut(weight, dp_me * slab, slab, 1).T

    attn_piece = jnp.concatenate([by_part(rows_piece(w_qkv)), columns_piece(w_out)], axis=1)
    attn_piece, up_early, down_early = tie(attn_piece, up_weight, down_weight)
    near_bits = bits_of(t_count)
    line_bits = near_bits[::-1]

    def widen_line(parts, bit):
        return parts + [swap(jnp.concatenate(parts, axis=1), bit, "tensor")]

    def line_order(bits):
        order = [0]
        for bit in bits:
            order += [item ^ bit for item in order]
        return order

    def by_distance(parts, columns, bits):
        wide = jnp.concatenate(parts, axis=1)
        order = line_order(bits)
        return [wide[:, order.index(d) * columns : (order.index(d) + 1) * columns] for d in range(t_count)]

    attn_parts = widen_line([attn_piece], line_bits[0])
    ffn_piece = jnp.concatenate([rows_piece(up_early), columns_piece(down_early)], axis=1)
    for bit in line_bits[1:]:
        attn_parts = widen_line(attn_parts, bit)
    ffn_parts = widen_line([ffn_piece], near_bits[0])
    bias_parts = widen_line([up_projection_bias.reshape(1, units)], near_bits[0])
    attn_line = jnp.concatenate(by_distance(attn_parts, block, line_bits)[1:], axis=1)

    order = np.arange(sentences)
    ahead = (lengths[None, :] > lengths[:, None]) | (
        (lengths[None, :] == lengths[:, None]) & (order[None, :] < order[:, None])
    )
    rank = jnp.sum(ahead.astype(jnp.int32), axis=1)
    row = rank // t_count
    column = rank % t_count
    column = jnp.where(row % 2 == 0, column, t_count - 1 - column)
    mine_here = (column == t_me)[None, :] & (row[None, :] == order[:mine, None])
    chosen = jnp.sum(jnp.where(mine_here, order[None, :], 0), axis=1)
    counts = jnp.sum(jnp.where(mine_here, lengths[None, :], 0), axis=1)
    source = (column ^ t_me) * mine + row
    taken = (counts + 15) & ~15
    ends = jnp.sum(jnp.where(np.tri(mine, dtype=bool), taken[None, :], 0), axis=1)
    devices = np.arange(dp_count)
    distance = 2 * np.arange(chips)
    near = devices[:, None] ^ distance[None, :]
    spots = np.concatenate([near, near ^ 1], axis=1)
    lines = np.arange(t_count)[:, None] ^ np.arange(t_count)[None, :]
    apart = devices[:, None] ^ devices[None, :]
    fixed = np.zeros((dp_count, DEST - PLACE + dp_count), np.int32)
    fixed[:, :dp_count] = spots
    fixed[:, DEST - PLACE :] = apart % 2 * chips + apart // 2
    line_fixed = np.zeros((t_count, CHOSEN - LINE), np.int32)
    line_fixed[:, :t_count] = lines
    table = jnp.concatenate(
        [
            ends - taken,
            np.zeros(LENS - mine, np.int32),
            counts,
            np.zeros(TILES - LENS - mine, np.int32),
            (ends[-1:] + (TILE - 1)) >> (TILE.bit_length() - 1),
            take(jnp.asarray(line_fixed), t_me),
            chosen,
            np.zeros(PLACE - CHOSEN - mine, np.int32),
            take(jnp.asarray(fixed), dp_me),
        ]
    ).astype(jnp.int32)
    attn_line, chosen = tie(attn_line, chosen)
    turn_shape = shape((dp_count, slab, rows), LOW)
    packed, packed_t = pl.pallas_call(
        pack,
        out_shape=(shape((pad, width), LOW), turn_shape),
        in_specs=[SMEM, SMEM, VMEM],
        out_specs=(VMEM,) * 2,
        scratch_shapes=[pltpu.VMEM((mine, length, width), LOW)],
        compiler_params=params(),
        cost_estimate=cost(0, 8 * rows * width),
        name="pack",
    )(table, chosen, tokens)

    attn_chips = gather_chips(attn_line)
    for bit in near_bits[1:]:
        ffn_parts = widen_line(ffn_parts, bit)
        bias_parts = widen_line(bias_parts, bit)
    ffn_parts[-1], bias_parts[-1], packed = tie(ffn_parts[-1], bias_parts[-1], packed)
    bias_all = jnp.stack(by_distance(bias_parts, units, near_bits))
    *attn_chips, packed = tie(*attn_chips, packed)
    attn_pieces = gather_cores(attn_chips)
    ffn_line = jnp.concatenate(by_distance(ffn_parts, 2 * units, near_bits)[1:], axis=1)
    middle = ffn_line.shape[1] // 2
    plane_bits = bits_of(chips)
    spread, orders = [], []
    for half, path in ((ffn_line[:, :middle], plane_bits), (ffn_line[:, middle:], plane_bits[::-1])):
        group, order = half[None], [0]
        for bit in path[:-1]:
            group = jnp.concatenate([group, swap(group, 2 * bit)])
            order = order + [item ^ bit for item in order]
        spread.append(group)
        orders += [order, [item ^ path[-1] for item in order]]
    attn_pieces[0], bias_all, *spread = tie(attn_pieces[0], bias_all, *spread)
    later = [swap(spread[0], 2 * plane_bits[-1]), swap(spread[1], 2 * plane_bits[0])]
    pairs = width // PAIR
    probs_shape = (mine, pairs, 2 * length, length)
    proj, ctx, probs, qkv, wo, z1, root1 = pl.pallas_call(
        attention_forward,
        out_shape=(
            shape((pad, 3 * width), LOW),
            shape((pad, width), LOW),
            shape(probs_shape, LOW),
            shape((width, 3 * width), LOW),
            shape((width, width), LOW),
            shape((rows, width), F32),
            shape((rows, 128), F32),
        ),
        in_specs=[SMEM, VMEM, VMEM, VMEM] + [ANY] * dp_count,
        out_specs=(ANY,) * 6 + (VMEM,),
        scratch_shapes=[
            pltpu.VMEM((pad, 3 * width), LOW),
            pltpu.VMEM((pad, width), LOW),
            pltpu.VMEM(probs_shape, LOW),
            pltpu.VMEM((width, 3 * width), LOW),
            pltpu.VMEM((width, width), LOW),
            pltpu.VMEM((rows, width), F32),
            pltpu.VMEM((dp_count, slab, (t_count - 1) * block), LOW),
            pltpu.SemaphoreType.DMA((dp_count,)),
            pltpu.SemaphoreType.DMA((3,)),
            pltpu.SemaphoreType.DMA((2,)),
            pltpu.SemaphoreType.DMA((rows // TILE,)),
        ],
        compiler_params=params(),
        cost_estimate=cost(8 * rows * width * width, 30 * rows * width),
        name="attention_forward",
    )(table, packed, w_qkv.T, w_out, *attn_pieces)
    *later, z1 = tie(*later, z1)
    ffn_pieces = [spread[0], later[0], spread[1], later[1]]
    ffn_pieces += [swap(item, 1) for item in ffn_pieces]

    gain1, bias1 = ln1_gain.reshape(1, width), ln1_bias.reshape(1, width)
    gain2, bias2 = ln2_gain.reshape(1, width), ln2_bias.reshape(1, width)

    def whole(*dims):
        return pl.BlockSpec(dims, lambda k, table: (0,) * len(dims))

    def call(kernel, outs, ins, out_specs, scratch, flops, nbytes):
        return pl.pallas_call(
            functools.partial(kernel, orders, t_count),
            out_shape=outs,
            grid_spec=pltpu.PrefetchScalarGridSpec(
                num_scalar_prefetch=1,
                grid=(t_count,),
                in_specs=ins,
                out_specs=out_specs,
                scratch_shapes=scratch,
            ),
            compiler_params=params(),
            cost_estimate=cost(flops, nbytes),
            name=kernel.__name__,
        )

    act_spec = pl.BlockSpec((1, rows, units), lambda k, table: (k, 0, 0))
    bias_spec = pl.BlockSpec((1, 1, units), lambda k, table: (k, 0, 0))
    line = whole(1, width)
    full = whole(rows, width)
    root_spec = whole(rows, 128)
    act_shape = shape((t_count, rows, units), LOW)
    weight_scratch = [
        pltpu.VMEM((units, width), LOW),
        pltpu.VMEM((dp_count, slab, (t_count - 1) * 2 * units), LOW),
        pltpu.SemaphoreType.DMA((2 * dp_count,)),
        pltpu.SemaphoreType.DMA((2,)),
        pltpu.SemaphoreType.DMA((rows // TILE,)),
        pltpu.SemaphoreType.DMA((rows // TILE,)),
    ]
    active, slope, z2, root2, pooled = call(
        ffn_forward,
        (
            act_shape,
            act_shape,
            shape((rows, width), F32),
            shape((rows, 128), F32),
            shape((mine, width), LOW),
        ),
        [ANY, line, line, ANY, ANY, bias_spec, line, line] + [ANY] * len(ffn_pieces),
        (act_spec, act_spec, ANY, root_spec, whole(mine, width)),
        [
            pltpu.VMEM((width, 2 * units), LOW),
            pltpu.VMEM((rows, width), LOW),
            pltpu.VMEM((rows, width), F32),
            pltpu.VMEM((rows, width), F32),
            pltpu.VMEM((pad, width), F32),
        ]
        + weight_scratch,
        4 * rows * width * units * t_count,
        40 * rows * width,
    )(table, z1, gain1, bias1, up_weight, down_weight, bias_all, gain2, bias2, *ffn_pieces)

    line_pooled = jnp.stack([pooled] + [swap(pooled, k, "tensor") for k in range(1, t_count)])
    returned = line_pooled.reshape(sentences, width)[source]
    both = jnp.concatenate([returned, cot_paired], axis=1)
    everyone = jnp.stack(gather_plane(both)).reshape(-1, 2 * width)
    apart = (partner // sentences) ^ dp_me
    base = ((apart & 1) * chips + (apart >> 1)) * sentences + partner % sentences
    partner_rows = everyone[base].astype(F32)
    partner_pooled, partner_cot = partner_rows[:, :width], partner_rows[:, width:]
    paired = (returned.astype(F32) * partner_pooled).astype(LOW)
    pool_grad = cot_pooled.astype(F32) + partner_pooled * (cot_paired.astype(F32) + partner_cot)
    pool_grad = pool_grad.astype(LOW).astype(F32)

    send_spec = pl.BlockSpec((chips, 1, slab, units), lambda k, table: (0, k, 0, 0))
    send_shape = shape((chips, t_count, slab, units), LOW)
    half_spec = pl.BlockSpec((chips // 2, 1, slab, units), lambda k, table: (0, k, 0, 0))
    half_shape = shape((chips // 2, t_count, slab, units), LOW)
    down_mine, down_early, down_late, up_mine, up_early, up_late, *small_parts = call(
        ffn_backward,
        (send_shape, half_shape, half_shape) * 2
        + (
            shape((rows, width), LOW),
            turn_shape,
            shape((4, width), F32),
            shape((t_count, 1, units), F32),
        ),
        [whole(sentences, width), ANY, root_spec, line, ANY, root_spec, line, line, ANY, ANY]
        + [act_spec, act_spec]
        + [ANY] * len(ffn_pieces),
        (send_spec, half_spec, half_spec) * 2
        + (full, whole(dp_count, slab, rows), whole(4, width), bias_spec),
        [
            pltpu.VMEM((width, 2 * units), LOW),
            pltpu.VMEM((rows, width), F32),
            pltpu.VMEM((rows, width), F32),
            pltpu.VMEM((pad, width), F32),
            pltpu.VMEM((rows, width), LOW),
            pltpu.VMEM((dp_count, slab, rows), LOW),
            pltpu.VMEM((dp_count, slab, rows), LOW),
            pltpu.VMEM((rows, units), LOW),
        ]
        + weight_scratch,
        8 * rows * width * units * t_count,
        60 * rows * width,
    )(
        table, pool_grad, z2, root2, gain2, z1, root1, gain1, bias1, up_weight, down_weight,
        active, slope, *ffn_pieces
    )

    attn_low, attn_t, sums, bias_sum = small_parts

    def small_step(norms, bias_part, mask):
        half = bias_part.shape[0] // 2
        split = bias_part.reshape(half, 2, units)
        got = swap(jnp.concatenate([split[:, 1], norms]), mask, "tensor")
        return norms, got, split[:, 0]

    def small_sum(norms, got, bias_part):
        half = bias_part.shape[0]
        return norms + got[half:], bias_part + got[:half]

    chip_bits = bits_of(chips)
    high = chip_bits[-1]
    down_early, up_early = swap(down_early, 1), swap(up_early, 1)
    small = jnp.concatenate([bias_sum.reshape(t_count, units), sums])
    down_sent, up_sent, small, attn_low = tie(
        add(pick(down_mine, 1, 1), down_early).astype(LOW),
        add(pick(up_mine, 1, high), up_early).astype(LOW),
        small,
        attn_low,
    )
    down_got, up_got = swap(down_sent, 2), swap(up_sent, 2 * high)
    down_late, up_late, small, attn_t = tie(down_late, up_late, small, attn_t)
    norms, small_got, bias_part = small_step(small[t_count:], small[:t_count], 1)
    down_late, up_late = swap(down_late, 1), swap(up_late, 1)

    share = length // t_count
    proj_grad, *input_blocks = pl.pallas_call(
        attention_backward,
        out_shape=(shape((pad, 3 * width), LOW),)
        + (shape((mine, share, width), LOW),) * t_count,
        in_specs=[SMEM, VMEM, VMEM, ANY, ANY, ANY],
        out_specs=(ANY,) + (VMEM,) * t_count,
        scratch_shapes=[
            pltpu.VMEM((pad, width), LOW),
            pltpu.VMEM((pad, 3 * width), LOW),
            pltpu.VMEM(probs_shape, LOW),
            pltpu.VMEM((width, 3 * width), LOW),
            pltpu.VMEM((pad, 3 * width), LOW),
            pltpu.SemaphoreType.DMA((3,)),
            pltpu.SemaphoreType.DMA((1,)),
        ],
        compiler_params=params(),
        cost_estimate=cost(12 * rows * width * width, 30 * rows * width),
        name="attention_backward",
    )(table, attn_low, wo, proj, probs, qkv)

    down_got, up_got, down_late, up_late, small_got, proj_grad, *input_blocks = tie(
        down_got, up_got, down_late, up_late, small_got, proj_grad, *input_blocks
    )
    norms, bias_part = small_sum(norms, small_got, bias_part)
    down_terms = [pick(down_mine, 0, 1), down_late, down_got]
    up_terms = [pick(up_mine, 0, high), up_late, up_got]
    for low, top in zip(chip_bits[1:-1], chip_bits[1:-1][::-1]):
        down_terms = kept(down_terms, 1, swap(sent(down_terms, 1), 2 * low))
        up_terms = kept(up_terms, top, swap(sent(up_terms, top), 2 * top))
    down_sent, up_sent, norms, proj_grad, *input_blocks = tie(
        sent(down_terms, 1), sent(up_terms, 1), norms, proj_grad, *input_blocks
    )
    norms, small_got, bias_part = small_step(norms, bias_part, 2)
    down_got, up_got = swap(down_sent, 2 * high), swap(up_sent, 2)
    input_landed = [input_blocks[0]] + [None] * (t_count - 1)
    input_landed[1] = swap(input_blocks[1], 1, "tensor")

    attn_mine, attn_other = pl.pallas_call(
        attention_weights,
        out_shape=(shape((chips, t_count, slab, block), LOW),) * 2,
        in_specs=[SMEM] + [ANY] * 4,
        out_specs=(VMEM,) * 2,
        scratch_shapes=[
            pltpu.VMEM((dp_count, slab, rows), LOW),
            pltpu.VMEM((dp_count, slab, rows), LOW),
            pltpu.VMEM((pad, width), LOW),
            pltpu.VMEM((pad, 3 * width), LOW),
            pltpu.SemaphoreType.DMA((6,)),
        ],
        compiler_params=params(),
        cost_estimate=cost(8 * rows * width * width, 30 * rows * width),
        name="attention_weights",
    )(table, packed_t, attn_t, ctx, proj_grad)

    def finish(kernel, near, outs, flat):
        near = jnp.stack(near)
        far = swap(near, 1)
        return pl.pallas_call(
            kernel,
            out_shape=tuple(shape(dims, F32) for dims in outs),
            in_specs=[SMEM, ANY, ANY],
            out_specs=(VMEM,) * 2,
            scratch_shapes=[
                pltpu.VMEM((dp_count,) + near.shape[1:], LOW),
                pltpu.VMEM((width, flat), F32),
                pltpu.SemaphoreType.DMA((dp_count,)),
            ],
            compiler_params=params(),
            cost_estimate=cost(0, 8 * width * near.shape[2]),
            name=kernel.__name__,
        )(table, near, far)

    attn_other, small_got, down_got, up_got, input_landed[1] = tie(
        attn_other, small_got, down_got, up_got, input_landed[1]
    )
    norms, bias_part = small_sum(norms, small_got, bias_part)
    small = jnp.concatenate([bias_part, norms])
    attn_got = swap(attn_other, 1)
    attn_sent = [add(attn_mine[m], attn_got[m]).astype(LOW) for m in range(1, chips)]
    ffn_line = jnp.concatenate(
        [add(*kept(up_terms, 1, up_got))[0], add(*kept(down_terms, 1, down_got))[0]], axis=2
    )
    ffn_line = [ffn_line.astype(LOW)]
    ffn_sent, input_blocks[2], *attn_sent = tie(
        sent(ffn_line, 1), input_blocks[2], *attn_sent
    )
    attn_got = [attn_got[0]] + [swap(item, 2 * m) for m, item in zip(range(1, chips), attn_sent)]
    ffn_got = swap(ffn_sent, 1, "tensor")
    input_landed[2] = swap(input_blocks[2], 2, "tensor")

    ffn_line = kept(ffn_line, 1, ffn_got)
    ffn_got = swap(sent(ffn_line, 1), 2, "tensor")
    *attn_got, ffn_got, small, input_landed[2] = tie(*attn_got, ffn_got, small, input_landed[2])
    attn_line = [add(attn_mine[0], *attn_got).astype(LOW)]
    ffn_sum = add(*kept(ffn_line, 1, ffn_got))[0].astype(LOW)
    attn_sent, ffn_sum, small = tie(sent(attn_line, 1), ffn_sum, small)
    small_got = swap(small, 2)
    attn_got = swap(attn_sent, 1, "tensor")
    ffn_chips = gather_chips(ffn_sum)
    attn_line = kept(attn_line, 1, attn_got)
    attn_got = swap(sent(attn_line, 1), 2, "tensor")
    attn_got, small_got, input_blocks[3], *ffn_chips = tie(
        attn_got, small_got, input_blocks[3], *ffn_chips
    )
    small = small + small_got
    for mask in bits_of(dp_count)[3:]:
        small = small + swap(small, mask)
    attn_sum = add(*kept(attn_line, 1, attn_got))[0].astype(LOW)
    attn_sum, input_blocks[3], ffn_chips[0] = tie(attn_sum, input_blocks[3], ffn_chips[0])
    attn_chips = gather_chips(attn_sum)
    input_landed[3] = swap(input_blocks[3], 3, "tensor")
    up_grad, down_grad = finish(place_grads, ffn_chips, ((width, units), (units, width)), units)
    small_got = swap(small, 4)
    attn_chips[0], up_grad, input_landed[3], small_got = tie(
        attn_chips[0], up_grad, input_landed[3], small_got
    )
    small = small + small_got
    small_got = swap(small, 1)
    qkv_grad, out_grad = finish(
        place_attention_grads, attn_chips, ((3 * ctx_cols, width), (ctx_cols, width)), block
    )
    home = pl.pallas_call(
        send_home,
        out_shape=shape((share, sentences, width), LOW),
        in_specs=[VMEM] * (1 + t_count),
        out_specs=VMEM,
        compiler_params=params(),
        cost_estimate=cost(0, 4 * share * sentences * width),
        name="send_home",
    )(jnp.tile(source, STEP).reshape(-1, 1), *input_landed)
    small = small + small_got
    bias_sum, norms = small[0], small[1:]
    return (
        returned,
        paired,
        home,
        qkv_grad.T,
        out_grad,
        norms[2],
        norms[3],
        up_grad,
        bias_sum,
        down_grad,
        norms[0],
        norms[1],
    )


def solution(mesh):
    placed = (
        P(None, "dp", None),
        P("dp"),
        P("dp"),
        P(None, "tensor"),
        P("tensor", None),
        P(),
        P(),
        P(None, "tensor"),
        P("tensor"),
        P("tensor", None),
        P(),
        P(),
        P("dp", None),
        P("dp", None),
    )
    return jax.shard_map(
        shards,
        mesh=mesh,
        in_specs=placed,
        out_specs=(
            P("dp", None),
            P("dp", None),
            P("tensor", "dp", None),
            P(None, "tensor"),
            P("tensor", None),
            P(),
            P(),
            P(None, "tensor"),
            P("tensor"),
            P("tensor", None),
            P(),
            P(),
        ),
        check_vma=False,
    )
```
